32 devices in a mesh: dp: 8 (over z, y), fsdp: 4 (over x, core).
Axes of the slice: x: 2, y: 2, z: 4, core: 2. Of those that a mesh axis runs over, the one named last changes fastest.
Arguments:
- buf_states: float32 [2048, 11], P(('dp', 'fsdp')), may hold values from -6 to 6
- buf_actions: float32 [2048, 3], P(('dp', 'fsdp')), may hold values from -0.95 to 0.95
- buf_returns: float32 [2048], P(('dp', 'fsdp')), may hold values from -6 to 6
- window_starts: int32 [512], P(('dp', 'fsdp')), may hold values from 0 to 44, as said below
- window_repeats: int32 [512], P(('dp', 'fsdp')), may hold values from 1 to 5
- valid_steps: int32 [512, 20], P(('dp', 'fsdp')), may hold values from 0 to 1, as said below
- matrix_groups: int32 [3, 4], replicated, may hold values from 0 to 2
- log_temp: float32 [1], replicated, may hold values from -2 to 0
- small_rows: float32 [85, 512], replicated
- head_bias: float32 [6], replicated, may hold values from -1.5 to 1.5
- qkv_weight: float32 [3, 512, 1536], P(None, ('dp', 'fsdp')), may hold values from -0.25 to 0.25
- out_weight: float32 [3, 512, 512], P(None, ('dp', 'fsdp')), may hold values from -0.5 to 0.5
- up_weight: float32 [3, 512, 2048], P(None, ('dp', 'fsdp')), may hold values from -0.25 to 0.25
- down_weight: float32 [3, 2048, 512], P(None, ('dp', 'fsdp')), may hold values from -0.125 to 0.125
- small_first: float32 [85, 512], replicated, may hold values from -0.005859375 to 0.005859375
- bias_first: float32 [6], replicated, may hold values from -0.005859375 to 0.005859375
- qkv_first: float32 [3, 512, 1536], P(None, ('dp', 'fsdp')), may hold values from -0.001953125 to 0.001953125
- out_first: float32 [3, 512, 512], P(None, ('dp', 'fsdp')), may hold values from -0.001953125 to 0.001953125
- up_first: float32 [3, 512, 2048], P(None, ('dp', 'fsdp')), may hold values from -0.001953125 to 0.001953125
- down_first: float32 [3, 2048, 512], P(None, ('dp', 'fsdp')), may hold values from -0.001953125 to 0.001953125
- small_second: float32 [85, 512], replicated, may hold values from 4.1007996e-07 to 1.6424391e-06
- bias_second: float32 [6], replicated, may hold values from 4.1007996e-07 to 1.6424391e-06
- qkv_second: float32 [3, 512, 1536], P(None, ('dp', 'fsdp')), may hold values from 4.556444e-08 to 1.8225776e-07
- out_second: float32 [3, 512, 512], P(None, ('dp', 'fsdp')), may hold values from 4.556444e-08 to 1.8225776e-07
- up_second: float32 [3, 512, 2048], P(None, ('dp', 'fsdp')), may hold values from 4.556444e-08 to 1.8225776e-07
- down_second: float32 [3, 2048, 512], P(None, ('dp', 'fsdp')), may hold values from 4.556444e-08 to 1.8225776e-07
Outputs:
- totals: float32 [3], replicated
- grad_norm: float32 [1], replicated
- next_temp: float32 [1], replicated
- small_next: float32 [85, 512], replicated
- small_first_next: float32 [85, 512], replicated
- small_second_next: float32 [85, 512], replicated
- bias_next: float32 [6], replicated
- bias_first_next: float32 [6], replicated
- bias_second_next: float32 [6], replicated
- qkv_next: float32 [3, 512, 1536], P(None, ('dp', 'fsdp'))
- out_next: float32 [3, 512, 512], P(None, ('dp', 'fsdp'))
- up_next: float32 [3, 512, 2048], P(None, ('dp', 'fsdp'))
- down_next: float32 [3, 2048, 512], P(None, ('dp', 'fsdp'))
- qkv_copy: bfloat16 [3, 512, 1536], P(None, ('dp', 'fsdp'))
- out_copy: bfloat16 [3, 512, 512], P(None, ('dp', 'fsdp'))
- up_copy: bfloat16 [3, 512, 2048], P(None, ('dp', 'fsdp'))
- down_copy: bfloat16 [3, 2048, 512], P(None, ('dp', 'fsdp'))
- qkv_first_next: float32 [3, 512, 1536], P(None, ('dp', 'fsdp'))
- out_first_next: float32 [3, 512, 512], P(None, ('dp', 'fsdp'))
- up_first_next: float32 [3, 512, 2048], P(None, ('dp', 'fsdp'))
- down_first_next: float32 [3, 2048, 512], P(None, ('dp', 'fsdp'))
- qkv_second_next: float32 [3, 512, 1536], P(None, ('dp', 'fsdp'))
- out_second_next: float32 [3, 512, 512], P(None, ('dp', 'fsdp'))
- up_second_next: float32 [3, 512, 2048], P(None, ('dp', 'fsdp'))
- down_second_next: float32 [3, 2048, 512], P(None, ('dp', 'fsdp'))
The draws below stay inside these ranges and needn't reach their ends.
Inputs may be any that keep to these rules, and one draw needn't show every extreme that they name: Window w reads rows of the buffer block of the device that holds it: (w // 16) * 64 + window_starts[w] + t. `valid_steps`: in each window the ones follow the zeros and the last timestep is 1.
All inputs are finite; a program needn't handle non-finite values.
Results may differ from the reference program's by a relative error of at most 0.0034.
The reference program's roundings to bfloat16 on the way count: a program that leaves them out, or rounds other values in their place, can miss the bound.
Values may be sent and summed in bfloat16 or wider, within the bound.
A program may use at most 256 MiB of HBM per device.

```python
import math
import jax
import jax.numpy as jnp
import numpy as np
from jax import lax

D = 512
H = 8
HD = 64
FF = 2048
S = 11
A = 3
L = 3
K = 20
STEP = 10
WIN_DEV = 16
BUF_DEV = 64
WINDOWS = 512
BUF = 2048
NROWS = 85
N_FSDP = 4


def draw_window_starts(key, part):
    key = jax.random.fold_in(key, 11)
    picks = jax.random.randint(key, (WINDOWS,), 0, BUF_DEV - K + 1)
    heads = jnp.arange(WINDOWS) % WIN_DEV == 0
    return jnp.where(heads, BUF_DEV - K, picks).astype(jnp.int32)


def draw_window_repeats(key, part):
    key = jax.random.fold_in(key, 12)
    index = jnp.arange(WINDOWS)
    device = index // WIN_DEV
    outer = 2 * index // WINDOWS
    inner = 2 * (device % N_FSDP) // N_FSDP
    ceiling = 1 + 2 * (outer + inner)
    picks = jax.random.randint(key, (WINDOWS,), 0, ceiling)
    return jnp.where(index == WINDOWS - 1, 5, 1 + picks).astype(jnp.int32)


def draw_valid_steps(key, part):
    key = jax.random.fold_in(key, 13)
    padding = jax.random.randint(key, (WINDOWS, 1), 0, K)
    return (jnp.arange(K)[None, :] >= padding).astype(jnp.int32)


def row_tables():
    first = S + A + 1 + K + 3
    per_layer = 9 + FF // D
    scale = np.full((NROWS,), 0.1, np.float32)
    ramp_rows = np.zeros((NROWS,), bool)
    scale[:S] = 0.3
    scale[S:S + A] = 0.6
    scale[S + A] = 1.0
    scale[S + A + 1:first] = 0.3
    ramp_rows[first] = True
    scale[first + 2:first + 2 + A] = D ** (-0.5)
    scale[first + 2 + A:first + 2 + 2 * A] = 0.5 * D ** (-0.5)
    for layer in range(L):
        base = first + 2 + 2 * A + layer * per_layer
        ramp_rows[base] = True
        ramp_rows[base + 2] = True
    return (scale, ramp_rows)


def draw_small_rows(key, part):
    key = jax.random.fold_in(key, 14)
    noise_key, factor_key = jax.random.split(key)
    scale, ramp_rows = row_tables()
    noise = jax.random.normal(noise_key, (NROWS, D), jnp.float32)
    ramp = jnp.linspace(0.6, 1.8, D)
    factor = jax.random.uniform(factor_key, (NROWS, D), jnp.float32, 0.8, 1.25)
    return jnp.where(jnp.asarray(ramp_rows)[:, None], ramp[None, :] * factor, noise * jnp.asarray(scale)[:, None])


def with_ends(array, key, low, top_value):
    index_at = [jax.random.randint(jax.random.fold_in(key, axis), (), 0, length) for axis, length in enumerate(array.shape)]
    widest = array.shape.index(max(array.shape))
    beside = index_at[:widest] + [(index_at[widest] + 1) % array.shape[widest]] + index_at[widest + 1:]
    return array.at[tuple(index_at)].set(low).at[tuple(beside)].set(top_value)


def level_of(own_key, dims, cuts, smallest, high):
    level = 1.0
    for axis_at, parts in cuts:
        steps = jax.random.uniform(jax.random.fold_in(jax.random.fold_in(own_key, 6), axis_at), (parts,), jnp.float32, smallest / len(cuts), high / len(cuts))
        level = level * jnp.repeat(jnp.exp(steps), dims[axis_at] // parts).reshape((-1,) + (1,) * (len(dims) - 1 - axis_at))
    return level


def normal_values(rng, dims, scale, bound, pieces=(), held_as=jnp.bfloat16):
    result = jax.random.normal(rng, dims, jnp.float32) * scale
    if len(pieces) > 0:
        result = level_of(rng, dims, pieces, -0.22, 0.18) * result
    return jnp.clip(result, min=-bound, max=bound).astype(held_as)


def setup_inputs(seed: int = 0) -> dict:
    streams_of = jax.random.split(jax.random.key(seed), 27)
    buf_states = normal_values(streams_of[0], (BUF, S), 1.0, 6.0, ((0, 32),), jnp.float32)
    buf_actions = jnp.clip(jax.random.uniform(streams_of[1], (BUF, A), jnp.float32, -0.95, 0.95) * level_of(streams_of[1], (BUF, A), ((0, 32),), -0.4, 0.0), -0.95, 0.95)
    buf_returns = normal_values(streams_of[2], (BUF,), 1.0, 6.0, ((0, 32),), jnp.float32)
    window_starts = draw_window_starts(jax.random.fold_in(streams_of[26], 71), 0)
    window_repeats = draw_window_repeats(jax.random.fold_in(streams_of[26], 71), 0)
    valid_steps = draw_valid_steps(jax.random.fold_in(streams_of[26], 71), 0)
    matrix_groups = with_ends(jax.random.randint(streams_of[6], (L, 4), 0, 3), jax.random.fold_in(streams_of[6], 1), 0, 2).astype(jnp.int32)
    log_temp = jnp.clip(jax.random.uniform(streams_of[7], (1,), jnp.float32, -2.0, 0.0), -2.0, 0.0)
    small_rows = draw_small_rows(jax.random.fold_in(streams_of[26], 71), 0)
    head_bias = normal_values(streams_of[9], (2 * A,), 0.3, 1.5, (), jnp.float32)
    qkv_weight = normal_values(streams_of[10], (L, D, 3 * D), D ** -0.5, 0.25, ((1, 32),), jnp.float32)
    out_weight = normal_values(streams_of[11], (L, D, D), (D // 4) ** -0.5, 0.5, ((1, 32),), jnp.float32)
    up_weight = normal_values(streams_of[12], (L, D, FF), D ** -0.5, 0.25, ((1, 32),), jnp.float32)
    down_weight = normal_values(streams_of[13], (L, FF, D), FF ** -0.5, 0.125, ((1, 32),), jnp.float32)
    small_first = normal_values(streams_of[14], (NROWS, D), (3 * (L * (4 * D * D + 2 * D * FF)) ** -0.5), 0.005859375, (), jnp.float32)
    bias_first = normal_values(streams_of[15], (2 * A,), (3 * (L * (4 * D * D + 2 * D * FF)) ** -0.5), 0.005859375, (), jnp.float32)
    qkv_first = normal_values(streams_of[16], (L, D, 3 * D), ((L * (4 * D * D + 2 * D * FF)) ** -0.5), 0.001953125, ((1, 32),), jnp.float32)
    out_first = normal_values(streams_of[17], (L, D, D), ((L * (4 * D * D + 2 * D * FF)) ** -0.5), 0.001953125, ((1, 32),), jnp.float32)
    up_first = normal_values(streams_of[18], (L, D, FF), ((L * (4 * D * D + 2 * D * FF)) ** -0.5), 0.001953125, ((1, 32),), jnp.float32)
    down_first = normal_values(streams_of[19], (L, FF, D), ((L * (4 * D * D + 2 * D * FF)) ** -0.5), 0.001953125, ((1, 32),), jnp.float32)
    small_second = jnp.clip(jnp.exp(jax.random.uniform(streams_of[20], (NROWS, D), jnp.float32, math.log(4.1007996287589776e-07), math.log(1.6424390878455597e-06))), 4.1007996287589776e-07, 1.6424390878455597e-06)
    bias_second = jnp.clip(jnp.exp(jax.random.uniform(streams_of[21], (2 * A,), jnp.float32, math.log(4.1007996287589776e-07), math.log(1.6424390878455597e-06))), 4.1007996287589776e-07, 1.6424390878455597e-06)
    qkv_second = jnp.clip(jnp.exp(math.log(1.822577644361445e-07) - 1.3862944 * jax.random.uniform(streams_of[22], (L, D, 3 * D), jnp.float32) ** level_of(streams_of[22], (L, D, 3 * D), ((1, 32),), -0.2, 0.2)), 4.5564441109036125e-08, 1.822577644361445e-07)
    out_second = jnp.clip(jnp.exp(math.log(1.822577644361445e-07) - 1.3862944 * jax.random.uniform(streams_of[23], (L, D, D), jnp.float32) ** level_of(streams_of[23], (L, D, D), ((1, 32),), -0.2, 0.2)), 4.5564441109036125e-08, 1.822577644361445e-07)
    up_second = jnp.clip(jnp.exp(math.log(1.822577644361445e-07) - 1.3862944 * jax.random.uniform(streams_of[24], (L, D, FF), jnp.float32) ** level_of(streams_of[24], (L, D, FF), ((1, 32),), -0.2, 0.2)), 4.5564441109036125e-08, 1.822577644361445e-07)
    down_second = jnp.clip(jnp.exp(math.log(1.822577644361445e-07) - 1.3862944 * jax.random.uniform(streams_of[25], (L, FF, D), jnp.float32) ** level_of(streams_of[25], (L, FF, D), ((1, 32),), -0.2, 0.2)), 4.5564441109036125e-08, 1.822577644361445e-07)
    return dict(buf_states=buf_states, buf_actions=buf_actions, buf_returns=buf_returns, window_starts=window_starts, window_repeats=window_repeats, valid_steps=valid_steps, matrix_groups=matrix_groups, log_temp=log_temp, small_rows=small_rows, head_bias=head_bias, qkv_weight=qkv_weight, out_weight=out_weight, up_weight=up_weight, down_weight=down_weight, small_first=small_first, bias_first=bias_first, qkv_first=qkv_first, out_first=out_first, up_first=up_first, down_first=down_first, small_second=small_second, bias_second=bias_second, qkv_second=qkv_second, out_second=out_second, up_second=up_second, down_second=down_second)


@jax.custom_vjp
def low(v):
    return lax.optimization_barrier(v.astype(jnp.bfloat16)).astype(jnp.float32)

@jax.custom_vjp
def low_back(v):
    return v

def low_keep(v):
    return (low(v), None)

def low_pass(kept, grad):
    return (grad,)

def back_keep(v):
    return (v, None)

def back_low(kept, grad):
    return (low(grad),)
low.defvjp(low_keep, low_pass)
low_back.defvjp(back_keep, back_low)
EPS = 1e-05
CLIP = 1.0
LEARN = 0.03
BETA_ONE = 0.5
BETA_TWO = 0.7
DECAY = 0.01
ADAM_EPS = 1e-08
TEMP_RATE = 0.1
MASKED = -1e+30
HALF_LOG_TAU = 0.5 * math.log(2.0 * math.pi)
HIGH = lax.Precision.HIGHEST

def norm_rows(stream, gain, bias):
    center = stream - lax.optimization_barrier(jnp.mean(stream, -1, keepdims=True))
    return center * lax.rsqrt(lax.optimization_barrier(jnp.mean(center * center, -1, keepdims=True)) + EPS) * gain + bias

def embed_tokens(states, actions, returns, small_rows):
    in_w = small_rows[:S + A + 1]
    position = small_rows[S + A + 1:S + A + 1 + K]
    kinds = small_rows[S + A + 1 + K:S + A + 4 + K]
    ret_tok = returns[..., None] * in_w[S + A] + kinds[0] + position
    state_tok = jnp.einsum('wts,sd->wtd', states, in_w[:S], precision=HIGH) + kinds[1] + position
    action_tok = jnp.einsum('wta,ad->wtd', actions, in_w[S:S + A], precision=HIGH) + kinds[2] + position
    return jnp.stack([ret_tok, state_tok, action_tok], 2)

def action_terms(head, actions, weight, temp):
    center = head[:, :A]
    spread = jnp.tanh(head[:, A:])
    target = 0.5 * (jnp.log(1.0 + actions) - jnp.log(1.0 - actions))
    scaled = (target - center) * jnp.exp(-spread)
    nll = lax.optimization_barrier(jnp.sum(0.5 * scaled * scaled + spread + HALF_LOG_TAU + jnp.log(1.0 - actions * actions), -1))
    entropy = lax.optimization_barrier(jnp.sum(spread, -1)) + A * (0.5 + HALF_LOG_TAU)
    return (jnp.sum(weight * (nll - temp * entropy)), jnp.sum(weight * entropy))

def layer_forward(stream, w_qkv, w_out, w_up, w_down, layer_rows, allowed):
    count = stream.shape[0]
    up_rows = FF // D
    normed = low(norm_rows(stream, layer_rows[0], layer_rows[1]))
    qkv_rows = low(low_back(jnp.einsum('bnd,de->bne', normed, low(w_qkv), precision=HIGH) + layer_rows[4:7].reshape(-1)))
    query = qkv_rows[..., :D].reshape(count, 3 * K, H, HD)
    keyed = qkv_rows[..., D:2 * D].reshape(count, 3 * K, H, HD)
    values = qkv_rows[..., 2 * D:].reshape(count, 3 * K, H, HD)
    scores = low_back(jnp.einsum('bqhe,bkhe->bhqk', query, keyed, precision=HIGH) * HD ** (-0.5))
    scores = jnp.where(allowed[:, None], scores, MASKED)
    probs = low(jax.nn.softmax(scores, -1))
    mixed = low(low_back(jnp.einsum('bhqk,bkhe->bqhe', probs, values, precision=HIGH))).reshape(count, 3 * K, D)
    stream = stream + low_back(jnp.einsum('bnd,de->bne', mixed, low(w_out), precision=HIGH) + layer_rows[7])
    second = low(norm_rows(stream, layer_rows[2], layer_rows[3]))
    hidden = low_back(jnp.einsum('bnd,df->bnf', second, low(w_up), precision=HIGH) + layer_rows[8:8 + up_rows].reshape(-1))
    acted = low(jax.nn.gelu(hidden))
    return stream + low_back(jnp.einsum('bnf,fd->bnd', acted, low(w_down), precision=HIGH) + layer_rows[8 + up_rows])

def forward_loss(params, states, actions, returns, weight, valid, temp):
    qkv_weight, out_weight, up_weight, down_weight, small_rows, head_bias = params
    count = states.shape[0]
    first = S + A + 1 + K + 3
    per_layer = 9 + FF // D
    layer_base = first + 2 + 2 * A
    stream = embed_tokens(states, actions, returns, small_rows).reshape(count, 3 * K, D)
    place = jnp.arange(3 * K, dtype=jnp.int32)
    live = jnp.repeat(valid, 3, axis=1) > 0
    causal = place[None, :] <= place[:, None]
    diagonal = place[None, :] == place[:, None]
    allowed = causal[None] & (live[:, None, :] | diagonal[None])
    for layer in range(L):
        layer_rows = small_rows[layer_base + layer * per_layer:layer_base + (layer + 1) * per_layer]
        stream = layer_forward(stream, qkv_weight[layer], out_weight[layer], up_weight[layer], down_weight[layer], layer_rows, allowed)
    state_rows = stream.reshape(count, K, 3, D)[:, :, 1].reshape(-1, D)
    feats = low(norm_rows(state_rows, small_rows[first], small_rows[first + 1]))
    head = low_back(jnp.dot(feats, low(small_rows[first + 2:first + 2 + 2 * A]).T, precision=HIGH) + head_bias)
    return action_terms(head, actions.reshape(-1, A), weight.reshape(-1), temp)

def adam_step(weight, grad, first, second, rate):
    first = BETA_ONE * first + (1.0 - BETA_ONE) * grad
    second = BETA_TWO * second + (1.0 - BETA_TWO) * grad * grad
    fix_one = 1.0 - BETA_ONE ** STEP
    fix_two = 1.0 - BETA_TWO ** STEP
    fresh = weight - rate * (first / fix_one / (jnp.sqrt(second / fix_two) + ADAM_EPS) + DECAY * weight)
    return (fresh, first, second)

def reference(buf_states, buf_actions, buf_returns, window_starts, window_repeats, valid_steps, matrix_groups, log_temp, small_rows, head_bias, qkv_weight, out_weight, up_weight, down_weight, small_first, bias_first, qkv_first, out_first, up_first, down_first, small_second, bias_second, qkv_second, out_second, up_second, down_second):
    blocks = WINDOWS // WIN_DEV
    window = jnp.arange(WINDOWS, dtype=jnp.int32)
    place = (window // WIN_DEV * BUF_DEV + window_starts.astype(jnp.int32))[:, None] + jnp.arange(K, dtype=jnp.int32)[None, :]
    states = buf_states[place].reshape(blocks, WIN_DEV, K, S)
    actions = buf_actions[place].reshape(blocks, WIN_DEV, K, A)
    returns = buf_returns[place].reshape(blocks, WIN_DEV, K)
    weight = (window_repeats.astype(jnp.float32)[:, None] * valid_steps.astype(jnp.float32)).reshape(blocks, WIN_DEV, K)
    valid = valid_steps.reshape(blocks, WIN_DEV, K)
    temp = jnp.exp(log_temp[0])
    params = (qkv_weight, out_weight, up_weight, down_weight, small_rows, head_bias)

    def step(carry, block):
        sums, totals = carry
        st, ac, rt, wt, vl = block
        loss, back, entropy = jax.vjp(lambda p: forward_loss(p, st, ac, rt, wt, vl, temp), params, has_aux=True)
        grads = back(jnp.ones_like(loss))[0]
        sums = jax.tree.map(lambda a, b: a + b, sums, grads)
        return ((sums, totals + jnp.stack([loss, entropy, jnp.sum(wt)])), None)
    zeros = jax.tree.map(jnp.zeros_like, params)
    (grads, totals), _ = lax.scan(step, (zeros, jnp.zeros((3,), jnp.float32)), (states, actions, returns, weight, valid))
    square = sum((jnp.sum(g * g) for g in grads))
    grad_norm = jnp.sqrt(square)
    clip = jnp.minimum(1.0, CLIP / (grad_norm + 1e-06))
    rates = LEARN * jnp.exp2(-matrix_groups.astype(jnp.float32))
    mats = (qkv_weight, out_weight, up_weight, down_weight)
    firsts = (qkv_first, out_first, up_first, down_first)
    seconds = (qkv_second, out_second, up_second, down_second)
    results = [adam_step(mats[kind], clip * grads[kind], firsts[kind], seconds[kind], rates[:, kind][:, None, None]) for kind in range(4)]
    small_new = adam_step(small_rows, clip * grads[4], small_first, small_second, LEARN)
    bias_new = adam_step(head_bias, clip * grads[5], bias_first, bias_second, LEARN)
    next_temp = log_temp - TEMP_RATE * temp * (totals[1] / totals[2] + A)
    return (totals, grad_norm[None], next_temp, small_new[0], small_new[1], small_new[2], bias_new[0], bias_new[1], bias_new[2], results[0][0], results[1][0], results[2][0], results[3][0], results[0][0].astype(jnp.bfloat16), results[1][0].astype(jnp.bfloat16), results[2][0].astype(jnp.bfloat16), results[3][0].astype(jnp.bfloat16), results[0][1], results[1][1], results[2][1], results[3][1], results[0][2], results[1][2], results[2][2], results[3][2])
```

```python
import functools
import math

import jax
import jax.numpy as jnp
from jax import lax
from jax.experimental import pallas as pl
from jax.experimental.pallas import tpu as pltpu
from jax.sharding import PartitionSpec as P

D = 512
H = 8
HD = 64
FF = 2048
S = 11
A = 3
K = 20
STEP = 10

EPS = 1e-05
CLIP = 1.0
LEARN = 0.03
BETA_ONE = 0.5
BETA_TWO = 0.7
DECAY = 0.01
ADAM_EPS = 1e-08
TEMP_RATE = 0.1
MASKED = -1e30
HALF_LOG_TAU = 0.5 * math.log(2.0 * math.pi)
GELU_C = math.sqrt(2.0 / math.pi)
GELU_A = 0.044715
HIGH = lax.Precision.HIGHEST
LOWER = jnp.bfloat16
WIDE = jnp.float32

LAYERS = 3
WINS = 16
SLOT = 64
ROWS = WINS * SLOT
CHUNK = 256
CHUNKS = ROWS // CHUNK
GROUP = 128
BLOCKS = 32
PACK = 192
EMB = S + A + 1 + K + 3
FIN = EMB
HEADW = EMB + 2
BASE = EMB + 2 + 2 * A
PER = 9 + FF // D
NROWS = BASE + LAYERS * PER
SMALL = 88


def dot(a, b, precision=None):
    return lax.dot_general(
        a, b, (((1,), (0,)), ((), ())), precision=precision, preferred_element_type=WIDE
    )


def dot_nt(a, b, precision=None):
    return lax.dot_general(
        a, b, (((1,), (1,)), ((), ())), precision=precision, preferred_element_type=WIDE
    )


def dot_tn(a, b, precision=None):
    return lax.dot_general(
        a, b, (((0,), (0,)), ((), ())), precision=precision, preferred_element_type=WIDE
    )


def iota(shape, dim):
    return lax.broadcasted_iota(jnp.int32, shape, dim)


def col_sum(v):
    return jnp.sum(v, 0, keepdims=True)


def row_mean(v):
    return jnp.mean(v, -1, keepdims=True)


def norm_parts(x):
    center = x - row_mean(x)
    scale = lax.rsqrt(row_mean(center * center) + EPS)
    return center * scale, scale


def norm_back(xhat, scale, gain, grad):
    scaled = grad * gain
    return scale * (scaled - row_mean(scaled) - xhat * row_mean(scaled * xhat))


def token_rows(at, count):
    row = at + iota((count, 128), 0)
    place = row & (SLOT - 1)
    step = (place * 21846) >> 16
    return row >> 6, step, place - 3 * step, place < 3 * K


def chunk_rows(c):
    return pl.ds(pl.multiple_of(c * CHUNK, CHUNK), CHUNK)


class Kit:
    def __init__(self, **refs):
        self.__dict__.update(refs)

    def row(self, l, k):
        return self.lrows[l, k : k + 1, :]

    def w(self, l, first, count=16):
        return self.wg[l, :, first : first + count, :].reshape(BLOCKS * count, D)

    def w_qkv(self, l, j):
        return self.w(l, 16 * j)

    def w_out(self, l):
        return self.w(l, 48)

    def w_up(self, l, j):
        return self.w(l, 64 + 16 * j)

    def w_down(self, l, j):
        return self.wg[l, pl.ds(8 * j, 8), 128:192, :].reshape(D, D)


def setup_stage(k):
    k.emb[...] = jnp.zeros_like(k.emb)
    k.emb[0:EMB, :] = k.small[0:EMB, :]
    k.headw[...] = jnp.zeros_like(k.headw)
    k.headw[0, 0:A, :] = k.small[HEADW : HEADW + A, :].astype(LOWER)
    k.headw[1, 0:A, :] = k.small[HEADW + A : HEADW + 2 * A, :].astype(LOWER)
    for l in range(LAYERS):
        k.lrows[l, 0:PER, :] = k.small[BASE + l * PER : BASE + (l + 1) * PER, :]
    k.sgl[...] = jnp.zeros_like(k.sgl)
    k.sgh[...] = jnp.zeros_like(k.sgh)
    k.sgw[...] = jnp.zeros_like(k.sgw)

    meta = k.meta[...].astype(LOWER)
    lane = iota((128, 128), 1)
    sub = iota((128, 128), 0)
    half = lane & (SLOT - 1)
    pick = sub - 2 == ((half * 21846) >> 16)
    pick_lo = (pick & (lane < SLOT)).astype(WIDE).astype(LOWER)
    pick_hi = (pick & (lane >= SLOT)).astype(WIDE).astype(LOWER)
    low = dot(meta, pick_lo).astype(LOWER)
    high = dot(meta, pick_hi).astype(LOWER)
    even = (lane == 2 * sub).astype(WIDE).astype(LOWER)
    odd = (lane == 2 * sub + 1).astype(WIDE).astype(LOWER)
    k.live[...] = (dot(even, low) + dot(odd, high))[0:8]
    same = (sub >> 6) == (lane >> 6)
    for g in range(ROWS // GROUP):
        live = k.live[g : g + 1, :] > 0.5
        allowed = same & (lane <= sub) & (live | (lane == sub))
        k.bias[g] = jnp.where(allowed, 0.0, MASKED)

    def chunk(c, carry):
        rows = chunk_rows(c)
        win, step, kind, real = token_rows(c * CHUNK, CHUNK)
        lane = iota((CHUNK, 128), 1)
        tok = dot((lane == win).astype(WIDE).astype(LOWER), meta)
        start, repeat = tok[:, 0:1], tok[:, 1:2]
        valid = jnp.sum(jnp.where(lane == step + 2, tok, 0.0), -1, keepdims=True)
        place = start.astype(jnp.int32) + step
        source = ((lane == place) & real).astype(WIDE)
        raw = dot(source, k.buf[...], HIGH)
        mine = (
            ((lane < S) & (kind == 1))
            | ((lane >= S) & (lane < S + A) & (kind == 2))
            | ((lane == S + A) & (kind == 0))
        )
        marks = ((lane == S + A + 1 + step) | (lane == S + A + 1 + K + kind)) & real
        feats = jnp.where(mine, raw, 0.0) + marks.astype(WIDE)
        k.feats[rows, :] = feats
        weight = jnp.where((kind == 1) & real, repeat * valid, 0.0)
        acts = pltpu.roll(raw, 128 - S, 1)
        k.acts[rows, :] = jnp.where(lane < A, acts, jnp.where(lane == A, weight, 0.0))
        k.xs[0, rows, :] = dot(feats, k.emb[...], HIGH)
        return carry

    lax.fori_loop(0, CHUNKS, chunk, 0)


def pair_masks(rows):
    lane = iota((rows, 128), 1)
    return lane < HD


def stack_pair(v, first):
    zero = jnp.zeros_like(v)
    return jnp.concatenate([jnp.where(first, v, zero), jnp.where(first, zero, v)], 0)


def forward_attn(k, l):
    def chunk(c, carry):
        rows = chunk_rows(c)
        xhat, _ = norm_parts(k.xs[l, rows, :])
        normed = (xhat * k.row(l, 0) + k.row(l, 1)).astype(LOWER)
        for j in range(3):
            part = dot(normed, k.w_qkv(l, j)) + k.row(l, 4 + j)
            k.qkv[l, rows, j * D : (j + 1) * D] = part.astype(LOWER)
        return carry

    lax.fori_loop(0, CHUNKS, chunk, 0)
    first = pair_masks(GROUP)

    def group(g, carry):
        rows = pl.ds(pl.multiple_of(g * GROUP, GROUP), GROUP)
        bias = k.bias[g]
        bias = jnp.concatenate([bias, bias], 0)
        lane = iota((GROUP, 128), 1)
        logs = jnp.zeros((GROUP, 128), WIDE)
        for p in range(H // 2):
            at = p * 128
            query = k.qkv[l, rows, at : at + 128] * jnp.asarray(HD**-0.5, LOWER)
            keyed = k.qkv[l, rows, D + at : D + at + 128]
            values = k.qkv[l, rows, 2 * D + at : 2 * D + at + 128]
            scores = dot_nt(stack_pair(query, first), keyed) + bias
            peak = jnp.max(scores, -1, keepdims=True)
            expo = jnp.exp(scores - peak)
            total = jnp.sum(expo, -1, keepdims=True)
            probs = (expo / total).astype(LOWER)
            out = dot(probs, values)
            k.mixed[l, rows, at : at + 128] = jnp.where(first, out[:GROUP], out[GROUP:]).astype(LOWER)
            lse = peak + jnp.log(total)
            logs = jnp.where(lane == 2 * p, lse[:GROUP], logs)
            logs = jnp.where(lane == 2 * p + 1, lse[GROUP:], logs)
        k.logs[l, rows, :] = logs
        return carry

    lax.fori_loop(0, ROWS // GROUP, group, 0)


def gelu_parts(h):
    square = h * h
    t = jnp.tanh(GELU_C * (h + GELU_A * h * square))
    return t, square


def forward_ffn(k, l, dest):
    def chunk(c, carry):
        rows = chunk_rows(c)
        mid = k.xs[l, rows, :] + dot(k.mixed[l, rows, :], k.w_out(l)) + k.row(l, 7)
        k.mid[l, rows, :] = mid
        xhat, _ = norm_parts(mid)
        second = (xhat * k.row(l, 2) + k.row(l, 3)).astype(LOWER)
        out = mid + k.row(l, 12)
        for j in range(4):
            h = dot(second, k.w_up(l, j)) + k.row(l, 8 + j)
            t, _ = gelu_parts(h)
            acted = (0.5 * h * (1.0 + t)).astype(LOWER)
            out = out + dot(acted, k.w_down(l, j))
        k.xs[dest, rows, :] = out
        return carry

    lax.fori_loop(0, CHUNKS, chunk, 0)


def head_stage(k, at):
    gain, bias = k.small[FIN : FIN + 1, :], k.small[FIN + 1 : FIN + 2, :]
    lane = iota((CHUNK, 128), 1)
    keep = lane < A

    def bias_row(first):
        row = jnp.zeros((1, 128), WIDE)
        at = iota((1, 128), 1)
        for a in range(A):
            row = jnp.where(at == a, k.head_bias[first + a], row)
        return row

    bias_mean, bias_spread = bias_row(0), bias_row(A)
    temp = jnp.exp(jnp.full((1, 128), k.log_temp[0], WIDE))

    def chunk(c, carry):
        rows = chunk_rows(c)
        xhat, scale = norm_parts(k.xs[at, rows, :])
        feats = (xhat * gain + bias).astype(LOWER)
        mean = dot_nt(feats, k.headw[0]) + bias_mean
        spread = jnp.tanh(dot_nt(feats, k.headw[1]) + bias_spread)
        acts = k.acts[rows, :]
        weight = acts[:, A : A + 1]
        acts = jnp.where(keep, acts, 0.0)
        target = 0.5 * (jnp.log(1.0 + acts) - jnp.log(1.0 - acts))
        shrink = jnp.exp(-spread)
        zed = (target - mean) * shrink
        terms = 0.5 * zed * zed + spread + HALF_LOG_TAU + jnp.log(1.0 - acts * acts)
        nll = jnp.sum(jnp.where(keep, terms, 0.0), -1, keepdims=True)
        entropy = jnp.sum(jnp.where(keep, spread, 0.0), -1, keepdims=True) + A * (0.5 + HALF_LOG_TAU)
        loss = weight * (nll - temp * entropy)
        sums = jnp.where(lane == 0, loss, jnp.where(lane == 1, weight * entropy, jnp.where(lane == 2, weight, 0.0)))
        d_mean = jnp.where(keep, weight * (-zed * shrink), 0.0).astype(LOWER)
        d_spread = weight * (1.0 - zed * zed - temp) * (1.0 - spread * spread)
        d_spread = jnp.where(keep, d_spread, 0.0).astype(LOWER)
        k.sgh[2:3, 0:128] += col_sum(sums)
        k.sgh[3:4, 0:128] += col_sum(d_mean.astype(WIDE))
        k.sgh[4:5, 0:128] += col_sum(d_spread.astype(WIDE))
        k.sgw[0] += dot_tn(d_mean, feats)[0:8]
        k.sgw[1] += dot_tn(d_spread, feats)[0:8]
        d_feats = dot(d_mean, k.headw[0]) + dot(d_spread, k.headw[1])
        k.sgh[0:1, :] += col_sum(d_feats * xhat)
        k.sgh[1:2, :] += col_sum(d_feats)
        k.xs[at, rows, :] = norm_back(xhat, scale, gain, d_feats)
        return carry

    lax.fori_loop(0, CHUNKS, chunk, 0)


def owner_place(i):
    z, y, x, c = i // 8, (i // 4) % 2, (i // 2) % 2, i % 2
    return c * 16 + x * 8 + y * 4 + z


def store_blocks(k, slot, first_block, first_row, count, value):
    value = value.astype(LOWER)
    for n in range(value.shape[0] // count):
        k.wg[slot, owner_place(first_block + n), first_row : first_row + count, :] = value[
            n * count : (n + 1) * count
        ]


def backward_ffn(k, l, grad):
    def before(c, carry):
        rows = chunk_rows(c)
        d_down = k.xs[grad, rows, :].astype(LOWER)
        k.work[rows, 2 * D : 3 * D] = d_down
        k.sgl[l, 12:13, :] += col_sum(d_down.astype(WIDE))
        xhat, _ = norm_parts(k.mid[l, rows, :])
        k.left[rows, :] = (xhat * k.row(l, 2) + k.row(l, 3)).astype(LOWER)
        k.dsec[rows, :] = jnp.zeros((CHUNK, D), WIDE)
        return carry

    lax.fori_loop(0, CHUNKS, before, 0)
    for j in range(4):

        def chunk(c, carry, j=j):
            rows = chunk_rows(c)
            h = dot(k.left[rows, :], k.w_up(l, j)) + k.row(l, 8 + j)
            t, square = gelu_parts(h)
            k.work[rows, 0:D] = (0.5 * h * (1.0 + t)).astype(LOWER)
            slope = 0.5 * (1.0 + t) + 0.5 * GELU_C * h * (1.0 - t * t) * (1.0 + 3.0 * GELU_A * square)
            d_acted = dot_nt(k.work[rows, 2 * D : 3 * D], k.w_down(l, j))
            d_hidden = (d_acted * slope).astype(LOWER)
            k.work[rows, D : 2 * D] = d_hidden
            k.sgl[l, 8 + j : 9 + j, :] += col_sum(d_hidden.astype(WIDE))
            k.dsec[rows, :] += dot_nt(d_hidden, k.w_up(l, j))
            return carry

        lax.fori_loop(0, CHUNKS, chunk, 0)
        store_blocks(k, l + 1, 0, 64 + 16 * j, 16, dot_tn(k.left[...], k.work[:, D : 2 * D]))
        store_blocks(k, l + 1, 8 * j, 128, 64, dot_tn(k.work[:, 0:D], k.work[:, 2 * D : 3 * D]))

    def after(c, carry):
        rows = chunk_rows(c)
        xhat, scale = norm_parts(k.mid[l, rows, :])
        d_second = k.dsec[rows, :]
        k.sgl[l, 2:3, :] += col_sum(d_second * xhat)
        k.sgl[l, 3:4, :] += col_sum(d_second)
        k.xs[grad, rows, :] += norm_back(xhat, scale, k.row(l, 2), d_second)
        return carry

    lax.fori_loop(0, CHUNKS, after, 0)


def backward_attn(k, l, grad):
    def before(c, carry):
        rows = chunk_rows(c)
        d_branch = k.xs[grad, rows, :].astype(LOWER)
        k.left[rows, :] = d_branch
        k.sgl[l, 7:8, :] += col_sum(d_branch.astype(WIDE))
        k.dmix[rows, :] = dot_nt(d_branch, k.w_out(l)).astype(LOWER)
        return carry

    lax.fori_loop(0, CHUNKS, before, 0)
    store_blocks(k, l + 1, 0, 48, 16, dot_tn(k.mixed[l], k.left[...]))
    first = pair_masks(GROUP)
    scale = HD**-0.5

    def group(g, carry):
        rows = pl.ds(pl.multiple_of(g * GROUP, GROUP), GROUP)
        bias = k.bias[g]
        bias = jnp.concatenate([bias, bias], 0)
        logs = k.logs[l, rows, :]
        for p in range(H // 2):
            at = p * 128
            query = stack_pair(k.qkv[l, rows, at : at + 128] * jnp.asarray(scale, LOWER), first)
            keyed = k.qkv[l, rows, D + at : D + at + 128]
            values = k.qkv[l, rows, 2 * D + at : 2 * D + at + 128]
            d_mixed = stack_pair(k.dmix[rows, at : at + 128], first)
            log_total = jnp.concatenate(
                [logs[:, 2 * p : 2 * p + 1], logs[:, 2 * p + 1 : 2 * p + 2]], 0
            )
            probs = jnp.exp(dot_nt(query, keyed) + bias - log_total)
            d_probs = dot_nt(d_mixed, values)
            d_values = dot_tn(probs.astype(LOWER), d_mixed)
            inner = probs * d_probs
            d_scores = (inner - probs * jnp.sum(inner, -1, keepdims=True)).astype(LOWER)
            d_query = dot(d_scores, keyed)
            d_query = jnp.where(first, d_query[:GROUP], d_query[GROUP:]) * scale
            d_keyed = dot_tn(d_scores, query)
            k.work[rows, at : at + 128] = d_query.astype(LOWER)
            k.work[rows, D + at : D + at + 128] = d_keyed.astype(LOWER)
            k.work[rows, 2 * D + at : 2 * D + at + 128] = d_values.astype(LOWER)
        return carry

    lax.fori_loop(0, ROWS // GROUP, group, 0)

    def again(c, carry):
        rows = chunk_rows(c)
        xhat, _ = norm_parts(k.xs[l, rows, :])
        k.left[rows, :] = (xhat * k.row(l, 0) + k.row(l, 1)).astype(LOWER)
        return carry

    lax.fori_loop(0, CHUNKS, again, 0)
    for j in range(3):
        store_blocks(k, l + 1, 0, 16 * j, 16, dot_tn(k.left[...], k.work[:, j * D : (j + 1) * D]))


def backward_input(k, l, grad):
    def chunk(c, carry):
        rows = chunk_rows(c)
        d_normed = jnp.zeros((CHUNK, D), WIDE)
        for j in range(3):
            d_part = k.work[rows, j * D : (j + 1) * D]
            k.sgl[l, 4 + j : 5 + j, :] += col_sum(d_part.astype(WIDE))
            d_normed = d_normed + dot_nt(d_part, k.w_qkv(l, j))
        xhat, scale = norm_parts(k.xs[l, rows, :])
        k.sgl[l, 0:1, :] += col_sum(d_normed * xhat)
        k.sgl[l, 1:2, :] += col_sum(d_normed)
        k.xs[grad, rows, :] += norm_back(xhat, scale, k.row(l, 0), d_normed)
        return carry

    lax.fori_loop(0, CHUNKS, chunk, 0)


def small_stage(k, out, grad):
    out[...] = jnp.zeros_like(out)
    out[0:EMB, :] = dot_tn(k.feats[...], k.xs[grad], HIGH)[0:EMB]
    out[FIN : FIN + 2, :] = k.sgh[0:2, :]
    out[HEADW : HEADW + A, :] = k.sgw[0, 0:A, :]
    out[HEADW + A : HEADW + 2 * A, :] = k.sgw[1, 0:A, :]
    for l in range(LAYERS):
        out[BASE + l * PER : BASE + (l + 1) * PER, :] = k.sgl[l, 0:PER, :]
    out[NROWS : NROWS + 3, :] = k.sgh[2:5, :]


WORK_SHAPES = dict(
    wg=((LAYERS + 1, BLOCKS, PACK, D), LOWER),
    xs=((LAYERS + 1, ROWS, D), WIDE),
    mid=((LAYERS, ROWS, D), WIDE),
    qkv=((LAYERS, ROWS, 3 * D), LOWER),
    mixed=((LAYERS, ROWS, D), LOWER),
    logs=((LAYERS, ROWS, 128), WIDE),
    work=((ROWS, 3 * D), LOWER),
    left=((ROWS, D), LOWER),
    dmix=((ROWS, D), LOWER),
    dsec=((ROWS, D), WIDE),
    feats=((ROWS, 128), WIDE),
    acts=((ROWS, 128), WIDE),
    bias=((ROWS // GROUP, GROUP, GROUP), WIDE),
    live=((8, 128), WIDE),
    emb=((128, D), WIDE),
    headw=((2, 128, D), LOWER),
    lrows=((LAYERS, 16, D), WIDE),
    sgl=((LAYERS, 16, D), WIDE),
    sgh=((8, D), WIDE),
    sgw=((2, 8, D), WIDE),
)


def compute_kernel(meta, buf, small, head_bias, log_temp, packed, grads, small_grad, *scratch):
    refs = dict(zip(WORK_SHAPES, scratch))
    load_sem, store_sem = scratch[len(WORK_SHAPES) :]
    k = Kit(meta=meta, buf=buf, small=small, head_bias=head_bias, log_temp=log_temp, **refs)
    loads = [
        pltpu.make_async_copy(packed.at[l], k.wg.at[l], load_sem.at[l]) for l in range(LAYERS)
    ]
    stores = [
        pltpu.make_async_copy(k.wg.at[l + 1], grads.at[l], store_sem.at[l]) for l in range(LAYERS)
    ]
    for copy in loads:
        copy.start()
    setup_stage(k)

    def forward(l, carry):
        pltpu.make_async_copy(packed.at[l], k.wg.at[l], load_sem.at[l]).wait()
        forward_attn(k, l)
        forward_ffn(k, l, l + 1)
        return carry

    lax.fori_loop(0, LAYERS, forward, 0)
    head_stage(k, LAYERS)

    def backward(n, carry):
        l = LAYERS - 1 - n
        backward_ffn(k, l, LAYERS)
        backward_attn(k, l, LAYERS)
        pltpu.make_async_copy(k.wg.at[l + 1], grads.at[l], store_sem.at[l]).start()
        backward_input(k, l, LAYERS)
        return carry

    lax.fori_loop(0, LAYERS, backward, 0)
    small_stage(k, small_grad, LAYERS)
    for copy in stores:
        copy.wait()


def vmem(shape, dtype):
    return pltpu.VMEM(shape, dtype)


def compute(meta, buf, small, head_bias, log_temp, packed):
    whole = pl.BlockSpec(memory_space=pltpu.VMEM)
    scalars = pl.BlockSpec(memory_space=pltpu.SMEM)
    anywhere = pl.BlockSpec(memory_space=pl.ANY)
    return pl.pallas_call(
        compute_kernel,
        name="train_pass",
        out_shape=(
            jax.ShapeDtypeStruct((LAYERS, BLOCKS, PACK, D), LOWER),
            jax.ShapeDtypeStruct((SMALL, D), WIDE),
        ),
        in_specs=[whole, whole, whole, scalars, scalars, anywhere],
        out_specs=(anywhere, whole),
        scratch_shapes=[vmem(*s) for s in WORK_SHAPES.values()]
        + [pltpu.SemaphoreType.DMA((LAYERS,)), pltpu.SemaphoreType.DMA((LAYERS,))],
        compiler_params=pltpu.CompilerParams(vmem_limit_bytes=66 * 1024 * 1024),
        cost_estimate=pl.CostEstimate(flops=6 * 10**10, bytes_accessed=4 * 10**7, transcendentals=10**7),
    )(meta, buf, small, head_bias, log_temp, packed)


def small_inputs(buf_states, buf_actions, buf_returns, window_starts, window_repeats, valid_steps):
    meta = jnp.concatenate(
        [window_starts[:, None], window_repeats[:, None], valid_steps], 1
    ).astype(WIDE)
    meta = jnp.pad(meta, ((0, 128 - meta.shape[0]), (0, 128 - meta.shape[1])))
    buf = jnp.concatenate([buf_states, buf_actions, buf_returns[:, None]], 1)
    buf = jnp.pad(buf, ((0, 128 - buf.shape[0]), (0, 128 - buf.shape[1])))
    return meta, buf


def adam_step(weight, grad, first, second, rate):
    first = BETA_ONE * first + (1.0 - BETA_ONE) * grad
    second = BETA_TWO * second + (1.0 - BETA_TWO) * grad * grad
    fix_one = 1.0 - BETA_ONE**STEP
    fix_two = 1.0 - BETA_TWO**STEP
    fresh = weight - rate * (
        first / fix_one / (jnp.sqrt(second / fix_two) + ADAM_EPS) + DECAY * weight
    )
    return (fresh, first, second)


def gather_packed(mats, axes, count):
    group = count // BLOCKS
    pieces = []
    for mat in mats:
        rows, wide = mat.shape[1], mat.shape[2] // D
        piece = mat.astype(LOWER).reshape(LAYERS, rows, wide, D)
        piece = lax.all_gather(piece, axes, axis=1, tiled=True)
        piece = piece.reshape(LAYERS, BLOCKS, group * rows, wide, D).transpose(0, 1, 3, 2, 4)
        pieces.append(piece.reshape(LAYERS, BLOCKS, wide * group * rows, D))
    return jnp.concatenate(pieces, 2)


def scatter_packed(grads, mats, axes):
    order = [owner_place(i) for i in range(BLOCKS)]
    grads = grads[:, jnp.array(order)].astype(WIDE)
    results, first = [], 0
    for mat in mats:
        rows, wide = mat.shape[1], mat.shape[2] // D
        total = lax.psum(1, axes) * rows
        deep = total // BLOCKS
        piece = grads[:, :, first : first + wide * deep]
        first += wide * deep
        piece = piece.reshape(LAYERS, BLOCKS, wide, deep, D).transpose(0, 1, 3, 2, 4)
        piece = piece.reshape(LAYERS, total, wide * D)
        results.append(lax.psum_scatter(piece, axes, scatter_dimension=1, tiled=True))
    return results


def local(
    buf_states,
    buf_actions,
    buf_returns,
    window_starts,
    window_repeats,
    valid_steps,
    matrix_groups,
    log_temp,
    small_rows,
    head_bias,
    qkv_weight,
    out_weight,
    up_weight,
    down_weight,
    small_first,
    bias_first,
    qkv_first,
    out_first,
    up_first,
    down_first,
    small_second,
    bias_second,
    qkv_second,
    out_second,
    up_second,
    down_second,
):
    axes = ("dp", "fsdp")
    mats = (qkv_weight, out_weight, up_weight, down_weight)
    firsts = (qkv_first, out_first, up_first, down_first)
    seconds = (qkv_second, out_second, up_second, down_second)
    meta, buf = small_inputs(
        buf_states, buf_actions, buf_returns, window_starts, window_repeats, valid_steps
    )
    packed = gather_packed(mats, axes, FF // down_weight.shape[1])
    grads, small = compute(meta, buf, small_rows, head_bias, log_temp, packed)
    big = scatter_packed(grads, mats, axes)
    small = lax.psum(small, axes)
    small_grad, totals = small[:NROWS], small[NROWS, :3]
    bias_grad = jnp.concatenate([small[NROWS + 1, :A], small[NROWS + 2, :A]])
    square = sum((jnp.sum(piece * piece) for piece in big))
    square = (
        lax.psum(square, axes) + jnp.sum(small_grad * small_grad) + jnp.sum(bias_grad * bias_grad)
    )
    grad_norm = jnp.sqrt(square)
    clip = jnp.minimum(1.0, CLIP / (grad_norm + 1e-06))
    rates = LEARN * jnp.exp2(-matrix_groups.astype(WIDE))
    results = [
        adam_step(
            mats[kind], clip * big[kind], firsts[kind], seconds[kind], rates[:, kind][:, None, None]
        )
        for kind in range(4)
    ]
    small_new = adam_step(small_rows, clip * small_grad, small_first, small_second, LEARN)
    bias_new = adam_step(head_bias, clip * bias_grad, bias_first, bias_second, LEARN)
    next_temp = log_temp - TEMP_RATE * jnp.exp(log_temp) * (totals[1] / totals[2] + A)
    return (
        (totals, grad_norm[None], next_temp)
        + small_new
        + bias_new
        + tuple(r[0] for r in results)
        + tuple(r[0].astype(LOWER) for r in results)
        + tuple(r[1] for r in results)
        + tuple(r[2] for r in results)
    )


def solution(mesh):
    rows = P(("dp", "fsdp"), None)
    vector = P(("dp", "fsdp"))
    stack = P(None, ("dp", "fsdp"), None)
    same = P()
    in_specs = (
        (rows, rows, vector, vector, vector, rows)
        + (same,) * 4
        + (stack,) * 4
        + (same,) * 2
        + (stack,) * 4
        + (same,) * 2
        + (stack,) * 4
    )
    out_specs = (same,) * 9 + (stack,) * 16
    return jax.shard_map(local, mesh=mesh, in_specs=in_specs, out_specs=out_specs, check_vma=False)
```

```python
import functools
import math

import jax
import jax.numpy as jnp
from jax import lax
from jax.experimental import pallas as pl
from jax.experimental.pallas import tpu as pltpu
from jax.sharding import PartitionSpec as P

D = 512
H = 8
HD = 64
FF = 2048
S = 11
A = 3
K = 20
STEP = 10

EPS = 1e-05
CLIP = 1.0
LEARN = 0.03
BETA_ONE = 0.5
BETA_TWO = 0.7
DECAY = 0.01
ADAM_EPS = 1e-08
TEMP_RATE = 0.1
MASKED = -1e30
HALF_LOG_TAU = 0.5 * math.log(2.0 * math.pi)
GELU_C = math.sqrt(2.0 / math.pi)
GELU_A = 0.044715
HIGH = lax.Precision.HIGHEST
LOWER = jnp.bfloat16
WIDE = jnp.float32

LAYERS = 3
WINS = 16
SLOT = 64
ROWS = WINS * SLOT
CHUNK = 256
CHUNKS = ROWS // CHUNK
GROUP = 128
BLOCKS = 32
PACK = 192
EMB = S + A + 1 + K + 3
FIN = EMB
HEADW = EMB + 2
BASE = EMB + 2 + 2 * A
PER = 9 + FF // D
NROWS = BASE + LAYERS * PER
SMALL = 88


def dot(a, b, precision=None):
    return lax.dot_general(
        a, b, (((1,), (0,)), ((), ())), precision=precision, preferred_element_type=WIDE
    )


def dot_nt(a, b, precision=None):
    return lax.dot_general(
        a, b, (((1,), (1,)), ((), ())), precision=precision, preferred_element_type=WIDE
    )


def dot_tn(a, b, precision=None):
    return lax.dot_general(
        a, b, (((0,), (0,)), ((), ())), precision=precision, preferred_element_type=WIDE
    )


def iota(shape, dim):
    return lax.broadcasted_iota(jnp.int32, shape, dim)


def col_sum(v):
    return jnp.sum(v, 0, keepdims=True)


def row_mean(v):
    return jnp.mean(v, -1, keepdims=True)


def norm_parts(x):
    center = x - row_mean(x)
    scale = lax.rsqrt(row_mean(center * center) + EPS)
    return center * scale, scale


def norm_back(xhat, scale, gain, grad):
    scaled = grad * gain
    return scale * (scaled - row_mean(scaled) - xhat * row_mean(scaled * xhat))


def token_rows(at, count):
    row = at + iota((count, 128), 0)
    place = row & (SLOT - 1)
    step = (place * 21846) >> 16
    return row >> 6, step, place - 3 * step, place < 3 * K


def chunk_rows(c):
    return pl.ds(pl.multiple_of(c * CHUNK, CHUNK), CHUNK)


class Kit:
    def __init__(self, **refs):
        self.__dict__.update(refs)

    def row(self, l, k):
        return self.lrows[l, k : k + 1, :]

    def w(self, l, first, count=16):
        return self.wg[l, :, :, first : first + count, :].reshape(BLOCKS * count, D)

    def w_qkv(self, l, j):
        return self.w(l, 16 * j)

    def w_out(self, l):
        return self.w(l, 48)

    def w_up(self, l, j):
        return self.w(l, 64 + 16 * j)

    def w_down(self, l, j):
        return self.wg[l, j, :, 128:192, :].reshape(D, D)


def setup_stage(k):
    k.emb[...] = jnp.zeros_like(k.emb)
    k.emb[0:EMB, :] = k.small[0:EMB, :]
    k.headw[...] = jnp.zeros_like(k.headw)
    k.headw[0, 0:A, :] = k.small[HEADW : HEADW + A, :].astype(LOWER)
    k.headw[1, 0:A, :] = k.small[HEADW + A : HEADW + 2 * A, :].astype(LOWER)
    for l in range(LAYERS):
        k.lrows[l, 0:PER, :] = k.small[BASE + l * PER : BASE + (l + 1) * PER, :]
    k.sgl[...] = jnp.zeros_like(k.sgl)
    k.sgh[...] = jnp.zeros_like(k.sgh)
    k.sgw[...] = jnp.zeros_like(k.sgw)

    meta = k.meta[...].astype(LOWER)
    lane = iota((128, 128), 1)
    sub = iota((128, 128), 0)
    half = lane & (SLOT - 1)
    pick = sub - 2 == ((half * 21846) >> 16)
    pick_lo = (pick & (lane < SLOT)).astype(WIDE).astype(LOWER)
    pick_hi = (pick & (lane >= SLOT)).astype(WIDE).astype(LOWER)
    low = dot(meta, pick_lo).astype(LOWER)
    high = dot(meta, pick_hi).astype(LOWER)
    even = (lane == 2 * sub).astype(WIDE).astype(LOWER)
    odd = (lane == 2 * sub + 1).astype(WIDE).astype(LOWER)
    k.live[...] = (dot(even, low) + dot(odd, high))[0:8]
    same = (sub >> 6) == (lane >> 6)
    for g in range(ROWS // GROUP):
        live = k.live[g : g + 1, :] > 0.5
        allowed = same & (lane <= sub) & (live | (lane == sub))
        k.bias[g] = jnp.where(allowed, 0.0, MASKED)

    def chunk(c, carry):
        rows = chunk_rows(c)
        win, step, kind, real = token_rows(c * CHUNK, CHUNK)
        lane = iota((CHUNK, 128), 1)
        tok = dot((lane == win).astype(WIDE).astype(LOWER), meta)
        start, repeat = tok[:, 0:1], tok[:, 1:2]
        valid = jnp.sum(jnp.where(lane == step + 2, tok, 0.0), -1, keepdims=True)
        place = start.astype(jnp.int32) + step
        source = ((lane == place) & real).astype(WIDE)
        raw = dot(source, k.buf[...], HIGH)
        mine = (
            ((lane < S) & (kind == 1))
            | ((lane >= S) & (lane < S + A) & (kind == 2))
            | ((lane == S + A) & (kind == 0))
        )
        marks = ((lane == S + A + 1 + step) | (lane == S + A + 1 + K + kind)) & real
        feats = jnp.where(mine, raw, 0.0) + marks.astype(WIDE)
        k.feats[rows, :] = feats
        weight = jnp.where((kind == 1) & real, repeat * valid, 0.0)
        acts = pltpu.roll(raw, 128 - S, 1)
        k.acts[rows, :] = jnp.where(lane < A, acts, jnp.where(lane == A, weight, 0.0))
        k.xs[0, rows, :] = dot(feats, k.emb[...], HIGH)
        return carry

    lax.fori_loop(0, CHUNKS, chunk, 0)


def pair_masks(rows):
    lane = iota((rows, 128), 1)
    return lane < HD


def stack_pair(v, first):
    zero = jnp.zeros_like(v)
    return jnp.concatenate([jnp.where(first, v, zero), jnp.where(first, zero, v)], 0)


def forward_attn(k, l):
    def chunk(c, carry):
        rows = chunk_rows(c)
        xhat, _ = norm_parts(k.xs[l, rows, :])
        normed = (xhat * k.row(l, 0) + k.row(l, 1)).astype(LOWER)
        for j in range(3):
            part = dot(normed, k.w_qkv(l, j)) + k.row(l, 4 + j)
            k.qkv[l, rows, j * D : (j + 1) * D] = part.astype(LOWER)
        return carry

    lax.fori_loop(0, CHUNKS, chunk, 0)
    first = pair_masks(GROUP)

    def group(g, carry):
        rows = pl.ds(pl.multiple_of(g * GROUP, GROUP), GROUP)
        bias = k.bias[g]
        bias = jnp.concatenate([bias, bias], 0)
        lane = iota((GROUP, 128), 1)
        logs = jnp.zeros((GROUP, 128), WIDE)
        for p in range(H // 2):
            at = p * 128
            query = k.qkv[l, rows, at : at + 128] * jnp.asarray(HD**-0.5, LOWER)
            keyed = k.qkv[l, rows, D + at : D + at + 128]
            values = k.qkv[l, rows, 2 * D + at : 2 * D + at + 128]
            scores = dot_nt(stack_pair(query, first), keyed) + bias
            peak = jnp.max(scores, -1, keepdims=True)
            expo = jnp.exp(scores - peak)
            total = jnp.sum(expo, -1, keepdims=True)
            probs = (expo / total).astype(LOWER)
            out = dot(probs, values)
            k.mixed[l, rows, at : at + 128] = jnp.where(first, out[:GROUP], out[GROUP:]).astype(LOWER)
            lse = peak + jnp.log(total)
            logs = jnp.where(lane == 2 * p, lse[:GROUP], logs)
            logs = jnp.where(lane == 2 * p + 1, lse[GROUP:], logs)
        k.logs[l, rows, :] = logs
        return carry

    lax.fori_loop(0, ROWS // GROUP, group, 0)


def gelu_parts(h):
    square = h * h
    t = jnp.tanh(GELU_C * (h + GELU_A * h * square))
    return t, square


def forward_ffn(k, l, dest):
    def chunk(c, carry):
        rows = chunk_rows(c)
        mid = k.xs[l, rows, :] + dot(k.mixed[l, rows, :], k.w_out(l)) + k.row(l, 7)
        k.mid[l, rows, :] = mid
        xhat, _ = norm_parts(mid)
        second = (xhat * k.row(l, 2) + k.row(l, 3)).astype(LOWER)
        out = mid + k.row(l, 12)
        for j in range(4):
            h = dot(second, k.w_up(l, j)) + k.row(l, 8 + j)
            t, _ = gelu_parts(h)
            acted = (0.5 * h * (1.0 + t)).astype(LOWER)
            out = out + dot(acted, k.w_down(l, j))
        k.xs[dest, rows, :] = out
        return carry

    lax.fori_loop(0, CHUNKS, chunk, 0)


def head_stage(k, at):
    gain, bias = k.small[FIN : FIN + 1, :], k.small[FIN + 1 : FIN + 2, :]
    lane = iota((CHUNK, 128), 1)
    keep = lane < A

    def bias_row(first):
        row = jnp.zeros((1, 128), WIDE)
        at = iota((1, 128), 1)
        for a in range(A):
            row = jnp.where(at == a, k.head_bias[first + a], row)
        return row

    bias_mean, bias_spread = bias_row(0), bias_row(A)
    temp = jnp.exp(jnp.full((1, 128), k.log_temp[0], WIDE))

    def chunk(c, carry):
        rows = chunk_rows(c)
        xhat, scale = norm_parts(k.xs[at, rows, :])
        feats = (xhat * gain + bias).astype(LOWER)
        mean = dot_nt(feats, k.headw[0]) + bias_mean
        spread = jnp.tanh(dot_nt(feats, k.headw[1]) + bias_spread)
        acts = k.acts[rows, :]
        weight = acts[:, A : A + 1]
        acts = jnp.where(keep, acts, 0.0)
        target = 0.5 * (jnp.log(1.0 + acts) - jnp.log(1.0 - acts))
        shrink = jnp.exp(-spread)
        zed = (target - mean) * shrink
        terms = 0.5 * zed * zed + spread + HALF_LOG_TAU + jnp.log(1.0 - acts * acts)
        nll = jnp.sum(jnp.where(keep, terms, 0.0), -1, keepdims=True)
        entropy = jnp.sum(jnp.where(keep, spread, 0.0), -1, keepdims=True) + A * (0.5 + HALF_LOG_TAU)
        loss = weight * (nll - temp * entropy)
        sums = jnp.where(lane == 0, loss, jnp.where(lane == 1, weight * entropy, jnp.where(lane == 2, weight, 0.0)))
        d_mean = jnp.where(keep, weight * (-zed * shrink), 0.0).astype(LOWER)
        d_spread = weight * (1.0 - zed * zed - temp) * (1.0 - spread * spread)
        d_spread = jnp.where(keep, d_spread, 0.0).astype(LOWER)
        k.sgh[2:3, 0:128] += col_sum(sums)
        k.sgh[3:4, 0:128] += col_sum(d_mean.astype(WIDE))
        k.sgh[4:5, 0:128] += col_sum(d_spread.astype(WIDE))
        k.sgw[0] += dot_tn(d_mean, feats)[0:8]
        k.sgw[1] += dot_tn(d_spread, feats)[0:8]
        d_feats = dot(d_mean, k.headw[0]) + dot(d_spread, k.headw[1])
        k.sgh[0:1, :] += col_sum(d_feats * xhat)
        k.sgh[1:2, :] += col_sum(d_feats)
        k.xs[at, rows, :] = norm_back(xhat, scale, gain, d_feats)
        return carry

    lax.fori_loop(0, CHUNKS, chunk, 0)


def owner_place(i):
    z, y, x, c = i // 8, (i // 4) % 2, (i // 2) % 2, i % 2
    return c * 16 + x * 8 + y * 4 + z


def store_blocks(k, slot, first_block, first_row, count, value):
    value = value.astype(LOWER)
    for n in range(value.shape[0] // count):
        place = owner_place(first_block + n)
        k.wg[slot, place // 8, place % 8, first_row : first_row + count, :] = value[
            n * count : (n + 1) * count
        ]


def backward_ffn(k, l, grad):
    def before(c, carry):
        rows = chunk_rows(c)
        d_down = k.xs[grad, rows, :].astype(LOWER)
        k.work[rows, 2 * D : 3 * D] = d_down
        k.sgl[l, 12:13, :] += col_sum(d_down.astype(WIDE))
        xhat, _ = norm_parts(k.mid[l, rows, :])
        k.left[rows, :] = (xhat * k.row(l, 2) + k.row(l, 3)).astype(LOWER)
        k.dsec[rows, :] = jnp.zeros((CHUNK, D), WIDE)
        return carry

    lax.fori_loop(0, CHUNKS, before, 0)
    for j in range(4):

        def chunk(c, carry, j=j):
            rows = chunk_rows(c)
            h = dot(k.left[rows, :], k.w_up(l, j)) + k.row(l, 8 + j)
            t, square = gelu_parts(h)
            k.work[rows, 0:D] = (0.5 * h * (1.0 + t)).astype(LOWER)
            slope = 0.5 * (1.0 + t) + 0.5 * GELU_C * h * (1.0 - t * t) * (1.0 + 3.0 * GELU_A * square)
            d_acted = dot_nt(k.work[rows, 2 * D : 3 * D], k.w_down(l, j))
            d_hidden = (d_acted * slope).astype(LOWER)
            k.work[rows, D : 2 * D] = d_hidden
            k.sgl[l, 8 + j : 9 + j, :] += col_sum(d_hidden.astype(WIDE))
            k.dsec[rows, :] += dot_nt(d_hidden, k.w_up(l, j))
            return carry

        lax.fori_loop(0, CHUNKS, chunk, 0)
        store_blocks(k, l + 1, 0, 64 + 16 * j, 16, dot_tn(k.left[...], k.work[:, D : 2 * D]))
        store_blocks(k, l + 1, 8 * j, 128, 64, dot_tn(k.work[:, 0:D], k.work[:, 2 * D : 3 * D]))

    def after(c, carry):
        rows = chunk_rows(c)
        xhat, scale = norm_parts(k.mid[l, rows, :])
        d_second = k.dsec[rows, :]
        k.sgl[l, 2:3, :] += col_sum(d_second * xhat)
        k.sgl[l, 3:4, :] += col_sum(d_second)
        k.xs[grad, rows, :] += norm_back(xhat, scale, k.row(l, 2), d_second)
        return carry

    lax.fori_loop(0, CHUNKS, after, 0)


def backward_attn(k, l, grad):
    def before(c, carry):
        rows = chunk_rows(c)
        d_branch = k.xs[grad, rows, :].astype(LOWER)
        k.left[rows, :] = d_branch
        k.sgl[l, 7:8, :] += col_sum(d_branch.astype(WIDE))
        k.dmix[rows, :] = dot_nt(d_branch, k.w_out(l)).astype(LOWER)
        return carry

    lax.fori_loop(0, CHUNKS, before, 0)
    store_blocks(k, l + 1, 0, 48, 16, dot_tn(k.mixed[l], k.left[...]))
    first = pair_masks(GROUP)
    scale = HD**-0.5

    def group(g, carry):
        rows = pl.ds(pl.multiple_of(g * GROUP, GROUP), GROUP)
        bias = k.bias[g]
        bias = jnp.concatenate([bias, bias], 0)
        logs = k.logs[l, rows, :]
        for p in range(H // 2):
            at = p * 128
            query = stack_pair(k.qkv[l, rows, at : at + 128] * jnp.asarray(scale, LOWER), first)
            keyed = k.qkv[l, rows, D + at : D + at + 128]
            values = k.qkv[l, rows, 2 * D + at : 2 * D + at + 128]
            d_mixed = stack_pair(k.dmix[rows, at : at + 128], first)
            log_total = jnp.concatenate(
                [logs[:, 2 * p : 2 * p + 1], logs[:, 2 * p + 1 : 2 * p + 2]], 0
            )
            probs = jnp.exp(dot_nt(query, keyed) + bias - log_total)
            d_probs = dot_nt(d_mixed, values)
            d_values = dot_tn(probs.astype(LOWER), d_mixed)
            inner = probs * d_probs
            d_scores = (inner - probs * jnp.sum(inner, -1, keepdims=True)).astype(LOWER)
            d_query = dot(d_scores, keyed)
            d_query = jnp.where(first, d_query[:GROUP], d_query[GROUP:]) * scale
            d_keyed = dot_tn(d_scores, query)
            k.work[rows, at : at + 128] = d_query.astype(LOWER)
            k.work[rows, D + at : D + at + 128] = d_keyed.astype(LOWER)
            k.work[rows, 2 * D + at : 2 * D + at + 128] = d_values.astype(LOWER)
        return carry

    lax.fori_loop(0, ROWS // GROUP, group, 0)

    def again(c, carry):
        rows = chunk_rows(c)
        xhat, _ = norm_parts(k.xs[l, rows, :])
        k.left[rows, :] = (xhat * k.row(l, 0) + k.row(l, 1)).astype(LOWER)
        return carry

    lax.fori_loop(0, CHUNKS, again, 0)
    for j in range(3):
        store_blocks(k, l + 1, 0, 16 * j, 16, dot_tn(k.left[...], k.work[:, j * D : (j + 1) * D]))


def backward_input(k, l, grad):
    def chunk(c, carry):
        rows = chunk_rows(c)
        d_normed = jnp.zeros((CHUNK, D), WIDE)
        for j in range(3):
            d_part = k.work[rows, j * D : (j + 1) * D]
            k.sgl[l, 4 + j : 5 + j, :] += col_sum(d_part.astype(WIDE))
            d_normed = d_normed + dot_nt(d_part, k.w_qkv(l, j))
        xhat, scale = norm_parts(k.xs[l, rows, :])
        k.sgl[l, 0:1, :] += col_sum(d_normed * xhat)
        k.sgl[l, 1:2, :] += col_sum(d_normed)
        k.xs[grad, rows, :] += norm_back(xhat, scale, k.row(l, 0), d_normed)
        return carry

    lax.fori_loop(0, CHUNKS, chunk, 0)


def small_stage(k, out, grad):
    out[...] = jnp.zeros_like(out)
    out[0:EMB, :] = dot_tn(k.feats[...], k.xs[grad], HIGH)[0:EMB]
    out[FIN : FIN + 2, :] = k.sgh[0:2, :]
    out[HEADW : HEADW + A, :] = k.sgw[0, 0:A, :]
    out[HEADW + A : HEADW + 2 * A, :] = k.sgw[1, 0:A, :]
    for l in range(LAYERS):
        out[BASE + l * PER : BASE + (l + 1) * PER, :] = k.sgl[l, 0:PER, :]
    out[NROWS : NROWS + 3, :] = k.sgh[2:5, :]


WORK_SHAPES = dict(
    wg=((LAYERS + 1, BLOCKS // 8, 8, PACK, D), LOWER),
    xs=((LAYERS + 1, ROWS, D), WIDE),
    mid=((LAYERS, ROWS, D), WIDE),
    qkv=((LAYERS, ROWS, 3 * D), LOWER),
    mixed=((LAYERS, ROWS, D), LOWER),
    logs=((LAYERS, ROWS, 128), WIDE),
    work=((ROWS, 3 * D), LOWER),
    left=((ROWS, D), LOWER),
    dmix=((ROWS, D), LOWER),
    dsec=((ROWS, D), WIDE),
    feats=((ROWS, 128), WIDE),
    acts=((ROWS, 128), WIDE),
    bias=((ROWS // GROUP, GROUP, GROUP), WIDE),
    live=((8, 128), WIDE),
    emb=((128, D), WIDE),
    headw=((2, 128, D), LOWER),
    lrows=((LAYERS, 16, D), WIDE),
    sgl=((LAYERS, 16, D), WIDE),
    sgh=((8, D), WIDE),
    sgw=((2, 8, D), WIDE),
)


def compute_kernel(meta, buf, small, head_bias, log_temp, packed, grads, small_grad, *scratch):
    refs = dict(zip(WORK_SHAPES, scratch))
    load_sem, store_sem = scratch[len(WORK_SHAPES) :]
    k = Kit(meta=meta, buf=buf, small=small, head_bias=head_bias, log_temp=log_temp, **refs)
    loads = [
        pltpu.make_async_copy(packed.at[l], k.wg.at[l], load_sem.at[l]) for l in range(LAYERS)
    ]
    stores = [
        pltpu.make_async_copy(k.wg.at[l + 1], grads.at[l], store_sem.at[l]) for l in range(LAYERS)
    ]
    for copy in loads:
        copy.start()
    setup_stage(k)

    def forward(l, carry):
        pltpu.make_async_copy(packed.at[l], k.wg.at[l], load_sem.at[l]).wait()
        forward_attn(k, l)
        forward_ffn(k, l, l + 1)
        return carry

    lax.fori_loop(0, LAYERS, forward, 0)
    head_stage(k, LAYERS)

    def backward(n, carry):
        l = LAYERS - 1 - n
        backward_ffn(k, l, LAYERS)
        backward_attn(k, l, LAYERS)
        pltpu.make_async_copy(k.wg.at[l + 1], grads.at[l], store_sem.at[l]).start()
        backward_input(k, l, LAYERS)
        return carry

    lax.fori_loop(0, LAYERS, backward, 0)
    small_stage(k, small_grad, LAYERS)
    for copy in stores:
        copy.wait()


def vmem(shape, dtype):
    return pltpu.VMEM(shape, dtype)


def compute(meta, buf, small, head_bias, log_temp, packed):
    whole = pl.BlockSpec(memory_space=pltpu.VMEM)
    scalars = pl.BlockSpec(memory_space=pltpu.SMEM)
    anywhere = pl.BlockSpec(memory_space=pl.ANY)
    return pl.pallas_call(
        compute_kernel,
        name="train_pass",
        out_shape=(
            jax.ShapeDtypeStruct((LAYERS, BLOCKS // 8, 8, PACK, D), LOWER),
            jax.ShapeDtypeStruct((SMALL, D), WIDE),
        ),
        in_specs=[whole, whole, whole, scalars, scalars, anywhere],
        out_specs=(anywhere, whole),
        scratch_shapes=[vmem(*s) for s in WORK_SHAPES.values()]
        + [pltpu.SemaphoreType.DMA((LAYERS,)), pltpu.SemaphoreType.DMA((LAYERS,))],
        compiler_params=pltpu.CompilerParams(vmem_limit_bytes=66 * 1024 * 1024),
        cost_estimate=pl.CostEstimate(flops=6 * 10**10, bytes_accessed=4 * 10**7, transcendentals=10**7),
    )(meta, buf, small, head_bias, log_temp, packed)


def small_inputs(buf_states, buf_actions, buf_returns, window_starts, window_repeats, valid_steps):
    meta = jnp.concatenate(
        [window_starts[:, None], window_repeats[:, None], valid_steps], 1
    ).astype(WIDE)
    meta = jnp.pad(meta, ((0, 128 - meta.shape[0]), (0, 128 - meta.shape[1])))
    buf = jnp.concatenate([buf_states, buf_actions, buf_returns[:, None]], 1)
    buf = jnp.pad(buf, ((0, 128 - buf.shape[0]), (0, 128 - buf.shape[1])))
    return meta, buf


MESH = pl.DeviceIdType.MESH
NZ, NY, NX, NC = 4, 2, 2, 2
NR = NY * NX * NC
SHARD = PACK
ATTN, FFN = (0, 64), (64, 128)


class Place:
    def __init__(self):
        dp, fsdp = lax.axis_index("dp"), lax.axis_index("fsdp")
        self.z, self.y = dp // NY, dp % NY
        self.x, self.c = fsdp // NC, fsdp % NC
        self.r = self.y * 4 + self.x * 2 + self.c
        self.r_x = self.y * 4 + (1 - self.x) * 2 + self.c
        self.r_y = (1 - self.y) * 4 + self.x * 2 + self.c
        self.r_xy = (1 - self.y) * 4 + (1 - self.x) * 2 + self.c
        self.to_x = (dp, (1 - self.x) * NC + self.c)
        self.to_y = (self.z * NY + 1 - self.y, fsdp)
        self.to_c = (dp, self.x * NC + 1 - self.c)
        self.to_z = [(((self.z + d) % NZ) * NY + self.y, fsdp) for d in range(1, NZ)]

    def barrier(self):
        partners = [self.to_x, self.to_y, self.to_c] + self.to_z
        sem = pltpu.get_barrier_semaphore()
        for partner in partners:
            pl.semaphore_signal(sem, inc=1, device_id=partner, device_id_type=MESH)
        pl.semaphore_wait(sem, len(partners))


class Gather:
    COPIES = 11

    def __init__(self, place, wg, send, recv):
        self.at, self.wg, self.send, self.recv = place, wg, send, recv

    def copy(self, l, part, n, z, r, rows, to):
        q = 2 * l + part
        ref = self.wg.at[l, z, r, pl.ds(*rows), :]
        return pltpu.make_async_remote_copy(
            src_ref=ref,
            dst_ref=ref,
            send_sem=self.send.at[q, n],
            recv_sem=self.recv.at[q, n],
            device_id=to,
            device_id_type=MESH,
        )

    def copies(self, l, part):
        at = self.at
        first, count = (ATTN, FFN)[part]
        rows, top, low = (first, count), (first, count // 2), (first + count // 2, count // 2)
        column = pl.ds(0, NZ)
        return (
            [self.copy(l, part, n, at.z, at.r, rows, at.to_z[n]) for n in range(3)]
            + [
                self.copy(l, part, 3, column, at.r, rows, at.to_x),
                self.copy(l, part, 4, column, at.r, rows, at.to_y),
                self.copy(l, part, 5, column, at.r, rows, at.to_c),
                self.copy(l, part, 6, column, at.r_x, top, at.to_y),
                self.copy(l, part, 7, column, at.r_y, low, at.to_x),
                self.copy(l, part, 8, column, at.r_x, rows, at.to_c),
                self.copy(l, part, 9, column, at.r_y, rows, at.to_c),
                self.copy(l, part, 10, column, at.r_xy, rows, at.to_c),
            ]
        )

    def first(self, l, part):
        for copy in self.copies(l, part)[0:3]:
            copy.start()

    def second(self, l, part):
        c = self.copies(l, part)
        for n in range(3):
            c[n].wait_recv()
        for n in (3, 4, 5):
            c[n].start()

    def third(self, l, part):
        c = self.copies(l, part)
        c[3].wait_recv()
        c[6].start()
        c[8].start()
        c[4].wait_recv()
        c[7].start()
        c[9].start()

    def fourth(self, l, part):
        c = self.copies(l, part)
        c[6].wait_recv()
        c[7].wait_recv()
        c[10].start()

    def last(self, l, part):
        c = self.copies(l, part)
        for n in (5, 8, 9, 10):
            c[n].wait_recv()

    def sent(self, l, part):
        for copy in self.copies(l, part):
            copy.wait_send()


def pack_rows(wg, l, z, r, mats):
    qkv, out, up, down = mats
    for j in range(3):
        wg[l, z, r, 16 * j : 16 * j + 16, :] = qkv[l, :, j * D : (j + 1) * D].astype(LOWER)
    wg[l, z, r, 48:64, :] = out[l].astype(LOWER)
    for j in range(4):
        wg[l, z, r, 64 + 16 * j : 80 + 16 * j, :] = up[l, :, j * D : (j + 1) * D].astype(LOWER)
    wg[l, z, r, 128:192, :] = down[l].astype(LOWER)


class Reduce:
    COPIES = 8

    def __init__(self, place, g, r0, r1a, r1b, r2, r3, send, recv):
        self.at, self.g, self.r0, self.r1a, self.r1b = place, g, r0, r1a, r1b
        self.r2, self.r3, self.send, self.recv = r2, r3, send, recv

    def rows(self, part):
        first, count = (ATTN, FFN)[part]
        half = count // 2
        return first, count, first, first + half, half, (0, 32)[part]

    def copies(self, slot, buf, part):
        at = self.at
        first, count, top, low, half, one = self.rows(part)
        rows, a, b, h = pl.ds(first, count), pl.ds(top, half), pl.ds(low, half), pl.ds(one, half)
        q = 2 * slot + part
        r0, r1a, r1b, r2, r3 = (
            ref.at[buf] for ref in (self.r0, self.r1a, self.r1b, self.r2, self.r3)
        )
        other = pl.ds(4 * (1 - at.y), 4)

        def copy(n, src, dst, to):
            return pltpu.make_async_remote_copy(
                src_ref=src,
                dst_ref=dst,
                send_sem=self.send.at[q, n],
                recv_sem=self.recv.at[q, n],
                device_id=to,
                device_id_type=MESH,
            )

        return [
            copy(0, self.g.at[slot, pl.ds(2 * (1 - at.c), 2), :, rows, :], r0.at[:, :, rows, :], at.to_c),
            copy(1, r0.at[1 - at.x, :, a, :], r1a.at[:, h, :], at.to_x),
            copy(2, r0.at[:, other, b, :], r1b.at[:, :, h, :], at.to_y),
            copy(3, r1a.at[other, h, :], r2.at[:, a, :], at.to_y),
            copy(4, r1b.at[1 - at.x, :, h, :], r2.at[:, b, :], at.to_x),
        ] + [
            copy(5 + n, r2.at[(at.z + n + 1) % NZ, rows, :], r3.at[n, rows, :], at.to_z[n])
            for n in range(3)
        ]

    def start(self, slot, buf, part):
        self.copies(slot, buf, part)[0].start()

    def wide(self, ref, *index):
        return ref[index].astype(WIDE)

    def first(self, slot, buf, part):
        at = self.at
        c = self.copies(slot, buf, part)
        _, _, top, low, half, _ = self.rows(part)
        a, b = pl.ds(top, half), pl.ds(low, half)
        c[0].wait_recv()

        def along_x(n, carry):
            total = self.wide(self.g, slot, 2 * at.c + 1 - at.x, n, a) + self.wide(
                self.r0, buf, 1 - at.x, n, a
            )
            self.r0[buf, 1 - at.x, n, a] = total.astype(LOWER)
            return carry

        lax.fori_loop(0, NR, along_x, 0)
        c[1].start()

        def along_y(n, carry):
            x, place = n // 4, 4 * (1 - at.y) + n % 4
            total = self.wide(self.g, slot, 2 * at.c + x, place, b) + self.wide(
                self.r0, buf, x, place, b
            )
            self.r0[buf, x, place, b] = total.astype(LOWER)
            return carry

        lax.fori_loop(0, NR, along_y, 0)
        c[2].start()

    def second(self, slot, buf, part):
        at = self.at
        c = self.copies(slot, buf, part)
        _, _, top, low, half, one = self.rows(part)
        a, b, h = pl.ds(top, half), pl.ds(low, half), pl.ds(one, half)
        c[1].wait_recv()

        def along_y(n, carry):
            place = 4 * (1 - at.y) + n
            total = (
                self.wide(self.g, slot, 2 * at.c + at.x, place, a)
                + self.wide(self.r0, buf, at.x, place, a)
                + self.wide(self.r1a, buf, place, h)
            )
            self.r1a[buf, place, h] = total.astype(LOWER)
            return carry

        lax.fori_loop(0, NZ, along_y, 0)
        c[3].start()
        c[2].wait_recv()

        def along_x(n, carry):
            place, x = 4 * at.y + n, 1 - at.x
            total = (
                self.wide(self.g, slot, 2 * at.c + x, place, b)
                + self.wide(self.r0, buf, x, place, b)
                + self.wide(self.r1b, buf, x, n, h)
            )
            self.r1b[buf, x, n, h] = total.astype(LOWER)
            return carry

        lax.fori_loop(0, NZ, along_x, 0)
        c[4].start()

    def chip_sums(self, slot, buf, part, z):
        at = self.at
        _, _, top, low, half, one = self.rows(part)
        a, b, h = pl.ds(top, half), pl.ds(low, half), pl.ds(one, half)
        place = 4 * at.y + z
        mine = 2 * at.c + at.x
        return (
            self.wide(self.g, slot, mine, place, a)
            + self.wide(self.r0, buf, at.x, place, a)
            + self.wide(self.r1a, buf, place, h)
            + self.wide(self.r2, buf, z, a),
            self.wide(self.g, slot, mine, place, b)
            + self.wide(self.r0, buf, at.x, place, b)
            + self.wide(self.r1b, buf, at.x, z, h)
            + self.wide(self.r2, buf, z, b),
        )

    def third(self, slot, buf, part):
        at = self.at
        c = self.copies(slot, buf, part)
        _, _, top, low, half, _ = self.rows(part)
        c[3].wait_recv()
        c[4].wait_recv()
        for n in range(3):
            z = (at.z + n + 1) % NZ
            upper, lower = self.chip_sums(slot, buf, part, z)
            self.r2[buf, z, pl.ds(top, half)] = upper.astype(LOWER)
            self.r2[buf, z, pl.ds(low, half)] = lower.astype(LOWER)
            c[5 + n].start()

    def last(self, slot, buf, part, out):
        c = self.copies(slot, buf, part)
        _, _, top, low, half, _ = self.rows(part)
        upper, lower = self.chip_sums(slot, buf, part, self.at.z)
        for n in range(3):
            c[5 + n].wait_recv()
            upper = upper + self.wide(self.r3, buf, n, pl.ds(top, half))
            lower = lower + self.wide(self.r3, buf, n, pl.ds(low, half))
        out[pl.ds(top, half), :] = upper
        out[pl.ds(low, half), :] = lower
        return col_sum(upper * upper) + col_sum(lower * lower)

    def sent(self, slot, buf, part):
        for copy in self.copies(slot, buf, part):
            copy.wait_send()


class Total:
    COPIES = 6

    def __init__(self, place, own, got, send, recv):
        self.at, self.own, self.got, self.send, self.recv = place, own, got, send, recv

    def copies(self):
        at = self.at

        def copy(n, dst, to):
            return pltpu.make_async_remote_copy(
                src_ref=self.own.at[min(n, 3)],
                dst_ref=self.got.at[dst],
                send_sem=self.send.at[n],
                recv_sem=self.recv.at[n],
                device_id=to,
                device_id_type=MESH,
            )

        return [copy(n, n, to) for n, to in enumerate((at.to_c, at.to_x, at.to_y))] + [
            copy(3 + n, 3 + n, to) for n, to in enumerate(at.to_z)
        ]

    def start(self):
        self.copies()[0].start()

    def step(self, n):
        c = self.copies()
        c[n].wait_recv()
        self.own[n + 1] = self.own[n] + self.got[n]
        if n < 2:
            c[n + 1].start()
        else:
            for m in (3, 4, 5):
                c[m].start()

    def last(self):
        c = self.copies()
        for m in (3, 4, 5):
            c[m].wait_recv()
        total = None
        for z in range(NZ):
            term = self.own[3]
            for n in range(3):
                from_z = (self.at.z + NZ - 1 - n) % NZ
                term = jnp.where(from_z == z, self.got[3 + n], term)
            total = term if total is None else total + term
        return total

    def sent(self):
        for copy in self.copies():
            copy.wait_send()


def gather_kernel(qkv, out, up, down, packed, wg, send, recv, store):
    place = Place()
    net = Gather(place, wg, send, recv)
    for l in range(LAYERS):
        pack_rows(wg, l, place.z, place.r, (qkv, out, up, down))
    place.barrier()
    parts = [(l, part) for l in range(LAYERS) for part in (0, 1)]

    def keep(l, part):
        rows = pl.ds(*(ATTN, FFN)[part])
        return pltpu.make_async_copy(
            wg.at[l, :, :, rows, :], packed.at[l, :, :, rows, :], store.at[2 * l + part]
        )

    for l, part in parts[:2]:
        net.first(l, part)
    for t in range(len(parts) + 3):
        if t < len(parts):
            net.second(*parts[t])
        if t + 2 < len(parts):
            net.first(*parts[t + 2])
        if 0 <= t - 1 < len(parts):
            net.third(*parts[t - 1])
        if 0 <= t - 2 < len(parts):
            net.fourth(*parts[t - 2])
        if 0 <= t - 3 < len(parts):
            net.last(*parts[t - 3])
            keep(*parts[t - 3]).start()
    for l, part in parts:
        net.sent(l, part)
        keep(l, part).wait()


def gather_all(mats):
    whole = pl.BlockSpec(memory_space=pltpu.VMEM)
    count = 2 * LAYERS
    return pl.pallas_call(
        gather_kernel,
        name="gather",
        out_shape=jax.ShapeDtypeStruct((LAYERS, NZ, NR, PACK, D), LOWER),
        in_specs=[whole] * 4,
        out_specs=pl.BlockSpec(memory_space=pl.ANY),
        scratch_shapes=[
            pltpu.VMEM((LAYERS, NZ, NR, PACK, D), LOWER),
            pltpu.SemaphoreType.DMA((count, Gather.COPIES)),
            pltpu.SemaphoreType.DMA((count, Gather.COPIES)),
            pltpu.SemaphoreType.DMA((count,)),
        ],
        compiler_params=pltpu.CompilerParams(
            collective_id=0, has_side_effects=True, vmem_limit_bytes=40 * 1024 * 1024
        ),
        cost_estimate=pl.CostEstimate(flops=0, bytes_accessed=4 * 10**7, transcendentals=0),
    )(*mats)


REDUCE_SHAPES = dict(
    r0=(NX, NR, PACK, D),
    r1a=(NR, PACK // 2, D),
    r1b=(NX, NZ, PACK // 2, D),
    r2=(NZ, PACK, D),
    r3=(3, PACK, D),
)


def reduce_kernel(grads, small, shard, totals, squares, g, *scratch):
    refs = scratch[: len(REDUCE_SHAPES)]
    send, recv, load, own_s, got_s, send_s, recv_s, own_n, got_n, send_n, recv_n = scratch[
        len(REDUCE_SHAPES) :
    ]
    place = Place()
    net = Reduce(place, g, *refs, send, recv)
    sums = Total(place, own_s, got_s, send_s, recv_s)
    norm = Total(place, own_n, got_n, send_n, recv_n)
    parts = [(l, part) for l in reversed(range(LAYERS)) for part in (1, 0)]

    def fetch(l, part):
        rows = pl.ds(*(ATTN, FFN)[part])
        return pltpu.make_async_copy(
            grads.at[l, :, :, rows, :], g.at[l, :, :, rows, :], load.at[2 * l + part]
        )

    for l, part in parts:
        fetch(l, part).start()
    own_s[0] = small[...]
    place.barrier()
    sums.start()
    square = jnp.zeros((1, D), WIDE)
    for t in range(len(parts) + 4):
        if t < len(parts):
            l, part = parts[t]
            fetch(l, part).wait()
            net.start(l, l, part)
        if 0 <= t - 1 < len(parts):
            l, part = parts[t - 1]
            net.first(l, l, part)
        if 0 <= t - 2 < len(parts):
            l, part = parts[t - 2]
            net.second(l, l, part)
        if 0 <= t - 3 < len(parts):
            l, part = parts[t - 3]
            net.third(l, l, part)
        if 0 <= t - 4 < len(parts):
            l, part = parts[t - 4]
            square = square + net.last(l, l, part, shard.at[l])
        if 1 <= t <= 3:
            sums.step(t - 1)
    own_n[0] = jnp.broadcast_to(square, own_n.shape[1:])
    norm.start()
    totals[...] = sums.last()
    for n in range(3):
        norm.step(n)
    squares[...] = norm.last()
    for l, part in parts:
        net.sent(l, l, part)
    sums.sent()
    norm.sent()


def reduce_all(grads, small):
    whole = pl.BlockSpec(memory_space=pltpu.VMEM)
    count = 2 * LAYERS
    dma = pltpu.SemaphoreType.DMA
    return pl.pallas_call(
        reduce_kernel,
        name="reduce",
        out_shape=(
            jax.ShapeDtypeStruct((LAYERS, PACK, D), WIDE),
            jax.ShapeDtypeStruct((SMALL, D), WIDE),
            jax.ShapeDtypeStruct((8, D), WIDE),
        ),
        in_specs=[pl.BlockSpec(memory_space=pl.ANY), whole],
        out_specs=(whole,) * 3,
        scratch_shapes=[pltpu.VMEM((LAYERS, NZ, NR, PACK, D), LOWER)]
        + [pltpu.VMEM((LAYERS,) + shape, LOWER) for shape in REDUCE_SHAPES.values()]
        + [dma((count, Reduce.COPIES)), dma((count, Reduce.COPIES)), dma((count,))]
        + [pltpu.VMEM((4, SMALL, D), WIDE), pltpu.VMEM((6, SMALL, D), WIDE), dma((6,)), dma((6,))]
        + [pltpu.VMEM((4, 8, D), WIDE), pltpu.VMEM((6, 8, D), WIDE), dma((6,)), dma((6,))],
        compiler_params=pltpu.CompilerParams(
            collective_id=1, has_side_effects=True, vmem_limit_bytes=56 * 1024 * 1024
        ),
        cost_estimate=pl.CostEstimate(flops=0, bytes_accessed=4 * 10**7, transcendentals=0),
    )(grads, small)


def adam_parts(weight, grad, first, second, rate):
    first = BETA_ONE * first + (1.0 - BETA_ONE) * grad
    second = BETA_TWO * second + (1.0 - BETA_TWO) * grad * grad
    fix_one = 1.0 - BETA_ONE**STEP
    fix_two = 1.0 - BETA_TWO**STEP
    fresh = weight - rate * (
        first / fix_one / (jnp.sqrt(second / fix_two) + ADAM_EPS) + DECAY * weight
    )
    return fresh, first, second


def adam_kernel(*refs):
    shard, small_grad, squares, groups, log_temp = refs[:5]
    small, small_first, small_second, bias, bias_first, bias_second = refs[5:11]
    mats, firsts, seconds = refs[11:15], refs[15:19], refs[19:23]
    totals, norm, next_temp, s_next, s_first, s_second, b_next, b_first, b_second = refs[23:32]
    m_next, m_copy, m_first, m_second = refs[32:36], refs[36:40], refs[40:44], refs[44:48]
    l = pl.program_id(0)
    extra = small_grad[NROWS : NROWS + 3, 0:128]
    lane = iota((1, 128), 1)
    bias_mean = jnp.where(lane < A, extra[1:2], 0.0)
    bias_spread = jnp.where(lane < A, extra[2:3], 0.0)

    def all_sum(v):
        return jnp.sum(jnp.sum(v, 0, keepdims=True), 1, keepdims=True)

    grads = small_grad[0:NROWS, :]
    square = (
        all_sum(squares[0:1, :])
        + all_sum(grads * grads)
        + all_sum(bias_mean * bias_mean)
        + all_sum(bias_spread * bias_spread)
    )
    length = jnp.sqrt(square)
    clip = jnp.minimum(1.0, CLIP / (length + 1e-06))

    def rate_of(kind):
        group = jnp.full((1, 1), groups[l, kind], jnp.int32).astype(WIDE)
        return LEARN * jnp.exp2(-group)

    def update(kind, rows, cols, grad):
        at = (0, rows, cols)
        fresh, first, second = adam_parts(
            mats[kind][at], clip * grad, firsts[kind][at], seconds[kind][at], rate_of(kind)
        )
        m_next[kind][at] = fresh
        m_copy[kind][at] = fresh.astype(LOWER)
        m_first[kind][at] = first
        m_second[kind][at] = second

    every = slice(0, 16)
    for j in range(3):
        update(0, every, slice(j * D, (j + 1) * D), shard[0, 16 * j : 16 * j + 16, :])
    update(1, every, slice(0, D), shard[0, 48:64, :])
    for j in range(4):
        update(2, every, slice(j * D, (j + 1) * D), shard[0, 64 + 16 * j : 80 + 16 * j, :])
    update(3, slice(0, 64), slice(0, D), shard[0, 128:192, :])

    @pl.when(l == 0)
    def _():
        s_next[...], s_first[...], s_second[...] = adam_parts(
            small[...], clip * grads, small_first[...], small_second[...], LEARN
        )

        def scalar(v, n):
            return jnp.sum(jnp.where(lane == n, v, 0.0))

        def row(ref):
            v = jnp.zeros((1, 128), WIDE)
            for n in range(2 * A):
                v = jnp.where(lane == n, ref[n], v)
            return v

        grad = bias_mean + pltpu.roll(bias_spread, A, 1)
        results = adam_parts(row(bias), clip * grad, row(bias_first), row(bias_second), LEARN)
        for ref, result in zip((b_next, b_first, b_second), results):
            for n in range(2 * A):
                ref[n] = scalar(result, n)
        sums = extra[0:1]
        for n in range(3):
            totals[n] = scalar(sums, n)
        norm[0] = jnp.sum(length)
        logs = jnp.full((1, 1), log_temp[0], WIDE)
        ratio = jnp.full((1, 1), scalar(sums, 1), WIDE) / jnp.full((1, 1), scalar(sums, 2), WIDE)
        next_temp[0] = jnp.sum(logs - TEMP_RATE * jnp.exp(logs) * (ratio + A))


def adam_all(shard, small_grad, squares, groups, log_temp, smalls, biases, mats, firsts, seconds):
    scalars = pl.BlockSpec(memory_space=pltpu.SMEM)

    def fixed(array):
        return pl.BlockSpec(array.shape, lambda l: (0,) * array.ndim)

    def layer(array):
        return pl.BlockSpec((1,) + array.shape[1:], lambda l: (l, 0, 0))

    def like(array, dtype=WIDE):
        return jax.ShapeDtypeStruct(array.shape, dtype)

    stacks = list(mats) + list(firsts) + list(seconds)
    small, bias = smalls[0], biases[0]
    return pl.pallas_call(
        adam_kernel,
        name="adam",
        grid=(LAYERS,),
        out_shape=(
            (jax.ShapeDtypeStruct((3,), WIDE),)
            + (jax.ShapeDtypeStruct((1,), WIDE),) * 2
            + (like(small),) * 3
            + (like(bias),) * 3
            + tuple(like(m) for m in mats)
            + tuple(like(m, LOWER) for m in mats)
            + tuple(like(m) for m in mats) * 2
        ),
        in_specs=[layer(shard), fixed(small_grad), fixed(squares), scalars, scalars]
        + [fixed(small)] * 3
        + [scalars] * 3
        + [layer(m) for m in stacks],
        out_specs=(scalars,) * 3
        + (fixed(small),) * 3
        + (scalars,) * 3
        + tuple(layer(m) for m in mats) * 4,
        compiler_params=pltpu.CompilerParams(vmem_limit_bytes=40 * 1024 * 1024),
        cost_estimate=pl.CostEstimate(flops=10**7, bytes_accessed=8 * 10**6, transcendentals=10**6),
    )(shard, small_grad, squares, groups, log_temp, *smalls, *biases, *stacks)


def gather_packed(mats, axes, count):
    group = count // BLOCKS
    pieces = []
    for mat in mats:
        rows, wide = mat.shape[1], mat.shape[2] // D
        piece = mat.astype(LOWER).reshape(LAYERS, rows, wide, D)
        piece = lax.all_gather(piece, axes, axis=1, tiled=True)
        piece = piece.reshape(LAYERS, BLOCKS, group * rows, wide, D).transpose(0, 1, 3, 2, 4)
        pieces.append(piece.reshape(LAYERS, BLOCKS, wide * group * rows, D))
    return jnp.concatenate(pieces, 2).reshape(LAYERS, BLOCKS // 8, 8, PACK, D)


def scatter_packed(grads, mats, axes):
    order = [owner_place(i) for i in range(BLOCKS)]
    grads = grads.reshape(LAYERS, BLOCKS, PACK, D)[:, jnp.array(order)].astype(WIDE)
    results, first = [], 0
    for mat in mats:
        rows, wide = mat.shape[1], mat.shape[2] // D
        total = lax.psum(1, axes) * rows
        deep = total // BLOCKS
        piece = grads[:, :, first : first + wide * deep]
        first += wide * deep
        piece = piece.reshape(LAYERS, BLOCKS, wide, deep, D).transpose(0, 1, 3, 2, 4)
        piece = piece.reshape(LAYERS, total, wide * D)
        results.append(lax.psum_scatter(piece, axes, scatter_dimension=1, tiled=True))
    return results


def local(
    buf_states,
    buf_actions,
    buf_returns,
    window_starts,
    window_repeats,
    valid_steps,
    matrix_groups,
    log_temp,
    small_rows,
    head_bias,
    qkv_weight,
    out_weight,
    up_weight,
    down_weight,
    small_first,
    bias_first,
    qkv_first,
    out_first,
    up_first,
    down_first,
    small_second,
    bias_second,
    qkv_second,
    out_second,
    up_second,
    down_second,
):
    axes = ("dp", "fsdp")
    mats = (qkv_weight, out_weight, up_weight, down_weight)
    firsts = (qkv_first, out_first, up_first, down_first)
    seconds = (qkv_second, out_second, up_second, down_second)
    meta, buf = small_inputs(
        buf_states, buf_actions, buf_returns, window_starts, window_repeats, valid_steps
    )
    if FF // down_weight.shape[1] == BLOCKS and lax.psum(1, "fsdp") == NX * NC:
        packed = gather_all(mats)
        grads, small = compute(meta, buf, small_rows, head_bias, log_temp, packed)
        shard, small, squares = reduce_all(grads, small)
        return adam_all(
            shard,
            small,
            squares,
            matrix_groups,
            log_temp,
            (small_rows, small_first, small_second),
            (head_bias, bias_first, bias_second),
            mats,
            firsts,
            seconds,
        )
    packed = gather_packed(mats, axes, FF // down_weight.shape[1])
    grads, small = compute(meta, buf, small_rows, head_bias, log_temp, packed)
    big = scatter_packed(grads, mats, axes)
    small = lax.psum(small, axes)
    small_grad, totals = small[:NROWS], small[NROWS, :3]
    bias_grad = jnp.concatenate([small[NROWS + 1, :A], small[NROWS + 2, :A]])
    square = sum((jnp.sum(piece * piece) for piece in big))
    square = (
        lax.psum(square, axes) + jnp.sum(small_grad * small_grad) + jnp.sum(bias_grad * bias_grad)
    )
    grad_norm = jnp.sqrt(square)
    clip = jnp.minimum(1.0, CLIP / (grad_norm + 1e-06))
    rates = LEARN * jnp.exp2(-matrix_groups.astype(WIDE))
    results = [
        adam_parts(
            mats[kind], clip * big[kind], firsts[kind], seconds[kind], rates[:, kind][:, None, None]
        )
        for kind in range(4)
    ]
    small_new = adam_parts(small_rows, clip * small_grad, small_first, small_second, LEARN)
    bias_new = adam_parts(head_bias, clip * bias_grad, bias_first, bias_second, LEARN)
    next_temp = log_temp - TEMP_RATE * jnp.exp(log_temp) * (totals[1] / totals[2] + A)
    return (
        (totals, grad_norm[None], next_temp)
        + small_new
        + bias_new
        + tuple(r[0] for r in results)
        + tuple(r[0].astype(LOWER) for r in results)
        + tuple(r[1] for r in results)
        + tuple(r[2] for r in results)
    )


def solution(mesh):
    rows = P(("dp", "fsdp"), None)
    vector = P(("dp", "fsdp"))
    stack = P(None, ("dp", "fsdp"), None)
    same = P()
    in_specs = (
        (rows, rows, vector, vector, vector, rows)
        + (same,) * 4
        + (stack,) * 4
        + (same,) * 2
        + (stack,) * 4
        + (same,) * 2
        + (stack,) * 4
    )
    out_specs = (same,) * 9 + (stack,) * 16
    return jax.shard_map(local, mesh=mesh, in_specs=in_specs, out_specs=out_specs, check_vma=False)
```

```python
import functools
import math

import jax
import jax.numpy as jnp
from jax import lax
from jax.experimental import pallas as pl
from jax.experimental.pallas import tpu as pltpu
from jax.sharding import PartitionSpec as P

D = 512
H = 8
HD = 64
FF = 2048
S = 11
A = 3
K = 20
STEP = 10

EPS = 1e-05
CLIP = 1.0
LEARN = 0.03
BETA_ONE = 0.5
BETA_TWO = 0.7
DECAY = 0.01
ADAM_EPS = 1e-08
TEMP_RATE = 0.1
MASKED = -1e30
HALF_LOG_TAU = 0.5 * math.log(2.0 * math.pi)
GELU_C = math.sqrt(2.0 / math.pi)
GELU_A = 0.044715
HIGH = lax.Precision.HIGHEST
LOWER = jnp.bfloat16
WIDE = jnp.float32

LAYERS = 3
WINS = 16
SLOT = 64
ROWS = WINS * SLOT
CHUNK = 256
CHUNKS = ROWS // CHUNK
UNROLL = 2
BLOCKS = 32
PACK = 192
ATTN, FFN = 64, 128
EMB = S + A + 1 + K + 3
FIN = EMB
HEADW = EMB + 2
BASE = EMB + 2 + 2 * A
PER = 9 + FF // D
NROWS = BASE + LAYERS * PER
SMALL = 88
VMEM_BYTES = 64 * 1024 * 1024


def dot(a, b, precision=None):
    return lax.dot_general(
        a, b, (((1,), (0,)), ((), ())), precision=precision, preferred_element_type=WIDE
    )


def dot_nt(a, b, precision=None):
    return lax.dot_general(
        a, b, (((1,), (1,)), ((), ())), precision=precision, preferred_element_type=WIDE
    )


def dot_tn(a, b, precision=None):
    return lax.dot_general(
        a, b, (((0,), (0,)), ((), ())), precision=precision, preferred_element_type=WIDE
    )


def iota(shape, dim):
    return lax.broadcasted_iota(jnp.int32, shape, dim)


def col_sum(v):
    return jnp.sum(v, 0, keepdims=True)


def row_mean(v):
    return jnp.mean(v, -1, keepdims=True)


def norm_parts(x):
    center = x - row_mean(x)
    scale = lax.rsqrt(row_mean(center * center) + EPS)
    return center * scale, scale


def norm_back(xhat, scale, gain, grad):
    scaled = grad * gain
    return scale * (scaled - row_mean(scaled) - xhat * row_mean(scaled * xhat))


def token_rows(at, count):
    row = at + iota((count, 128), 0)
    place = row & (SLOT - 1)
    step = (place * 21846) >> 16
    return row >> 6, step, place - 3 * step, place < 3 * K


def chunk_rows(c):
    return pl.ds(pl.multiple_of(c * CHUNK, CHUNK), CHUNK)


def owner_place(i):
    z, y, x, c = i // 8, (i // 4) % 2, (i // 2) % 2, i % 2
    return 2 * c + x, 4 * y + z


class Kit:
    def __init__(self, **refs):
        self.__dict__.update(refs)

    def row(self, l, k):
        return self.lrows[l, k : k + 1, :]

    def blocks(self, ref, l, first, count, owners):
        places = [owner_place(i) for i in owners]
        return jnp.concatenate([ref[l, a, b, first : first + count, :] for a, b in places], 0)

    def w_qkv(self, l, j):
        return self.blocks(self.wa, l, 16 * j, 16, range(BLOCKS))

    def w_out(self, l):
        return self.blocks(self.wa, l, 48, 16, range(BLOCKS))

    def w_up(self, l, j):
        return self.blocks(self.wf, l, 16 * j, 16, range(BLOCKS))

    def w_down(self, l, j):
        return self.blocks(self.wf, l, 64, 64, range(8 * j, 8 * j + 8))


def slot(l):
    return l % 2


def setup_stage(k):
    k.emb[...] = jnp.zeros_like(k.emb)
    k.emb[0:EMB, :] = k.small[0:EMB, :]
    k.headw[...] = jnp.zeros_like(k.headw)
    k.headw[0, 0:A, :] = k.small[HEADW : HEADW + A, :].astype(LOWER)
    k.headw[1, 0:A, :] = k.small[HEADW + A : HEADW + 2 * A, :].astype(LOWER)
    for l in range(LAYERS):
        k.lrows[l, 0:PER, :] = k.small[BASE + l * PER : BASE + (l + 1) * PER, :]
    k.sgl[...] = jnp.zeros_like(k.sgl)
    k.sgh[...] = jnp.zeros_like(k.sgh)
    k.sgw[...] = jnp.zeros_like(k.sgw)

    meta = k.meta[...].astype(LOWER)

    def chunk(c, carry):
        rows = chunk_rows(c)
        win, step, kind, real = token_rows(c * CHUNK, CHUNK)
        lane = iota((CHUNK, 128), 1)
        tok = dot((lane == win).astype(WIDE).astype(LOWER), meta)
        start, repeat = tok[:, 0:1], tok[:, 1:2]
        valid = jnp.sum(jnp.where(lane == step + 2, tok, 0.0), -1, keepdims=True)
        key = iota((CHUNK, 128), 0) & (SLOT - 1)
        query = lane & (SLOT - 1)
        allowed = (key <= query) & (((valid > 0.5) & real) | (key == query))
        k.bias[rows, :] = jnp.where(allowed, 0.0, MASKED)
        place = start.astype(jnp.int32) + step
        source = ((lane == place) & real).astype(WIDE)
        raw = dot(source, k.buf[...], HIGH)
        mine = (
            ((lane < S) & (kind == 1))
            | ((lane >= S) & (lane < S + A) & (kind == 2))
            | ((lane == S + A) & (kind == 0))
        )
        marks = ((lane == S + A + 1 + step) | (lane == S + A + 1 + K + kind)) & real
        feats = jnp.where(mine, raw, 0.0) + marks.astype(WIDE)
        k.feats[rows, :] = feats
        weight = jnp.where((kind == 1) & real, repeat * valid, 0.0)
        acts = pltpu.roll(raw, 128 - S, 1)
        k.acts[rows, :] = jnp.where(lane < A, acts, jnp.where(lane == A, weight, 0.0))
        k.xs[0, rows, :] = dot(feats, k.emb[...], HIGH)
        return carry

    lax.fori_loop(0, CHUNKS, chunk, 0)


def stack_pair(v, first):
    zero = jnp.zeros_like(v)
    return jnp.concatenate([jnp.where(first, v, zero), jnp.where(first, zero, v)], 0)


def join_pair(v, first):
    return jnp.where(first, v[:SLOT], v[SLOT:])


def window_rows(w):
    return pl.ds(pl.multiple_of(w * SLOT, SLOT), SLOT)


def each_chunk(body):
    def some(n, carry):
        for c in range(UNROLL):
            body(UNROLL * n + c, chunk_rows(UNROLL * n + c))
        return carry

    lax.fori_loop(0, CHUNKS // UNROLL, some, 0)


def each_window(body):
    def pair(n, carry):
        body(2 * n)
        body(2 * n + 1)
        return carry

    lax.fori_loop(0, WINS // 2, pair, 0)


def forward_attn(k, l):
    def chunk(c, rows):
        xhat, _ = norm_parts(k.xs[slot(l), rows, :])
        normed = (xhat * k.row(l, 0) + k.row(l, 1)).astype(LOWER)
        k.normed_t[slot(l), :, rows] = normed.T
        for j in range(3):
            part = dot(normed, k.w_qkv(l, j)) + k.row(l, 4 + j)
            k.qkv[slot(l), rows, j * D : (j + 1) * D] = part.astype(LOWER)

    each_chunk(chunk)
    first = iota((SLOT, 128), 1) < HD

    def window(w):
        rows = window_rows(w)
        bias = k.bias[rows, :]
        scores = []
        for p in range(H // 2):
            at = p * 128
            query = stack_pair(k.qkv[slot(l), rows, at : at + 128] * jnp.asarray(HD**-0.5, LOWER), first)
            scores.append(dot_nt(k.qkv[slot(l), rows, D + at : D + at + 128], query) + bias)
        for p in range(H // 2):
            at = p * 128
            peak = jnp.max(scores[p], 0, keepdims=True)
            expo = jnp.exp(scores[p] - peak)
            total = jnp.sum(expo, 0, keepdims=True)
            probs = (expo * (1.0 / total)).astype(LOWER)
            k.logs[l, w, p : p + 1, :] = peak + jnp.log(total)
            out = dot_tn(probs, k.qkv[slot(l), rows, 2 * D + at : 2 * D + at + 128])
            k.left[rows, at : at + 128] = join_pair(out, first).astype(LOWER)

    each_window(window)


def gelu_parts(h):
    square = h * h
    t = jnp.tanh(GELU_C * (h + GELU_A * h * square))
    return t, square


def forward_ffn(k, l, dest):
    def chunk(c, rows):
        mixed = k.left[rows, :]
        k.mixed_t[slot(l), :, rows] = mixed.T
        mid = k.xs[slot(l), rows, :] + dot(mixed, k.w_out(l)) + k.row(l, 7)
        k.mid[slot(l), rows, :] = mid
        xhat, _ = norm_parts(mid)
        second = (xhat * k.row(l, 2) + k.row(l, 3)).astype(LOWER)
        out = mid + k.row(l, 12)
        for j in range(4):
            h = dot(second, k.w_up(l, j)) + k.row(l, 8 + j)
            t, _ = gelu_parts(h)
            acted = (0.5 * h * (1.0 + t)).astype(LOWER)
            out = out + dot(acted, k.w_down(l, j))
        k.xs[dest, rows, :] = out

    each_chunk(chunk)


def head_stage(k, at):
    gain, bias = k.small[FIN : FIN + 1, :], k.small[FIN + 1 : FIN + 2, :]
    lane = iota((CHUNK, 128), 1)
    keep = lane < A

    def bias_row(first):
        row = jnp.zeros((1, 128), WIDE)
        at = iota((1, 128), 1)
        for a in range(A):
            row = jnp.where(at == a, k.head_bias[first + a], row)
        return row

    bias_mean, bias_spread = bias_row(0), bias_row(A)
    temp = jnp.exp(jnp.full((1, 128), k.log_temp[0], WIDE))

    def chunk(c, carry):
        rows = chunk_rows(c)
        xhat, scale = norm_parts(k.xs[at, rows, :])
        feats = (xhat * gain + bias).astype(LOWER)
        mean = dot_nt(feats, k.headw[0]) + bias_mean
        spread = jnp.tanh(dot_nt(feats, k.headw[1]) + bias_spread)
        acts = k.acts[rows, :]
        weight = acts[:, A : A + 1]
        acts = jnp.where(keep, acts, 0.0)
        target = 0.5 * (jnp.log(1.0 + acts) - jnp.log(1.0 - acts))
        shrink = jnp.exp(-spread)
        zed = (target - mean) * shrink
        terms = 0.5 * zed * zed + spread + HALF_LOG_TAU + jnp.log(1.0 - acts * acts)
        nll = jnp.sum(jnp.where(keep, terms, 0.0), -1, keepdims=True)
        entropy = jnp.sum(jnp.where(keep, spread, 0.0), -1, keepdims=True) + A * (0.5 + HALF_LOG_TAU)
        loss = weight * (nll - temp * entropy)
        sums = jnp.where(lane == 0, loss, jnp.where(lane == 1, weight * entropy, jnp.where(lane == 2, weight, 0.0)))
        d_mean = jnp.where(keep, weight * (-zed * shrink), 0.0).astype(LOWER)
        d_spread = weight * (1.0 - zed * zed - temp) * (1.0 - spread * spread)
        d_spread = jnp.where(keep, d_spread, 0.0).astype(LOWER)
        k.sgh[2:3, 0:128] += col_sum(sums)
        k.sgh[3:4, 0:128] += col_sum(d_mean.astype(WIDE))
        k.sgh[4:5, 0:128] += col_sum(d_spread.astype(WIDE))
        k.sgw[0] += dot_tn(d_mean, feats)[0:8]
        k.sgw[1] += dot_tn(d_spread, feats)[0:8]
        d_feats = dot(d_mean, k.headw[0]) + dot(d_spread, k.headw[1])
        k.sgh[0:1, :] += col_sum(d_feats * xhat)
        k.sgh[1:2, :] += col_sum(d_feats)
        k.xs[at, rows, :] = norm_back(xhat, scale, gain, d_feats)
        return carry

    lax.fori_loop(0, CHUNKS, chunk, 0)


def store_blocks(ref, l, owners, first, count, value):
    value = value.astype(LOWER)
    for n, i in enumerate(owners):
        a, b = owner_place(i)
        ref[l, a, b, first : first + count, :] = value[n * count : (n + 1) * count]


def backward_ffn_start(k, l, grad):
    def before(c, rows):
        d_down = k.xs[grad, rows, :].astype(LOWER)
        k.dout[rows, :] = d_down
        k.sgl[l, 12:13, :] += col_sum(d_down.astype(WIDE))
        xhat, _ = norm_parts(k.mid[slot(l), rows, :])
        second = (xhat * k.row(l, 2) + k.row(l, 3)).astype(LOWER)
        k.left[rows, :] = second
        k.left_t[:, rows] = second.T
        k.dsec[rows, :] = jnp.zeros((CHUNK, D), WIDE)

    each_chunk(before)


def backward_ffn_block(k, l, j):
    def chunk(c, rows):
        h = dot(k.left[rows, :], k.w_up(l, j)) + k.row(l, 8 + j)
        t, square = gelu_parts(h)
        half, over = 0.5 * h, 1.0 + t
        k.act_t[:, rows] = (half * over).astype(LOWER).T
        slope = over * (0.5 + half * (2.0 - over) * (GELU_C + 3.0 * GELU_A * GELU_C * square))
        d_acted = dot_nt(k.dout[rows, :], k.w_down(l, j))
        d_hidden = (d_acted * slope).astype(LOWER)
        k.work[rows, 0:D] = d_hidden
        k.sgl[l, 8 + j : 9 + j, :] += col_sum(d_hidden.astype(WIDE))
        k.dsec[rows, :] += dot_nt(d_hidden, k.w_up(l, j))

    each_chunk(chunk)
    store_blocks(k.wf, l, range(BLOCKS), 16 * j, 16, dot(k.left_t[...], k.work[:, 0:D]))
    store_blocks(k.wf, l, range(8 * j, 8 * j + 8), 64, 64, dot(k.act_t[...], k.dout[...]))


def backward_ffn_end(k, l, grad):
    def after(c, rows):
        xhat, scale = norm_parts(k.mid[slot(l), rows, :])
        d_second = k.dsec[rows, :]
        k.sgl[l, 2:3, :] += col_sum(d_second * xhat)
        k.sgl[l, 3:4, :] += col_sum(d_second)
        k.xs[grad, rows, :] += norm_back(xhat, scale, k.row(l, 2), d_second)

    each_chunk(after)


def backward_attn(k, l, grad):
    def before(c, rows):
        d_branch = k.xs[grad, rows, :].astype(LOWER)
        k.left[rows, :] = d_branch
        k.sgl[l, 7:8, :] += col_sum(d_branch.astype(WIDE))
        k.dout[rows, :] = dot_nt(d_branch, k.w_out(l)).astype(LOWER)

    each_chunk(before)
    store_blocks(k.wa, l + 1, range(BLOCKS), 48, 16, dot(k.mixed_t[slot(l)], k.left[...]))
    first = iota((SLOT, 128), 1) < HD
    scale = HD**-0.5

    def window(w):
        rows = window_rows(w)
        bias = k.bias[rows, :]
        for p in range(H // 2):
            at = p * 128
            query = stack_pair(k.qkv[slot(l), rows, at : at + 128] * jnp.asarray(scale, LOWER), first)
            keyed = k.qkv[slot(l), rows, D + at : D + at + 128]
            values = k.qkv[slot(l), rows, 2 * D + at : 2 * D + at + 128]
            d_mixed = stack_pair(k.dout[rows, at : at + 128], first)
            probs = jnp.exp(dot_nt(keyed, query) + bias - k.logs[l, w, p : p + 1, :])
            d_probs = dot_nt(values, d_mixed)
            d_values = dot(probs.astype(LOWER), d_mixed)
            inner = probs * d_probs
            d_scores = (inner - probs * jnp.sum(inner, 0, keepdims=True)).astype(LOWER)
            d_keyed = dot(d_scores, query)
            d_query = join_pair(dot_tn(d_scores, keyed), first) * scale
            k.work[rows, at : at + 128] = d_query.astype(LOWER)
            k.work[rows, D + at : D + at + 128] = d_keyed.astype(LOWER)
            k.work[rows, 2 * D + at : 2 * D + at + 128] = d_values.astype(LOWER)

    each_window(window)
    for j in range(3):
        store_blocks(k.wa, l + 1, range(BLOCKS), 16 * j, 16, dot(k.normed_t[slot(l)], k.work[:, j * D : (j + 1) * D]))


def backward_input(k, l, grad):
    def chunk(c, rows):
        d_normed = jnp.zeros((CHUNK, D), WIDE)
        for j in range(3):
            d_part = k.work[rows, j * D : (j + 1) * D]
            k.sgl[l, 4 + j : 5 + j, :] += col_sum(d_part.astype(WIDE))
            d_normed = d_normed + dot_nt(d_part, k.w_qkv(l, j))
        xhat, scale = norm_parts(k.xs[slot(l), rows, :])
        k.sgl[l, 0:1, :] += col_sum(d_normed * xhat)
        k.sgl[l, 1:2, :] += col_sum(d_normed)
        k.xs[grad, rows, :] += norm_back(xhat, scale, k.row(l, 0), d_normed)

    each_chunk(chunk)


def small_stage(k, out, grad):
    out[...] = jnp.zeros_like(out)
    out[0:EMB, :] = dot_tn(k.feats[...], k.xs[grad], HIGH)[0:EMB]
    out[FIN : FIN + 2, :] = k.sgh[0:2, :]
    out[HEADW : HEADW + A, :] = k.sgw[0, 0:A, :]
    out[HEADW + A : HEADW + 2 * A, :] = k.sgw[1, 0:A, :]
    for l in range(LAYERS):
        out[BASE + l * PER : BASE + (l + 1) * PER, :] = k.sgl[l, 0:PER, :]
    out[NROWS : NROWS + 3, :] = k.sgh[2:5, :]


WORK_SHAPES = dict(
    wa=((LAYERS + 1, 4, 8, ATTN, D), LOWER),
    wf=((LAYERS, 4, 8, FFN, D), LOWER),
    xs=((3, ROWS, D), WIDE),
    mid=((2, ROWS, D), WIDE),
    qkv=((2, ROWS, 3 * D), LOWER),
    normed_t=((2, D, ROWS), LOWER),
    mixed_t=((2, D, ROWS), LOWER),
    logs=((LAYERS, WINS, 8, 128), WIDE),
    work=((ROWS, 3 * D), LOWER),
    left=((ROWS, D), LOWER),
    left_t=((D, ROWS), LOWER),
    act_t=((D, ROWS), LOWER),
    dout=((ROWS, D), LOWER),
    dsec=((ROWS, D), WIDE),
    feats=((ROWS, 128), WIDE),
    acts=((ROWS, 128), WIDE),
    bias=((ROWS, 128), WIDE),
    emb=((128, D), WIDE),
    headw=((2, 128, D), LOWER),
    lrows=((LAYERS, 16, D), WIDE),
    sgl=((LAYERS, 16, D), WIDE),
    sgh=((8, D), WIDE),
    sgw=((2, 8, D), WIDE),
)
SAVED = ("xs", "mid", "qkv", "normed_t", "mixed_t")


MESH = pl.DeviceIdType.MESH
NZ, NY, NX, NC = 4, 2, 2, 2
NR = NY * NX * NC
SHARD = PACK
PART = (ATTN, FFN)


class Place:
    def __init__(self):
        dp, fsdp = lax.axis_index("dp"), lax.axis_index("fsdp")
        self.z, self.y = dp // NY, dp % NY
        self.x, self.c = fsdp // NC, fsdp % NC
        self.a, self.b = 2 * self.c + self.x, 4 * self.y + self.z
        self.to_x = (dp, (1 - self.x) * NC + self.c)
        self.to_y = (self.z * NY + 1 - self.y, fsdp)
        self.to_c = (dp, self.x * NC + 1 - self.c)
        self.to_z = [(((self.z + d) % NZ) * NY + self.y, fsdp) for d in range(1, NZ)]
        self.partners = [self.to_c, self.to_x, self.to_y] + self.to_z

    def barrier(self):
        sem = pltpu.get_barrier_semaphore()
        for partner in self.partners:
            pl.semaphore_signal(sem, inc=1, device_id=partner, device_id_type=MESH)
        pl.semaphore_wait(sem, len(self.partners))


def remote(src, dst, send, recv, to):
    return pltpu.make_async_remote_copy(
        src_ref=src, dst_ref=dst, send_sem=send, recv_sem=recv, device_id=to, device_id_type=MESH
    )


class Gather:
    COPIES = 11

    def __init__(self, place, weights, send, recv):
        self.at, self.weights, self.send, self.recv = place, weights, send, recv

    def copy(self, l, part, n):
        at, count = self.at, PART[part]
        half = count // 2
        a, b, rows, to = at.a, pl.ds(4 * at.y, 4), pl.ds(0, count), at.to_c
        if n < 3:
            b, to = at.b, at.to_z[n]
        elif n < 5:
            to = (at.to_x, at.to_y)[n - 3]
        if n in (6, 8, 10):
            a = 2 * at.c + 1 - at.x
        if n in (7, 9, 10):
            b = pl.ds(4 * (1 - at.y), 4)
        if n in (6, 7):
            rows, to = pl.ds((n - 6) * half, half), (at.to_y, at.to_x)[n - 6]
        ref = self.weights[part].at[l, a, b, rows, :]
        q = 2 * l + part
        return remote(ref, ref, self.send.at[q, n], self.recv.at[q, n], to)

    def start(self, l, part, *ns):
        for n in ns:
            self.copy(l, part, n).start()

    def wait(self, l, part, *ns):
        for n in ns:
            self.copy(l, part, n).wait_recv()

    def first(self, l, part):
        self.start(l, part, 0, 1, 2)

    def second(self, l, part):
        self.wait(l, part, 0, 1, 2)
        self.start(l, part, 3, 4, 5)

    def third(self, l, part):
        self.wait(l, part, 3)
        self.start(l, part, 6, 8)
        self.wait(l, part, 4)
        self.start(l, part, 7, 9)

    def fourth(self, l, part):
        self.wait(l, part, 6, 7)
        self.start(l, part, 10)

    def last(self, l, part):
        self.wait(l, part, 5, 8, 9, 10)

    def sent(self, l, part):
        for n in range(self.COPIES):
            self.copy(l, part, n).wait_send()


class Reduce:
    COPIES = 8

    def __init__(self, place, grads, landing, send, recv, credit):
        self.at, self.grads, self.landing = place, grads, landing
        self.send, self.recv, self.credit = send, recv, credit

    def refs(self, l, part):
        grads = self.grads[part].at[l + 1 - part]
        r0, r1a, r1b, r2, r3 = self.landing[part]
        return grads, r0, r1a, r1b, r2, r3

    def copy(self, l, part, n):
        at, half = self.at, PART[part] // 2
        g, r0, r1a, r1b, r2, r3 = self.refs(l, part)
        top, low, other = pl.ds(0, half), pl.ds(half, half), pl.ds(4 * (1 - at.y), 4)
        if n == 0:
            src, dst, to = g.at[pl.ds(2 * (1 - at.c), 2)], r0, at.to_c
        elif n == 1:
            src, dst, to = r0.at[1 - at.x, :, top, :], r1a, at.to_x
        elif n == 2:
            src, dst, to = r0.at[:, other, low, :], r1b, at.to_y
        elif n == 3:
            src, dst, to = r1a.at[other], r2.at[:, top, :], at.to_y
        elif n == 4:
            src, dst, to = r1b.at[1 - at.x], r2.at[:, low, :], at.to_x
        else:
            src, dst, to = r2.at[(at.z + n - 4) % NZ], r3.at[n - 5], at.to_z[n - 5]
        q = 2 * l + part
        return remote(src, dst, self.send.at[q, n], self.recv.at[q, n], to)

    def may_send(self, l, part, *partners):
        @pl.when(l < LAYERS - 1)
        def _():
            for n in partners:
                pl.semaphore_wait(self.credit.at[part, n], 1)

    def start(self, l, part):
        self.may_send(l, part, 0)
        self.copy(l, part, 0).start()

    def first(self, l, part):
        at, half = self.at, PART[part] // 2
        g, r0, _, _, _, _ = self.refs(l, part)
        top, low = pl.ds(0, half), pl.ds(half, half)
        self.copy(l, part, 0).wait_recv()

        def along_x(n, carry):
            x = 1 - at.x
            total = g[2 * at.c + x, n, top].astype(WIDE) + r0[x, n, top].astype(WIDE)
            r0[x, n, top] = total.astype(LOWER)
            return carry

        def along_y(n, carry):
            x, b = n // 4, 4 * (1 - at.y) + n % 4
            total = g[2 * at.c + x, b, low].astype(WIDE) + r0[x, b, low].astype(WIDE)
            r0[x, b, low] = total.astype(LOWER)
            return carry

        lax.fori_loop(0, 8, along_x, 0)
        self.may_send(l, part, 1, 2)
        self.copy(l, part, 1).start()
        lax.fori_loop(0, 8, along_y, 0)
        self.copy(l, part, 2).start()

    def second(self, l, part):
        at, half = self.at, PART[part] // 2
        g, r0, r1a, r1b, _, _ = self.refs(l, part)
        top, low = pl.ds(0, half), pl.ds(half, half)

        def along_y(n, carry):
            b = 4 * (1 - at.y) + n
            total = g[at.a, b, top].astype(WIDE) + r0[at.x, b, top].astype(WIDE)
            r1a[b] = (total + r1a[b].astype(WIDE)).astype(LOWER)
            return carry

        def along_x(n, carry):
            x, b = 1 - at.x, 4 * at.y + n
            total = g[2 * at.c + x, b, low].astype(WIDE) + r0[x, b, low].astype(WIDE)
            r1b[x, n] = (total + r1b[x, n].astype(WIDE)).astype(LOWER)
            return carry

        self.copy(l, part, 1).wait_recv()
        lax.fori_loop(0, NZ, along_y, 0)
        self.copy(l, part, 3).start()
        self.copy(l, part, 2).wait_recv()
        lax.fori_loop(0, NZ, along_x, 0)
        self.copy(l, part, 4).start()

    def chip_sums(self, l, part, z):
        at, half = self.at, PART[part] // 2
        g, r0, r1a, r1b, r2, _ = self.refs(l, part)
        top, low, b = pl.ds(0, half), pl.ds(half, half), 4 * at.y + z
        upper = g[at.a, b, top].astype(WIDE) + r0[at.x, b, top].astype(WIDE)
        lower = g[at.a, b, low].astype(WIDE) + r0[at.x, b, low].astype(WIDE)
        return (
            upper + r1a[b].astype(WIDE) + r2[z, top].astype(WIDE),
            lower + r1b[at.x, z].astype(WIDE) + r2[z, low].astype(WIDE),
        )

    def third(self, l, part):
        half = PART[part] // 2
        r2 = self.landing[part][3]
        for n in (3, 4):
            self.copy(l, part, n).wait_recv()
        self.may_send(l, part, 3, 4, 5)
        for n in range(3):
            z = (self.at.z + n + 1) % NZ
            upper, lower = self.chip_sums(l, part, z)
            r2[z, pl.ds(0, half)] = upper.astype(LOWER)
            r2[z, pl.ds(half, half)] = lower.astype(LOWER)
            self.copy(l, part, 5 + n).start()

    def last(self, l, part, out, squares):
        half, row = PART[part] // 2, (0, ATTN)[part]
        r3 = self.landing[part][4]
        upper, lower = self.chip_sums(l, part, self.at.z)
        for n in range(3):
            self.copy(l, part, 5 + n).wait_recv()
            upper = upper + r3[n, pl.ds(0, half)].astype(WIDE)
            lower = lower + r3[n, pl.ds(half, half)].astype(WIDE)
        out[l, row : row + half, :] = upper
        out[l, row + half : row + 2 * half, :] = lower
        squares[0:1, :] += col_sum(upper * upper) + col_sum(lower * lower)
        for n in range(self.COPIES):
            self.copy(l, part, n).wait_send()

        @pl.when(l > 0)
        def _():
            for n, to in zip((0, 1, 2, 5, 4, 3), self.at.partners):
                pl.semaphore_signal(
                    self.credit.at[part, n], inc=1, device_id=to, device_id_type=MESH
                )


class Total:
    COPIES = 6

    def __init__(self, place, own, got, send, recv):
        self.at, self.own, self.got, self.send, self.recv = place, own, got, send, recv

    def copy(self, n):
        src = self.own.at[min(n, 3)]
        return remote(src, self.got.at[n], self.send.at[n], self.recv.at[n], self.at.partners[n])

    def start(self):
        self.copy(0).start()

    def step(self, n):
        self.copy(n).wait_recv()
        self.own[n + 1] = self.own[n] + self.got[n]
        for m in ((1,), (2,), (3, 4, 5))[n]:
            self.copy(m).start()

    def last(self):
        for m in (3, 4, 5):
            self.copy(m).wait_recv()
        total = None
        for z in range(NZ):
            term = self.own[3]
            for n in range(3):
                from_z = (self.at.z + NZ - 1 - n) % NZ
                term = jnp.where(from_z == z, self.got[3 + n], term)
            total = term if total is None else total + term
        return total

    def sent(self):
        for n in range(self.COPIES):
            self.copy(n).wait_send()


def landing_shapes(count):
    half = count // 2
    return [
        (NX, 8, count, D),
        (8, half, D),
        (NX, NZ, half, D),
        (NZ, count, D),
        (3, count, D),
    ]


def stage_rows(qkv, out, up, down, l):
    return (
        [(qkv.at[l, :, pl.ds(j * D, D)], 16 * j, 16) for j in range(3)]
        + [(out.at[l], 48, 16)]
        + [(up.at[l, :, pl.ds(j * D, D)], 64 + 16 * j, 16) for j in range(4)]
        + [(down.at[l], 128, 64)]
    )


def train_kernel(refs, alone):
    k = Kit(**refs)

    def saved(back):
        copies = []
        for n, name in enumerate(SAVED):
            here, there = refs[name].at[0], refs["save_" + name]
            src, dst = (there, here) if back else (here, there)
            copies.append(pltpu.make_async_copy(src, dst, k.save_sem.at[n]))
        return copies

    parts = [(l, part) for l in range(LAYERS) for part in (0, 1)]
    weights = (k.wa, k.wf)
    if alone:
        loads = [
            pltpu.make_async_copy(ref, weights[part].at[l], k.load_sem.at[2 * l + part])
            for l, part in parts
            for ref in [(k.all_a, k.all_f)[part].at[l]]
        ]
        stores = [
            pltpu.make_async_copy(
                weights[part].at[l + 1 - part],
                (k.grad_a, k.grad_f)[part].at[l],
                k.load_sem.at[2 * l + part],
            )
            for l, part in parts
        ]
        for copy in loads:
            copy.start()
    else:
        place = Place()
        gather = Gather(place, weights, k.gather_send, k.gather_recv)
        reduce = Reduce(
            place, weights, (k.land_a, k.land_f), k.reduce_send, k.reduce_recv, k.credit
        )
        sums = Total(place, k.sum_own, k.sum_got, k.sum_send, k.sum_recv)
        norm = Total(place, k.norm_own, k.norm_got, k.norm_send, k.norm_recv)
        staged = []
        for l in range(LAYERS):
            for n, (src, row, count) in enumerate(stage_rows(k.qkv_w, k.out_w, k.up_w, k.down_w, l)):
                dst = k.dsec.at[pl.ds(l * PACK + row, count), :]
                staged.append(pltpu.make_async_copy(src, dst, k.stage_sem.at[l, n]))
        for copy in staged:
            copy.start()
        place.barrier()
        for l in range(LAYERS):
            for copy in staged[9 * l : 9 * l + 9]:
                copy.wait()
            row = l * PACK
            k.wa[l, place.a, place.b] = k.dsec[row : row + ATTN, :].astype(LOWER)
            gather.first(l, 0)
            k.wf[l, place.a, place.b] = k.dsec[row + ATTN : row + PACK, :].astype(LOWER)
            if l < LAYERS - 1:
                gather.first(l, 1)
        k.squares_sum[...] = jnp.zeros_like(k.squares_sum)

    setup_stage(k)
    if not alone:
        gather.second(0, 0)
        gather.second(0, 1)
        gather.third(0, 0)
        gather.second(1, 0)
        gather.third(0, 1)
        gather.fourth(0, 0)

    def forward(l, carry):
        def ahead(n, *stages):
            for stage, part in stages:

                @pl.when(l + n < LAYERS)
                def _(stage=stage, part=part):
                    stage(l + n, part)

        if alone:
            pltpu.make_async_copy(k.all_a.at[l], k.wa.at[l], k.load_sem.at[2 * l]).wait()
        else:
            ahead(1, (gather.second, 1))
            ahead(2, (gather.first, 1))
            ahead(1, (gather.third, 0))
            gather.fourth(l, 1)
            gather.last(l, 0)
        forward_attn(k, l)

        @pl.when(l == 1)
        def _():
            for copy in saved(False):
                copy.wait()

        if alone:
            pltpu.make_async_copy(k.all_f.at[l], k.wf.at[l], k.load_sem.at[2 * l + 1]).wait()
        else:
            ahead(2, (gather.second, 0))
            ahead(1, (gather.third, 1), (gather.fourth, 0))
            gather.last(l, 1)
        forward_ffn(k, l, (l + 1) % 2 + l // 2)

        @pl.when(l == 0)
        def _():
            for copy in saved(False):
                copy.start()

        return carry

    lax.fori_loop(0, LAYERS, forward, 0)
    if not alone:
        for l, part in parts:
            gather.sent(l, part)
    grad = 2
    head_stage(k, grad)

    def backward(n, carry):
        l = LAYERS - 1 - n

        def behind(*stages):
            if alone:
                return

            @pl.when(n > 0)
            def _():
                for stage, part, *more in stages:
                    stage(l + 1, part, *more)

        def now(*stages):
            if not alone:
                for stage, part in stages:
                    stage(l, part)

        finish = () if alone else (k.shard, k.squares_sum)

        @pl.when(n == 2)
        def _():
            for copy in saved(True):
                copy.wait()

        backward_ffn_start(k, l, grad)
        backward_ffn_block(k, l, 0)
        backward_ffn_block(k, l, 1)
        if not alone:
            behind((reduce.third, 1), (reduce.second, 0))
        backward_ffn_block(k, l, 2)
        backward_ffn_block(k, l, 3)
        if not alone:
            behind((reduce.last, 1, *finish), (reduce.third, 0))
            now((reduce.start, 1))
        backward_ffn_end(k, l, grad)
        backward_attn(k, l, grad)
        if not alone:
            behind((reduce.last, 0, *finish))
            now((reduce.first, 1), (reduce.start, 0))
        backward_input(k, l, grad)

        @pl.when(n == 0)
        def _():
            for copy in saved(True):
                copy.start()

        if not alone:
            now((reduce.second, 1), (reduce.first, 0))
        return carry

    lax.fori_loop(0, LAYERS, backward, 0)
    if alone:
        for copy in stores:
            copy.start()
        small_stage(k, k.small_out, grad)
        for copy in stores:
            copy.wait()
        return
    reduce.third(0, 1)
    small_stage(k, k.sum_own.at[0], grad)
    sums.start()
    reduce.second(0, 0)
    reduce.last(0, 1, k.shard, k.squares_sum)
    sums.step(0)
    reduce.third(0, 0)
    sums.step(1)
    reduce.last(0, 0, k.shard, k.squares_sum)
    k.norm_own[0] = k.squares_sum[...]
    norm.start()
    sums.step(2)
    norm.step(0)
    norm.step(1)
    k.small_out[...] = sums.last()
    norm.step(2)
    k.squares[...] = norm.last()
    sums.sent()
    norm.sent()


def train_pass(meta, buf, small, head_bias, log_temp, weights, alone):
    whole = pl.BlockSpec(memory_space=pltpu.VMEM)
    scalars = pl.BlockSpec(memory_space=pltpu.SMEM)
    anywhere = pl.BlockSpec(memory_space=pl.ANY)
    dma = pltpu.SemaphoreType.DMA
    count = 2 * LAYERS
    names = ["meta", "buf", "small", "head_bias", "log_temp"]
    out_shape = {"small_out": ((SMALL, D), WIDE)}
    for name in SAVED:
        shape, dtype = WORK_SHAPES[name]
        out_shape["save_" + name] = (shape[1:], dtype)
    scratch = {name: pltpu.VMEM(*shape) for name, shape in WORK_SHAPES.items()}
    scratch["save_sem"] = dma((len(SAVED),))
    if alone:
        names += ["all_a", "all_f"]
        out_shape["grad_a"] = ((LAYERS, 4, 8, ATTN, D), LOWER)
        out_shape["grad_f"] = ((LAYERS, 4, 8, FFN, D), LOWER)
        scratch["load_sem"] = dma((count,))
    else:
        names += ["qkv_w", "out_w", "up_w", "down_w"]
        out_shape["shard"] = ((LAYERS, PACK, D), WIDE)
        out_shape["squares"] = ((8, D), WIDE)
        for part, name in enumerate("af"):
            for n, shape in enumerate(landing_shapes(PART[part])):
                scratch["land_%s%d" % (name, n)] = pltpu.VMEM(shape, LOWER)
        scratch["stage_sem"] = dma((LAYERS, 9))
        scratch["squares_sum"] = pltpu.VMEM((8, D), WIDE)
        for name, copies in (("gather", Gather.COPIES), ("reduce", Reduce.COPIES)):
            scratch[name + "_send"] = dma((count, copies))
            scratch[name + "_recv"] = dma((count, copies))
        scratch["credit"] = pltpu.SemaphoreType.REGULAR((2, 6))
        for name, rows in (("sum", SMALL), ("norm", 8)):
            scratch[name + "_own"] = pltpu.VMEM((4, rows, D), WIDE)
            scratch[name + "_got"] = pltpu.VMEM((6, rows, D), WIDE)
            scratch[name + "_send"] = dma((6,))
            scratch[name + "_recv"] = dma((6,))
    spaces = dict(head_bias=scalars, log_temp=scalars)
    for name in ("all_a", "all_f", "grad_a", "grad_f", "qkv_w", "out_w", "up_w", "down_w"):
        spaces[name] = anywhere
    for name in SAVED:
        spaces["save_" + name] = anywhere
    every = names + list(out_shape) + list(scratch)

    def kernel(*given):
        refs = dict(zip(every, given))
        for name in "af":
            refs["land_" + name] = [refs.get("land_%s%d" % (name, n)) for n in range(5)]
        train_kernel(refs, alone)

    results = pl.pallas_call(
        kernel,
        name="train_pass",
        out_shape=tuple(jax.ShapeDtypeStruct(*shape) for shape in out_shape.values()),
        in_specs=[spaces.get(name, whole) for name in names],
        out_specs=tuple(spaces.get(name, whole) for name in out_shape),
        scratch_shapes=list(scratch.values()),
        compiler_params=pltpu.CompilerParams(
            vmem_limit_bytes=VMEM_BYTES,
            collective_id=None if alone else 0,
            has_side_effects=not alone,
        ),
        cost_estimate=pl.CostEstimate(
            flops=6 * 10**10, bytes_accessed=4 * 10**7, transcendentals=10**7
        ),
    )(meta, buf, small, head_bias, log_temp, *weights)
    return dict(zip(out_shape, results))


def small_inputs(buf_states, buf_actions, buf_returns, window_starts, window_repeats, valid_steps):
    meta = jnp.concatenate(
        [window_starts[:, None], window_repeats[:, None], valid_steps], 1
    ).astype(WIDE)
    meta = jnp.pad(meta, ((0, 128 - meta.shape[0]), (0, 128 - meta.shape[1])))
    buf = jnp.concatenate([buf_states, buf_actions, buf_returns[:, None]], 1)
    buf = jnp.pad(buf, ((0, 128 - buf.shape[0]), (0, 128 - buf.shape[1])))
    return meta, buf


def adam_parts(weight, grad, first, second, rate):
    first = BETA_ONE * first + (1.0 - BETA_ONE) * grad
    second = BETA_TWO * second + (1.0 - BETA_TWO) * grad * grad
    fix_one = 1.0 - BETA_ONE**STEP
    fix_two = 1.0 - BETA_TWO**STEP
    fresh = weight - rate * (
        first / fix_one / (jnp.sqrt(second / fix_two) + ADAM_EPS) + DECAY * weight
    )
    return fresh, first, second


def adam_kernel(*refs):
    shard, small_grad, squares, groups, log_temp = refs[:5]
    small, small_first, small_second, bias, bias_first, bias_second = refs[5:11]
    mats, firsts, seconds = refs[11:15], refs[15:19], refs[19:23]
    totals, norm, next_temp, s_next, s_first, s_second, b_next, b_first, b_second = refs[23:32]
    m_next, m_copy, m_first, m_second = refs[32:36], refs[36:40], refs[40:44], refs[44:48]
    l = pl.program_id(0)
    extra = small_grad[NROWS : NROWS + 3, 0:128]
    lane = iota((1, 128), 1)
    bias_mean = jnp.where(lane < A, extra[1:2], 0.0)
    bias_spread = jnp.where(lane < A, extra[2:3], 0.0)

    def all_sum(v):
        return jnp.sum(jnp.sum(v, 0, keepdims=True), 1, keepdims=True)

    grads = small_grad[0:NROWS, :]
    square = (
        all_sum(squares[0:1, :])
        + all_sum(grads * grads)
        + all_sum(bias_mean * bias_mean)
        + all_sum(bias_spread * bias_spread)
    )
    length = jnp.sqrt(square)
    clip = jnp.minimum(1.0, CLIP / (length + 1e-06))

    def rate_of(kind):
        group = jnp.full((1, 1), groups[l, kind], jnp.int32).astype(WIDE)
        return LEARN * jnp.exp2(-group)

    def update(kind, rows, cols, grad):
        at = (0, rows, cols)
        fresh, first, second = adam_parts(
            mats[kind][at], clip * grad, firsts[kind][at], seconds[kind][at], rate_of(kind)
        )
        m_next[kind][at] = fresh
        m_copy[kind][at] = fresh.astype(LOWER)
        m_first[kind][at] = first
        m_second[kind][at] = second

    every = slice(0, 16)
    for j in range(3):
        update(0, every, slice(j * D, (j + 1) * D), shard[0, 16 * j : 16 * j + 16, :])
    update(1, every, slice(0, D), shard[0, 48:64, :])
    for j in range(4):
        update(2, every, slice(j * D, (j + 1) * D), shard[0, 64 + 16 * j : 80 + 16 * j, :])
    update(3, slice(0, 64), slice(0, D), shard[0, 128:192, :])

    @pl.when(l == 0)
    def _():
        s_next[...], s_first[...], s_second[...] = adam_parts(
            small[...], clip * grads, small_first[...], small_second[...], LEARN
        )

        def scalar(v, n):
            return jnp.sum(jnp.where(lane == n, v, 0.0))

        def row(ref):
            v = jnp.zeros((1, 128), WIDE)
            for n in range(2 * A):
                v = jnp.where(lane == n, ref[n], v)
            return v

        grad = bias_mean + pltpu.roll(bias_spread, A, 1)
        results = adam_parts(row(bias), clip * grad, row(bias_first), row(bias_second), LEARN)
        for ref, result in zip((b_next, b_first, b_second), results):
            for n in range(2 * A):
                ref[n] = scalar(result, n)
        sums = extra[0:1]
        for n in range(3):
            totals[n] = scalar(sums, n)
        norm[0] = jnp.sum(length)
        logs = jnp.full((1, 1), log_temp[0], WIDE)
        ratio = jnp.full((1, 1), scalar(sums, 1), WIDE) / jnp.full((1, 1), scalar(sums, 2), WIDE)
        next_temp[0] = jnp.sum(logs - TEMP_RATE * jnp.exp(logs) * (ratio + A))


def adam_all(shard, small_grad, squares, groups, log_temp, smalls, biases, mats, firsts, seconds):
    scalars = pl.BlockSpec(memory_space=pltpu.SMEM)

    def fixed(array):
        return pl.BlockSpec(array.shape, lambda l: (0,) * array.ndim)

    def layer(array):
        return pl.BlockSpec((1,) + array.shape[1:], lambda l: (l, 0, 0))

    def like(array, dtype=WIDE):
        return jax.ShapeDtypeStruct(array.shape, dtype)

    stacks = list(mats) + list(firsts) + list(seconds)
    small, bias = smalls[0], biases[0]
    return pl.pallas_call(
        adam_kernel,
        name="adam",
        grid=(LAYERS,),
        out_shape=(
            (jax.ShapeDtypeStruct((3,), WIDE),)
            + (jax.ShapeDtypeStruct((1,), WIDE),) * 2
            + (like(small),) * 3
            + (like(bias),) * 3
            + tuple(like(m) for m in mats)
            + tuple(like(m, LOWER) for m in mats)
            + tuple(like(m) for m in mats) * 2
        ),
        in_specs=[layer(shard), fixed(small_grad), fixed(squares), scalars, scalars]
        + [fixed(small)] * 3
        + [scalars] * 3
        + [layer(m) for m in stacks],
        out_specs=(scalars,) * 3
        + (fixed(small),) * 3
        + (scalars,) * 3
        + tuple(layer(m) for m in mats) * 4,
        compiler_params=pltpu.CompilerParams(vmem_limit_bytes=40 * 1024 * 1024),
        cost_estimate=pl.CostEstimate(flops=10**7, bytes_accessed=8 * 10**6, transcendentals=10**6),
    )(shard, small_grad, squares, groups, log_temp, *smalls, *biases, *stacks)


def gather_packed(mats, axes, count):
    group = count // BLOCKS
    pieces = []
    for mat in mats:
        rows, wide = mat.shape[1], mat.shape[2] // D
        piece = mat.astype(LOWER).reshape(LAYERS, rows, wide, D)
        piece = lax.all_gather(piece, axes, axis=1, tiled=True)
        piece = piece.reshape(LAYERS, NZ, NY, NX, NC, group * rows, wide, D)
        piece = piece.transpose(0, 4, 3, 2, 1, 6, 5, 7)
        pieces.append(piece.reshape(LAYERS, 4, 8, wide * group * rows, D))
    return jnp.concatenate(pieces[:2], 3), jnp.concatenate(pieces[2:], 3)


def scatter_packed(grads, mats, axes):
    results, first = [], 0
    for n, mat in enumerate(mats):
        rows, wide = mat.shape[1], mat.shape[2] // D
        total = lax.psum(1, axes) * rows
        deep = total // BLOCKS
        first = 0 if n % 2 == 0 else first
        piece = grads[n // 2][:, :, :, first : first + wide * deep].astype(WIDE)
        first += wide * deep
        piece = piece.reshape(LAYERS, NC, NX, NY, NZ, wide, deep, D)
        piece = piece.transpose(0, 4, 3, 2, 1, 6, 5, 7).reshape(LAYERS, total, wide * D)
        results.append(lax.psum_scatter(piece, axes, scatter_dimension=1, tiled=True))
    return results


def local(
    buf_states,
    buf_actions,
    buf_returns,
    window_starts,
    window_repeats,
    valid_steps,
    matrix_groups,
    log_temp,
    small_rows,
    head_bias,
    qkv_weight,
    out_weight,
    up_weight,
    down_weight,
    small_first,
    bias_first,
    qkv_first,
    out_first,
    up_first,
    down_first,
    small_second,
    bias_second,
    qkv_second,
    out_second,
    up_second,
    down_second,
):
    axes = ("dp", "fsdp")
    mats = (qkv_weight, out_weight, up_weight, down_weight)
    firsts = (qkv_first, out_first, up_first, down_first)
    seconds = (qkv_second, out_second, up_second, down_second)
    meta, buf = small_inputs(
        buf_states, buf_actions, buf_returns, window_starts, window_repeats, valid_steps
    )
    pass_inputs = (meta, buf, small_rows, head_bias, log_temp)
    if FF // down_weight.shape[1] == BLOCKS and lax.psum(1, "fsdp") == NX * NC:
        made = train_pass(*pass_inputs, mats, False)
        return adam_all(
            made["shard"],
            made["small_out"],
            made["squares"],
            matrix_groups,
            log_temp,
            (small_rows, small_first, small_second),
            (head_bias, bias_first, bias_second),
            mats,
            firsts,
            seconds,
        )
    packed = gather_packed(mats, axes, FF // down_weight.shape[1])
    made = train_pass(*pass_inputs, packed, True)
    big = scatter_packed((made["grad_a"], made["grad_f"]), mats, axes)
    small = made["small_out"]
    small = lax.psum(small, axes)
    small_grad, totals = small[:NROWS], small[NROWS, :3]
    bias_grad = jnp.concatenate([small[NROWS + 1, :A], small[NROWS + 2, :A]])
    square = sum((jnp.sum(piece * piece) for piece in big))
    square = (
        lax.psum(square, axes) + jnp.sum(small_grad * small_grad) + jnp.sum(bias_grad * bias_grad)
    )
    grad_norm = jnp.sqrt(square)
    clip = jnp.minimum(1.0, CLIP / (grad_norm + 1e-06))
    rates = LEARN * jnp.exp2(-matrix_groups.astype(WIDE))
    results = [
        adam_parts(
            mats[kind], clip * big[kind], firsts[kind], seconds[kind], rates[:, kind][:, None, None]
        )
        for kind in range(4)
    ]
    small_new = adam_parts(small_rows, clip * small_grad, small_first, small_second, LEARN)
    bias_new = adam_parts(head_bias, clip * bias_grad, bias_first, bias_second, LEARN)
    next_temp = log_temp - TEMP_RATE * jnp.exp(log_temp) * (totals[1] / totals[2] + A)
    return (
        (totals, grad_norm[None], next_temp)
        + small_new
        + bias_new
        + tuple(r[0] for r in results)
        + tuple(r[0].astype(LOWER) for r in results)
        + tuple(r[1] for r in results)
        + tuple(r[2] for r in results)
    )


def solution(mesh):
    rows = P(("dp", "fsdp"), None)
    vector = P(("dp", "fsdp"))
    stack = P(None, ("dp", "fsdp"), None)
    same = P()
    in_specs = (
        (rows, rows, vector, vector, vector, rows)
        + (same,) * 4
        + (stack,) * 4
        + (same,) * 2
        + (stack,) * 4
        + (same,) * 2
        + (stack,) * 4
    )
    out_specs = (same,) * 9 + (stack,) * 16
    return jax.shard_map(local, mesh=mesh, in_specs=in_specs, out_specs=out_specs, check_vma=False)
```

```python
import functools
import math

import jax
import jax.numpy as jnp
from jax import lax
from jax.experimental import pallas as pl
from jax.experimental.pallas import tpu as pltpu
from jax.sharding import PartitionSpec as P

D = 512
H = 8
HD = 64
FF = 2048
S = 11
A = 3
K = 20
STEP = 10

EPS = 1e-05
CLIP = 1.0
LEARN = 0.03
BETA_ONE = 0.5
BETA_TWO = 0.7
DECAY = 0.01
ADAM_EPS = 1e-08
TEMP_RATE = 0.1
MASKED = -1e30
HALF_LOG_TAU = 0.5 * math.log(2.0 * math.pi)
GELU_C = math.sqrt(2.0 / math.pi)
GELU_A = 0.044715
HIGH = lax.Precision.HIGHEST
LOWER = jnp.bfloat16
WIDE = jnp.float32

LAYERS = 3
WINS = 16
SLOT = 64
ROWS = WINS * SLOT
CHUNK = 256
CHUNKS = ROWS // CHUNK
UNROLL = 2
BLOCKS = 32
PACK = 192
ATTN, FFN = 64, 128
EMB = S + A + 1 + K + 3
FIN = EMB
HEADW = EMB + 2
BASE = EMB + 2 + 2 * A
PER = 9 + FF // D
NROWS = BASE + LAYERS * PER
SMALL = 88
VMEM_BYTES = 64 * 1024 * 1024


def dot(a, b, precision=None):
    return lax.dot_general(
        a, b, (((1,), (0,)), ((), ())), precision=precision, preferred_element_type=WIDE
    )


def dot_nt(a, b, precision=None):
    return lax.dot_general(
        a, b, (((1,), (1,)), ((), ())), precision=precision, preferred_element_type=WIDE
    )


def dot_tn(a, b, precision=None):
    return lax.dot_general(
        a, b, (((0,), (0,)), ((), ())), precision=precision, preferred_element_type=WIDE
    )


def iota(shape, dim):
    return lax.broadcasted_iota(jnp.int32, shape, dim)


def col_sum(v):
    return jnp.sum(v, 0, keepdims=True)


def row_mean(v):
    return jnp.mean(v, -1, keepdims=True)


def norm_parts(x):
    center = x - row_mean(x)
    scale = lax.rsqrt(row_mean(center * center) + EPS)
    return center * scale, scale


def norm_back(xhat, scale, gain, grad):
    scaled = grad * gain
    return scale * (scaled - row_mean(scaled) - xhat * row_mean(scaled * xhat))


def token_rows(at, count):
    row = at + iota((count, 128), 0)
    place = row & (SLOT - 1)
    step = (place * 21846) >> 16
    return row >> 6, step, place - 3 * step, place < 3 * K


def chunk_rows(c):
    return pl.ds(pl.multiple_of(c * CHUNK, CHUNK), CHUNK)


def owner_place(i):
    z, y, x, c = i // 8, (i // 4) % 2, (i // 2) % 2, i % 2
    return 2 * c + x, 4 * y + z


class Kit:
    def __init__(self, **refs):
        self.__dict__.update(refs)

    def row(self, l, k):
        return self.lrows[l, k : k + 1, :]

    def blocks(self, ref, l, first, count, owners):
        places = [owner_place(i) for i in owners]
        return jnp.concatenate([ref[l, a, b, first : first + count, :] for a, b in places], 0)

    def w_qkv(self, l, j):
        return self.blocks(self.wa, l, 16 * j, 16, range(BLOCKS))

    def w_out(self, l):
        return self.blocks(self.wa, l, 48, 16, range(BLOCKS))

    def w_up(self, l, j):
        return self.blocks(self.wf, l, 16 * j, 16, range(BLOCKS))

    def w_down(self, l, j):
        return self.blocks(self.wf, l, 64, 64, range(8 * j, 8 * j + 8))


def slot(l):
    return l % 2


def setup_stage(k):
    k.emb[...] = jnp.zeros_like(k.emb)
    k.emb[0:EMB, :] = k.small[0:EMB, :]
    k.headw[...] = jnp.zeros_like(k.headw)
    k.headw[0, 0:A, :] = k.small[HEADW : HEADW + A, :].astype(LOWER)
    k.headw[1, 0:A, :] = k.small[HEADW + A : HEADW + 2 * A, :].astype(LOWER)
    for l in range(LAYERS):
        k.lrows[l, 0:PER, :] = k.small[BASE + l * PER : BASE + (l + 1) * PER, :]
    k.sgl[...] = jnp.zeros_like(k.sgl)
    k.sgh[...] = jnp.zeros_like(k.sgh)
    k.sgw[...] = jnp.zeros_like(k.sgw)

    meta = k.meta[...].astype(LOWER)

    def chunk(c, carry):
        rows = chunk_rows(c)
        win, step, kind, real = token_rows(c * CHUNK, CHUNK)
        lane = iota((CHUNK, 128), 1)
        tok = dot((lane == win).astype(WIDE).astype(LOWER), meta)
        start, repeat = tok[:, 0:1], tok[:, 1:2]
        valid = jnp.sum(jnp.where(lane == step + 2, tok, 0.0), -1, keepdims=True)
        key = iota((CHUNK, 128), 0) & (SLOT - 1)
        query = lane & (SLOT - 1)
        allowed = (key <= query) & (((valid > 0.5) & real) | (key == query))
        k.bias[rows, :] = jnp.where(allowed, 0.0, MASKED)
        place = start.astype(jnp.int32) + step
        source = ((lane == place) & real).astype(WIDE)
        raw = dot(source, k.buf[...], HIGH)
        mine = (
            ((lane < S) & (kind == 1))
            | ((lane >= S) & (lane < S + A) & (kind == 2))
            | ((lane == S + A) & (kind == 0))
        )
        marks = ((lane == S + A + 1 + step) | (lane == S + A + 1 + K + kind)) & real
        feats = jnp.where(mine, raw, 0.0) + marks.astype(WIDE)
        k.feats[rows, :] = feats
        weight = jnp.where((kind == 1) & real, repeat * valid, 0.0)
        acts = pltpu.roll(raw, 128 - S, 1)
        k.acts[rows, :] = jnp.where(lane < A, acts, jnp.where(lane == A, weight, 0.0))
        k.xs[0, rows, :] = dot(feats, k.emb[...], HIGH)
        return carry

    lax.fori_loop(0, CHUNKS, chunk, 0)


def stack_pair(v, first):
    zero = jnp.zeros_like(v)
    return jnp.concatenate([jnp.where(first, v, zero), jnp.where(first, zero, v)], 0)


def join_pair(v, first):
    return jnp.where(first, v[:SLOT], v[SLOT:])


def window_rows(w):
    return pl.ds(pl.multiple_of(w * SLOT, SLOT), SLOT)


def each_chunk(body):
    def some(n, carry):
        for c in range(UNROLL):
            body(UNROLL * n + c, chunk_rows(UNROLL * n + c))
        return carry

    lax.fori_loop(0, CHUNKS // UNROLL, some, 0)


def each_window(body):
    def pair(n, carry):
        body(2 * n)
        body(2 * n + 1)
        return carry

    lax.fori_loop(0, WINS // 2, pair, 0)


def forward_attn(k, l):
    def chunk(c, rows):
        xhat, _ = norm_parts(k.xs[slot(l), rows, :])
        normed = (xhat * k.row(l, 0) + k.row(l, 1)).astype(LOWER)
        k.normed_t[slot(l), :, rows] = normed.T
        for j in range(3):
            part = dot(normed, k.w_qkv(l, j)) + k.row(l, 4 + j)
            k.qkv[slot(l), rows, j * D : (j + 1) * D] = part.astype(LOWER)

    each_chunk(chunk)
    first = iota((SLOT, 128), 1) < HD

    def window(w):
        rows = window_rows(w)
        bias = k.bias[rows, :]
        scores = []
        for p in range(H // 2):
            at = p * 128
            query = stack_pair(k.qkv[slot(l), rows, at : at + 128] * jnp.asarray(HD**-0.5, LOWER), first)
            scores.append(dot_nt(k.qkv[slot(l), rows, D + at : D + at + 128], query) + bias)
        for p in range(H // 2):
            at = p * 128
            peak = jnp.max(scores[p], 0, keepdims=True)
            expo = jnp.exp(scores[p] - peak)
            total = jnp.sum(expo, 0, keepdims=True)
            probs = (expo * (1.0 / total)).astype(LOWER)
            k.logs[l, w, p : p + 1, :] = peak + jnp.log(total)
            out = dot_tn(probs, k.qkv[slot(l), rows, 2 * D + at : 2 * D + at + 128])
            k.left[rows, at : at + 128] = join_pair(out, first).astype(LOWER)

    each_window(window)


def gelu_parts(h):
    square = h * h
    t = jnp.tanh(GELU_C * (h + GELU_A * h * square))
    return t, square


def forward_ffn(k, l, dest):
    def chunk(c, rows):
        mixed = k.left[rows, :]
        k.mixed_t[slot(l), :, rows] = mixed.T
        mid = k.xs[slot(l), rows, :] + dot(mixed, k.w_out(l)) + k.row(l, 7)
        k.mid[slot(l), rows, :] = mid
        xhat, _ = norm_parts(mid)
        second = (xhat * k.row(l, 2) + k.row(l, 3)).astype(LOWER)
        out = mid + k.row(l, 12)
        for j in range(4):
            h = dot(second, k.w_up(l, j)) + k.row(l, 8 + j)
            t, _ = gelu_parts(h)
            acted = (0.5 * h * (1.0 + t)).astype(LOWER)
            out = out + dot(acted, k.w_down(l, j))
        k.xs[dest, rows, :] = out

    each_chunk(chunk)


def head_stage(k, at):
    gain, bias = k.small[FIN : FIN + 1, :], k.small[FIN + 1 : FIN + 2, :]
    lane = iota((CHUNK, 128), 1)
    keep = lane < A

    def bias_row(first):
        row = jnp.zeros((1, 128), WIDE)
        at = iota((1, 128), 1)
        for a in range(A):
            row = jnp.where(at == a, k.head_bias[first + a], row)
        return row

    bias_mean, bias_spread = bias_row(0), bias_row(A)
    temp = jnp.exp(jnp.full((1, 128), k.log_temp[0], WIDE))

    def chunk(c, carry):
        rows = chunk_rows(c)
        xhat, scale = norm_parts(k.xs[at, rows, :])
        feats = (xhat * gain + bias).astype(LOWER)
        mean = dot_nt(feats, k.headw[0]) + bias_mean
        spread = jnp.tanh(dot_nt(feats, k.headw[1]) + bias_spread)
        acts = k.acts[rows, :]
        weight = acts[:, A : A + 1]
        acts = jnp.where(keep, acts, 0.0)
        target = 0.5 * (jnp.log(1.0 + acts) - jnp.log(1.0 - acts))
        shrink = jnp.exp(-spread)
        zed = (target - mean) * shrink
        terms = 0.5 * zed * zed + spread + HALF_LOG_TAU + jnp.log(1.0 - acts * acts)
        nll = jnp.sum(jnp.where(keep, terms, 0.0), -1, keepdims=True)
        entropy = jnp.sum(jnp.where(keep, spread, 0.0), -1, keepdims=True) + A * (0.5 + HALF_LOG_TAU)
        loss = weight * (nll - temp * entropy)
        sums = jnp.where(lane == 0, loss, jnp.where(lane == 1, weight * entropy, jnp.where(lane == 2, weight, 0.0)))
        d_mean = jnp.where(keep, weight * (-zed * shrink), 0.0).astype(LOWER)
        d_spread = weight * (1.0 - zed * zed - temp) * (1.0 - spread * spread)
        d_spread = jnp.where(keep, d_spread, 0.0).astype(LOWER)
        k.sgh[2:3, 0:128] += col_sum(sums)
        k.sgh[3:4, 0:128] += col_sum(d_mean.astype(WIDE))
        k.sgh[4:5, 0:128] += col_sum(d_spread.astype(WIDE))
        k.sgw[0] += dot_tn(d_mean, feats)[0:8]
        k.sgw[1] += dot_tn(d_spread, feats)[0:8]
        d_feats = dot(d_mean, k.headw[0]) + dot(d_spread, k.headw[1])
        k.sgh[0:1, :] += col_sum(d_feats * xhat)
        k.sgh[1:2, :] += col_sum(d_feats)
        k.xs[at, rows, :] = norm_back(xhat, scale, gain, d_feats)
        return carry

    lax.fori_loop(0, CHUNKS, chunk, 0)


def store_blocks(ref, l, owners, first, count, value):
    value = value.astype(LOWER)
    for n, i in enumerate(owners):
        a, b = owner_place(i)
        ref[l, a, b, first : first + count, :] = value[n * count : (n + 1) * count]


def backward_ffn_start(k, l, grad):
    def before(c, rows):
        d_down = k.xs[grad, rows, :].astype(LOWER)
        k.dout[rows, :] = d_down
        k.sgl[l, 12:13, :] += col_sum(d_down.astype(WIDE))
        xhat, _ = norm_parts(k.mid[slot(l), rows, :])
        second = (xhat * k.row(l, 2) + k.row(l, 3)).astype(LOWER)
        k.left[rows, :] = second
        k.left_t[:, rows] = second.T
        k.dsec[rows, :] = jnp.zeros((CHUNK, D), WIDE)

    each_chunk(before)


def backward_ffn_block(k, l, j):
    def chunk(c, rows):
        h = dot(k.left[rows, :], k.w_up(l, j)) + k.row(l, 8 + j)
        t, square = gelu_parts(h)
        half, over = 0.5 * h, 1.0 + t
        k.act_t[:, rows] = (half * over).astype(LOWER).T
        slope = over * (0.5 + half * (2.0 - over) * (GELU_C + 3.0 * GELU_A * GELU_C * square))
        d_acted = dot_nt(k.dout[rows, :], k.w_down(l, j))
        d_hidden = (d_acted * slope).astype(LOWER)
        k.work[rows, 0:D] = d_hidden
        k.sgl[l, 8 + j : 9 + j, :] += col_sum(d_hidden.astype(WIDE))
        k.dsec[rows, :] += dot_nt(d_hidden, k.w_up(l, j))

    each_chunk(chunk)
    store_blocks(k.wf, l, range(BLOCKS), 16 * j, 16, dot(k.left_t[...], k.work[:, 0:D]))
    store_blocks(k.wf, l, range(8 * j, 8 * j + 8), 64, 64, dot(k.act_t[...], k.dout[...]))


def backward_ffn_end(k, l, grad):
    def after(c, rows):
        xhat, scale = norm_parts(k.mid[slot(l), rows, :])
        d_second = k.dsec[rows, :]
        k.sgl[l, 2:3, :] += col_sum(d_second * xhat)
        k.sgl[l, 3:4, :] += col_sum(d_second)
        k.xs[grad, rows, :] += norm_back(xhat, scale, k.row(l, 2), d_second)

    each_chunk(after)


def backward_attn(k, l, grad):
    def before(c, rows):
        d_branch = k.xs[grad, rows, :].astype(LOWER)
        k.left[rows, :] = d_branch
        k.sgl[l, 7:8, :] += col_sum(d_branch.astype(WIDE))
        k.dout[rows, :] = dot_nt(d_branch, k.w_out(l)).astype(LOWER)

    each_chunk(before)
    store_blocks(k.wa, l + 1, range(BLOCKS), 48, 16, dot(k.mixed_t[slot(l)], k.left[...]))
    first = iota((SLOT, 128), 1) < HD
    scale = HD**-0.5

    def window(w):
        rows = window_rows(w)
        bias = k.bias[rows, :]
        for p in range(H // 2):
            at = p * 128
            query = stack_pair(k.qkv[slot(l), rows, at : at + 128] * jnp.asarray(scale, LOWER), first)
            keyed = k.qkv[slot(l), rows, D + at : D + at + 128]
            values = k.qkv[slot(l), rows, 2 * D + at : 2 * D + at + 128]
            d_mixed = stack_pair(k.dout[rows, at : at + 128], first)
            probs = jnp.exp(dot_nt(keyed, query) + bias - k.logs[l, w, p : p + 1, :])
            d_probs = dot_nt(values, d_mixed)
            d_values = dot(probs.astype(LOWER), d_mixed)
            inner = probs * d_probs
            d_scores = (inner - probs * jnp.sum(inner, 0, keepdims=True)).astype(LOWER)
            d_keyed = dot(d_scores, query)
            d_query = join_pair(dot_tn(d_scores, keyed), first) * scale
            k.work[rows, at : at + 128] = d_query.astype(LOWER)
            k.work[rows, D + at : D + at + 128] = d_keyed.astype(LOWER)
            k.work[rows, 2 * D + at : 2 * D + at + 128] = d_values.astype(LOWER)

    each_window(window)
    for j in range(3):
        store_blocks(k.wa, l + 1, range(BLOCKS), 16 * j, 16, dot(k.normed_t[slot(l)], k.work[:, j * D : (j + 1) * D]))


def backward_input(k, l, grad):
    def chunk(c, rows):
        d_normed = jnp.zeros((CHUNK, D), WIDE)
        for j in range(3):
            d_part = k.work[rows, j * D : (j + 1) * D]
            k.sgl[l, 4 + j : 5 + j, :] += col_sum(d_part.astype(WIDE))
            d_normed = d_normed + dot_nt(d_part, k.w_qkv(l, j))
        xhat, scale = norm_parts(k.xs[slot(l), rows, :])
        k.sgl[l, 0:1, :] += col_sum(d_normed * xhat)
        k.sgl[l, 1:2, :] += col_sum(d_normed)
        k.xs[grad, rows, :] += norm_back(xhat, scale, k.row(l, 0), d_normed)

    each_chunk(chunk)


def small_stage(k, out, grad):
    out[...] = jnp.zeros_like(out)
    out[0:EMB, :] = dot_tn(k.feats[...], k.xs[grad], HIGH)[0:EMB]
    out[FIN : FIN + 2, :] = k.sgh[0:2, :]
    out[HEADW : HEADW + A, :] = k.sgw[0, 0:A, :]
    out[HEADW + A : HEADW + 2 * A, :] = k.sgw[1, 0:A, :]
    for l in range(LAYERS):
        out[BASE + l * PER : BASE + (l + 1) * PER, :] = k.sgl[l, 0:PER, :]
    out[NROWS : NROWS + 3, :] = k.sgh[2:5, :]


WORK_SHAPES = dict(
    wa=((LAYERS + 1, 4, 8, ATTN, D), LOWER),
    wf=((LAYERS, 4, 8, FFN, D), LOWER),
    xs=((3, ROWS, D), WIDE),
    mid=((2, ROWS, D), WIDE),
    qkv=((2, ROWS, 3 * D), LOWER),
    normed_t=((2, D, ROWS), LOWER),
    mixed_t=((2, D, ROWS), LOWER),
    logs=((LAYERS, WINS, 8, 128), WIDE),
    work=((ROWS, 3 * D), LOWER),
    left=((ROWS, D), LOWER),
    left_t=((D, ROWS), LOWER),
    act_t=((D, ROWS), LOWER),
    dout=((ROWS, D), LOWER),
    dsec=((ROWS, D), WIDE),
    feats=((ROWS, 128), WIDE),
    acts=((ROWS, 128), WIDE),
    bias=((ROWS, 128), WIDE),
    emb=((128, D), WIDE),
    headw=((2, 128, D), LOWER),
    lrows=((LAYERS, 16, D), WIDE),
    sgl=((LAYERS, 16, D), WIDE),
    sgh=((8, D), WIDE),
    sgw=((2, 8, D), WIDE),
)
SAVED = ("xs", "mid", "qkv", "normed_t", "mixed_t")


MESH = pl.DeviceIdType.MESH
NZ, NY, NX, NC = 4, 2, 2, 2
NR = NY * NX * NC
SHARD = PACK
PART = (ATTN, FFN)


class Place:
    def __init__(self):
        dp, fsdp = lax.axis_index("dp"), lax.axis_index("fsdp")
        self.z, self.y = dp // NY, dp % NY
        self.x, self.c = fsdp // NC, fsdp % NC
        self.a, self.b = 2 * self.c + self.x, 4 * self.y + self.z
        self.to_x = (dp, (1 - self.x) * NC + self.c)
        self.to_y = (self.z * NY + 1 - self.y, fsdp)
        self.to_c = (dp, self.x * NC + 1 - self.c)
        self.to_z = [(((self.z + d) % NZ) * NY + self.y, fsdp) for d in range(1, NZ)]
        self.partners = [self.to_c, self.to_x, self.to_y] + self.to_z

    def barrier(self):
        sem = pltpu.get_barrier_semaphore()
        for partner in self.partners:
            pl.semaphore_signal(sem, inc=1, device_id=partner, device_id_type=MESH)
        pl.semaphore_wait(sem, len(self.partners))


def remote(src, dst, send, recv, to):
    return pltpu.make_async_remote_copy(
        src_ref=src, dst_ref=dst, send_sem=send, recv_sem=recv, device_id=to, device_id_type=MESH
    )


class Gather:
    COPIES = 11

    def __init__(self, place, weights, send, recv):
        self.at, self.weights, self.send, self.recv = place, weights, send, recv

    def copy(self, l, part, n):
        at, count = self.at, PART[part]
        half = count // 2
        a, b, rows, to = at.a, pl.ds(4 * at.y, 4), pl.ds(0, count), at.to_c
        if n < 3:
            b, to = at.b, at.to_z[n]
        elif n < 5:
            to = (at.to_x, at.to_y)[n - 3]
        if n in (6, 8, 10):
            a = 2 * at.c + 1 - at.x
        if n in (7, 9, 10):
            b = pl.ds(4 * (1 - at.y), 4)
        if n in (6, 7):
            rows, to = pl.ds((n - 6) * half, half), (at.to_y, at.to_x)[n - 6]
        ref = self.weights[part].at[l, a, b, rows, :]
        q = 2 * l + part
        return remote(ref, ref, self.send.at[q, n], self.recv.at[q, n], to)

    def start(self, l, part, *ns):
        for n in ns:
            self.copy(l, part, n).start()

    def wait(self, l, part, *ns):
        for n in ns:
            self.copy(l, part, n).wait_recv()

    def first(self, l, part):
        self.start(l, part, 0, 1, 2)

    def second(self, l, part):
        self.wait(l, part, 0, 1, 2)
        self.start(l, part, 3, 4, 5)

    def third(self, l, part):
        self.wait(l, part, 3)
        self.start(l, part, 6, 8)
        self.wait(l, part, 4)
        self.start(l, part, 7, 9)

    def fourth(self, l, part):
        self.wait(l, part, 6, 7)
        self.start(l, part, 10)

    def last(self, l, part):
        self.wait(l, part, 5, 8, 9, 10)

    def sent(self, l, part):
        for n in range(self.COPIES):
            self.copy(l, part, n).wait_send()


class Reduce:
    COPIES = 8

    def __init__(self, place, grads, landing, send, recv, credit):
        self.at, self.grads, self.landing = place, grads, landing
        self.send, self.recv, self.credit = send, recv, credit

    def refs(self, l, part):
        grads = self.grads[part].at[l + 1 - part]
        landing = self.landing[part]
        if self.credit is None:
            landing = [ref.at[l] for ref in landing]
        return (grads, *landing)

    def copy(self, l, part, n):
        at, half = self.at, PART[part] // 2
        g, r0, r1a, r1b, r2, r3 = self.refs(l, part)
        top, low, other = pl.ds(0, half), pl.ds(half, half), pl.ds(4 * (1 - at.y), 4)
        if n == 0:
            src, dst, to = g.at[pl.ds(2 * (1 - at.c), 2)], r0, at.to_c
        elif n == 1:
            src, dst, to = r0.at[1 - at.x, :, top, :], r1a, at.to_x
        elif n == 2:
            src, dst, to = r0.at[:, other, low, :], r1b, at.to_y
        elif n == 3:
            src, dst, to = r1a.at[other], r2.at[:, top, :], at.to_y
        elif n == 4:
            src, dst, to = r1b.at[1 - at.x], r2.at[:, low, :], at.to_x
        else:
            src, dst, to = r2.at[(at.z + n - 4) % NZ], r3.at[n - 5], at.to_z[n - 5]
        q = 2 * l + part
        return remote(src, dst, self.send.at[q, n], self.recv.at[q, n], to)

    def may_send(self, l, part, *partners):
        if self.credit is None:
            return

        @pl.when(l < LAYERS - 1)
        def _():
            for n in partners:
                pl.semaphore_wait(self.credit.at[part, n], 1)

    def start(self, l, part):
        self.may_send(l, part, 0)
        self.copy(l, part, 0).start()

    def first(self, l, part):
        at, half = self.at, PART[part] // 2
        g, r0, _, _, _, _ = self.refs(l, part)
        top, low = pl.ds(0, half), pl.ds(half, half)
        self.copy(l, part, 0).wait_recv()

        def along_x(n, carry):
            x = 1 - at.x
            total = g[2 * at.c + x, n, top].astype(WIDE) + r0[x, n, top].astype(WIDE)
            r0[x, n, top] = total.astype(LOWER)
            return carry

        def along_y(n, carry):
            x, b = n // 4, 4 * (1 - at.y) + n % 4
            total = g[2 * at.c + x, b, low].astype(WIDE) + r0[x, b, low].astype(WIDE)
            r0[x, b, low] = total.astype(LOWER)
            return carry

        lax.fori_loop(0, 8, along_x, 0)
        self.may_send(l, part, 1, 2)
        self.copy(l, part, 1).start()
        lax.fori_loop(0, 8, along_y, 0)
        self.copy(l, part, 2).start()

    def second(self, l, part):
        at, half = self.at, PART[part] // 2
        g, r0, r1a, r1b, _, _ = self.refs(l, part)
        top, low = pl.ds(0, half), pl.ds(half, half)

        def along_y(n, carry):
            b = 4 * (1 - at.y) + n
            total = g[at.a, b, top].astype(WIDE) + r0[at.x, b, top].astype(WIDE)
            r1a[b] = (total + r1a[b].astype(WIDE)).astype(LOWER)
            return carry

        def along_x(n, carry):
            x, b = 1 - at.x, 4 * at.y + n
            total = g[2 * at.c + x, b, low].astype(WIDE) + r0[x, b, low].astype(WIDE)
            r1b[x, n] = (total + r1b[x, n].astype(WIDE)).astype(LOWER)
            return carry

        self.copy(l, part, 1).wait_recv()
        lax.fori_loop(0, NZ, along_y, 0)
        self.copy(l, part, 3).start()
        self.copy(l, part, 2).wait_recv()
        lax.fori_loop(0, NZ, along_x, 0)
        self.copy(l, part, 4).start()

    def chip_sums(self, l, part, z):
        at, half = self.at, PART[part] // 2
        g, r0, r1a, r1b, r2, _ = self.refs(l, part)
        top, low, b = pl.ds(0, half), pl.ds(half, half), 4 * at.y + z
        upper = g[at.a, b, top].astype(WIDE) + r0[at.x, b, top].astype(WIDE)
        lower = g[at.a, b, low].astype(WIDE) + r0[at.x, b, low].astype(WIDE)
        return (
            upper + r1a[b].astype(WIDE) + r2[z, top].astype(WIDE),
            lower + r1b[at.x, z].astype(WIDE) + r2[z, low].astype(WIDE),
        )

    def third(self, l, part):
        half = PART[part] // 2
        r2 = self.refs(l, part)[4]
        for n in (3, 4):
            self.copy(l, part, n).wait_recv()
        self.may_send(l, part, 3, 4, 5)
        for n in range(3):
            z = (self.at.z + n + 1) % NZ
            upper, lower = self.chip_sums(l, part, z)
            r2[z, pl.ds(0, half)] = upper.astype(LOWER)
            r2[z, pl.ds(half, half)] = lower.astype(LOWER)
            self.copy(l, part, 5 + n).start()

    def last(self, l, part, out, squares):
        half, row = PART[part] // 2, (0, ATTN)[part]
        r3 = self.refs(l, part)[5]
        upper, lower = self.chip_sums(l, part, self.at.z)
        for n in range(3):
            self.copy(l, part, 5 + n).wait_recv()
            upper = upper + r3[n, pl.ds(0, half)].astype(WIDE)
            lower = lower + r3[n, pl.ds(half, half)].astype(WIDE)
        out[l, row : row + half, :] = upper
        out[l, row + half : row + 2 * half, :] = lower
        squares[0:1, :] += col_sum(upper * upper) + col_sum(lower * lower)
        for n in range(self.COPIES):
            self.copy(l, part, n).wait_send()
        if self.credit is None:
            return

        @pl.when(l > 0)
        def _():
            for n, to in zip((0, 1, 2, 5, 4, 3), self.at.partners):
                pl.semaphore_signal(
                    self.credit.at[part, n], inc=1, device_id=to, device_id_type=MESH
                )


class Total:
    COPIES = 6

    def __init__(self, place, own, got, send, recv):
        self.at, self.own, self.got, self.send, self.recv = place, own, got, send, recv

    def copy(self, n):
        src = self.own.at[min(n, 3)]
        return remote(src, self.got.at[n], self.send.at[n], self.recv.at[n], self.at.partners[n])

    def start(self):
        self.copy(0).start()

    def step(self, n):
        self.copy(n).wait_recv()
        self.own[n + 1] = self.own[n] + self.got[n]
        for m in ((1,), (2,), (3, 4, 5))[n]:
            self.copy(m).start()

    def last(self):
        for m in (3, 4, 5):
            self.copy(m).wait_recv()
        total = None
        for z in range(NZ):
            term = self.own[3]
            for n in range(3):
                from_z = (self.at.z + NZ - 1 - n) % NZ
                term = jnp.where(from_z == z, self.got[3 + n], term)
            total = term if total is None else total + term
        return total

    def sent(self):
        for n in range(self.COPIES):
            self.copy(n).wait_send()


def landing_shapes(count):
    half = count // 2
    return [
        (NX, 8, count, D),
        (8, half, D),
        (NX, NZ, half, D),
        (NZ, count, D),
        (3, count, D),
    ]


def stage_rows(qkv, out, up, down, l):
    return (
        [(qkv.at[l, :, pl.ds(j * D, D)], 16 * j, 16) for j in range(3)]
        + [(out.at[l], 48, 16)]
        + [(up.at[l, :, pl.ds(j * D, D)], 64 + 16 * j, 16) for j in range(4)]
        + [(down.at[l], 128, 64)]
    )


def train_kernel(refs, alone):
    k = Kit(**refs)

    def saved(back):
        copies = []
        for n, name in enumerate(SAVED):
            here, there = refs[name].at[0], refs["save_" + name]
            src, dst = (there, here) if back else (here, there)
            copies.append(pltpu.make_async_copy(src, dst, k.save_sem.at[n]))
        return copies

    parts = [(l, part) for l in range(LAYERS) for part in (0, 1)]
    weights = (k.wa, k.wf)
    if alone:
        loads = [
            pltpu.make_async_copy(ref, weights[part].at[l], k.load_sem.at[2 * l + part])
            for l, part in parts
            for ref in [(k.all_a, k.all_f)[part].at[l]]
        ]
        stores = [
            pltpu.make_async_copy(
                weights[part].at[l + 1 - part],
                (k.grad_a, k.grad_f)[part].at[l],
                k.load_sem.at[2 * l + part],
            )
            for l, part in parts
        ]
        for copy in loads:
            copy.start()
    else:
        place = Place()
        gather = Gather(place, weights, k.gather_send, k.gather_recv)
        reduce = Reduce(
            place, weights, (k.land_a, k.land_f), k.reduce_send, k.reduce_recv, k.credit
        )
        sums = Total(place, k.sum_own, k.sum_got, k.sum_send, k.sum_recv)
        norm = Total(place, k.norm_own, k.norm_got, k.norm_send, k.norm_recv)
        staged = []
        for l in range(LAYERS):
            for n, (src, row, count) in enumerate(stage_rows(k.qkv_w, k.out_w, k.up_w, k.down_w, l)):
                dst = k.dsec.at[pl.ds(l * PACK + row, count), :]
                staged.append(pltpu.make_async_copy(src, dst, k.stage_sem.at[l, n]))
        for copy in staged:
            copy.start()
        place.barrier()
        for l in range(LAYERS):
            for copy in staged[9 * l : 9 * l + 9]:
                copy.wait()
            row = l * PACK
            k.wa[l, place.a, place.b] = k.dsec[row : row + ATTN, :].astype(LOWER)
            gather.first(l, 0)
            k.wf[l, place.a, place.b] = k.dsec[row + ATTN : row + PACK, :].astype(LOWER)
            if l < LAYERS - 1:
                gather.first(l, 1)
        k.squares_sum[...] = jnp.zeros_like(k.squares_sum)

    setup_stage(k)
    if not alone:
        gather.second(0, 0)
        gather.second(0, 1)
        gather.third(0, 0)
        gather.second(1, 0)
        gather.third(0, 1)
        gather.fourth(0, 0)

    def forward(l, carry):
        def ahead(n, *stages):
            for stage, part in stages:

                @pl.when(l + n < LAYERS)
                def _(stage=stage, part=part):
                    stage(l + n, part)

        if alone:
            pltpu.make_async_copy(k.all_a.at[l], k.wa.at[l], k.load_sem.at[2 * l]).wait()
        else:
            ahead(1, (gather.second, 1))
            ahead(2, (gather.first, 1))
            ahead(1, (gather.third, 0))
            gather.fourth(l, 1)
            gather.last(l, 0)
        forward_attn(k, l)

        @pl.when(l == 1)
        def _():
            for copy in saved(False):
                copy.wait()

        if alone:
            pltpu.make_async_copy(k.all_f.at[l], k.wf.at[l], k.load_sem.at[2 * l + 1]).wait()
        else:
            ahead(2, (gather.second, 0))
            ahead(1, (gather.third, 1), (gather.fourth, 0))
            gather.last(l, 1)
        forward_ffn(k, l, (l + 1) % 2 + l // 2)

        @pl.when(l == 0)
        def _():
            for copy in saved(False):
                copy.start()

        return carry

    lax.fori_loop(0, LAYERS, forward, 0)
    if not alone:
        for l, part in parts:
            gather.sent(l, part)
    grad = 2
    head_stage(k, grad)

    def backward(n, carry):
        l = LAYERS - 1 - n

        def behind(*stages):
            if alone:
                return

            @pl.when(n > 0)
            def _():
                for stage, part, *more in stages:
                    stage(l + 1, part, *more)

        def now(*stages):
            if not alone:
                for stage, part in stages:
                    stage(l, part)

        finish = () if alone else (k.shard, k.squares_sum)

        @pl.when(n == 2)
        def _():
            for copy in saved(True):
                copy.wait()

        backward_ffn_start(k, l, grad)
        backward_ffn_block(k, l, 0)
        backward_ffn_block(k, l, 1)
        if not alone:
            behind((reduce.third, 1), (reduce.second, 0))
        backward_ffn_block(k, l, 2)
        backward_ffn_block(k, l, 3)
        if not alone:
            behind((reduce.last, 1, *finish), (reduce.third, 0))
            now((reduce.start, 1))
        backward_ffn_end(k, l, grad)
        backward_attn(k, l, grad)
        if not alone:
            behind((reduce.last, 0, *finish))
            now((reduce.first, 1), (reduce.start, 0))
        backward_input(k, l, grad)

        @pl.when(n == 0)
        def _():
            for copy in saved(True):
                copy.start()

        if not alone:
            now((reduce.second, 1), (reduce.first, 0))
        return carry

    lax.fori_loop(0, LAYERS, backward, 0)
    if alone:
        for copy in stores:
            copy.start()
        small_stage(k, k.small_out, grad)
        for copy in stores:
            copy.wait()
        return
    reduce.third(0, 1)
    small_stage(k, k.sum_own.at[0], grad)
    sums.start()
    reduce.second(0, 0)
    reduce.last(0, 1, k.shard, k.squares_sum)
    sums.step(0)
    reduce.third(0, 0)
    sums.step(1)
    reduce.last(0, 0, k.shard, k.squares_sum)
    k.norm_own[0] = k.squares_sum[...]
    norm.start()
    sums.step(2)
    norm.step(0)
    norm.step(1)
    k.small_out[...] = sums.last()
    norm.step(2)
    k.squares[...] = norm.last()
    sums.sent()
    norm.sent()


def train_pass(meta, buf, small, head_bias, log_temp, weights, alone):
    whole = pl.BlockSpec(memory_space=pltpu.VMEM)
    scalars = pl.BlockSpec(memory_space=pltpu.SMEM)
    anywhere = pl.BlockSpec(memory_space=pl.ANY)
    dma = pltpu.SemaphoreType.DMA
    count = 2 * LAYERS
    names = ["meta", "buf", "small", "head_bias", "log_temp"]
    out_shape = {"small_out": ((SMALL, D), WIDE)}
    for name in SAVED:
        shape, dtype = WORK_SHAPES[name]
        out_shape["save_" + name] = (shape[1:], dtype)
    scratch = {name: pltpu.VMEM(*shape) for name, shape in WORK_SHAPES.items()}
    scratch["save_sem"] = dma((len(SAVED),))
    if alone:
        names += ["all_a", "all_f"]
        out_shape["grad_a"] = ((LAYERS, 4, 8, ATTN, D), LOWER)
        out_shape["grad_f"] = ((LAYERS, 4, 8, FFN, D), LOWER)
        scratch["load_sem"] = dma((count,))
    else:
        names += ["qkv_w", "out_w", "up_w", "down_w"]
        out_shape["shard"] = ((LAYERS, PACK, D), WIDE)
        out_shape["squares"] = ((8, D), WIDE)
        for part, name in enumerate("af"):
            for n, shape in enumerate(landing_shapes(PART[part])):
                scratch["land_%s%d" % (name, n)] = pltpu.VMEM(shape, LOWER)
        scratch["stage_sem"] = dma((LAYERS, 9))
        scratch["squares_sum"] = pltpu.VMEM((8, D), WIDE)
        for name, copies in (("gather", Gather.COPIES), ("reduce", Reduce.COPIES)):
            scratch[name + "_send"] = dma((count, copies))
            scratch[name + "_recv"] = dma((count, copies))
        scratch["credit"] = pltpu.SemaphoreType.REGULAR((2, 6))
        for name, rows in (("sum", SMALL), ("norm", 8)):
            scratch[name + "_own"] = pltpu.VMEM((4, rows, D), WIDE)
            scratch[name + "_got"] = pltpu.VMEM((6, rows, D), WIDE)
            scratch[name + "_send"] = dma((6,))
            scratch[name + "_recv"] = dma((6,))
    spaces = dict(head_bias=scalars, log_temp=scalars)
    for name in ("all_a", "all_f", "grad_a", "grad_f", "qkv_w", "out_w", "up_w", "down_w"):
        spaces[name] = anywhere
    for name in SAVED:
        spaces["save_" + name] = anywhere
    every = names + list(out_shape) + list(scratch)

    def kernel(*given):
        refs = dict(zip(every, given))
        for name in "af":
            refs["land_" + name] = [refs.get("land_%s%d" % (name, n)) for n in range(5)]
        train_kernel(refs, alone)

    results = pl.pallas_call(
        kernel,
        name="train_pass",
        out_shape=tuple(jax.ShapeDtypeStruct(*shape) for shape in out_shape.values()),
        in_specs=[spaces.get(name, whole) for name in names],
        out_specs=tuple(spaces.get(name, whole) for name in out_shape),
        scratch_shapes=list(scratch.values()),
        compiler_params=pltpu.CompilerParams(
            vmem_limit_bytes=VMEM_BYTES,
            collective_id=None if alone else 0,
            has_side_effects=not alone,
        ),
        cost_estimate=pl.CostEstimate(
            flops=6 * 10**10, bytes_accessed=4 * 10**7, transcendentals=10**7
        ),
    )(meta, buf, small, head_bias, log_temp, *weights)
    return dict(zip(out_shape, results))


def packed_shape(part, layers=LAYERS):
    return (layers, 4, 8, PART[part], D)


def gather_kernel(qkv, out, up, down, all_a, all_f, wa, wf, stage, send, recv, stage_sem, store):
    place = Place()
    weights, results = (wa, wf), (all_a, all_f)
    net = Gather(place, weights, send, recv)
    staged = []
    for l in range(LAYERS):
        for n, (src, row, count) in enumerate(stage_rows(qkv, out, up, down, l)):
            dst = stage.at[pl.ds(l * PACK + row, count), :]
            staged.append(pltpu.make_async_copy(src, dst, stage_sem.at[l, n]))
    for copy in staged:
        copy.start()
    place.barrier()
    parts = [(l, part) for l in range(LAYERS) for part in (0, 1)]
    for l in range(LAYERS):
        for copy in staged[9 * l : 9 * l + 9]:
            copy.wait()
        row = l * PACK
        wa[l, place.a, place.b] = stage[row : row + ATTN, :].astype(LOWER)
        wf[l, place.a, place.b] = stage[row + ATTN : row + PACK, :].astype(LOWER)

    def keep(l, part):
        return pltpu.make_async_copy(
            weights[part].at[l], results[part].at[l], store.at[2 * l + part]
        )

    for l, part in parts[:3]:
        net.first(l, part)
    for t in range(len(parts) + 3):
        if t < len(parts):
            net.second(*parts[t])
        if t + 3 < len(parts):
            net.first(*parts[t + 3])
        if 0 <= t - 1 < len(parts):
            net.third(*parts[t - 1])
        if 0 <= t - 2 < len(parts):
            net.fourth(*parts[t - 2])
        if 0 <= t - 3 < len(parts):
            net.last(*parts[t - 3])
            keep(*parts[t - 3]).start()
    for l, part in parts:
        net.sent(l, part)
        keep(l, part).wait()


def gather_all(mats):
    anywhere = pl.BlockSpec(memory_space=pl.ANY)
    dma = pltpu.SemaphoreType.DMA
    count = 2 * LAYERS
    return pl.pallas_call(
        gather_kernel,
        name="gather",
        out_shape=tuple(jax.ShapeDtypeStruct(packed_shape(part), LOWER) for part in (0, 1)),
        in_specs=[anywhere] * 4,
        out_specs=(anywhere,) * 2,
        scratch_shapes=[pltpu.VMEM(packed_shape(part), LOWER) for part in (0, 1)]
        + [pltpu.VMEM((LAYERS * PACK, D), WIDE)]
        + [dma((count, Gather.COPIES))] * 2
        + [dma((LAYERS, 9)), dma((count,))],
        compiler_params=pltpu.CompilerParams(
            collective_id=0, has_side_effects=True, vmem_limit_bytes=VMEM_BYTES
        ),
        cost_estimate=pl.CostEstimate(flops=0, bytes_accessed=4 * 10**7, transcendentals=0),
    )(*mats)


def reduce_kernel(refs):
    k = Kit(**refs)
    place = Place()
    net = Reduce(place, (k.wa, k.wf), (k.land_a, k.land_f), k.send, k.recv, None)
    sums = Total(place, k.sum_own, k.sum_got, k.sum_send, k.sum_recv)
    norm = Total(place, k.norm_own, k.norm_got, k.norm_send, k.norm_recv)
    parts = [(l, part) for l in reversed(range(LAYERS)) for part in (1, 0)]

    def fetch(l, part):
        return pltpu.make_async_copy(
            (k.grad_a, k.grad_f)[part].at[l],
            (k.wa, k.wf)[part].at[l + 1 - part],
            k.load.at[2 * l + part],
        )

    for l, part in parts:
        fetch(l, part).start()
    k.sum_own[0] = k.small[...]
    k.squares_sum[...] = jnp.zeros_like(k.squares_sum)
    place.barrier()
    sums.start()
    stages = (net.first, net.second, net.third)
    for t in range(len(parts) + 4):
        if t >= 4:
            net.last(*parts[t - 4], k.shard, k.squares_sum)
        if t < len(parts):
            fetch(*parts[t]).wait()
            net.start(*parts[t])
        for n, stage in enumerate(stages):
            if 0 <= t - 1 - n < len(parts):
                stage(*parts[t - 1 - n])
        if 1 <= t <= 3:
            sums.step(t - 1)
    k.norm_own[0] = k.squares_sum[...]
    norm.start()
    k.small_out[...] = sums.last()
    for n in range(3):
        norm.step(n)
    k.squares[...] = norm.last()
    sums.sent()
    norm.sent()


def reduce_all(grad_a, grad_f, small):
    whole = pl.BlockSpec(memory_space=pltpu.VMEM)
    anywhere = pl.BlockSpec(memory_space=pl.ANY)
    dma = pltpu.SemaphoreType.DMA
    count = 2 * LAYERS
    out_shape = {
        "shard": (LAYERS, PACK, D),
        "small_out": (SMALL, D),
        "squares": (8, D),
    }
    scratch = dict(
        wa=pltpu.VMEM(packed_shape(0, LAYERS + 1), LOWER),
        wf=pltpu.VMEM(packed_shape(1), LOWER),
        squares_sum=pltpu.VMEM((8, D), WIDE),
        send=dma((count, Reduce.COPIES)),
        recv=dma((count, Reduce.COPIES)),
        load=dma((count,)),
    )
    for part, name in enumerate("af"):
        for n, shape in enumerate(landing_shapes(PART[part])):
            scratch["land_%s%d" % (name, n)] = pltpu.VMEM((LAYERS,) + shape, LOWER)
    for name, rows in (("sum", SMALL), ("norm", 8)):
        scratch[name + "_own"] = pltpu.VMEM((4, rows, D), WIDE)
        scratch[name + "_got"] = pltpu.VMEM((6, rows, D), WIDE)
        scratch[name + "_send"] = dma((6,))
        scratch[name + "_recv"] = dma((6,))
    every = ["grad_a", "grad_f", "small"] + list(out_shape) + list(scratch)

    def kernel(*given):
        refs = dict(zip(every, given))
        for name in "af":
            refs["land_" + name] = [refs["land_%s%d" % (name, n)] for n in range(5)]
        reduce_kernel(refs)

    return pl.pallas_call(
        kernel,
        name="reduce",
        out_shape=tuple(jax.ShapeDtypeStruct(shape, WIDE) for shape in out_shape.values()),
        in_specs=[anywhere, anywhere, whole],
        out_specs=(whole,) * 3,
        scratch_shapes=list(scratch.values()),
        compiler_params=pltpu.CompilerParams(
            collective_id=1, has_side_effects=True, vmem_limit_bytes=VMEM_BYTES
        ),
        cost_estimate=pl.CostEstimate(flops=0, bytes_accessed=4 * 10**7, transcendentals=0),
    )(grad_a, grad_f, small)


def small_inputs(buf_states, buf_actions, buf_returns, window_starts, window_repeats, valid_steps):
    meta = jnp.concatenate(
        [window_starts[:, None], window_repeats[:, None], valid_steps], 1
    ).astype(WIDE)
    meta = jnp.pad(meta, ((0, 128 - meta.shape[0]), (0, 128 - meta.shape[1])))
    buf = jnp.concatenate([buf_states, buf_actions, buf_returns[:, None]], 1)
    buf = jnp.pad(buf, ((0, 128 - buf.shape[0]), (0, 128 - buf.shape[1])))
    return meta, buf


def adam_parts(weight, grad, first, second, rate):
    first = BETA_ONE * first + (1.0 - BETA_ONE) * grad
    second = BETA_TWO * second + (1.0 - BETA_TWO) * grad * grad
    fix_one = 1.0 - BETA_ONE**STEP
    fix_two = 1.0 - BETA_TWO**STEP
    fresh = weight - rate * (
        first / fix_one / (jnp.sqrt(second / fix_two) + ADAM_EPS) + DECAY * weight
    )
    return fresh, first, second


def adam_kernel(*refs):
    shard, small_grad, squares, groups, log_temp = refs[:5]
    small, small_first, small_second, bias, bias_first, bias_second = refs[5:11]
    mats, firsts, seconds = refs[11:15], refs[15:19], refs[19:23]
    totals, norm, next_temp, s_next, s_first, s_second, b_next, b_first, b_second = refs[23:32]
    m_next, m_copy, m_first, m_second = refs[32:36], refs[36:40], refs[40:44], refs[44:48]
    l = pl.program_id(0)
    extra = small_grad[NROWS : NROWS + 3, 0:128]
    lane = iota((1, 128), 1)
    bias_mean = jnp.where(lane < A, extra[1:2], 0.0)
    bias_spread = jnp.where(lane < A, extra[2:3], 0.0)

    def all_sum(v):
        return jnp.sum(jnp.sum(v, 0, keepdims=True), 1, keepdims=True)

    grads = small_grad[0:NROWS, :]
    square = (
        all_sum(squares[0:1, :])
        + all_sum(grads * grads)
        + all_sum(bias_mean * bias_mean)
        + all_sum(bias_spread * bias_spread)
    )
    length = jnp.sqrt(square)
    clip = jnp.minimum(1.0, CLIP / (length + 1e-06))

    def rate_of(kind):
        group = jnp.full((1, 1), groups[l, kind], jnp.int32).astype(WIDE)
        return LEARN * jnp.exp2(-group)

    def update(kind, rows, cols, grad):
        at = (0, rows, cols)
        fresh, first, second = adam_parts(
            mats[kind][at], clip * grad, firsts[kind][at], seconds[kind][at], rate_of(kind)
        )
        m_next[kind][at] = fresh
        m_copy[kind][at] = fresh.astype(LOWER)
        m_first[kind][at] = first
        m_second[kind][at] = second

    every = slice(0, 16)
    for j in range(3):
        update(0, every, slice(j * D, (j + 1) * D), shard[0, 16 * j : 16 * j + 16, :])
    update(1, every, slice(0, D), shard[0, 48:64, :])
    for j in range(4):
        update(2, every, slice(j * D, (j + 1) * D), shard[0, 64 + 16 * j : 80 + 16 * j, :])
    update(3, slice(0, 64), slice(0, D), shard[0, 128:192, :])

    @pl.when(l == 0)
    def _():
        s_next[...], s_first[...], s_second[...] = adam_parts(
            small[...], clip * grads, small_first[...], small_second[...], LEARN
        )

        def scalar(v, n):
            return jnp.sum(jnp.where(lane == n, v, 0.0))

        def row(ref):
            v = jnp.zeros((1, 128), WIDE)
            for n in range(2 * A):
                v = jnp.where(lane == n, ref[n], v)
            return v

        grad = bias_mean + pltpu.roll(bias_spread, A, 1)
        results = adam_parts(row(bias), clip * grad, row(bias_first), row(bias_second), LEARN)
        for ref, result in zip((b_next, b_first, b_second), results):
            for n in range(2 * A):
                ref[n] = scalar(result, n)
        sums = extra[0:1]
        for n in range(3):
            totals[n] = scalar(sums, n)
        norm[0] = jnp.sum(length)
        logs = jnp.full((1, 1), log_temp[0], WIDE)
        ratio = jnp.full((1, 1), scalar(sums, 1), WIDE) / jnp.full((1, 1), scalar(sums, 2), WIDE)
        next_temp[0] = jnp.sum(logs - TEMP_RATE * jnp.exp(logs) * (ratio + A))


def adam_all(shard, small_grad, squares, groups, log_temp, smalls, biases, mats, firsts, seconds):
    scalars = pl.BlockSpec(memory_space=pltpu.SMEM)

    def fixed(array):
        return pl.BlockSpec(array.shape, lambda l: (0,) * array.ndim)

    def layer(array):
        return pl.BlockSpec((1,) + array.shape[1:], lambda l: (l, 0, 0))

    def like(array, dtype=WIDE):
        return jax.ShapeDtypeStruct(array.shape, dtype)

    stacks = list(mats) + list(firsts) + list(seconds)
    small, bias = smalls[0], biases[0]
    return pl.pallas_call(
        adam_kernel,
        name="adam",
        grid=(LAYERS,),
        out_shape=(
            (jax.ShapeDtypeStruct((3,), WIDE),)
            + (jax.ShapeDtypeStruct((1,), WIDE),) * 2
            + (like(small),) * 3
            + (like(bias),) * 3
            + tuple(like(m) for m in mats)
            + tuple(like(m, LOWER) for m in mats)
            + tuple(like(m) for m in mats) * 2
        ),
        in_specs=[layer(shard), fixed(small_grad), fixed(squares), scalars, scalars]
        + [fixed(small)] * 3
        + [scalars] * 3
        + [layer(m) for m in stacks],
        out_specs=(scalars,) * 3
        + (fixed(small),) * 3
        + (scalars,) * 3
        + tuple(layer(m) for m in mats) * 4,
        compiler_params=pltpu.CompilerParams(vmem_limit_bytes=VMEM_BYTES),
        cost_estimate=pl.CostEstimate(flops=10**7, bytes_accessed=8 * 10**6, transcendentals=10**6),
    )(shard, small_grad, squares, groups, log_temp, *smalls, *biases, *stacks)


def gather_packed(mats, axes, count):
    group = count // BLOCKS
    pieces = []
    for mat in mats:
        rows, wide = mat.shape[1], mat.shape[2] // D
        piece = mat.astype(LOWER).reshape(LAYERS, rows, wide, D)
        piece = lax.all_gather(piece, axes, axis=1, tiled=True)
        piece = piece.reshape(LAYERS, NZ, NY, NX, NC, group * rows, wide, D)
        piece = piece.transpose(0, 4, 3, 2, 1, 6, 5, 7)
        pieces.append(piece.reshape(LAYERS, 4, 8, wide * group * rows, D))
    return jnp.concatenate(pieces[:2], 3), jnp.concatenate(pieces[2:], 3)


def scatter_packed(grads, mats, axes):
    results, first = [], 0
    for n, mat in enumerate(mats):
        rows, wide = mat.shape[1], mat.shape[2] // D
        total = lax.psum(1, axes) * rows
        deep = total // BLOCKS
        first = 0 if n % 2 == 0 else first
        piece = grads[n // 2][:, :, :, first : first + wide * deep].astype(WIDE)
        first += wide * deep
        piece = piece.reshape(LAYERS, NC, NX, NY, NZ, wide, deep, D)
        piece = piece.transpose(0, 4, 3, 2, 1, 6, 5, 7).reshape(LAYERS, total, wide * D)
        results.append(lax.psum_scatter(piece, axes, scatter_dimension=1, tiled=True))
    return results


def local(
    buf_states,
    buf_actions,
    buf_returns,
    window_starts,
    window_repeats,
    valid_steps,
    matrix_groups,
    log_temp,
    small_rows,
    head_bias,
    qkv_weight,
    out_weight,
    up_weight,
    down_weight,
    small_first,
    bias_first,
    qkv_first,
    out_first,
    up_first,
    down_first,
    small_second,
    bias_second,
    qkv_second,
    out_second,
    up_second,
    down_second,
):
    axes = ("dp", "fsdp")
    mats = (qkv_weight, out_weight, up_weight, down_weight)
    firsts = (qkv_first, out_first, up_first, down_first)
    seconds = (qkv_second, out_second, up_second, down_second)
    meta, buf = small_inputs(
        buf_states, buf_actions, buf_returns, window_starts, window_repeats, valid_steps
    )
    pass_inputs = (meta, buf, small_rows, head_bias, log_temp)
    if FF // down_weight.shape[1] == BLOCKS and lax.psum(1, "fsdp") == NX * NC:
        made = train_pass(*pass_inputs, gather_all(mats), True)
        shard, small, squares = reduce_all(made["grad_a"], made["grad_f"], made["small_out"])
        return adam_all(
            shard,
            small,
            squares,
            matrix_groups,
            log_temp,
            (small_rows, small_first, small_second),
            (head_bias, bias_first, bias_second),
            mats,
            firsts,
            seconds,
        )
    packed = gather_packed(mats, axes, FF // down_weight.shape[1])
    made = train_pass(*pass_inputs, packed, True)
    big = scatter_packed((made["grad_a"], made["grad_f"]), mats, axes)
    small = made["small_out"]
    small = lax.psum(small, axes)
    small_grad, totals = small[:NROWS], small[NROWS, :3]
    bias_grad = jnp.concatenate([small[NROWS + 1, :A], small[NROWS + 2, :A]])
    square = sum((jnp.sum(piece * piece) for piece in big))
    square = (
        lax.psum(square, axes) + jnp.sum(small_grad * small_grad) + jnp.sum(bias_grad * bias_grad)
    )
    grad_norm = jnp.sqrt(square)
    clip = jnp.minimum(1.0, CLIP / (grad_norm + 1e-06))
    rates = LEARN * jnp.exp2(-matrix_groups.astype(WIDE))
    results = [
        adam_parts(
            mats[kind], clip * big[kind], firsts[kind], seconds[kind], rates[:, kind][:, None, None]
        )
        for kind in range(4)
    ]
    small_new = adam_parts(small_rows, clip * small_grad, small_first, small_second, LEARN)
    bias_new = adam_parts(head_bias, clip * bias_grad, bias_first, bias_second, LEARN)
    next_temp = log_temp - TEMP_RATE * jnp.exp(log_temp) * (totals[1] / totals[2] + A)
    return (
        (totals, grad_norm[None], next_temp)
        + small_new
        + bias_new
        + tuple(r[0] for r in results)
        + tuple(r[0].astype(LOWER) for r in results)
        + tuple(r[1] for r in results)
        + tuple(r[2] for r in results)
    )


def solution(mesh):
    rows = P(("dp", "fsdp"), None)
    vector = P(("dp", "fsdp"))
    stack = P(None, ("dp", "fsdp"), None)
    same = P()
    in_specs = (
        (rows, rows, vector, vector, vector, rows)
        + (same,) * 4
        + (stack,) * 4
        + (same,) * 2
        + (stack,) * 4
        + (same,) * 2
        + (stack,) * 4
    )
    out_specs = (same,) * 9 + (stack,) * 16
    return jax.shard_map(local, mesh=mesh, in_specs=in_specs, out_specs=out_specs, check_vma=False)
```

```python
import functools
import math

import jax
import jax.numpy as jnp
from jax import lax
from jax.experimental import pallas as pl
from jax.experimental.pallas import tpu as pltpu
from jax.sharding import PartitionSpec as P

D = 512
H = 8
HD = 64
FF = 2048
S = 11
A = 3
K = 20
STEP = 10

EPS = 1e-05
CLIP = 1.0
LEARN = 0.03
BETA_ONE = 0.5
BETA_TWO = 0.7
DECAY = 0.01
ADAM_EPS = 1e-08
TEMP_RATE = 0.1
MASKED = -1e30
HALF_LOG_TAU = 0.5 * math.log(2.0 * math.pi)
GELU_C = math.sqrt(2.0 / math.pi)
GELU_A = 0.044715
HIGH = lax.Precision.HIGHEST
LOWER = jnp.bfloat16
WIDE = jnp.float32

LAYERS = 3
WINS = 16
SLOT = 64
ROWS = WINS * SLOT
CHUNK = 512
CHUNKS = ROWS // CHUNK
BLOCKS = 32
PACK = 192
ATTN, FFN = 64, 128
EMB = S + A + 1 + K + 3
FIN = EMB
HEADW = EMB + 2
BASE = EMB + 2 + 2 * A
PER = 9 + FF // D
NROWS = BASE + LAYERS * PER
SMALL = 88
HEAD_AT = 64
EMB_AT = ROWS - 128
VMEM_BYTES = 64 * 1024 * 1024


def dot(a, b, precision=None):
    return lax.dot_general(
        a, b, (((1,), (0,)), ((), ())), precision=precision, preferred_element_type=WIDE
    )


def dot_nt(a, b, precision=None):
    return lax.dot_general(
        a, b, (((1,), (1,)), ((), ())), precision=precision, preferred_element_type=WIDE
    )


def dot_tn(a, b, precision=None):
    return lax.dot_general(
        a, b, (((0,), (0,)), ((), ())), precision=precision, preferred_element_type=WIDE
    )


def iota(shape, dim):
    return lax.broadcasted_iota(jnp.int32, shape, dim)


def col_sum(v):
    return jnp.sum(v, 0, keepdims=True)


def row_mean(v):
    return jnp.mean(v, -1, keepdims=True)


def norm_parts(x):
    center = x - row_mean(x)
    scale = lax.rsqrt(row_mean(center * center) + EPS)
    return center * scale, scale


def norm_back(xhat, scale, gain, grad):
    scaled = grad * gain
    return scale * (scaled - row_mean(scaled) - xhat * row_mean(scaled * xhat))


def token_rows(at, count):
    row = at + iota((count, 128), 0)
    place = row & (SLOT - 1)
    step = (place * 21846) >> 16
    return row >> 6, step, place - 3 * step, place < 3 * K


def chunk_rows(c):
    return pl.ds(pl.multiple_of(c * CHUNK, CHUNK), CHUNK)


def owner_place(i):
    z, y, x, c = i // 8, (i // 4) % 2, (i // 2) % 2, i % 2
    return 2 * c + x, 4 * y + z


class Kit:
    def __init__(self, **refs):
        self.__dict__.update(refs)

    def row(self, l, k):
        return self.lrows[l, k : k + 1, :]

    def blocks(self, ref, l, first, count, owners):
        places = [owner_place(i) for i in owners]
        return jnp.concatenate([ref[l, a, b, first : first + count, :] for a, b in places], 0)

    def w_qkv(self, l, j):
        return self.blocks(self.wa, l, 16 * j, 16, range(BLOCKS))

    def w_out(self, l):
        return self.blocks(self.wa, l, 48, 16, range(BLOCKS))

    def w_up(self, l, j):
        return self.blocks(self.wf, l, 16 * j, 16, range(BLOCKS))

    def w_down(self, l, j):
        return self.blocks(self.wf, l, 64, 64, range(8 * j, 8 * j + 8))


def slot(l):
    return l % 2


def setup_stage(k):
    k.xs[2, EMB_AT:ROWS, :] = jnp.zeros((128, D), WIDE)
    k.xs[2, EMB_AT : EMB_AT + EMB, :] = k.small[0:EMB, :]
    k.headw[...] = jnp.zeros_like(k.headw)
    k.headw[0, 0:A, :] = k.small[HEADW : HEADW + A, :].astype(LOWER)
    k.headw[1, 0:A, :] = k.small[HEADW + A : HEADW + 2 * A, :].astype(LOWER)
    for l in range(LAYERS):
        k.lrows[l, 0:PER, :] = k.small[BASE + l * PER : BASE + (l + 1) * PER, :]
    k.sgl[...] = jnp.zeros_like(k.sgl)
    k.sgh[...] = jnp.zeros_like(k.sgh)
    k.sgw[...] = jnp.zeros_like(k.sgw)

    meta = k.meta[...].astype(LOWER)

    def chunk(c, carry):
        rows = chunk_rows(c)
        win, step, kind, real = token_rows(c * CHUNK, CHUNK)
        lane = iota((CHUNK, 128), 1)
        tok = dot((lane == win).astype(WIDE).astype(LOWER), meta)
        start, repeat = tok[:, 0:1], tok[:, 1:2]
        valid = jnp.sum(jnp.where(lane == step + 2, tok, 0.0), -1, keepdims=True)
        key = iota((CHUNK, 128), 0) & (SLOT - 1)
        query = lane & (SLOT - 1)
        allowed = (key <= query) & (((valid > 0.5) & real) | (key == query))
        k.bias[rows, :] = jnp.where(allowed, 0.0, MASKED)
        place = start.astype(jnp.int32) + step
        source = ((lane == place) & real).astype(WIDE)
        raw = dot(source, k.buf[...], HIGH)
        mine = (
            ((lane < S) & (kind == 1))
            | ((lane >= S) & (lane < S + A) & (kind == 2))
            | ((lane == S + A) & (kind == 0))
        )
        marks = ((lane == S + A + 1 + step) | (lane == S + A + 1 + K + kind)) & real
        feats = jnp.where(mine, raw, 0.0) + marks.astype(WIDE)
        weight = jnp.where((kind == 1) & real, repeat * valid, 0.0)
        acts = pltpu.roll(raw, HEAD_AT - S, 1)
        ours = (lane >= HEAD_AT) & (lane < HEAD_AT + A)
        feats = jnp.where(ours, acts, jnp.where(lane == HEAD_AT + A, weight, feats))
        k.feats[rows, :] = feats
        k.xs[0, rows, :] = dot(feats, k.xs[2, EMB_AT:ROWS, :], HIGH)
        return carry

    lax.fori_loop(0, CHUNKS, chunk, 0)


def stack_pair(v, first):
    zero = jnp.zeros_like(v)
    return jnp.concatenate([jnp.where(first, v, zero), jnp.where(first, zero, v)], 0)


def join_pair(v, first):
    return jnp.where(first, v[:SLOT], v[SLOT:])


def window_rows(w):
    return pl.ds(pl.multiple_of(w * SLOT, SLOT), SLOT)


def each_chunk(body, between=None):
    def step(c, carry):
        body(c, chunk_rows(c))
        if between is not None:

            @pl.when(c < CHUNKS - 1)
            def _():
                between()

        return carry

    lax.fori_loop(0, CHUNKS, step, 0)


def each_window(body, after=None):
    def pair(n, carry):
        body(2 * n)
        body(2 * n + 1)
        if after is not None:
            after(pl.ds(pl.multiple_of(n * 128, 128), 128))
        return carry

    lax.fori_loop(0, WINS // 2, pair, 0)


def forward_qkv(k, l):
    def chunk(c, rows):
        xhat, _ = norm_parts(k.xs[slot(l), rows, :])
        normed = (xhat * k.row(l, 0) + k.row(l, 1)).astype(LOWER)
        k.normed_t[:, rows] = normed.T
        for j in range(3):
            part = dot(normed, k.w_qkv(l, j)) + k.row(l, 4 + j)
            k.qkv[rows, j * D : (j + 1) * D] = part.astype(LOWER)

    each_chunk(chunk)


def forward_windows(k, l):
    first = iota((SLOT, 128), 1) < HD

    def window(w):
        rows = window_rows(w)
        bias = k.bias[rows, :]
        scores = []
        for p in range(H // 2):
            at = p * 128
            query = stack_pair(k.qkv[rows, at : at + 128] * jnp.asarray(HD**-0.5, LOWER), first)
            scores.append(dot_nt(k.qkv[rows, D + at : D + at + 128], query) + bias)
        for p in range(H // 2):
            at = p * 128
            peak = jnp.max(scores[p], 0, keepdims=True)
            expo = jnp.exp(scores[p] - peak)
            total = jnp.sum(expo, 0, keepdims=True)
            probs = (expo * (1.0 / total)).astype(LOWER)
            k.logs[l, w, p : p + 1, :] = peak + jnp.log(total)
            out = dot_tn(probs, k.qkv[rows, 2 * D + at : 2 * D + at + 128])
            k.left[rows, at : at + 128] = join_pair(out, first).astype(LOWER)

    def turn(rows):
        k.mixed_t[:, rows] = k.left[rows, :].T

    each_window(window, turn)


def forward_ffn(k, l, dest, between=None):
    def chunk(c, rows):
        mid = k.xs[slot(l), rows, :] + dot(k.left[rows, :], k.w_out(l)) + k.row(l, 7)
        k.mid[rows, :] = mid
        xhat, _ = norm_parts(mid)
        second = (xhat * k.row(l, 2) + k.row(l, 3)).astype(LOWER)
        k.second_t[:, rows] = second.T
        out = mid + k.row(l, 12)
        for j in range(4):
            cols = slice(j * D, (j + 1) * D)
            h = dot(second, k.w_up(l, j)) + k.row(l, 8 + j)
            square = h * h
            over = 1.0 + jnp.tanh(h * (GELU_C + GELU_C * GELU_A * square))
            half = 0.5 * h
            acted = (half * over).astype(LOWER)
            slope = over * (0.5 + half * (2.0 - over) * (GELU_C + 3.0 * GELU_A * GELU_C * square))
            k.slope[rows, cols] = slope.astype(LOWER)
            k.act_t[cols, rows] = acted.T
            out = out + dot(acted, k.w_down(l, j))
        k.xs[dest, rows, :] = out

    each_chunk(chunk, between)


def head_stage(k, at):
    gain, bias = k.small[FIN : FIN + 1, :], k.small[FIN + 1 : FIN + 2, :]
    lane = iota((CHUNK, 128), 1)
    keep = lane < A

    def bias_row(first):
        row = jnp.zeros((1, 128), WIDE)
        at = iota((1, 128), 1)
        for a in range(A):
            row = jnp.where(at == a, k.head_bias[first + a], row)
        return row

    bias_mean, bias_spread = bias_row(0), bias_row(A)
    temp = jnp.exp(jnp.full((1, 128), k.log_temp[0], WIDE))

    def chunk(c, carry):
        rows = chunk_rows(c)
        xhat, scale = norm_parts(k.xs[at, rows, :])
        feats = (xhat * gain + bias).astype(LOWER)
        mean = dot_nt(feats, k.headw[0]) + bias_mean
        spread = jnp.tanh(dot_nt(feats, k.headw[1]) + bias_spread)
        acts = pltpu.roll(k.feats[rows, :], 128 - HEAD_AT, 1)
        weight = acts[:, A : A + 1]
        acts = jnp.where(keep, acts, 0.0)
        target = 0.5 * (jnp.log(1.0 + acts) - jnp.log(1.0 - acts))
        shrink = jnp.exp(-spread)
        zed = (target - mean) * shrink
        terms = 0.5 * zed * zed + spread + HALF_LOG_TAU + jnp.log(1.0 - acts * acts)
        nll = jnp.sum(jnp.where(keep, terms, 0.0), -1, keepdims=True)
        entropy = jnp.sum(jnp.where(keep, spread, 0.0), -1, keepdims=True) + A * (0.5 + HALF_LOG_TAU)
        loss = weight * (nll - temp * entropy)
        sums = jnp.where(lane == 0, loss, jnp.where(lane == 1, weight * entropy, jnp.where(lane == 2, weight, 0.0)))
        d_mean = jnp.where(keep, weight * (-zed * shrink), 0.0).astype(LOWER)
        d_spread = weight * (1.0 - zed * zed - temp) * (1.0 - spread * spread)
        d_spread = jnp.where(keep, d_spread, 0.0).astype(LOWER)
        k.sgh[2:3, 0:128] += col_sum(sums)
        k.sgh[3:4, 0:128] += col_sum(d_mean.astype(WIDE))
        k.sgh[4:5, 0:128] += col_sum(d_spread.astype(WIDE))
        k.sgw[0] += dot_tn(d_mean, feats)[0:8]
        k.sgw[1] += dot_tn(d_spread, feats)[0:8]
        d_feats = dot(d_mean, k.headw[0]) + dot(d_spread, k.headw[1])
        k.sgh[0:1, :] += col_sum(d_feats * xhat)
        k.sgh[1:2, :] += col_sum(d_feats)
        k.xs[at, rows, :] = norm_back(xhat, scale, gain, d_feats)
        return carry

    lax.fori_loop(0, CHUNKS, chunk, 0)


def store_blocks(ref, l, owners, first, count, value):
    value = value.astype(LOWER)
    for n, i in enumerate(owners):
        a, b = owner_place(i)
        ref[l, a, b, first : first + count, :] = value[n * count : (n + 1) * count]


def backward_ffn(k, l, grad, between=None):
    def chunk(c, rows):
        d_down = k.xs[grad, rows, :].astype(LOWER)
        k.dout[rows, :] = d_down
        k.sgl[l, 12:13, :] += col_sum(d_down.astype(WIDE))
        d_second = jnp.zeros((CHUNK, D), WIDE)
        for j in range(4):
            cols = slice(j * D, (j + 1) * D)
            d_acted = dot_nt(d_down, k.w_down(l, j))
            d_hidden = (d_acted * k.slope[rows, cols].astype(WIDE)).astype(LOWER)
            k.work[rows, cols] = d_hidden
            k.sgl[l, 8 + j : 9 + j, :] += col_sum(d_hidden.astype(WIDE))
            d_second = d_second + dot_nt(d_hidden, k.w_up(l, j))
        xhat, scale = norm_parts(k.mid[rows, :])
        k.sgl[l, 2:3, :] += col_sum(d_second * xhat)
        k.sgl[l, 3:4, :] += col_sum(d_second)
        k.xs[grad, rows, :] += norm_back(xhat, scale, k.row(l, 2), d_second)

    each_chunk(chunk, between)


def backward_ffn_grads(k, l):
    for j in range(4):
        cols = slice(j * D, (j + 1) * D)
        store_blocks(k.wf, l, range(BLOCKS), 16 * j, 16, dot(k.second_t[...], k.work[:, cols]))
        store_blocks(k.wf, l, range(8 * j, 8 * j + 8), 64, 64, dot(k.act_t[cols, :], k.dout[...]))


def backward_attn(k, l, grad):
    def before(c, rows):
        d_branch = k.xs[grad, rows, :].astype(LOWER)
        k.left[rows, :] = d_branch
        k.sgl[l, 7:8, :] += col_sum(d_branch.astype(WIDE))
        k.dout[rows, :] = dot_nt(d_branch, k.w_out(l)).astype(LOWER)

    each_chunk(before)
    store_blocks(k.wa, l + 1, range(BLOCKS), 48, 16, dot(k.mixed_t[...], k.left[...]))
    first = iota((SLOT, 128), 1) < HD
    scale = HD**-0.5

    def window(w):
        rows = window_rows(w)
        bias = k.bias[rows, :]
        for p in range(H // 2):
            at = p * 128
            query = stack_pair(k.qkv[rows, at : at + 128] * jnp.asarray(scale, LOWER), first)
            keyed = k.qkv[rows, D + at : D + at + 128]
            values = k.qkv[rows, 2 * D + at : 2 * D + at + 128]
            d_mixed = stack_pair(k.dout[rows, at : at + 128], first)
            probs = jnp.exp(dot_nt(keyed, query) + bias - k.logs[l, w, p : p + 1, :])
            d_probs = dot_nt(values, d_mixed)
            d_values = dot(probs.astype(LOWER), d_mixed)
            inner = probs * d_probs
            d_scores = (inner - probs * jnp.sum(inner, 0, keepdims=True)).astype(LOWER)
            d_keyed = dot(d_scores, query)
            d_query = join_pair(dot_tn(d_scores, keyed), first) * scale
            k.work[rows, at : at + 128] = d_query.astype(LOWER)
            k.work[rows, D + at : D + at + 128] = d_keyed.astype(LOWER)
            k.work[rows, 2 * D + at : 2 * D + at + 128] = d_values.astype(LOWER)

    each_window(window)


def backward_attn_grads(k, l):
    for j in range(3):
        part = dot(k.normed_t[...], k.work[:, j * D : (j + 1) * D])
        store_blocks(k.wa, l + 1, range(BLOCKS), 16 * j, 16, part)


def backward_input(k, l, grad):
    def chunk(c, rows):
        d_normed = jnp.zeros((CHUNK, D), WIDE)
        for j in range(3):
            d_part = k.work[rows, j * D : (j + 1) * D]
            k.sgl[l, 4 + j : 5 + j, :] += col_sum(d_part.astype(WIDE))
            d_normed = d_normed + dot_nt(d_part, k.w_qkv(l, j))
        xhat, scale = norm_parts(k.xs[slot(l), rows, :])
        k.sgl[l, 0:1, :] += col_sum(d_normed * xhat)
        k.sgl[l, 1:2, :] += col_sum(d_normed)
        k.xs[grad, rows, :] += norm_back(xhat, scale, k.row(l, 0), d_normed)

    each_chunk(chunk)


def small_stage(k, out, grad):
    out[...] = jnp.zeros_like(out)
    out[0:EMB, :] = dot_tn(k.feats[...], k.xs[grad], HIGH)[0:EMB]
    out[FIN : FIN + 2, :] = k.sgh[0:2, :]
    out[HEADW : HEADW + A, :] = k.sgw[0, 0:A, :]
    out[HEADW + A : HEADW + 2 * A, :] = k.sgw[1, 0:A, :]
    for l in range(LAYERS):
        out[BASE + l * PER : BASE + (l + 1) * PER, :] = k.sgl[l, 0:PER, :]
    out[NROWS : NROWS + 3, :] = k.sgh[2:5, :]


WORK_SHAPES = dict(
    wa=((LAYERS + 1, 4, 8, ATTN, D), LOWER),
    wf=((LAYERS, 4, 8, FFN, D), LOWER),
    xs=((3, ROWS, D), WIDE),
    qkv=((ROWS, 3 * D), LOWER),
    normed_t=((D, ROWS), LOWER),
    mixed_t=((D, ROWS), LOWER),
    slope=((ROWS, FF), LOWER),
    act_t=((FF, ROWS), LOWER),
    second_t=((D, ROWS), LOWER),
    mid=((ROWS, D), WIDE),
    logs=((LAYERS, WINS, 8, 128), WIDE),
    work=((ROWS, FF), LOWER),
    left=((ROWS, D), LOWER),
    dout=((ROWS, D), LOWER),
    feats=((ROWS, 128), WIDE),
    bias=((ROWS, 128), WIDE),
    headw=((2, 128, D), LOWER),
    lrows=((LAYERS, 16, D), WIDE),
    sgl=((LAYERS, 16, D), WIDE),
    sgh=((8, D), WIDE),
    sgw=((2, 8, D), WIDE),
)
KEEP_ATTN = ("qkv", "normed_t", "mixed_t")
KEEP_FFN = ("slope", "act_t", "second_t", "mid")
KEEP = KEEP_ATTN + KEEP_FFN


MESH = pl.DeviceIdType.MESH
NZ, NY, NX, NC = 4, 2, 2, 2
NR = NY * NX * NC
SHARD = PACK
PART = (ATTN, FFN)


class Place:
    def __init__(self):
        dp, fsdp = lax.axis_index("dp"), lax.axis_index("fsdp")
        self.z, self.y = dp // NY, dp % NY
        self.x, self.c = fsdp // NC, fsdp % NC
        self.a, self.b = 2 * self.c + self.x, 4 * self.y + self.z
        self.to_x = (dp, (1 - self.x) * NC + self.c)
        self.to_y = (self.z * NY + 1 - self.y, fsdp)
        self.to_c = (dp, self.x * NC + 1 - self.c)
        self.to_z = [(((self.z + d) % NZ) * NY + self.y, fsdp) for d in range(1, NZ)]
        self.partners = [self.to_c, self.to_x, self.to_y] + self.to_z

    def barrier(self):
        sem = pltpu.get_barrier_semaphore()
        for partner in self.partners:
            pl.semaphore_signal(sem, inc=1, device_id=partner, device_id_type=MESH)
        pl.semaphore_wait(sem, len(self.partners))


def remote(src, dst, send, recv, to):
    return pltpu.make_async_remote_copy(
        src_ref=src, dst_ref=dst, send_sem=send, recv_sem=recv, device_id=to, device_id_type=MESH
    )


class Gather:
    COPIES = 11

    def __init__(self, place, weights, send, recv):
        self.at, self.weights, self.send, self.recv = place, weights, send, recv

    def copy(self, l, part, n):
        at, count = self.at, PART[part]
        half = count // 2
        a, b, rows, to = at.a, pl.ds(4 * at.y, 4), pl.ds(0, count), at.to_c
        if n < 3:
            b, to = at.b, at.to_z[n]
        elif n < 5:
            to = (at.to_x, at.to_y)[n - 3]
        if n in (6, 8, 10):
            a = 2 * at.c + 1 - at.x
        if n in (7, 9, 10):
            b = pl.ds(4 * (1 - at.y), 4)
        if n in (6, 7):
            rows, to = pl.ds((n - 6) * half, half), (at.to_y, at.to_x)[n - 6]
        ref = self.weights[part].at[l, a, b, rows, :]
        q = 2 * l + part
        return remote(ref, ref, self.send.at[q, n], self.recv.at[q, n], to)

    def start(self, l, part, *ns):
        for n in ns:
            self.copy(l, part, n).start()

    def wait(self, l, part, *ns):
        for n in ns:
            self.copy(l, part, n).wait_recv()

    def first(self, l, part):
        self.start(l, part, 0, 1, 2)

    def second(self, l, part):
        self.wait(l, part, 0, 1, 2)
        self.start(l, part, 3, 4, 5)

    def third(self, l, part):
        self.wait(l, part, 3)
        self.start(l, part, 6, 8)
        self.wait(l, part, 4)
        self.start(l, part, 7, 9)

    def fourth(self, l, part):
        self.wait(l, part, 6, 7)
        self.start(l, part, 10)

    def last(self, l, part):
        self.wait(l, part, 5, 8, 9, 10)

    def sent(self, l, part):
        for n in range(self.COPIES):
            self.copy(l, part, n).wait_send()


class Reduce:
    COPIES = 8

    def __init__(self, place, grads, landing, send, recv, credit):
        self.at, self.grads, self.landing = place, grads, landing
        self.send, self.recv, self.credit = send, recv, credit

    def refs(self, l, part):
        grads = self.grads[part].at[l + 1 - part]
        r0, r1a, r1b, r2, r3 = self.landing[part]
        return grads, r0, r1a, r1b, r2, r3

    def copy(self, l, part, n):
        at, half = self.at, PART[part] // 2
        g, r0, r1a, r1b, r2, r3 = self.refs(l, part)
        top, low, other = pl.ds(0, half), pl.ds(half, half), pl.ds(4 * (1 - at.y), 4)
        if n == 0:
            src, dst, to = g.at[pl.ds(2 * (1 - at.c), 2)], r0, at.to_c
        elif n == 1:
            src, dst, to = r0.at[1 - at.x, :, top, :], r1a, at.to_x
        elif n == 2:
            src, dst, to = r0.at[:, other, low, :], r1b, at.to_y
        elif n == 3:
            src, dst, to = r1a.at[other], r2.at[:, top, :], at.to_y
        elif n == 4:
            src, dst, to = r1b.at[1 - at.x], r2.at[:, low, :], at.to_x
        else:
            src, dst, to = r2.at[(at.z + n - 4) % NZ], r3.at[n - 5], at.to_z[n - 5]
        q = 2 * l + part
        return remote(src, dst, self.send.at[q, n], self.recv.at[q, n], to)

    def may_send(self, l, part, *partners):
        @pl.when(l < LAYERS - 1)
        def _():
            for n in partners:
                pl.semaphore_wait(self.credit.at[part, n], 1)

    def allow(self, l, part, *credits):
        at = self.at

        @pl.when(l > 0)
        def _():
            for n, to in credits:
                pl.semaphore_signal(
                    self.credit.at[part, n], inc=1, device_id=to, device_id_type=MESH
                )

    def start(self, l, part):
        self.may_send(l, part, 0)
        self.copy(l, part, 0).start()

    def first(self, l, part):
        at, half = self.at, PART[part] // 2
        g, r0, _, _, _, _ = self.refs(l, part)
        top, low = pl.ds(0, half), pl.ds(half, half)
        self.copy(l, part, 0).wait_recv()

        def along_x(n, carry):
            x = 1 - at.x
            total = g[2 * at.c + x, n, top].astype(WIDE) + r0[x, n, top].astype(WIDE)
            r0[x, n, top] = total.astype(LOWER)
            return carry

        def along_y(n, carry):
            x, b = n // 4, 4 * (1 - at.y) + n % 4
            total = g[2 * at.c + x, b, low].astype(WIDE) + r0[x, b, low].astype(WIDE)
            r0[x, b, low] = total.astype(LOWER)
            return carry

        lax.fori_loop(0, 8, along_x, 0)
        self.may_send(l, part, 1, 2)
        self.copy(l, part, 1).start()
        lax.fori_loop(0, 8, along_y, 0)
        self.copy(l, part, 2).start()

    def second(self, l, part):
        at, half = self.at, PART[part] // 2
        g, r0, r1a, r1b, _, _ = self.refs(l, part)
        top, low = pl.ds(0, half), pl.ds(half, half)

        def along_y(n, carry):
            b = 4 * (1 - at.y) + n
            total = g[at.a, b, top].astype(WIDE) + r0[at.x, b, top].astype(WIDE)
            r1a[b] = (total + r1a[b].astype(WIDE)).astype(LOWER)
            return carry

        def along_x(n, carry):
            x, b = 1 - at.x, 4 * at.y + n
            total = g[2 * at.c + x, b, low].astype(WIDE) + r0[x, b, low].astype(WIDE)
            r1b[x, n] = (total + r1b[x, n].astype(WIDE)).astype(LOWER)
            return carry

        self.copy(l, part, 1).wait_recv()
        lax.fori_loop(0, NZ, along_y, 0)
        self.may_send(l, part, 6, 7)
        self.copy(l, part, 3).start()
        self.copy(l, part, 2).wait_recv()
        lax.fori_loop(0, NZ, along_x, 0)
        self.copy(l, part, 4).start()

    def chip_sums(self, l, part, z):
        at, half = self.at, PART[part] // 2
        g, r0, r1a, r1b, r2, _ = self.refs(l, part)
        top, low, b = pl.ds(0, half), pl.ds(half, half), 4 * at.y + z
        upper = g[at.a, b, top].astype(WIDE) + r0[at.x, b, top].astype(WIDE)
        lower = g[at.a, b, low].astype(WIDE) + r0[at.x, b, low].astype(WIDE)
        return (
            upper + r1a[b].astype(WIDE) + r2[z, top].astype(WIDE),
            lower + r1b[at.x, z].astype(WIDE) + r2[z, low].astype(WIDE),
        )

    def third(self, l, part, out):
        at, half, row = self.at, PART[part] // 2, (0, ATTN)[part]
        r2 = self.landing[part][3]
        for n in (3, 4):
            self.copy(l, part, n).wait_recv()
        self.may_send(l, part, 3, 4, 5)
        for n in range(3):
            z = (at.z + n + 1) % NZ
            upper, lower = self.chip_sums(l, part, z)
            r2[z, pl.ds(0, half)] = upper.astype(LOWER)
            r2[z, pl.ds(half, half)] = lower.astype(LOWER)
            self.copy(l, part, 5 + n).start()
        upper, lower = self.chip_sums(l, part, at.z)
        out[l, row : row + half, :] = upper
        out[l, row + half : row + 2 * half, :] = lower
        for n in range(5):
            self.copy(l, part, n).wait_send()
        self.allow(l, part, (0, at.to_c), (1, at.to_x), (2, at.to_y))

    def last(self, l, part, out, squares):
        at, row = self.at, (0, ATTN)[part]
        r3 = self.landing[part][4]
        rows = slice(row, row + PART[part])
        total = out[l, rows, :]
        for n in range(3):
            self.copy(l, part, 5 + n).wait_recv()
            total = total + r3[n].astype(WIDE)
        out[l, rows, :] = total
        squares[0:1, :] += col_sum(total * total)
        for n in range(5, self.COPIES):
            self.copy(l, part, n).wait_send()
        late = [(6, at.to_x), (7, at.to_y)] + [(5 - n, at.to_z[n]) for n in range(3)]
        self.allow(l, part, *late)


class Total:
    COPIES = 6

    def __init__(self, place, ref, first, rows, send, recv):
        self.at, self.ref, self.first, self.rows = place, ref, first, rows
        self.send, self.recv = send, recv

    def own(self, n):
        return self.ref.at[pl.ds(self.first + n * self.rows, self.rows), :]

    def got(self, n):
        return self.own(4 + n)

    def copy(self, n):
        src, dst = self.own(min(n, 3)), self.got(n)
        return remote(src, dst, self.send.at[n], self.recv.at[n], self.at.partners[n])

    def start(self):
        self.copy(0).start()

    def step(self, n):
        self.copy(n).wait_recv()
        self.own(n + 1)[...] = self.own(n)[...] + self.got(n)[...]
        for m in ((1,), (2,), (3, 4, 5))[n]:
            self.copy(m).start()

    def last(self):
        for m in (3, 4, 5):
            self.copy(m).wait_recv()
        total = None
        for z in range(NZ):
            term = self.own(3)[...]
            for n in range(3):
                from_z = (self.at.z + NZ - 1 - n) % NZ
                term = jnp.where(from_z == z, self.got(3 + n)[...], term)
            total = term if total is None else total + term
        return total

    def sent(self):
        for n in range(self.COPIES):
            self.copy(n).wait_send()


def landing_shapes(count):
    half = count // 2
    return [
        (NX, 8, count, D),
        (8, half, D),
        (NX, NZ, half, D),
        (NZ, count, D),
        (3, count, D),
    ]


def stage_rows(qkv, out, up, down, l):
    return (
        [(qkv.at[l, :, pl.ds(j * D, D)], 16 * j, 16) for j in range(3)]
        + [(out.at[l], 48, 16)]
        + [(up.at[l, :, pl.ds(j * D, D)], 64 + 16 * j, 16) for j in range(4)]
        + [(down.at[l], 128, 64)]
    )


GATHER_PLAN = {
    (-1, "start"): [("first", 0, 0), ("first", 0, 1), ("first", 1, 0), ("first", 1, 1)],
    (-1, "setup"): [("second", 0, 0), ("third", 0, 0), ("fourth", 0, 0), ("last", 0, 0)],
    (0, "qkv"): [("second", 0, 1), ("first", 2, 0), ("second", 1, 0)],
    (0, "windows"): [("third", 0, 1), ("first", 2, 1), ("fourth", 0, 1), ("last", 0, 1)],
    (0, "half"): [("third", 1, 0), ("second", 1, 1)],
    (0, "ffn"): [("fourth", 1, 0), ("second", 2, 0), ("last", 1, 0)],
    (1, "qkv"): [("third", 1, 1), ("fourth", 1, 1)],
    (1, "windows"): [("third", 2, 0), ("second", 2, 1), ("last", 1, 1)],
    (1, "half"): [("fourth", 2, 0)],
    (1, "ffn"): [("last", 2, 0), ("third", 2, 1)],
    (2, "qkv"): [("fourth", 2, 1)],
    (2, "windows"): [("last", 2, 1)],
}


def train_kernel(refs, alone):
    k = Kit(**refs)

    def kept(names, l, back):
        copies = []
        for name in names:
            here, there = refs[name], refs["keep_" + name].at[l]
            src, dst = (there, here) if back else (here, there)
            copies.append(pltpu.make_async_copy(src, dst, k.keep_sem.at[KEEP.index(name)]))
        return copies

    def start(copies):
        for copy in copies:
            copy.start()

    def wait(copies):
        for copy in copies:
            copy.wait()

    def kept_x(back):
        here, there = k.xs.at[0], k.keep_x
        src, dst = (there, here) if back else (here, there)
        return [pltpu.make_async_copy(src, dst, k.keep_sem.at[len(KEEP)])]

    parts = [(l, part) for l in range(LAYERS) for part in (0, 1)]
    weights = (k.wa, k.wf)
    if alone:
        loads = [
            pltpu.make_async_copy(ref, weights[part].at[l], k.load_sem.at[2 * l + part])
            for l, part in parts
            for ref in [(k.all_a, k.all_f)[part].at[l]]
        ]
        stores = [
            pltpu.make_async_copy(
                weights[part].at[l + 1 - part],
                (k.grad_a, k.grad_f)[part].at[l],
                k.load_sem.at[2 * l + part],
            )
            for l, part in parts
        ]
        start(loads)
    else:
        place = Place()
        gather = Gather(place, weights, k.gather_send, k.gather_recv)
        reduce = Reduce(
            place, weights, (k.land_a, k.land_f), k.reduce_send, k.reduce_recv, k.credit
        )
        sums = Total(place, k.mid, 0, SMALL, k.sum_send, k.sum_recv)
        norm = Total(place, k.mid, 10 * SMALL, 8, k.norm_send, k.norm_recv)

    def run(plan):
        for stage, l, part in plan:
            getattr(gather, stage)(l, part)

    def poll(l, point):
        if alone:
            return
        for layer in range(LAYERS):
            plan = GATHER_PLAN.get((layer, point))
            if plan:

                @pl.when(l == layer)
                def _(plan=plan):
                    run(plan)

    if not alone:
        staged = []
        for l in range(LAYERS):
            for n, (src, row, count) in enumerate(stage_rows(k.qkv_w, k.out_w, k.up_w, k.down_w, l)):
                dst = k.xs.at[2, pl.ds(l * PACK + row, count), :]
                staged.append(pltpu.make_async_copy(src, dst, k.stage_sem.at[l, n]))
        start(staged)
        place.barrier()
        for l in range(LAYERS):
            wait(staged[9 * l : 9 * l + 9])
            row = l * PACK
            for part, (low, high) in enumerate(((0, ATTN), (ATTN, PACK))):
                weights[part][l, place.a, place.b] = k.xs[2, row + low : row + high, :].astype(LOWER)
                if ("first", l, part) in GATHER_PLAN[-1, "start"]:
                    gather.first(l, part)
        k.squares_sum[...] = jnp.zeros_like(k.squares_sum)

    setup_stage(k)
    start(kept_x(False))
    if not alone:
        run(GATHER_PLAN[-1, "setup"])

    def forward(l, carry):
        if alone:
            pltpu.make_async_copy(k.all_a.at[l], k.wa.at[l], k.load_sem.at[2 * l]).wait()

        @pl.when(l > 0)
        def _():
            wait(kept(KEEP_ATTN, l - 1, False))

        forward_qkv(k, l)
        poll(l, "qkv")
        forward_windows(k, l)

        @pl.when(l < LAYERS - 1)
        def _():
            start(kept(KEEP_ATTN, l, False))

        @pl.when(l > 0)
        def _():
            wait(kept(KEEP_FFN, l - 1, False))

        @pl.when(l == 1)
        def _():
            wait(kept_x(False))

        if alone:
            pltpu.make_async_copy(k.all_f.at[l], k.wf.at[l], k.load_sem.at[2 * l + 1]).wait()
        poll(l, "windows")
        forward_ffn(k, l, (l + 1) % 2 + l // 2, lambda: poll(l, "half"))

        @pl.when(l < LAYERS - 1)
        def _():
            start(kept(KEEP_FFN, l, False))

        poll(l, "ffn")
        return carry

    lax.fori_loop(0, LAYERS, forward, 0)
    if not alone:
        for l, part in parts:
            gather.sent(l, part)
    grad = 2
    head_stage(k, grad)

    def backward(n, carry):
        l = LAYERS - 1 - n

        def behind(*stages):
            if alone:
                return

            @pl.when(n > 0)
            def _():
                for stage, part, *more in stages:
                    stage(l + 1, part, *more)

        @pl.when(n > 0)
        def _():
            wait(kept(KEEP_FFN, l, True))

        backward_ffn(k, l, grad)
        if not alone:
            behind((reduce.second, 1), (reduce.second, 0))
        backward_ffn_grads(k, l)

        @pl.when(n < LAYERS - 1)
        def _():
            start(kept(KEEP_FFN, l - 1, True))

        if not alone:
            behind((reduce.third, 1, k.shard), (reduce.third, 0, k.shard))
            reduce.start(l, 1)

        @pl.when(n > 0)
        def _():
            wait(kept(KEEP_ATTN, l, True))

        backward_attn(k, l, grad)
        if not alone:
            reduce.first(l, 1)
        backward_attn_grads(k, l)

        @pl.when(n < LAYERS - 1)
        def _():
            start(kept(KEEP_ATTN, l - 1, True))

        if not alone:
            reduce.start(l, 0)
            behind((reduce.last, 1, k.shard, k.squares_sum), (reduce.last, 0, k.shard, k.squares_sum))

        @pl.when(n == LAYERS - 1)
        def _():
            wait(kept_x(True))

        backward_input(k, l, grad)

        @pl.when(n == 0)
        def _():
            start(kept_x(True))

        if not alone:
            reduce.first(l, 0)
        return carry

    lax.fori_loop(0, LAYERS, backward, 0)
    if alone:
        start(stores)
        small_stage(k, k.small_out, grad)
        wait(stores)
        return
    small_stage(k, sums.own(0), grad)
    sums.start()
    reduce.second(0, 1)
    reduce.second(0, 0)
    sums.step(0)
    reduce.third(0, 1, k.shard)
    reduce.third(0, 0, k.shard)
    sums.step(1)
    reduce.last(0, 1, k.shard, k.squares_sum)
    reduce.last(0, 0, k.shard, k.squares_sum)
    norm.own(0)[...] = k.squares_sum[...]
    norm.start()
    sums.step(2)
    norm.step(0)
    norm.step(1)
    k.small_out[...] = sums.last()
    norm.step(2)
    k.squares[...] = norm.last()
    sums.sent()
    norm.sent()


def train_pass(meta, buf, small, head_bias, log_temp, weights, alone):
    whole = pl.BlockSpec(memory_space=pltpu.VMEM)
    scalars = pl.BlockSpec(memory_space=pltpu.SMEM)
    anywhere = pl.BlockSpec(memory_space=pl.ANY)
    dma = pltpu.SemaphoreType.DMA
    count = 2 * LAYERS
    names = ["meta", "buf", "small", "head_bias", "log_temp"]
    out_shape = {"small_out": ((SMALL, D), WIDE)}
    for name in KEEP:
        shape, dtype = WORK_SHAPES[name]
        out_shape["keep_" + name] = ((LAYERS - 1,) + shape, dtype)
    out_shape["keep_x"] = ((ROWS, D), WIDE)
    scratch = {name: pltpu.VMEM(*shape) for name, shape in WORK_SHAPES.items()}
    scratch["keep_sem"] = dma((len(KEEP) + 1,))
    if alone:
        names += ["all_a", "all_f"]
        out_shape["grad_a"] = ((LAYERS, 4, 8, ATTN, D), LOWER)
        out_shape["grad_f"] = ((LAYERS, 4, 8, FFN, D), LOWER)
        scratch["load_sem"] = dma((count,))
    else:
        names += ["qkv_w", "out_w", "up_w", "down_w"]
        out_shape["shard"] = ((LAYERS, PACK, D), WIDE)
        out_shape["squares"] = ((8, D), WIDE)
        for part, name in enumerate("af"):
            for n, shape in enumerate(landing_shapes(PART[part])):
                scratch["land_%s%d" % (name, n)] = pltpu.VMEM(shape, LOWER)
        scratch["stage_sem"] = dma((LAYERS, 9))
        scratch["squares_sum"] = pltpu.VMEM((8, D), WIDE)
        for name, copies in (("gather", Gather.COPIES), ("reduce", Reduce.COPIES)):
            scratch[name + "_send"] = dma((count, copies))
            scratch[name + "_recv"] = dma((count, copies))
        scratch["credit"] = pltpu.SemaphoreType.REGULAR((2, 8))
        for name in ("sum", "norm"):
            scratch[name + "_send"] = dma((6,))
            scratch[name + "_recv"] = dma((6,))
    spaces = dict(head_bias=scalars, log_temp=scalars)
    for name in ("all_a", "all_f", "grad_a", "grad_f", "qkv_w", "out_w", "up_w", "down_w"):
        spaces[name] = anywhere
    for name in KEEP + ("x",):
        spaces["keep_" + name] = anywhere
    every = names + list(out_shape) + list(scratch)

    def kernel(*given):
        refs = dict(zip(every, given))
        for name in "af":
            refs["land_" + name] = [refs.get("land_%s%d" % (name, n)) for n in range(5)]
        train_kernel(refs, alone)

    results = pl.pallas_call(
        kernel,
        name="train_pass",
        out_shape=tuple(jax.ShapeDtypeStruct(*shape) for shape in out_shape.values()),
        in_specs=[spaces.get(name, whole) for name in names],
        out_specs=tuple(spaces.get(name, whole) for name in out_shape),
        scratch_shapes=list(scratch.values()),
        compiler_params=pltpu.CompilerParams(
            vmem_limit_bytes=VMEM_BYTES,
            collective_id=None if alone else 0,
            has_side_effects=not alone,
        ),
        cost_estimate=pl.CostEstimate(
            flops=6 * 10**10, bytes_accessed=4 * 10**7, transcendentals=10**7
        ),
    )(meta, buf, small, head_bias, log_temp, *weights)
    return dict(zip(out_shape, results))


def small_inputs(buf_states, buf_actions, buf_returns, window_starts, window_repeats, valid_steps):
    meta = jnp.concatenate(
        [window_starts[:, None], window_repeats[:, None], valid_steps], 1
    ).astype(WIDE)
    meta = jnp.pad(meta, ((0, 128 - meta.shape[0]), (0, 128 - meta.shape[1])))
    buf = jnp.concatenate([buf_states, buf_actions, buf_returns[:, None]], 1)
    buf = jnp.pad(buf, ((0, 128 - buf.shape[0]), (0, 128 - buf.shape[1])))
    return meta, buf


def adam_parts(weight, grad, first, second, rate):
    first = BETA_ONE * first + (1.0 - BETA_ONE) * grad
    second = BETA_TWO * second + (1.0 - BETA_TWO) * grad * grad
    fix_one = 1.0 - BETA_ONE**STEP
    fix_two = 1.0 - BETA_TWO**STEP
    fresh = weight - rate * (
        first / fix_one / (jnp.sqrt(second / fix_two) + ADAM_EPS) + DECAY * weight
    )
    return fresh, first, second


def adam_kernel(*refs):
    shard, small_grad, squares, groups, log_temp = refs[:5]
    small, small_first, small_second, bias, bias_first, bias_second = refs[5:11]
    mats, firsts, seconds = refs[11:15], refs[15:19], refs[19:23]
    totals, norm, next_temp, s_next, s_first, s_second, b_next, b_first, b_second = refs[23:32]
    m_next, m_copy, m_first, m_second = refs[32:36], refs[36:40], refs[40:44], refs[44:48]
    l = pl.program_id(0)
    extra = small_grad[NROWS : NROWS + 3, 0:128]
    lane = iota((1, 128), 1)
    bias_mean = jnp.where(lane < A, extra[1:2], 0.0)
    bias_spread = jnp.where(lane < A, extra[2:3], 0.0)

    def all_sum(v):
        return jnp.sum(jnp.sum(v, 0, keepdims=True), 1, keepdims=True)

    grads = small_grad[0:NROWS, :]
    square = (
        all_sum(squares[0:1, :])
        + all_sum(grads * grads)
        + all_sum(bias_mean * bias_mean)
        + all_sum(bias_spread * bias_spread)
    )
    length = jnp.sqrt(square)
    clip = jnp.minimum(1.0, CLIP / (length + 1e-06))

    def rate_of(kind):
        group = jnp.full((1, 1), groups[l, kind], jnp.int32).astype(WIDE)
        return LEARN * jnp.exp2(-group)

    def update(kind, rows, cols, grad):
        at = (0, rows, cols)
        fresh, first, second = adam_parts(
            mats[kind][at], clip * grad, firsts[kind][at], seconds[kind][at], rate_of(kind)
        )
        m_next[kind][at] = fresh
        m_copy[kind][at] = fresh.astype(LOWER)
        m_first[kind][at] = first
        m_second[kind][at] = second

    every = slice(0, 16)
    for j in range(3):
        update(0, every, slice(j * D, (j + 1) * D), shard[0, 16 * j : 16 * j + 16, :])
    update(1, every, slice(0, D), shard[0, 48:64, :])
    for j in range(4):
        update(2, every, slice(j * D, (j + 1) * D), shard[0, 64 + 16 * j : 80 + 16 * j, :])
    update(3, slice(0, 64), slice(0, D), shard[0, 128:192, :])

    @pl.when(l == 0)
    def _():
        s_next[...], s_first[...], s_second[...] = adam_parts(
            small[...], clip * grads, small_first[...], small_second[...], LEARN
        )

        def scalar(v, n):
            return jnp.sum(jnp.where(lane == n, v, 0.0))

        def row(ref):
            v = jnp.zeros((1, 128), WIDE)
            for n in range(2 * A):
                v = jnp.where(lane == n, ref[n], v)
            return v

        grad = bias_mean + pltpu.roll(bias_spread, A, 1)
        results = adam_parts(row(bias), clip * grad, row(bias_first), row(bias_second), LEARN)
        for ref, result in zip((b_next, b_first, b_second), results):
            for n in range(2 * A):
                ref[n] = scalar(result, n)
        sums = extra[0:1]
        for n in range(3):
            totals[n] = scalar(sums, n)
        norm[0] = jnp.sum(length)
        logs = jnp.full((1, 1), log_temp[0], WIDE)
        ratio = jnp.full((1, 1), scalar(sums, 1), WIDE) / jnp.full((1, 1), scalar(sums, 2), WIDE)
        next_temp[0] = jnp.sum(logs - TEMP_RATE * jnp.exp(logs) * (ratio + A))


def adam_all(shard, small_grad, squares, groups, log_temp, smalls, biases, mats, firsts, seconds):
    scalars = pl.BlockSpec(memory_space=pltpu.SMEM)

    def fixed(array):
        return pl.BlockSpec(array.shape, lambda l: (0,) * array.ndim)

    def layer(array):
        return pl.BlockSpec((1,) + array.shape[1:], lambda l: (l, 0, 0))

    def like(array, dtype=WIDE):
        return jax.ShapeDtypeStruct(array.shape, dtype)

    stacks = list(mats) + list(firsts) + list(seconds)
    small, bias = smalls[0], biases[0]
    return pl.pallas_call(
        adam_kernel,
        name="adam",
        grid=(LAYERS,),
        out_shape=(
            (jax.ShapeDtypeStruct((3,), WIDE),)
            + (jax.ShapeDtypeStruct((1,), WIDE),) * 2
            + (like(small),) * 3
            + (like(bias),) * 3
            + tuple(like(m) for m in mats)
            + tuple(like(m, LOWER) for m in mats)
            + tuple(like(m) for m in mats) * 2
        ),
        in_specs=[layer(shard), fixed(small_grad), fixed(squares), scalars, scalars]
        + [fixed(small)] * 3
        + [scalars] * 3
        + [layer(m) for m in stacks],
        out_specs=(scalars,) * 3
        + (fixed(small),) * 3
        + (scalars,) * 3
        + tuple(layer(m) for m in mats) * 4,
        compiler_params=pltpu.CompilerParams(vmem_limit_bytes=VMEM_BYTES),
        cost_estimate=pl.CostEstimate(flops=10**7, bytes_accessed=8 * 10**6, transcendentals=10**6),
    )(shard, small_grad, squares, groups, log_temp, *smalls, *biases, *stacks)


def gather_packed(mats, axes, count):
    group = count // BLOCKS
    pieces = []
    for mat in mats:
        rows, wide = mat.shape[1], mat.shape[2] // D
        piece = mat.astype(LOWER).reshape(LAYERS, rows, wide, D)
        piece = lax.all_gather(piece, axes, axis=1, tiled=True)
        piece = piece.reshape(LAYERS, NZ, NY, NX, NC, group * rows, wide, D)
        piece = piece.transpose(0, 4, 3, 2, 1, 6, 5, 7)
        pieces.append(piece.reshape(LAYERS, 4, 8, wide * group * rows, D))
    return jnp.concatenate(pieces[:2], 3), jnp.concatenate(pieces[2:], 3)


def scatter_packed(grads, mats, axes):
    results, first = [], 0
    for n, mat in enumerate(mats):
        rows, wide = mat.shape[1], mat.shape[2] // D
        total = lax.psum(1, axes) * rows
        deep = total // BLOCKS
        first = 0 if n % 2 == 0 else first
        piece = grads[n // 2][:, :, :, first : first + wide * deep].astype(WIDE)
        first += wide * deep
        piece = piece.reshape(LAYERS, NC, NX, NY, NZ, wide, deep, D)
        piece = piece.transpose(0, 4, 3, 2, 1, 6, 5, 7).reshape(LAYERS, total, wide * D)
        results.append(lax.psum_scatter(piece, axes, scatter_dimension=1, tiled=True))
    return results


def local(
    buf_states,
    buf_actions,
    buf_returns,
    window_starts,
    window_repeats,
    valid_steps,
    matrix_groups,
    log_temp,
    small_rows,
    head_bias,
    qkv_weight,
    out_weight,
    up_weight,
    down_weight,
    small_first,
    bias_first,
    qkv_first,
    out_first,
    up_first,
    down_first,
    small_second,
    bias_second,
    qkv_second,
    out_second,
    up_second,
    down_second,
):
    axes = ("dp", "fsdp")
    mats = (qkv_weight, out_weight, up_weight, down_weight)
    firsts = (qkv_first, out_first, up_first, down_first)
    seconds = (qkv_second, out_second, up_second, down_second)
    meta, buf = small_inputs(
        buf_states, buf_actions, buf_returns, window_starts, window_repeats, valid_steps
    )
    pass_inputs = (meta, buf, small_rows, head_bias, log_temp)
    if FF // down_weight.shape[1] == BLOCKS and lax.psum(1, "fsdp") == NX * NC:
        made = train_pass(*pass_inputs, mats, False)
        return adam_all(
            made["shard"],
            made["small_out"],
            made["squares"],
            matrix_groups,
            log_temp,
            (small_rows, small_first, small_second),
            (head_bias, bias_first, bias_second),
            mats,
            firsts,
            seconds,
        )
    packed = gather_packed(mats, axes, FF // down_weight.shape[1])
    made = train_pass(*pass_inputs, packed, True)
    big = scatter_packed((made["grad_a"], made["grad_f"]), mats, axes)
    small = made["small_out"]
    small = lax.psum(small, axes)
    small_grad, totals = small[:NROWS], small[NROWS, :3]
    bias_grad = jnp.concatenate([small[NROWS + 1, :A], small[NROWS + 2, :A]])
    square = sum((jnp.sum(piece * piece) for piece in big))
    square = (
        lax.psum(square, axes) + jnp.sum(small_grad * small_grad) + jnp.sum(bias_grad * bias_grad)
    )
    grad_norm = jnp.sqrt(square)
    clip = jnp.minimum(1.0, CLIP / (grad_norm + 1e-06))
    rates = LEARN * jnp.exp2(-matrix_groups.astype(WIDE))
    results = [
        adam_parts(
            mats[kind], clip * big[kind], firsts[kind], seconds[kind], rates[:, kind][:, None, None]
        )
        for kind in range(4)
    ]
    small_new = adam_parts(small_rows, clip * small_grad, small_first, small_second, LEARN)
    bias_new = adam_parts(head_bias, clip * bias_grad, bias_first, bias_second, LEARN)
    next_temp = log_temp - TEMP_RATE * jnp.exp(log_temp) * (totals[1] / totals[2] + A)
    return (
        (totals, grad_norm[None], next_temp)
        + small_new
        + bias_new
        + tuple(r[0] for r in results)
        + tuple(r[0].astype(LOWER) for r in results)
        + tuple(r[1] for r in results)
        + tuple(r[2] for r in results)
    )


def solution(mesh):
    rows = P(("dp", "fsdp"), None)
    vector = P(("dp", "fsdp"))
    stack = P(None, ("dp", "fsdp"), None)
    same = P()
    in_specs = (
        (rows, rows, vector, vector, vector, rows)
        + (same,) * 4
        + (stack,) * 4
        + (same,) * 2
        + (stack,) * 4
        + (same,) * 2
        + (stack,) * 4
    )
    out_specs = (same,) * 9 + (stack,) * 16
    return jax.shard_map(local, mesh=mesh, in_specs=in_specs, out_specs=out_specs, check_vma=False)
```

```python
import functools
import math

import jax
import jax.numpy as jnp
from jax import lax
from jax.experimental import pallas as pl
from jax.experimental.pallas import tpu as pltpu
from jax.sharding import PartitionSpec as P

D = 512
H = 8
HD = 64
FF = 2048
S = 11
A = 3
K = 20
STEP = 10

EPS = 1e-05
CLIP = 1.0
LEARN = 0.03
BETA_ONE = 0.5
BETA_TWO = 0.7
DECAY = 0.01
ADAM_EPS = 1e-08
TEMP_RATE = 0.1
MASKED = -1e30
HALF_LOG_TAU = 0.5 * math.log(2.0 * math.pi)
GELU_C = math.sqrt(2.0 / math.pi)
GELU_A = 0.044715
HIGH = lax.Precision.HIGHEST
LOWER = jnp.bfloat16
WIDE = jnp.float32

LAYERS = 3
WINS = 16
BUF_DEV = 64
SLOT = 64
ROWS = WINS * SLOT
CHUNK = 512
CHUNKS = ROWS // CHUNK
BLOCKS = 32
PACK = 192
ATTN, FFN = 64, 128
EMB = S + A + 1 + K + 3
FIN = EMB
HEADW = EMB + 2
BASE = EMB + 2 + 2 * A
PER = 9 + FF // D
NROWS = BASE + LAYERS * PER
SMALL = 88
HEAD_AT = 64
EMB_AT = ROWS - 128
VMEM_BYTES = 64 * 1024 * 1024


def dot(a, b, precision=None):
    return lax.dot_general(
        a, b, (((1,), (0,)), ((), ())), precision=precision, preferred_element_type=WIDE
    )


def dot_nt(a, b, precision=None):
    return lax.dot_general(
        a, b, (((1,), (1,)), ((), ())), precision=precision, preferred_element_type=WIDE
    )


def dot_tn(a, b, precision=None):
    return lax.dot_general(
        a, b, (((0,), (0,)), ((), ())), precision=precision, preferred_element_type=WIDE
    )


def iota(shape, dim):
    return lax.broadcasted_iota(jnp.int32, shape, dim)


def col_sum(v):
    return jnp.sum(v, 0, keepdims=True)


def row_mean(v):
    return jnp.mean(v, -1, keepdims=True)


def norm_parts(x):
    center = x - row_mean(x)
    scale = lax.rsqrt(row_mean(center * center) + EPS)
    return center * scale, scale


def norm_back(xhat, scale, gain, grad):
    scaled = grad * gain
    return scale * (scaled - row_mean(scaled) - xhat * row_mean(scaled * xhat))


def token_rows(at, count):
    row = at + iota((count, 128), 0)
    place = row & (SLOT - 1)
    step = (place * 21846) >> 16
    return row >> 6, step, place - 3 * step, place < 3 * K


def chunk_rows(c):
    return pl.ds(pl.multiple_of(c * CHUNK, CHUNK), CHUNK)


def owner_place(i):
    z, y, x, c = i // 8, (i // 4) % 2, (i // 2) % 2, i % 2
    return 2 * c + x, 4 * y + z


class Kit:
    def __init__(self, **refs):
        self.__dict__.update(refs)

    def row(self, l, k):
        return self.lrows[l, k : k + 1, :]

    def blocks(self, ref, l, first, count, owners):
        places = [owner_place(i) for i in owners]
        return jnp.concatenate([ref[l, a, b, first : first + count, :] for a, b in places], 0)

    def w_qkv(self, l, j):
        return self.blocks(self.wa, l, 16 * j, 16, range(BLOCKS))

    def w_out(self, l):
        return self.blocks(self.wa, l, 48, 16, range(BLOCKS))

    def w_up(self, l, j):
        return self.blocks(self.wf, l, 16 * j, 16, range(BLOCKS))

    def w_down(self, l, j):
        return self.blocks(self.wf, l, 64, 64, range(8 * j, 8 * j + 8))


def slot(l):
    return l % 2


def setup_stage(k):
    k.xs[2, EMB_AT:ROWS, :] = jnp.zeros((128, D), WIDE)
    k.xs[2, EMB_AT : EMB_AT + EMB, :] = k.small[0:EMB, :]
    k.headw[...] = jnp.zeros_like(k.headw)
    k.headw[0, 0:A, :] = k.small[HEADW : HEADW + A, :].astype(LOWER)
    k.headw[1, 0:A, :] = k.small[HEADW + A : HEADW + 2 * A, :].astype(LOWER)
    for l in range(LAYERS):
        k.lrows[l, 0:PER, :] = k.small[BASE + l * PER : BASE + (l + 1) * PER, :]
    k.sgl[...] = jnp.zeros_like(k.sgl)
    k.sgh[...] = jnp.zeros_like(k.sgh)
    k.sgw[...] = jnp.zeros_like(k.sgw)

    lane, sub = iota((WINS, 128), 1), iota((WINS, 128), 0)
    k.meta[...] = jnp.zeros_like(k.meta)
    k.meta[0:WINS, 0:K] = k.valid[...].astype(WIDE)
    meta = k.meta[0:WINS, :]
    for w in range(WINS):
        for n, ref in enumerate((k.starts, k.repeats)):
            meta = jnp.where((sub == w) & (lane == K + n), ref[w].astype(WIDE), meta)
    k.meta[0:WINS, :] = meta
    meta = k.meta[...].astype(LOWER)
    k.buf[...] = jnp.zeros_like(k.buf)
    k.buf[0, 0:S, 0:BUF_DEV] = k.states[...]
    k.buf[0, S + A : S + A + 1, 0:BUF_DEV] = k.returns[...]
    k.buf[1, 0:A, 0:BUF_DEV] = k.actions[...]

    def chunk(c, carry):
        rows = chunk_rows(c)
        win, step, kind, real = token_rows(c * CHUNK, CHUNK)
        lane = iota((CHUNK, 128), 1)
        tok = dot((lane == win).astype(WIDE).astype(LOWER), meta)
        start, repeat = tok[:, K : K + 1], tok[:, K + 1 : K + 2]
        valid = jnp.sum(jnp.where(lane == step, tok, 0.0), -1, keepdims=True)
        key = iota((CHUNK, 128), 0) & (SLOT - 1)
        query = lane & (SLOT - 1)
        allowed = (key <= query) & (((valid > 0.5) & real) | (key == query))
        k.bias[rows, :] = jnp.where(allowed, 0.0, MASKED)
        place = start.astype(jnp.int32) + step
        source = ((lane == place) & real).astype(WIDE)
        raw = dot_nt(source, k.buf[0], HIGH)
        acts = dot_nt(source, k.buf[1], HIGH)
        mine = (
            ((lane < S) & (kind == 1))
            | ((lane >= S) & (lane < S + A) & (kind == 2))
            | ((lane == S + A) & (kind == 0))
        )
        raw = raw + pltpu.roll(acts, S, 1)
        marks = ((lane == S + A + 1 + step) | (lane == S + A + 1 + K + kind)) & real
        feats = jnp.where(mine, raw, 0.0) + marks.astype(WIDE)
        weight = jnp.where((kind == 1) & real, repeat * valid, 0.0)
        acts = pltpu.roll(acts, HEAD_AT, 1)
        ours = (lane >= HEAD_AT) & (lane < HEAD_AT + A)
        feats = jnp.where(ours, acts, jnp.where(lane == HEAD_AT + A, weight, feats))
        k.feats[rows, :] = feats
        k.xs[0, rows, :] = dot(feats, k.xs[2, EMB_AT:ROWS, :], HIGH)
        return carry

    lax.fori_loop(0, CHUNKS, chunk, 0)


def stack_pair(v, first):
    zero = jnp.zeros_like(v)
    return jnp.concatenate([jnp.where(first, v, zero), jnp.where(first, zero, v)], 0)


def join_pair(v, first):
    return jnp.where(first, v[:SLOT], v[SLOT:])


def window_rows(w):
    return pl.ds(pl.multiple_of(w * SLOT, SLOT), SLOT)


def each_chunk(body, between=None):
    def step(c, carry):
        body(c, chunk_rows(c))
        if between is not None:

            @pl.when(c < CHUNKS - 1)
            def _():
                between()

        return carry

    lax.fori_loop(0, CHUNKS, step, 0)


def each_window(body, after=None, between=None):
    def pair(n, carry):
        body(2 * n)
        body(2 * n + 1)
        if between is not None:

            @pl.when(n == WINS // 4 - 1)
            def _():
                between()

        if after is not None:
            after(pl.ds(pl.multiple_of(n * 128, 128), 128))
        return carry

    lax.fori_loop(0, WINS // 2, pair, 0)


def forward_qkv(k, l):
    def chunk(c, rows):
        xhat, _ = norm_parts(k.xs[slot(l), rows, :])
        normed = (xhat * k.row(l, 0) + k.row(l, 1)).astype(LOWER)
        k.normed_t[:, rows] = normed.T
        for j in range(3):
            part = dot(normed, k.w_qkv(l, j)) + k.row(l, 4 + j)
            k.qkv[rows, j * D : (j + 1) * D] = part.astype(LOWER)

    each_chunk(chunk)


def forward_windows(k, l):
    first = iota((SLOT, 128), 1) < HD

    def window(w):
        rows = window_rows(w)
        bias = k.bias[rows, :]
        scores = []
        for p in range(H // 2):
            at = p * 128
            query = stack_pair(k.qkv[rows, at : at + 128] * jnp.asarray(HD**-0.5, LOWER), first)
            scores.append(dot_nt(k.qkv[rows, D + at : D + at + 128], query) + bias)
        for p in range(H // 2):
            at = p * 128
            peak = jnp.max(scores[p], 0, keepdims=True)
            expo = jnp.exp(scores[p] - peak)
            total = jnp.sum(expo, 0, keepdims=True)
            probs = (expo * (1.0 / total)).astype(LOWER)
            k.logs[l, w, p : p + 1, :] = peak + jnp.log(total)
            out = dot_tn(probs, k.qkv[rows, 2 * D + at : 2 * D + at + 128])
            k.left[rows, at : at + 128] = join_pair(out, first).astype(LOWER)

    def turn(rows):
        k.mixed_t[:, rows] = k.left[rows, :].T

    each_window(window, turn)


def forward_ffn(k, l, dest, between=None):
    def chunk(c, rows):
        mid = k.xs[slot(l), rows, :] + dot(k.left[rows, :], k.w_out(l)) + k.row(l, 7)
        k.mid[rows, :] = mid
        xhat, _ = norm_parts(mid)
        second = (xhat * k.row(l, 2) + k.row(l, 3)).astype(LOWER)
        k.second_t[:, rows] = second.T
        out = mid + k.row(l, 12)
        for j in range(4):
            cols = slice(j * D, (j + 1) * D)
            h = dot(second, k.w_up(l, j)) + k.row(l, 8 + j)
            square = h * h
            over = 1.0 + jnp.tanh(h * (GELU_C + GELU_C * GELU_A * square))
            half = 0.5 * h
            acted = (half * over).astype(LOWER)
            slope = over * (0.5 + half * (2.0 - over) * (GELU_C + 3.0 * GELU_A * GELU_C * square))
            k.slope[rows, cols] = slope.astype(LOWER)
            k.act_t[cols, rows] = acted.T
            out = out + dot(acted, k.w_down(l, j))
        k.xs[dest, rows, :] = out

    each_chunk(chunk, between)


def head_stage(k, at):
    gain, bias = k.small[FIN : FIN + 1, :], k.small[FIN + 1 : FIN + 2, :]
    lane = iota((CHUNK, 128), 1)
    keep = lane < A

    def bias_row(first):
        row = jnp.zeros((1, 128), WIDE)
        at = iota((1, 128), 1)
        for a in range(A):
            row = jnp.where(at == a, k.head_bias[first + a], row)
        return row

    bias_mean, bias_spread = bias_row(0), bias_row(A)
    temp = jnp.exp(jnp.full((1, 128), k.log_temp[0], WIDE))

    def chunk(c, carry):
        rows = chunk_rows(c)
        xhat, scale = norm_parts(k.xs[at, rows, :])
        feats = (xhat * gain + bias).astype(LOWER)
        mean = dot_nt(feats, k.headw[0]) + bias_mean
        spread = jnp.tanh(dot_nt(feats, k.headw[1]) + bias_spread)
        acts = pltpu.roll(k.feats[rows, :], 128 - HEAD_AT, 1)
        weight = acts[:, A : A + 1]
        acts = jnp.where(keep, acts, 0.0)
        target = 0.5 * (jnp.log(1.0 + acts) - jnp.log(1.0 - acts))
        shrink = jnp.exp(-spread)
        zed = (target - mean) * shrink
        terms = 0.5 * zed * zed + spread + HALF_LOG_TAU + jnp.log(1.0 - acts * acts)
        nll = jnp.sum(jnp.where(keep, terms, 0.0), -1, keepdims=True)
        entropy = jnp.sum(jnp.where(keep, spread, 0.0), -1, keepdims=True) + A * (0.5 + HALF_LOG_TAU)
        loss = weight * (nll - temp * entropy)
        sums = jnp.where(lane == 0, loss, jnp.where(lane == 1, weight * entropy, jnp.where(lane == 2, weight, 0.0)))
        d_mean = jnp.where(keep, weight * (-zed * shrink), 0.0).astype(LOWER)
        d_spread = weight * (1.0 - zed * zed - temp) * (1.0 - spread * spread)
        d_spread = jnp.where(keep, d_spread, 0.0).astype(LOWER)
        k.sgh[2:3, 0:128] += col_sum(sums)
        k.sgh[3:4, 0:128] += col_sum(d_mean.astype(WIDE))
        k.sgh[4:5, 0:128] += col_sum(d_spread.astype(WIDE))
        k.sgw[0] += dot_tn(d_mean, feats)[0:8]
        k.sgw[1] += dot_tn(d_spread, feats)[0:8]
        d_feats = dot(d_mean, k.headw[0]) + dot(d_spread, k.headw[1])
        k.sgh[0:1, :] += col_sum(d_feats * xhat)
        k.sgh[1:2, :] += col_sum(d_feats)
        k.xs[at, rows, :] = norm_back(xhat, scale, gain, d_feats)
        return carry

    lax.fori_loop(0, CHUNKS, chunk, 0)


def store_blocks(ref, l, owners, first, count, value):
    value = value.astype(LOWER)
    for n, i in enumerate(owners):
        a, b = owner_place(i)
        ref[l, a, b, first : first + count, :] = value[n * count : (n + 1) * count]


def backward_ffn(k, l, grad, between=None):
    def chunk(c, rows):
        d_down = k.xs[grad, rows, :].astype(LOWER)
        k.dout[rows, :] = d_down
        k.sgl[l, 12:13, :] += col_sum(d_down.astype(WIDE))
        d_second = jnp.zeros((CHUNK, D), WIDE)
        for j in range(4):
            cols = slice(j * D, (j + 1) * D)
            d_acted = dot_nt(d_down, k.w_down(l, j))
            d_hidden = (d_acted * k.slope[rows, cols].astype(WIDE)).astype(LOWER)
            k.work[rows, cols] = d_hidden
            k.sgl[l, 8 + j : 9 + j, :] += col_sum(d_hidden.astype(WIDE))
            d_second = d_second + dot_nt(d_hidden, k.w_up(l, j))
        xhat, scale = norm_parts(k.mid[rows, :])
        k.sgl[l, 2:3, :] += col_sum(d_second * xhat)
        k.sgl[l, 3:4, :] += col_sum(d_second)
        k.xs[grad, rows, :] += norm_back(xhat, scale, k.row(l, 2), d_second)

    each_chunk(chunk, between)


def backward_ffn_grads(k, l):
    for j in range(4):
        cols = slice(j * D, (j + 1) * D)
        store_blocks(k.wf, l, range(BLOCKS), 16 * j, 16, dot(k.second_t[...], k.work[:, cols]))
        store_blocks(k.wf, l, range(8 * j, 8 * j + 8), 64, 64, dot(k.act_t[cols, :], k.dout[...]))


def backward_attn(k, l, grad, between=None):
    def before(c, rows):
        d_branch = k.xs[grad, rows, :].astype(LOWER)
        k.left[rows, :] = d_branch
        k.sgl[l, 7:8, :] += col_sum(d_branch.astype(WIDE))
        k.dout[rows, :] = dot_nt(d_branch, k.w_out(l)).astype(LOWER)

    each_chunk(before)
    store_blocks(k.wa, l + 1, range(BLOCKS), 48, 16, dot(k.mixed_t[...], k.left[...]))
    first = iota((SLOT, 128), 1) < HD
    scale = HD**-0.5

    def window(w):
        rows = window_rows(w)
        bias = k.bias[rows, :]
        for p in range(H // 2):
            at = p * 128
            query = stack_pair(k.qkv[rows, at : at + 128] * jnp.asarray(scale, LOWER), first)
            keyed = k.qkv[rows, D + at : D + at + 128]
            values = k.qkv[rows, 2 * D + at : 2 * D + at + 128]
            d_mixed = stack_pair(k.dout[rows, at : at + 128], first)
            probs = jnp.exp(dot_nt(keyed, query) + bias - k.logs[l, w, p : p + 1, :])
            d_probs = dot_nt(values, d_mixed)
            d_values = dot(probs.astype(LOWER), d_mixed)
            inner = probs * d_probs
            d_scores = (inner - probs * jnp.sum(inner, 0, keepdims=True)).astype(LOWER)
            d_keyed = dot(d_scores, query)
            d_query = join_pair(dot_tn(d_scores, keyed), first) * scale
            k.work[rows, at : at + 128] = d_query.astype(LOWER)
            k.work[rows, D + at : D + at + 128] = d_keyed.astype(LOWER)
            k.work[rows, 2 * D + at : 2 * D + at + 128] = d_values.astype(LOWER)

    each_window(window, None, between)


def backward_attn_grads(k, l):
    for j in range(3):
        part = dot(k.normed_t[...], k.work[:, j * D : (j + 1) * D])
        store_blocks(k.wa, l + 1, range(BLOCKS), 16 * j, 16, part)


def backward_input(k, l, grad):
    def chunk(c, rows):
        d_normed = jnp.zeros((CHUNK, D), WIDE)
        for j in range(3):
            d_part = k.work[rows, j * D : (j + 1) * D]
            k.sgl[l, 4 + j : 5 + j, :] += col_sum(d_part.astype(WIDE))
            d_normed = d_normed + dot_nt(d_part, k.w_qkv(l, j))
        xhat, scale = norm_parts(k.xs[slot(l), rows, :])
        k.sgl[l, 0:1, :] += col_sum(d_normed * xhat)
        k.sgl[l, 1:2, :] += col_sum(d_normed)
        k.xs[grad, rows, :] += norm_back(xhat, scale, k.row(l, 0), d_normed)

    each_chunk(chunk)


def small_stage(k, out, grad):
    out[...] = jnp.zeros_like(out)
    out[0:EMB, :] = dot_tn(k.feats[...], k.xs[grad], HIGH)[0:EMB]
    out[FIN : FIN + 2, :] = k.sgh[0:2, :]
    out[HEADW : HEADW + A, :] = k.sgw[0, 0:A, :]
    out[HEADW + A : HEADW + 2 * A, :] = k.sgw[1, 0:A, :]
    for l in range(LAYERS):
        out[BASE + l * PER : BASE + (l + 1) * PER, :] = k.sgl[l, 0:PER, :]
    out[NROWS : NROWS + 3, :] = k.sgh[2:5, :]


WORK_SHAPES = dict(
    wa=((LAYERS + 1, 4, 8, ATTN, D), LOWER),
    wf=((LAYERS, 4, 8, FFN, D), LOWER),
    xs=((3, ROWS, D), WIDE),
    qkv=((ROWS, 3 * D), LOWER),
    normed_t=((D, ROWS), LOWER),
    mixed_t=((D, ROWS), LOWER),
    slope=((ROWS, FF), LOWER),
    act_t=((FF, ROWS), LOWER),
    second_t=((D, ROWS), LOWER),
    mid=((ROWS, D), WIDE),
    logs=((LAYERS, WINS, 8, 128), WIDE),
    work=((ROWS, FF), LOWER),
    left=((ROWS, D), LOWER),
    dout=((ROWS, D), LOWER),
    feats=((ROWS, 128), WIDE),
    bias=((ROWS, 128), WIDE),
    headw=((2, 128, D), LOWER),
    lrows=((LAYERS, 16, D), WIDE),
    sgl=((LAYERS, 16, D), WIDE),
    sgh=((8, D), WIDE),
    sgw=((2, 8, D), WIDE),
    meta=((128, 128), WIDE),
    buf=((2, 128, 128), WIDE),
)
KEEP_ATTN = ("qkv", "normed_t", "mixed_t")
KEEP_FFN = ("slope", "act_t", "second_t", "mid")
KEEP = KEEP_ATTN + KEEP_FFN


MESH = pl.DeviceIdType.MESH
NZ, NY, NX, NC = 4, 2, 2, 2
NR = NY * NX * NC
SHARD = PACK
PART = (ATTN, FFN)


class Place:
    def __init__(self):
        dp, fsdp = lax.axis_index("dp"), lax.axis_index("fsdp")
        self.z, self.y = dp // NY, dp % NY
        self.x, self.c = fsdp // NC, fsdp % NC
        self.a, self.b = 2 * self.c + self.x, 4 * self.y + self.z
        self.to_x = (dp, (1 - self.x) * NC + self.c)
        self.to_y = (self.z * NY + 1 - self.y, fsdp)
        self.to_c = (dp, self.x * NC + 1 - self.c)
        self.to_z = [(((self.z + d) % NZ) * NY + self.y, fsdp) for d in range(1, NZ)]
        self.partners = [self.to_c, self.to_x, self.to_y] + self.to_z

    def barrier(self):
        sem = pltpu.get_barrier_semaphore()
        for partner in self.partners:
            pl.semaphore_signal(sem, inc=1, device_id=partner, device_id_type=MESH)
        pl.semaphore_wait(sem, len(self.partners))


def remote(src, dst, send, recv, to):
    return pltpu.make_async_remote_copy(
        src_ref=src, dst_ref=dst, send_sem=send, recv_sem=recv, device_id=to, device_id_type=MESH
    )


class Gather:
    COPIES = 11

    def __init__(self, place, weights, send, recv):
        self.at, self.weights, self.send, self.recv = place, weights, send, recv

    def copy(self, l, part, n):
        at, count = self.at, PART[part]
        half = count // 2
        a, b, rows, to = at.a, pl.ds(4 * at.y, 4), pl.ds(0, count), at.to_c
        if n < 3:
            b, to = at.b, at.to_z[n]
        elif n < 5:
            to = (at.to_x, at.to_y)[n - 3]
        if n in (6, 8, 10):
            a = 2 * at.c + 1 - at.x
        if n in (7, 9, 10):
            b = pl.ds(4 * (1 - at.y), 4)
        if n in (6, 7):
            rows, to = pl.ds((n - 6) * half, half), (at.to_y, at.to_x)[n - 6]
        ref = self.weights[part].at[l, a, b, rows, :]
        q = 2 * l + part
        return remote(ref, ref, self.send.at[q, n], self.recv.at[q, n], to)

    def start(self, l, part, *ns):
        for n in ns:
            self.copy(l, part, n).start()

    def wait(self, l, part, *ns):
        for n in ns:
            self.copy(l, part, n).wait_recv()

    def first(self, l, part):
        self.start(l, part, 0, 1, 2)

    def second(self, l, part):
        self.wait(l, part, 0, 1, 2)
        self.start(l, part, 3, 4, 5)

    def third(self, l, part):
        self.wait(l, part, 3)
        self.start(l, part, 6, 8)
        self.wait(l, part, 4)
        self.start(l, part, 7, 9)

    def fourth(self, l, part):
        self.wait(l, part, 6, 7)
        self.start(l, part, 10)

    def last(self, l, part):
        self.wait(l, part, 5, 8, 9, 10)

    def sent(self, l, part):
        for n in range(self.COPIES):
            self.copy(l, part, n).wait_send()


class Reduce:
    COPIES = 8

    def __init__(self, place, grads, landing, send, recv, credit):
        self.at, self.grads, self.landing = place, grads, landing
        self.send, self.recv, self.credit = send, recv, credit

    def refs(self, l, part):
        grads = self.grads[part].at[l + 1 - part]
        r0, r1a, r1b, r2, r3 = self.landing[part]
        return grads, r0, r1a, r1b, r2, r3

    def copy(self, l, part, n):
        at, half = self.at, PART[part] // 2
        g, r0, r1a, r1b, r2, r3 = self.refs(l, part)
        top, low, other = pl.ds(0, half), pl.ds(half, half), pl.ds(4 * (1 - at.y), 4)
        if n == 0:
            src, dst, to = g.at[pl.ds(2 * (1 - at.c), 2)], r0, at.to_c
        elif n == 1:
            src, dst, to = r0.at[1 - at.x, :, top, :], r1a, at.to_x
        elif n == 2:
            src, dst, to = r0.at[:, other, low, :], r1b, at.to_y
        elif n == 3:
            src, dst, to = r1a.at[other], r2.at[:, top, :], at.to_y
        elif n == 4:
            src, dst, to = r1b.at[1 - at.x], r2.at[:, low, :], at.to_x
        else:
            src, dst, to = r2.at[(at.z + n - 4) % NZ], r3.at[n - 5], at.to_z[n - 5]
        q = 2 * l + part
        return remote(src, dst, self.send.at[q, n], self.recv.at[q, n], to)

    def may_send(self, l, part, *partners):
        @pl.when(l < LAYERS - 1)
        def _():
            for n in partners:
                pl.semaphore_wait(self.credit.at[part, n], 1)

    def allow(self, l, part, *credits):
        at = self.at

        @pl.when(l > 0)
        def _():
            for n, to in credits:
                pl.semaphore_signal(
                    self.credit.at[part, n], inc=1, device_id=to, device_id_type=MESH
                )

    def start(self, l, part):
        self.may_send(l, part, 0)
        self.copy(l, part, 0).start()

    def first(self, l, part):
        at, half = self.at, PART[part] // 2
        g, r0, _, _, _, _ = self.refs(l, part)
        top, low = pl.ds(0, half), pl.ds(half, half)
        self.copy(l, part, 0).wait_recv()

        def along_x(n, carry):
            x = 1 - at.x
            total = g[2 * at.c + x, n, top].astype(WIDE) + r0[x, n, top].astype(WIDE)
            r0[x, n, top] = total.astype(LOWER)
            return carry

        def along_y(n, carry):
            x, b = n // 4, 4 * (1 - at.y) + n % 4
            total = g[2 * at.c + x, b, low].astype(WIDE) + r0[x, b, low].astype(WIDE)
            r0[x, b, low] = total.astype(LOWER)
            return carry

        lax.fori_loop(0, 8, along_x, 0)
        self.may_send(l, part, 1, 2)
        self.copy(l, part, 1).start()
        lax.fori_loop(0, 8, along_y, 0)
        self.copy(l, part, 2).start()

    def second(self, l, part):
        at, half = self.at, PART[part] // 2
        g, r0, r1a, r1b, _, _ = self.refs(l, part)
        top, low = pl.ds(0, half), pl.ds(half, half)

        def along_y(n, carry):
            b = 4 * (1 - at.y) + n
            total = g[at.a, b, top].astype(WIDE) + r0[at.x, b, top].astype(WIDE)
            r1a[b] = (total + r1a[b].astype(WIDE)).astype(LOWER)
            return carry

        def along_x(n, carry):
            x, b = 1 - at.x, 4 * at.y + n
            total = g[2 * at.c + x, b, low].astype(WIDE) + r0[x, b, low].astype(WIDE)
            r1b[x, n] = (total + r1b[x, n].astype(WIDE)).astype(LOWER)
            return carry

        self.copy(l, part, 1).wait_recv()
        lax.fori_loop(0, NZ, along_y, 0)
        self.may_send(l, part, 6, 7)
        self.copy(l, part, 3).start()
        self.copy(l, part, 2).wait_recv()
        lax.fori_loop(0, NZ, along_x, 0)
        self.copy(l, part, 4).start()

    def chip_sums(self, l, part, z):
        at, half = self.at, PART[part] // 2
        g, r0, r1a, r1b, r2, _ = self.refs(l, part)
        top, low, b = pl.ds(0, half), pl.ds(half, half), 4 * at.y + z
        upper = g[at.a, b, top].astype(WIDE) + r0[at.x, b, top].astype(WIDE)
        lower = g[at.a, b, low].astype(WIDE) + r0[at.x, b, low].astype(WIDE)
        return (
            upper + r1a[b].astype(WIDE) + r2[z, top].astype(WIDE),
            lower + r1b[at.x, z].astype(WIDE) + r2[z, low].astype(WIDE),
        )

    def third(self, l, part, out):
        at, half, row = self.at, PART[part] // 2, (0, ATTN)[part]
        r2 = self.landing[part][3]
        for n in (3, 4):
            self.copy(l, part, n).wait_recv()
        self.may_send(l, part, 3, 4, 5)
        for n in range(3):
            z = (at.z + n + 1) % NZ
            upper, lower = self.chip_sums(l, part, z)
            r2[z, pl.ds(0, half)] = upper.astype(LOWER)
            r2[z, pl.ds(half, half)] = lower.astype(LOWER)
            self.copy(l, part, 5 + n).start()
        upper, lower = self.chip_sums(l, part, at.z)
        out[l, row : row + half, :] = upper
        out[l, row + half : row + 2 * half, :] = lower
        for n in range(5):
            self.copy(l, part, n).wait_send()
        self.allow(l, part, (0, at.to_c), (1, at.to_x), (2, at.to_y))

    def last(self, l, part, out, squares):
        at, row = self.at, (0, ATTN)[part]
        r3 = self.landing[part][4]
        rows = slice(row, row + PART[part])
        total = out[l, rows, :]
        for n in range(3):
            self.copy(l, part, 5 + n).wait_recv()
            total = total + r3[n].astype(WIDE)
        out[l, rows, :] = total
        squares[0:1, :] += col_sum(total * total)
        for n in range(5, self.COPIES):
            self.copy(l, part, n).wait_send()
        late = [(6, at.to_x), (7, at.to_y)] + [(5 - n, at.to_z[n]) for n in range(3)]
        self.allow(l, part, *late)


class Total:
    COPIES = 6

    def __init__(self, place, ref, first, rows, send, recv):
        self.at, self.ref, self.first, self.rows = place, ref, first, rows
        self.send, self.recv = send, recv

    def own(self, n):
        return self.ref.at[pl.ds(self.first + n * self.rows, self.rows), :]

    def got(self, n):
        return self.own(4 + n)

    def copy(self, n):
        src, dst = self.own(min(n, 3)), self.got(n)
        return remote(src, dst, self.send.at[n], self.recv.at[n], self.at.partners[n])

    def start(self):
        self.copy(0).start()

    def step(self, n):
        self.copy(n).wait_recv()
        self.own(n + 1)[...] = self.own(n)[...] + self.got(n)[...]
        for m in ((1,), (2,), (3, 4, 5))[n]:
            self.copy(m).start()

    def last(self):
        for m in (3, 4, 5):
            self.copy(m).wait_recv()
        total = None
        for z in range(NZ):
            term = self.own(3)[...]
            for n in range(3):
                from_z = (self.at.z + NZ - 1 - n) % NZ
                term = jnp.where(from_z == z, self.got(3 + n)[...], term)
            total = term if total is None else total + term
        return total

    def sent(self):
        for n in range(self.COPIES):
            self.copy(n).wait_send()


def landing_shapes(count):
    half = count // 2
    return [
        (NX, 8, count, D),
        (8, half, D),
        (NX, NZ, half, D),
        (NZ, count, D),
        (3, count, D),
    ]


def stage_rows(qkv, out, up, down, l):
    return (
        [(qkv.at[l, :, pl.ds(j * D, D)], 16 * j, 16) for j in range(3)]
        + [(out.at[l], 48, 16)]
        + [(up.at[l, :, pl.ds(j * D, D)], 64 + 16 * j, 16) for j in range(4)]
        + [(down.at[l], 128, 64)]
    )


GATHER_PLAN = {
    (-1, "start"): [("first", 0, 0), ("first", 0, 1), ("first", 1, 0), ("first", 1, 1)],
    (-1, "setup"): [("second", 0, 0), ("third", 0, 0), ("fourth", 0, 0), ("last", 0, 0)],
    (0, "qkv"): [("second", 0, 1), ("first", 2, 0), ("second", 1, 0)],
    (0, "windows"): [("third", 0, 1), ("first", 2, 1), ("fourth", 0, 1), ("last", 0, 1)],
    (0, "half"): [("third", 1, 0), ("second", 1, 1)],
    (0, "ffn"): [("fourth", 1, 0), ("second", 2, 0), ("last", 1, 0)],
    (1, "qkv"): [("third", 1, 1), ("fourth", 1, 1)],
    (1, "windows"): [("third", 2, 0), ("second", 2, 1), ("last", 1, 1)],
    (1, "half"): [("fourth", 2, 0)],
    (1, "ffn"): [("last", 2, 0), ("third", 2, 1)],
    (2, "qkv"): [("fourth", 2, 1)],
    (2, "windows"): [("last", 2, 1)],
}


def train_kernel(refs, alone):
    k = Kit(**refs)

    def kept(names, l, back):
        copies = []
        for name in names:
            here, there = refs[name], refs["keep_" + name].at[l]
            src, dst = (there, here) if back else (here, there)
            copies.append(pltpu.make_async_copy(src, dst, k.keep_sem.at[KEEP.index(name)]))
        return copies

    def start(copies):
        for copy in copies:
            copy.start()

    def wait(copies):
        for copy in copies:
            copy.wait()

    def kept_x(back):
        here, there = k.xs.at[0], k.keep_x
        src, dst = (there, here) if back else (here, there)
        return [pltpu.make_async_copy(src, dst, k.keep_sem.at[len(KEEP)])]

    parts = [(l, part) for l in range(LAYERS) for part in (0, 1)]
    weights = (k.wa, k.wf)
    if alone:
        loads = [
            pltpu.make_async_copy(ref, weights[part].at[l], k.load_sem.at[2 * l + part])
            for l, part in parts
            for ref in [(k.all_a, k.all_f)[part].at[l]]
        ]
        stores = [
            pltpu.make_async_copy(
                weights[part].at[l + 1 - part],
                (k.grad_a, k.grad_f)[part].at[l],
                k.load_sem.at[2 * l + part],
            )
            for l, part in parts
        ]
        start(loads)
    else:
        place = Place()
        gather = Gather(place, weights, k.gather_send, k.gather_recv)
        reduce = Reduce(
            place, weights, (k.land_a, k.land_f), k.reduce_send, k.reduce_recv, k.credit
        )
        sums = Total(place, k.mid, 0, SMALL, k.sum_send, k.sum_recv)
        norm = Total(place, k.mid, 10 * SMALL, 8, k.norm_send, k.norm_recv)

    def run(plan):
        for stage, l, part in plan:
            getattr(gather, stage)(l, part)

    def poll(l, point):
        if alone:
            return
        for layer in range(LAYERS):
            plan = GATHER_PLAN.get((layer, point))
            if plan:

                @pl.when(l == layer)
                def _(plan=plan):
                    with jax.named_scope("gather_" + point):
                        run(plan)

    if not alone:
        staged = []
        for l in range(LAYERS):
            for n, (src, row, count) in enumerate(stage_rows(k.qkv_w, k.out_w, k.up_w, k.down_w, l)):
                dst = k.xs.at[2, pl.ds(l * PACK + row, count), :]
                staged.append(pltpu.make_async_copy(src, dst, k.stage_sem.at[l, n]))
        start(staged)
        place.barrier()
        for l in range(LAYERS):
            wait(staged[9 * l : 9 * l + 9])
            row = l * PACK
            for part, (low, high) in enumerate(((0, ATTN), (ATTN, PACK))):
                weights[part][l, place.a, place.b] = k.xs[2, row + low : row + high, :].astype(LOWER)
                if ("first", l, part) in GATHER_PLAN[-1, "start"]:
                    gather.first(l, part)
        k.squares_sum[...] = jnp.zeros_like(k.squares_sum)

    with jax.named_scope("embedding"):
        setup_stage(k)
    start(kept_x(False))
    if not alone:
        with jax.named_scope("gather_setup"):
            run(GATHER_PLAN[-1, "setup"])

    def forward(l, carry):
        if alone:
            pltpu.make_async_copy(k.all_a.at[l], k.wa.at[l], k.load_sem.at[2 * l]).wait()

        @pl.when(l > 0)
        def _():
            wait(kept(KEEP_ATTN, l - 1, False))

        with jax.named_scope("qkv"):
            forward_qkv(k, l)
        poll(l, "qkv")
        with jax.named_scope("attention"):
            forward_windows(k, l)

        @pl.when(l < LAYERS - 1)
        def _():
            start(kept(KEEP_ATTN, l, False))

        @pl.when(l > 0)
        def _():
            wait(kept(KEEP_FFN, l - 1, False))

        @pl.when(l == 1)
        def _():
            wait(kept_x(False))

        if alone:
            pltpu.make_async_copy(k.all_f.at[l], k.wf.at[l], k.load_sem.at[2 * l + 1]).wait()
        poll(l, "windows")
        with jax.named_scope("ffn"):
            forward_ffn(k, l, (l + 1) % 2 + l // 2, lambda: poll(l, "half"))

        @pl.when(l < LAYERS - 1)
        def _():
            start(kept(KEEP_FFN, l, False))

        poll(l, "ffn")
        return carry

    lax.fori_loop(0, LAYERS, forward, 0)
    if not alone:
        for l, part in parts:
            gather.sent(l, part)
    grad = 2
    with jax.named_scope("head"):
        head_stage(k, grad)

    def backward(n, carry):
        l = LAYERS - 1 - n

        def behind(name, *stages):
            @pl.when(n > 0)
            def _():
                with jax.named_scope(name):
                    for stage, part, *more in stages:
                        stage(l + 1, part, *more)

        @pl.when(n > 0)
        def _():
            wait(kept(KEEP_FFN, l, True))

        finish = () if alone else (k.shard, k.squares_sum)

        def ffn_between():
            if not alone:
                behind("reduce_third", (reduce.third, 1, k.shard))

        def attn_between():
            if not alone:
                with jax.named_scope("reduce_first"):
                    reduce.first(l, 1)
                behind("reduce_last", (reduce.last, 1, *finish))

        with jax.named_scope("ffn_back"):
            backward_ffn(k, l, grad, ffn_between)
        if not alone:
            behind("reduce_second", (reduce.second, 0))
        with jax.named_scope("ffn_grads"):
            backward_ffn_grads(k, l)

        @pl.when(n < LAYERS - 1)
        def _():
            start(kept(KEEP_FFN, l - 1, True))

        if not alone:
            with jax.named_scope("reduce_start"):
                reduce.start(l, 1)
            behind("reduce_third", (reduce.third, 0, k.shard))

        @pl.when(n > 0)
        def _():
            wait(kept(KEEP_ATTN, l, True))

        with jax.named_scope("attention_back"):
            backward_attn(k, l, grad, attn_between)
        with jax.named_scope("qkv_grads"):
            backward_attn_grads(k, l)

        @pl.when(n < LAYERS - 1)
        def _():
            start(kept(KEEP_ATTN, l - 1, True))

        if not alone:
            with jax.named_scope("reduce_start"):
                reduce.start(l, 0)
            behind("reduce_last", (reduce.last, 0, *finish))

        @pl.when(n == LAYERS - 1)
        def _():
            wait(kept_x(True))

        with jax.named_scope("qkv_back"):
            backward_input(k, l, grad)

        @pl.when(n == 0)
        def _():
            start(kept_x(True))

        if not alone:
            with jax.named_scope("reduce_second"):
                reduce.second(l, 1)
            with jax.named_scope("reduce_first"):
                reduce.first(l, 0)
        return carry

    lax.fori_loop(0, LAYERS, backward, 0)
    if alone:
        start(stores)
        small_stage(k, k.small_out, grad)
        wait(stores)
        return
    with jax.named_scope("small_grads"):
        small_stage(k, sums.own(0), grad)
    sums.start()
    with jax.named_scope("reduce_third"):
        reduce.third(0, 1, k.shard)
    with jax.named_scope("reduce_second"):
        reduce.second(0, 0)
    sums.step(0)
    with jax.named_scope("reduce_third"):
        reduce.third(0, 0, k.shard)
    sums.step(1)
    with jax.named_scope("reduce_last"):
        reduce.last(0, 1, k.shard, k.squares_sum)
        reduce.last(0, 0, k.shard, k.squares_sum)
    with jax.named_scope("norm_sums"):
        norm.own(0)[...] = k.squares_sum[...]
        norm.start()
        sums.step(2)
        norm.step(0)
        norm.step(1)
        k.small_out[...] = sums.last()
        norm.step(2)
        k.squares[...] = norm.last()
    sums.sent()
    norm.sent()


def train_pass(inputs, weights, alone):
    whole = pl.BlockSpec(memory_space=pltpu.VMEM)
    scalars = pl.BlockSpec(memory_space=pltpu.SMEM)
    anywhere = pl.BlockSpec(memory_space=pl.ANY)
    dma = pltpu.SemaphoreType.DMA
    count = 2 * LAYERS
    names = ["states", "actions", "returns", "starts", "repeats", "valid"]
    names += ["log_temp", "small", "head_bias"]
    out_shape = {"small_out": ((SMALL, D), WIDE)}
    for name in KEEP:
        shape, dtype = WORK_SHAPES[name]
        out_shape["keep_" + name] = ((LAYERS - 1,) + shape, dtype)
    out_shape["keep_x"] = ((ROWS, D), WIDE)
    scratch = {name: pltpu.VMEM(*shape) for name, shape in WORK_SHAPES.items()}
    scratch["keep_sem"] = dma((len(KEEP) + 1,))
    if alone:
        names += ["all_a", "all_f"]
        out_shape["grad_a"] = ((LAYERS, 4, 8, ATTN, D), LOWER)
        out_shape["grad_f"] = ((LAYERS, 4, 8, FFN, D), LOWER)
        scratch["load_sem"] = dma((count,))
    else:
        names += ["qkv_w", "out_w", "up_w", "down_w"]
        out_shape["shard"] = ((LAYERS, PACK, D), WIDE)
        out_shape["squares"] = ((8, D), WIDE)
        for part, name in enumerate("af"):
            for n, shape in enumerate(landing_shapes(PART[part])):
                scratch["land_%s%d" % (name, n)] = pltpu.VMEM(shape, LOWER)
        scratch["stage_sem"] = dma((LAYERS, 9))
        scratch["squares_sum"] = pltpu.VMEM((8, D), WIDE)
        for name, copies in (("gather", Gather.COPIES), ("reduce", Reduce.COPIES)):
            scratch[name + "_send"] = dma((count, copies))
            scratch[name + "_recv"] = dma((count, copies))
        scratch["credit"] = pltpu.SemaphoreType.REGULAR((2, 8))
        for name in ("sum", "norm"):
            scratch[name + "_send"] = dma((6,))
            scratch[name + "_recv"] = dma((6,))
    spaces = dict.fromkeys(("starts", "repeats", "head_bias", "log_temp"), scalars)
    for name in ("all_a", "all_f", "grad_a", "grad_f", "qkv_w", "out_w", "up_w", "down_w"):
        spaces[name] = anywhere
    for name in KEEP + ("x",):
        spaces["keep_" + name] = anywhere
    every = names + list(out_shape) + list(scratch)

    def kernel(*given):
        refs = dict(zip(every, given))
        for name in "af":
            refs["land_" + name] = [refs.get("land_%s%d" % (name, n)) for n in range(5)]
        train_kernel(refs, alone)

    results = pl.pallas_call(
        kernel,
        name="train_pass",
        out_shape=tuple(jax.ShapeDtypeStruct(*shape) for shape in out_shape.values()),
        in_specs=[spaces.get(name, whole) for name in names],
        out_specs=tuple(spaces.get(name, whole) for name in out_shape),
        scratch_shapes=list(scratch.values()),
        compiler_params=pltpu.CompilerParams(
            vmem_limit_bytes=VMEM_BYTES,
            collective_id=None if alone else 0,
            has_side_effects=not alone,
        ),
        cost_estimate=pl.CostEstimate(
            flops=6 * 10**10, bytes_accessed=4 * 10**7, transcendentals=10**7
        ),
    )(*inputs, *weights)
    return dict(zip(out_shape, results))


def adam_parts(weight, grad, first, second, rate):
    first = BETA_ONE * first + (1.0 - BETA_ONE) * grad
    second = BETA_TWO * second + (1.0 - BETA_TWO) * grad * grad
    fix_one = 1.0 - BETA_ONE**STEP
    fix_two = 1.0 - BETA_TWO**STEP
    fresh = weight - rate * (
        first / fix_one / (jnp.sqrt(second / fix_two) + ADAM_EPS) + DECAY * weight
    )
    return fresh, first, second


def adam_kernel(*refs):
    shard, small_grad, squares, groups, log_temp = refs[:5]
    small, small_first, small_second, bias, bias_first, bias_second = refs[5:11]
    mats, firsts, seconds = refs[11:15], refs[15:19], refs[19:23]
    totals, norm, next_temp, s_next, s_first, s_second, b_next, b_first, b_second = refs[23:32]
    m_next, m_copy, m_first, m_second = refs[32:36], refs[36:40], refs[40:44], refs[44:48]
    l = pl.program_id(0)
    extra = small_grad[NROWS : NROWS + 3, 0:128]
    lane = iota((1, 128), 1)
    bias_mean = jnp.where(lane < A, extra[1:2], 0.0)
    bias_spread = jnp.where(lane < A, extra[2:3], 0.0)

    def all_sum(v):
        return jnp.sum(jnp.sum(v, 0, keepdims=True), 1, keepdims=True)

    grads = small_grad[0:NROWS, :]
    square = (
        all_sum(squares[0:1, :])
        + all_sum(grads * grads)
        + all_sum(bias_mean * bias_mean)
        + all_sum(bias_spread * bias_spread)
    )
    length = jnp.sqrt(square)
    clip = jnp.minimum(1.0, CLIP / (length + 1e-06))

    def rate_of(kind):
        group = jnp.full((1, 1), groups[l, kind], jnp.int32).astype(WIDE)
        return LEARN * jnp.exp2(-group)

    def update(kind, rows, cols, grad):
        at = (0, rows, cols)
        fresh, first, second = adam_parts(
            mats[kind][at], clip * grad, firsts[kind][at], seconds[kind][at], rate_of(kind)
        )
        m_next[kind][at] = fresh
        m_copy[kind][at] = fresh.astype(LOWER)
        m_first[kind][at] = first
        m_second[kind][at] = second

    every = slice(0, 16)
    for j in range(3):
        update(0, every, slice(j * D, (j + 1) * D), shard[0, 16 * j : 16 * j + 16, :])
    update(1, every, slice(0, D), shard[0, 48:64, :])
    for j in range(4):
        update(2, every, slice(j * D, (j + 1) * D), shard[0, 64 + 16 * j : 80 + 16 * j, :])
    update(3, slice(0, 64), slice(0, D), shard[0, 128:192, :])

    @pl.when(l == 0)
    def _():
        s_next[...], s_first[...], s_second[...] = adam_parts(
            small[...], clip * grads, small_first[...], small_second[...], LEARN
        )

        def scalar(v, n):
            return jnp.sum(jnp.where(lane == n, v, 0.0))

        def row(ref):
            v = jnp.zeros((1, 128), WIDE)
            for n in range(2 * A):
                v = jnp.where(lane == n, ref[n], v)
            return v

        grad = bias_mean + pltpu.roll(bias_spread, A, 1)
        results = adam_parts(row(bias), clip * grad, row(bias_first), row(bias_second), LEARN)
        for ref, result in zip((b_next, b_first, b_second), results):
            for n in range(2 * A):
                ref[n] = scalar(result, n)
        sums = extra[0:1]
        for n in range(3):
            totals[n] = scalar(sums, n)
        norm[0] = jnp.sum(length)
        logs = jnp.full((1, 1), log_temp[0], WIDE)
        ratio = jnp.full((1, 1), scalar(sums, 1), WIDE) / jnp.full((1, 1), scalar(sums, 2), WIDE)
        next_temp[0] = jnp.sum(logs - TEMP_RATE * jnp.exp(logs) * (ratio + A))


def adam_all(shard, small_grad, squares, groups, log_temp, smalls, biases, mats, firsts, seconds):
    scalars = pl.BlockSpec(memory_space=pltpu.SMEM)

    def fixed(array):
        return pl.BlockSpec(array.shape, lambda l: (0,) * array.ndim)

    def layer(array):
        return pl.BlockSpec((1,) + array.shape[1:], lambda l: (l, 0, 0))

    def like(array, dtype=WIDE):
        return jax.ShapeDtypeStruct(array.shape, dtype)

    stacks = list(mats) + list(firsts) + list(seconds)
    small, bias = smalls[0], biases[0]
    return pl.pallas_call(
        adam_kernel,
        name="adam",
        grid=(LAYERS,),
        out_shape=(
            (jax.ShapeDtypeStruct((3,), WIDE),)
            + (jax.ShapeDtypeStruct((1,), WIDE),) * 2
            + (like(small),) * 3
            + (like(bias),) * 3
            + tuple(like(m) for m in mats)
            + tuple(like(m, LOWER) for m in mats)
            + tuple(like(m) for m in mats) * 2
        ),
        in_specs=[layer(shard), fixed(small_grad), fixed(squares), scalars, scalars]
        + [fixed(small)] * 3
        + [scalars] * 3
        + [layer(m) for m in stacks],
        out_specs=(scalars,) * 3
        + (fixed(small),) * 3
        + (scalars,) * 3
        + tuple(layer(m) for m in mats) * 4,
        compiler_params=pltpu.CompilerParams(vmem_limit_bytes=VMEM_BYTES),
        cost_estimate=pl.CostEstimate(flops=10**7, bytes_accessed=8 * 10**6, transcendentals=10**6),
    )(shard, small_grad, squares, groups, log_temp, *smalls, *biases, *stacks)


def gather_packed(mats, axes, count):
    group = count // BLOCKS
    pieces = []
    for mat in mats:
        rows, wide = mat.shape[1], mat.shape[2] // D
        piece = mat.astype(LOWER).reshape(LAYERS, rows, wide, D)
        piece = lax.all_gather(piece, axes, axis=1, tiled=True)
        piece = piece.reshape(LAYERS, NZ, NY, NX, NC, group * rows, wide, D)
        piece = piece.transpose(0, 4, 3, 2, 1, 6, 5, 7)
        pieces.append(piece.reshape(LAYERS, 4, 8, wide * group * rows, D))
    return jnp.concatenate(pieces[:2], 3), jnp.concatenate(pieces[2:], 3)


def scatter_packed(grads, mats, axes):
    results, first = [], 0
    for n, mat in enumerate(mats):
        rows, wide = mat.shape[1], mat.shape[2] // D
        total = lax.psum(1, axes) * rows
        deep = total // BLOCKS
        first = 0 if n % 2 == 0 else first
        piece = grads[n // 2][:, :, :, first : first + wide * deep].astype(WIDE)
        first += wide * deep
        piece = piece.reshape(LAYERS, NC, NX, NY, NZ, wide, deep, D)
        piece = piece.transpose(0, 4, 3, 2, 1, 6, 5, 7).reshape(LAYERS, total, wide * D)
        results.append(lax.psum_scatter(piece, axes, scatter_dimension=1, tiled=True))
    return results


def local(
    buf_states,
    buf_actions,
    buf_returns,
    window_starts,
    window_repeats,
    valid_steps,
    matrix_groups,
    log_temp,
    small_rows,
    head_bias,
    qkv_weight,
    out_weight,
    up_weight,
    down_weight,
    small_first,
    bias_first,
    qkv_first,
    out_first,
    up_first,
    down_first,
    small_second,
    bias_second,
    qkv_second,
    out_second,
    up_second,
    down_second,
):
    axes = ("dp", "fsdp")
    mats = (qkv_weight, out_weight, up_weight, down_weight)
    firsts = (qkv_first, out_first, up_first, down_first)
    seconds = (qkv_second, out_second, up_second, down_second)
    pass_inputs = (
        buf_states.T,
        buf_actions.T,
        buf_returns[None],
        window_starts,
        window_repeats,
        valid_steps,
        log_temp,
        small_rows,
        head_bias,
    )
    if FF // down_weight.shape[1] == BLOCKS and lax.psum(1, "fsdp") == NX * NC:
        made = train_pass(pass_inputs, mats, False)
        return adam_all(
            made["shard"],
            made["small_out"],
            made["squares"],
            matrix_groups,
            log_temp,
            (small_rows, small_first, small_second),
            (head_bias, bias_first, bias_second),
            mats,
            firsts,
            seconds,
        )
    packed = gather_packed(mats, axes, FF // down_weight.shape[1])
    made = train_pass(pass_inputs, packed, True)
    big = scatter_packed((made["grad_a"], made["grad_f"]), mats, axes)
    small = made["small_out"]
    small = lax.psum(small, axes)
    small_grad, totals = small[:NROWS], small[NROWS, :3]
    bias_grad = jnp.concatenate([small[NROWS + 1, :A], small[NROWS + 2, :A]])
    square = sum((jnp.sum(piece * piece) for piece in big))
    square = (
        lax.psum(square, axes) + jnp.sum(small_grad * small_grad) + jnp.sum(bias_grad * bias_grad)
    )
    grad_norm = jnp.sqrt(square)
    clip = jnp.minimum(1.0, CLIP / (grad_norm + 1e-06))
    rates = LEARN * jnp.exp2(-matrix_groups.astype(WIDE))
    results = [
        adam_parts(
            mats[kind], clip * big[kind], firsts[kind], seconds[kind], rates[:, kind][:, None, None]
        )
        for kind in range(4)
    ]
    small_new = adam_parts(small_rows, clip * small_grad, small_first, small_second, LEARN)
    bias_new = adam_parts(head_bias, clip * bias_grad, bias_first, bias_second, LEARN)
    next_temp = log_temp - TEMP_RATE * jnp.exp(log_temp) * (totals[1] / totals[2] + A)
    return (
        (totals, grad_norm[None], next_temp)
        + small_new
        + bias_new
        + tuple(r[0] for r in results)
        + tuple(r[0].astype(LOWER) for r in results)
        + tuple(r[1] for r in results)
        + tuple(r[2] for r in results)
    )


def solution(mesh):
    rows = P(("dp", "fsdp"), None)
    vector = P(("dp", "fsdp"))
    stack = P(None, ("dp", "fsdp"), None)
    same = P()
    in_specs = (
        (rows, rows, vector, vector, vector, rows)
        + (same,) * 4
        + (stack,) * 4
        + (same,) * 2
        + (stack,) * 4
        + (same,) * 2
        + (stack,) * 4
    )
    out_specs = (same,) * 9 + (stack,) * 16
    return jax.shard_map(local, mesh=mesh, in_specs=in_specs, out_specs=out_specs, check_vma=False)
```

```python
import math

import jax
import jax.numpy as jnp
from jax import lax
from jax.experimental import pallas as pl
from jax.experimental.pallas import tpu as pltpu
from jax.sharding import PartitionSpec as P

D = 512
H = 8
HD = 64
FF = 2048
S = 11
A = 3
K = 20
STEP = 10

EPS = 1e-05
CLIP = 1.0
LEARN = 0.03
BETA_ONE = 0.5
BETA_TWO = 0.7
DECAY = 0.01
ADAM_EPS = 1e-08
TEMP_RATE = 0.1
MASKED = -1e30
HALF_LOG_TAU = 0.5 * math.log(2.0 * math.pi)
GELU_C = math.sqrt(2.0 / math.pi)
GELU_A = 0.044715
HIGH = lax.Precision.HIGHEST
LOWER = jnp.bfloat16
WIDE = jnp.float32

LAYERS = 3
WINS = 16
BUF_DEV = 64
SLOT = 64
ROWS = WINS * SLOT
CHUNK = 512
CHUNKS = ROWS // CHUNK
BLOCKS = 32
PACK = 192
ATTN, FFN = 64, 128
EMB = S + A + 1 + K + 3
FIN = EMB
HEADW = EMB + 2
BASE = EMB + 2 + 2 * A
PER = 9 + FF // D
NROWS = BASE + LAYERS * PER
SMALL = 96
HEAD_AT = 64
EMB_AT = ROWS - 128
VMEM_BYTES = 64 * 1024 * 1024


def dot(a, b, precision=None):
    return lax.dot_general(
        a, b, (((1,), (0,)), ((), ())), precision=precision, preferred_element_type=WIDE
    )


def dot_nt(a, b, precision=None):
    return lax.dot_general(
        a, b, (((1,), (1,)), ((), ())), precision=precision, preferred_element_type=WIDE
    )


def dot_tn(a, b, precision=None):
    return lax.dot_general(
        a, b, (((0,), (0,)), ((), ())), precision=precision, preferred_element_type=WIDE
    )


def iota(shape, dim):
    return lax.broadcasted_iota(jnp.int32, shape, dim)


def col_sum(v):
    return jnp.sum(v, 0, keepdims=True)


def row_mean(v):
    return jnp.mean(v, -1, keepdims=True)


def norm_parts(x):
    center = x - row_mean(x)
    scale = lax.rsqrt(row_mean(center * center) + EPS)
    return center * scale, scale


def norm_back(xhat, scale, gain, grad):
    scaled = grad * gain
    return scale * (scaled - row_mean(scaled) - xhat * row_mean(scaled * xhat))


def token_rows(at, count):
    row = at + iota((count, 128), 0)
    place = row & (SLOT - 1)
    step = (place * 21846) >> 16
    return row >> 6, step, place - 3 * step, place < 3 * K


def chunk_rows(c):
    return pl.ds(pl.multiple_of(c * CHUNK, CHUNK), CHUNK)


def owner_place(i):
    z, y, x, c = i // 8, (i // 4) % 2, (i // 2) % 2, i % 2
    return 2 * c + x, 4 * y + z


class Kit:
    def __init__(self, **refs):
        self.__dict__.update(refs)

    def row(self, l, k):
        return self.lrows[l, k : k + 1, :]

    def blocks(self, ref, l, first, count, owners):
        places = [owner_place(i) for i in owners]
        return jnp.concatenate([ref[l, a, b, first : first + count, :] for a, b in places], 0)

    def w_qkv(self, l, j):
        return self.blocks(self.wa, l, 16 * j, 16, range(BLOCKS))

    def w_out(self, l):
        return self.blocks(self.wa, l, 48, 16, range(BLOCKS))

    def w_up(self, l, j):
        return self.blocks(self.wf, l, 16 * j, 16, range(BLOCKS))

    def w_down(self, l, j):
        return self.blocks(self.wf, l, 64, 64, range(8 * j, 8 * j + 8))


def slot(l):
    return l % 2


def setup_stage(k):
    k.xs[2, EMB_AT:ROWS, :] = jnp.zeros((128, D), WIDE)
    k.xs[2, EMB_AT : EMB_AT + EMB, :] = k.small[0:EMB, :]
    k.headw[...] = jnp.zeros_like(k.headw)
    k.headw[0, 0:A, :] = k.small[HEADW : HEADW + A, :].astype(LOWER)
    k.headw[1, 0:A, :] = k.small[HEADW + A : HEADW + 2 * A, :].astype(LOWER)
    for l in range(LAYERS):
        k.lrows[l, 0:PER, :] = k.small[BASE + l * PER : BASE + (l + 1) * PER, :]
    k.sgl[...] = jnp.zeros_like(k.sgl)
    k.sgh[...] = jnp.zeros_like(k.sgh)
    k.sgw[...] = jnp.zeros_like(k.sgw)

    lane, sub = iota((WINS, 128), 1), iota((WINS, 128), 0)
    k.meta[...] = jnp.zeros_like(k.meta)
    k.meta[0:WINS, 0:K] = k.valid[...].astype(WIDE)
    meta = k.meta[0:WINS, :]
    for w in range(WINS):
        for n, ref in enumerate((k.starts, k.repeats)):
            meta = jnp.where((sub == w) & (lane == K + n), ref[w].astype(WIDE), meta)
    k.meta[0:WINS, :] = meta
    meta = k.meta[...].astype(LOWER)
    k.buf[...] = jnp.zeros_like(k.buf)
    k.buf[0, 0:S, 0:BUF_DEV] = k.states[...]
    k.buf[0, S + A : S + A + 1, 0:BUF_DEV] = k.returns[...]
    k.buf[1, 0:A, 0:BUF_DEV] = k.actions[...]

    def chunk(c, carry):
        rows = chunk_rows(c)
        win, step, kind, real = token_rows(c * CHUNK, CHUNK)
        lane = iota((CHUNK, 128), 1)
        tok = dot((lane == win).astype(WIDE).astype(LOWER), meta)
        start, repeat = tok[:, K : K + 1], tok[:, K + 1 : K + 2]
        valid = jnp.sum(jnp.where(lane == step, tok, 0.0), -1, keepdims=True)
        key = iota((CHUNK, 128), 0) & (SLOT - 1)
        query = lane & (SLOT - 1)
        allowed = (key <= query) & (((valid > 0.5) & real) | (key == query))
        k.bias[rows, :] = jnp.where(allowed, 0.0, MASKED)
        place = start.astype(jnp.int32) + step
        source = ((lane == place) & real).astype(WIDE)
        raw = dot_nt(source, k.buf[0], HIGH)
        acts = dot_nt(source, k.buf[1], HIGH)
        mine = (
            ((lane < S) & (kind == 1))
            | ((lane >= S) & (lane < S + A) & (kind == 2))
            | ((lane == S + A) & (kind == 0))
        )
        raw = raw + pltpu.roll(acts, S, 1)
        marks = ((lane == S + A + 1 + step) | (lane == S + A + 1 + K + kind)) & real
        feats = jnp.where(mine, raw, 0.0) + marks.astype(WIDE)
        weight = jnp.where((kind == 1) & real, repeat * valid, 0.0)
        acts = pltpu.roll(acts, HEAD_AT, 1)
        ours = (lane >= HEAD_AT) & (lane < HEAD_AT + A)
        feats = jnp.where(ours, acts, jnp.where(lane == HEAD_AT + A, weight, feats))
        k.feats[rows, :] = feats
        k.xs[0, rows, :] = dot(feats, k.xs[2, EMB_AT:ROWS, :], HIGH)
        return carry

    lax.fori_loop(0, CHUNKS, chunk, 0)


def stack_pair(v, first):
    zero = jnp.zeros_like(v)
    return jnp.concatenate([jnp.where(first, v, zero), jnp.where(first, zero, v)], 0)


def join_pair(v, first):
    return jnp.where(first, v[:SLOT], v[SLOT:])


def window_rows(w):
    return pl.ds(pl.multiple_of(w * SLOT, SLOT), SLOT)


def each_chunk(body, between=None):
    def step(c, carry):
        body(c, chunk_rows(c))
        if between is not None:

            @pl.when(c < CHUNKS - 1)
            def _():
                between()

        return carry

    lax.fori_loop(0, CHUNKS, step, 0)


def each_window(body, after=None, between=None):
    def pair(n, carry):
        body(2 * n)
        body(2 * n + 1)
        if between is not None:

            @pl.when(n == WINS // 4 - 1)
            def _():
                between()

        if after is not None:
            after(pl.ds(pl.multiple_of(n * 128, 128), 128))
        return carry

    lax.fori_loop(0, WINS // 2, pair, 0)


def forward_qkv(k, l, between):
    def chunk(c, rows):
        xhat, _ = norm_parts(k.xs[slot(l), rows, :])
        normed = (xhat * k.row(l, 0) + k.row(l, 1)).astype(LOWER)
        k.normed_t[:, rows] = normed.T
        for j in range(3):
            part = dot(normed, k.w_qkv(l, j)) + k.row(l, 4 + j)
            k.qkv[rows, j * D : (j + 1) * D] = part.astype(LOWER)

    each_chunk(chunk, between)


def forward_windows(k, l, between):
    first = iota((SLOT, 128), 1) < HD

    def window(w):
        rows = window_rows(w)
        bias = k.bias[rows, :]
        scores = []
        for p in range(H // 2):
            at = p * 128
            query = stack_pair(k.qkv[rows, at : at + 128] * jnp.asarray(HD**-0.5, LOWER), first)
            scores.append(dot_nt(k.qkv[rows, D + at : D + at + 128], query) + bias)
        for p in range(H // 2):
            at = p * 128
            peak = jnp.max(scores[p], 0, keepdims=True)
            expo = jnp.exp(scores[p] - peak)
            total = jnp.sum(expo, 0, keepdims=True)
            probs = (expo * (1.0 / total)).astype(LOWER)
            k.logs[l, w, p : p + 1, :] = peak + jnp.log(total)
            out = dot_tn(probs, k.qkv[rows, 2 * D + at : 2 * D + at + 128])
            k.left[rows, at : at + 128] = join_pair(out, first).astype(LOWER)

    def turn(rows):
        k.mixed_t[:, rows] = k.left[rows, :].T

    each_window(window, turn, between)


def forward_up(k, l, between):
    def chunk(c, rows):
        mid = k.xs[slot(l), rows, :] + dot(k.left[rows, :], k.w_out(l)) + k.row(l, 7)
        k.mid[rows, :] = mid
        xhat, _ = norm_parts(mid)
        second = (xhat * k.row(l, 2) + k.row(l, 3)).astype(LOWER)
        k.second_t[:, rows] = second.T
        for j in range(4):
            cols = slice(j * D, (j + 1) * D)
            h = dot(second, k.w_up(l, j)) + k.row(l, 8 + j)
            square = h * h
            over = 1.0 + jnp.tanh(h * (GELU_C + GELU_C * GELU_A * square))
            half = 0.5 * h
            acted = (half * over).astype(LOWER)
            slope = over * (0.5 + half * (2.0 - over) * (GELU_C + 3.0 * GELU_A * GELU_C * square))
            k.work[rows, cols] = acted
            k.slope[rows, cols] = slope.astype(LOWER)
            k.act_t[cols, rows] = acted.T

    each_chunk(chunk, between)


def forward_down(k, l, dest):
    def chunk(c, rows):
        w_down = jnp.concatenate([k.w_down(l, j) for j in range(4)], 0)
        k.xs[dest, rows, :] = k.mid[rows, :] + k.row(l, 12) + dot(k.work[rows, :], w_down)

    each_chunk(chunk)


def head_stage(k, at):
    gain, bias = k.small[FIN : FIN + 1, :], k.small[FIN + 1 : FIN + 2, :]
    lane = iota((CHUNK, 128), 1)
    keep = lane < A

    def bias_row(first):
        row = jnp.zeros((1, 128), WIDE)
        at = iota((1, 128), 1)
        for a in range(A):
            row = jnp.where(at == a, k.head_bias[first + a], row)
        return row

    bias_mean, bias_spread = bias_row(0), bias_row(A)
    temp = jnp.exp(jnp.full((1, 128), k.log_temp[0], WIDE))

    def chunk(c, carry):
        rows = chunk_rows(c)
        xhat, scale = norm_parts(k.xs[at, rows, :])
        feats = (xhat * gain + bias).astype(LOWER)
        mean = dot_nt(feats, k.headw[0]) + bias_mean
        spread = jnp.tanh(dot_nt(feats, k.headw[1]) + bias_spread)
        acts = pltpu.roll(k.feats[rows, :], 128 - HEAD_AT, 1)
        weight = acts[:, A : A + 1]
        acts = jnp.where(keep, acts, 0.0)
        target = 0.5 * (jnp.log(1.0 + acts) - jnp.log(1.0 - acts))
        shrink = jnp.exp(-spread)
        zed = (target - mean) * shrink
        terms = 0.5 * zed * zed + spread + HALF_LOG_TAU + jnp.log(1.0 - acts * acts)
        nll = jnp.sum(jnp.where(keep, terms, 0.0), -1, keepdims=True)
        entropy = jnp.sum(jnp.where(keep, spread, 0.0), -1, keepdims=True) + A * (0.5 + HALF_LOG_TAU)
        loss = weight * (nll - temp * entropy)
        sums = jnp.where(lane == 0, loss, jnp.where(lane == 1, weight * entropy, jnp.where(lane == 2, weight, 0.0)))
        d_mean = jnp.where(keep, weight * (-zed * shrink), 0.0).astype(LOWER)
        d_spread = weight * (1.0 - zed * zed - temp) * (1.0 - spread * spread)
        d_spread = jnp.where(keep, d_spread, 0.0).astype(LOWER)
        k.sgh[2:3, 0:128] += col_sum(sums)
        k.sgh[3:4, 0:128] += col_sum(d_mean.astype(WIDE))
        k.sgh[4:5, 0:128] += col_sum(d_spread.astype(WIDE))
        k.sgw[0] += dot_tn(d_mean, feats)[0:8]
        k.sgw[1] += dot_tn(d_spread, feats)[0:8]
        d_feats = dot(d_mean, k.headw[0]) + dot(d_spread, k.headw[1])
        k.sgh[0:1, :] += col_sum(d_feats * xhat)
        k.sgh[1:2, :] += col_sum(d_feats)
        k.xs[at, rows, :] = norm_back(xhat, scale, gain, d_feats)
        return carry

    lax.fori_loop(0, CHUNKS, chunk, 0)


def store_blocks(ref, l, owners, first, count, value):
    value = value.astype(LOWER)
    for n, i in enumerate(owners):
        a, b = owner_place(i)
        ref[l, a, b, first : first + count, :] = value[n * count : (n + 1) * count]


def backward_ffn(k, l, grad, between=None):
    def chunk(c, rows):
        d_down = k.xs[grad, rows, :].astype(LOWER)
        k.dout[rows, :] = d_down
        k.sgl[l, 12:13, :] += col_sum(d_down.astype(WIDE))
        d_second = jnp.zeros((CHUNK, D), WIDE)
        for j in range(4):
            cols = slice(j * D, (j + 1) * D)
            d_acted = dot_nt(d_down, k.w_down(l, j))
            d_hidden = (d_acted * k.slope[rows, cols].astype(WIDE)).astype(LOWER)
            k.work[rows, cols] = d_hidden
            k.sgl[l, 8 + j : 9 + j, :] += col_sum(d_hidden.astype(WIDE))
            d_second = d_second + dot_nt(d_hidden, k.w_up(l, j))
        xhat, scale = norm_parts(k.mid[rows, :])
        k.sgl[l, 2:3, :] += col_sum(d_second * xhat)
        k.sgl[l, 3:4, :] += col_sum(d_second)
        k.xs[grad, rows, :] += norm_back(xhat, scale, k.row(l, 2), d_second)

    each_chunk(chunk, between)


def backward_down_grads(k, l):
    for j in range(4):
        part = dot(k.act_t[j * D : (j + 1) * D, :], k.dout[...])
        store_blocks(k.wf, l, range(8 * j, 8 * j + 8), 64, 64, part)


def backward_up_grads(k, l):
    for j in range(4):
        part = dot(k.second_t[...], k.work[:, j * D : (j + 1) * D])
        store_blocks(k.wf, l, range(BLOCKS), 16 * j, 16, part)


def backward_out(k, l, grad):
    def before(c, rows):
        d_branch = k.xs[grad, rows, :].astype(LOWER)
        k.left[rows, :] = d_branch
        k.sgl[l, 7:8, :] += col_sum(d_branch.astype(WIDE))
        k.dout[rows, :] = dot_nt(d_branch, k.w_out(l)).astype(LOWER)

    each_chunk(before)
    store_blocks(k.wa, l + 1, range(BLOCKS), 48, 16, dot(k.mixed_t[...], k.left[...]))


def backward_windows(k, l, between):
    first = iota((SLOT, 128), 1) < HD
    scale = HD**-0.5

    def window(w):
        rows = window_rows(w)
        bias = k.bias[rows, :]
        for p in range(H // 2):
            at = p * 128
            query = stack_pair(k.qkv[rows, at : at + 128] * jnp.asarray(scale, LOWER), first)
            keyed = k.qkv[rows, D + at : D + at + 128]
            values = k.qkv[rows, 2 * D + at : 2 * D + at + 128]
            d_mixed = stack_pair(k.dout[rows, at : at + 128], first)
            probs = jnp.exp(dot_nt(keyed, query) + bias - k.logs[l, w, p : p + 1, :])
            d_probs = dot_nt(values, d_mixed)
            d_values = dot(probs.astype(LOWER), d_mixed)
            inner = probs * d_probs
            d_scores = (inner - probs * jnp.sum(inner, 0, keepdims=True)).astype(LOWER)
            d_keyed = dot(d_scores, query)
            d_query = join_pair(dot_tn(d_scores, keyed), first) * scale
            k.work[rows, at : at + 128] = d_query.astype(LOWER)
            k.work[rows, D + at : D + at + 128] = d_keyed.astype(LOWER)
            k.work[rows, 2 * D + at : 2 * D + at + 128] = d_values.astype(LOWER)

    each_window(window, None, between)


def backward_attn_grads(k, l):
    for j in range(3):
        part = dot(k.normed_t[...], k.work[:, j * D : (j + 1) * D])
        store_blocks(k.wa, l + 1, range(BLOCKS), 16 * j, 16, part)


def backward_input(k, l, grad):
    def chunk(c, rows):
        d_normed = jnp.zeros((CHUNK, D), WIDE)
        for j in range(3):
            d_part = k.work[rows, j * D : (j + 1) * D]
            k.sgl[l, 4 + j : 5 + j, :] += col_sum(d_part.astype(WIDE))
            d_normed = d_normed + dot_nt(d_part, k.w_qkv(l, j))
        xhat, scale = norm_parts(k.xs[slot(l), rows, :])
        k.sgl[l, 0:1, :] += col_sum(d_normed * xhat)
        k.sgl[l, 1:2, :] += col_sum(d_normed)
        k.xs[grad, rows, :] += norm_back(xhat, scale, k.row(l, 0), d_normed)

    each_chunk(chunk)


def small_stage(k, out, grad):
    out[...] = jnp.zeros_like(out)
    out[0:EMB, :] = dot_tn(k.feats[...], k.xs[grad], HIGH)[0:EMB]
    out[FIN : FIN + 2, :] = k.sgh[0:2, :]
    out[HEADW : HEADW + A, :] = k.sgw[0, 0:A, :]
    out[HEADW + A : HEADW + 2 * A, :] = k.sgw[1, 0:A, :]
    for l in range(LAYERS):
        out[BASE + l * PER : BASE + (l + 1) * PER, :] = k.sgl[l, 0:PER, :]
    out[NROWS : NROWS + 3, :] = k.sgh[2:5, :]


WORK_SHAPES = dict(
    wa=((LAYERS + 1, 4, 8, ATTN, D), LOWER),
    wf=((LAYERS, 4, 8, FFN, D), LOWER),
    xs=((3, ROWS, D), WIDE),
    qkv=((ROWS, 3 * D), LOWER),
    normed_t=((D, ROWS), LOWER),
    mixed_t=((D, ROWS), LOWER),
    slope=((ROWS, FF), LOWER),
    act_t=((FF, ROWS), LOWER),
    second_t=((D, ROWS), LOWER),
    mid=((ROWS, D), WIDE),
    logs=((LAYERS, WINS, 8, 128), WIDE),
    work=((ROWS, FF), LOWER),
    left=((ROWS, D), LOWER),
    dout=((ROWS, D), LOWER),
    feats=((ROWS, 128), WIDE),
    bias=((ROWS, 128), WIDE),
    headw=((2, 128, D), LOWER),
    lrows=((LAYERS, 16, D), WIDE),
    sgl=((LAYERS, 16, D), WIDE),
    sgh=((8, D), WIDE),
    sgw=((2, 8, D), WIDE),
    meta=((128, 128), WIDE),
    buf=((2, 128, 128), WIDE),
)
KEEP_ATTN = ("qkv", "normed_t", "mixed_t")
KEEP_FFN = ("slope", "act_t", "second_t", "mid")
KEEP = KEEP_ATTN + KEEP_FFN


MESH = pl.DeviceIdType.MESH
NZ, NY, NX, NC = 4, 2, 2, 2
NR = NY * NX * NC
SHARD = PACK
PARTS, DEEP = 3, 64
HALF = DEEP // 2


class Place:
    def __init__(self):
        dp, fsdp = lax.axis_index("dp"), lax.axis_index("fsdp")
        self.z, self.y = dp // NY, dp % NY
        self.x, self.c = fsdp // NC, fsdp % NC
        self.a, self.b = 2 * self.c + self.x, 4 * self.y + self.z
        self.r = 4 * self.y + fsdp
        self.to_z = [(((self.z + d) % NZ) * NY + self.y, fsdp) for d in range(1, NZ)]
        self.odd = self.z % 2
        self.to_pair = ((self.z + 1 - 2 * self.odd) * NY + self.y, fsdp)
        self.plane = []
        for d in range(1, 8):
            y, x, c = [
                1 - v if d & bit else v for v, bit in ((self.y, 4), (self.x, 2), (self.c, 1))
            ]
            self.plane.append((self.z * NY + y, x * NC + c))
        self.to_c, self.to_x, self.to_y = self.plane[0], self.plane[1], self.plane[3]

    def barrier(self):
        sem = pltpu.get_barrier_semaphore()
        for partner in self.plane + self.to_z:
            pl.semaphore_signal(sem, inc=1, device_id=partner, device_id_type=MESH)
        pl.semaphore_wait(sem, len(self.plane) + len(self.to_z))


def remote(src, dst, send, recv, to):
    return pltpu.make_async_remote_copy(
        src_ref=src, dst_ref=dst, send_sem=send, recv_sem=recv, device_id=to, device_id_type=MESH
    )


def part_ref(weights, part):
    return weights[min(part, 1)], (0, 0, DEEP)[part]


class Gather:
    COPIES = 13

    def __init__(self, place, weights, send, recv):
        self.at, self.weights, self.send, self.recv = place, weights, send, recv

    def copy(self, l, part, n):
        at = self.at
        array, row = part_ref(self.weights, part)
        a, b, rows, to = at.a, pl.ds(4 * at.y, 4), pl.ds(row, DEEP), at.to_c
        if n < 3:
            b, to = at.b, at.to_z[n]
        elif n < 5:
            to = (at.to_x, at.to_y)[n - 3]
        if n in (6, 8, 10, 11, 12):
            a = 2 * at.c + 1 - at.x
        if n in (7, 9, 10, 11, 12):
            b = pl.ds(4 * (1 - at.y), 4)
        if n in (6, 7):
            first = row + at.odd * HALF + (n - 6) * (HALF // 2)
            rows = pl.ds(pl.multiple_of(first, HALF // 2), HALF // 2)
            to = (at.to_y, at.to_x)[n - 6]
        if n in (10, 11):
            rows = pl.ds(pl.multiple_of(row + at.odd * HALF, HALF), HALF)
        if n == 11:
            to = at.to_pair
        if n == 12:
            rows = pl.ds(pl.multiple_of(row + (1 - at.odd) * HALF, HALF), HALF)
        ref = array.at[l, a, b, rows, :]
        q = PARTS * l + part
        return remote(ref, ref, self.send.at[q, n], self.recv.at[q, n], to)

    def start(self, l, part, *ns):
        for n in ns:
            self.copy(l, part, n).start()

    def wait(self, l, part, *ns):
        for n in ns:
            self.copy(l, part, n).wait_recv()

    def first(self, l, part):
        self.start(l, part, 0, 1, 2)

    def second(self, l, part):
        self.wait(l, part, 0, 1, 2)
        self.start(l, part, 3, 4, 5)

    def third(self, l, part):
        self.wait(l, part, 3)
        self.start(l, part, 6, 8)
        self.wait(l, part, 4)
        self.start(l, part, 7, 9)

    def fourth(self, l, part):
        self.wait(l, part, 6, 7)
        self.start(l, part, 11, 10)

    def fifth(self, l, part):
        self.wait(l, part, 11)
        self.start(l, part, 12)

    def last(self, l, part):
        self.wait(l, part, 5, 8, 9, 10, 12)

    def sent(self, l, part):
        for n in range(self.COPIES):
            self.copy(l, part, n).wait_send()


class Reduce:
    COPIES = 8

    def __init__(self, place, grads, landing, send, recv, credit):
        self.at, self.grads, self.landing = place, grads, landing
        self.send, self.recv, self.credit = send, recv, credit

    def refs(self, l, part):
        array, row = part_ref(self.grads, part)
        grads = array.at[l + 1 - min(part, 1), :, :, pl.ds(row, DEEP), :]
        return (grads, *self.landing[part])

    def copy(self, l, part, n):
        at, half = self.at, HALF
        g, r0, r1a, r1b, r2, r3 = self.refs(l, part)
        top, low, other = pl.ds(0, half), pl.ds(half, half), pl.ds(4 * (1 - at.y), 4)
        if n == 0:
            src, dst, to = g.at[pl.ds(2 * (1 - at.c), 2)], r0, at.to_c
        elif n == 1:
            src, dst, to = r0.at[1 - at.x, :, top, :], r1a, at.to_x
        elif n == 2:
            src, dst, to = r0.at[:, other, low, :], r1b, at.to_y
        elif n == 3:
            src, dst, to = r1a.at[other], r2.at[:, top, :], at.to_y
        elif n == 4:
            src, dst, to = r1b.at[1 - at.x], r2.at[:, low, :], at.to_x
        else:
            src, dst, to = r2.at[(at.z + n - 4) % NZ], r3.at[n - 5], at.to_z[n - 5]
        q = PARTS * l + part
        return remote(src, dst, self.send.at[q, n], self.recv.at[q, n], to)

    def may_send(self, l, part, *partners):
        @pl.when(l < LAYERS - 1)
        def _():
            for n in partners:
                pl.semaphore_wait(self.credit.at[part, n], 1)

    def allow(self, l, part, *credits):
        at = self.at

        @pl.when(l > 0)
        def _():
            for n, to in credits:
                pl.semaphore_signal(
                    self.credit.at[part, n], inc=1, device_id=to, device_id_type=MESH
                )

    def start(self, l, part):
        self.may_send(l, part, 0)
        self.copy(l, part, 0).start()

    def first(self, l, part):
        at, half = self.at, HALF
        g, r0, _, _, _, _ = self.refs(l, part)
        top, low = pl.ds(0, half), pl.ds(half, half)
        self.copy(l, part, 0).wait_recv()

        def along_x(n, carry):
            x = 1 - at.x
            total = g[2 * at.c + x, n, top].astype(WIDE) + r0[x, n, top].astype(WIDE)
            r0[x, n, top] = total.astype(LOWER)
            return carry

        def along_y(n, carry):
            x, b = n // 4, 4 * (1 - at.y) + n % 4
            total = g[2 * at.c + x, b, low].astype(WIDE) + r0[x, b, low].astype(WIDE)
            r0[x, b, low] = total.astype(LOWER)
            return carry

        lax.fori_loop(0, 8, along_x, 0)
        self.may_send(l, part, 1, 2)
        self.copy(l, part, 1).start()
        lax.fori_loop(0, 8, along_y, 0)
        self.copy(l, part, 2).start()

    def second(self, l, part):
        at, half = self.at, HALF
        g, r0, r1a, r1b, _, _ = self.refs(l, part)
        top, low = pl.ds(0, half), pl.ds(half, half)

        def along_y(n, carry):
            b = 4 * (1 - at.y) + n
            total = g[at.a, b, top].astype(WIDE) + r0[at.x, b, top].astype(WIDE)
            r1a[b] = (total + r1a[b].astype(WIDE)).astype(LOWER)
            return carry

        def along_x(n, carry):
            x, b = 1 - at.x, 4 * at.y + n
            total = g[2 * at.c + x, b, low].astype(WIDE) + r0[x, b, low].astype(WIDE)
            r1b[x, n] = (total + r1b[x, n].astype(WIDE)).astype(LOWER)
            return carry

        self.copy(l, part, 1).wait_recv()
        lax.fori_loop(0, NZ, along_y, 0)
        self.may_send(l, part, 6, 7)
        self.copy(l, part, 3).start()
        self.copy(l, part, 2).wait_recv()
        lax.fori_loop(0, NZ, along_x, 0)
        self.copy(l, part, 4).start()

    def chip_sums(self, l, part, z):
        at, half = self.at, HALF
        g, r0, r1a, r1b, r2, _ = self.refs(l, part)
        top, low, b = pl.ds(0, half), pl.ds(half, half), 4 * at.y + z
        upper = g[at.a, b, top].astype(WIDE) + r0[at.x, b, top].astype(WIDE)
        lower = g[at.a, b, low].astype(WIDE) + r0[at.x, b, low].astype(WIDE)
        return (
            upper + r1a[b].astype(WIDE) + r2[z, top].astype(WIDE),
            lower + r1b[at.x, z].astype(WIDE) + r2[z, low].astype(WIDE),
        )

    def third(self, l, part, out):
        at, half, row = self.at, HALF, DEEP * part
        r2 = self.landing[part][3]
        for n in (3, 4):
            self.copy(l, part, n).wait_recv()
        self.may_send(l, part, 3, 4, 5)
        for n in range(3):
            z = (at.z + n + 1) % NZ
            upper, lower = self.chip_sums(l, part, z)
            r2[z, pl.ds(0, half)] = upper.astype(LOWER)
            r2[z, pl.ds(half, half)] = lower.astype(LOWER)
            self.copy(l, part, 5 + n).start()
        upper, lower = self.chip_sums(l, part, at.z)
        out[l, row : row + half, :] = upper
        out[l, row + half : row + 2 * half, :] = lower
        for n in range(5):
            self.copy(l, part, n).wait_send()
        self.allow(l, part, (0, at.to_c), (1, at.to_x), (2, at.to_y))

    def last(self, l, part, out, squares):
        at, row = self.at, DEEP * part
        r3 = self.landing[part][4]
        rows = slice(row, row + DEEP)
        total = out[l, rows, :]
        for n in range(3):
            self.copy(l, part, 5 + n).wait_recv()
            total = total + r3[n].astype(WIDE)
        out[l, rows, :] = total
        squares[0:1, :] += col_sum(total * total)
        for n in range(5, self.COPIES):
            self.copy(l, part, n).wait_send()
        late = [(6, at.to_x), (7, at.to_y)] + [(5 - n, at.to_z[n]) for n in range(3)]
        self.allow(l, part, *late)


class Total:
    COPIES = 7

    def __init__(self, place, ref, rows, send, recv):
        self.at, self.ref, self.rows = place, ref, rows // 2
        self.send, self.recv = send, recv

    def half(self, n):
        return self.ref.at[pl.ds(pl.multiple_of(n * self.rows, 8), self.rows), :]

    def whole(self):
        return self.ref.at[pl.ds(0, 2 * self.rows), :]

    def copy(self, n):
        at = self.at
        mine, other = self.half(at.c), self.half(1 - at.c)
        src, dst, to = (
            (other, self.half(2), at.to_c),
            (self.half(8), self.half(3), at.to_x),
            (self.half(9), self.half(4), at.to_y),
            (self.half(10), self.half(5), at.to_z[0]),
            (self.half(10), self.half(6), at.to_z[1]),
            (self.half(10), self.half(7), at.to_z[2]),
            (mine, self.half(11), at.to_c),
        )[n]
        return remote(src, dst, self.send.at[n], self.recv.at[n], to)

    def start(self):
        self.copy(0).start()

    def step(self, n):
        self.copy(n).wait_recv()
        own = self.half(self.at.c) if n == 0 else self.half(7 + n)
        self.half(8 + n)[...] = own[...] + self.half(2 + n)[...]
        for m in ((1,), (2,), (3, 4, 5))[n]:
            self.copy(m).start()

    def back(self):
        for m in (3, 4, 5):
            self.copy(m).wait_recv()
        self.copy(0).wait_send()
        total = None
        for z in range(NZ):
            term = self.half(10)[...]
            for n in range(3):
                from_z = (self.at.z + NZ - 1 - n) % NZ
                term = jnp.where(from_z == z, self.half(5 + n)[...], term)
            total = term if total is None else total + term
        self.half(self.at.c)[...] = total
        self.copy(6).start()

    def last(self):
        self.copy(6).wait_recv()
        self.half(1 - self.at.c)[...] = self.half(11)[...]
        for n in range(1, self.COPIES):
            self.copy(n).wait_send()


class Norm:
    COPIES = 10

    def __init__(self, place, plane, column, send, recv):
        self.at, self.plane, self.column = place, plane, column
        self.send, self.recv = send, recv

    def copy(self, n):
        at = self.at
        if n < 7:
            ref, to = self.plane.at[at.r], at.plane[n]
        else:
            ref, to = self.column.at[at.z], at.to_z[n - 7]
        return remote(ref, ref, self.send.at[n], self.recv.at[n], to)

    def start(self, tile):
        self.plane[self.at.r] = tile
        for n in range(7):
            self.copy(n).start()

    def total(self, ref, ns):
        for n in ns:
            self.copy(n).wait_recv()
        total = ref[0]
        for n in range(1, ref.shape[0]):
            total = total + ref[n]
        return total

    def step(self):
        self.column[self.at.z] = self.total(self.plane, range(7))
        for n in range(7, self.COPIES):
            self.copy(n).start()

    def last(self):
        total = self.total(self.column, range(7, self.COPIES))
        for n in range(self.COPIES):
            self.copy(n).wait_send()
        return total


LANDING = (
    (NX, 8, DEEP, D),
    (8, HALF, D),
    (NX, NZ, HALF, D),
    (NZ, DEEP, D),
    (3, DEEP, D),
)


def stage_rows(qkv, out, up, down, l):
    return (
        [(qkv.at[l, :, pl.ds(j * D, D)], 16 * j, 16) for j in range(3)]
        + [(out.at[l], 48, 16)]
        + [(up.at[l, :, pl.ds(j * D, D)], 64 + 16 * j, 16) for j in range(4)]
        + [(down.at[l], 128, 64)]
    )


GATHER_PLAN = {
    (-1, "begin"): [("first", 0, 0), ("first", 0, 1)],
    (-1, "setup"): [("first", 0, 2), ("first", 1, 0), ("second", 0, 0)],
    (0, "start"): [("second", 0, 1), ("first", 1, 1), ("third", 0, 0), ("fourth", 0, 0), ("second", 0, 2), ("first", 1, 2), ("third", 0, 1), ("fifth", 0, 0), ("last", 0, 0), ("second", 1, 0), ("fourth", 0, 1)],
    (0, "qkv"): [("first", 2, 0), ("third", 0, 2), ("fifth", 0, 1)],
    (0, "windows_half"): [("second", 1, 1), ("last", 0, 1)],
    (0, "windows"): [("fourth", 0, 2)],
    (0, "up_half"): [("first", 2, 1), ("third", 1, 0), ("fifth", 0, 2), ("second", 1, 2)],
    (0, "up"): [("last", 0, 2), ("fourth", 1, 0), ("second", 2, 0)],
    (0, "down"): [("first", 2, 2), ("third", 1, 1), ("fifth", 1, 0)],
    (1, "start"): [("last", 1, 0), ("fourth", 1, 1)],
    (1, "qkv_half"): [("second", 2, 1)],
    (1, "qkv"): [("third", 1, 2), ("fifth", 1, 1)],
    (1, "windows_half"): [("last", 1, 1)],
    (1, "windows"): [("second", 2, 2), ("fourth", 1, 2)],
    (1, "up_half"): [("third", 2, 0), ("fifth", 1, 2), ("last", 1, 2)],
    (1, "up"): [("fourth", 2, 0)],
    (1, "down"): [("third", 2, 1), ("fifth", 2, 0)],
    (2, "start"): [("last", 2, 0), ("fourth", 2, 1)],
    (2, "qkv"): [("third", 2, 2), ("fifth", 2, 1)],
    (2, "windows_half"): [("last", 2, 1)],
    (2, "windows"): [("fourth", 2, 2)],
    (2, "up_half"): [("fifth", 2, 2), ("last", 2, 2)],
}


def train_kernel(refs, alone):
    k = Kit(**refs)

    def kept(names, l, back):
        copies = []
        for name in names:
            here, there = refs[name], refs["keep_" + name].at[l]
            src, dst = (there, here) if back else (here, there)
            copies.append(pltpu.make_async_copy(src, dst, k.keep_sem.at[KEEP.index(name)]))
        return copies

    def start(copies):
        for copy in copies:
            copy.start()

    def wait(copies):
        for copy in copies:
            copy.wait()

    def kept_x(back):
        here, there = k.xs.at[0], k.keep_x
        src, dst = (there, here) if back else (here, there)
        return [pltpu.make_async_copy(src, dst, k.keep_sem.at[len(KEEP)])]

    arrays = [(l, n) for l in range(LAYERS) for n in (0, 1)]
    parts = [(l, part) for l in range(LAYERS) for part in range(PARTS)]
    weights = (k.wa, k.wf)
    if alone:
        loads = [
            pltpu.make_async_copy((k.all_a, k.all_f)[n].at[l], weights[n].at[l], k.load_sem.at[2 * l + n])
            for l, n in arrays
        ]
        stores = [
            pltpu.make_async_copy(
                weights[n].at[l + 1 - n], (k.grad_a, k.grad_f)[n].at[l], k.load_sem.at[2 * l + n]
            )
            for l, n in arrays
        ]
        start(loads)
    else:
        place = Place()
        gather = Gather(place, weights, k.gather_send, k.gather_recv)
        reduce = Reduce(
            place, weights, k.landing, k.reduce_send, k.reduce_recv, k.credit
        )
        sums = Total(place, k.mid, SMALL, k.sum_send, k.sum_recv)
        norm = Norm(place, k.norm_plane, k.norm_column, k.norm_send, k.norm_recv)

    def run(plan):
        for stage, l, part in plan:
            getattr(gather, stage)(l, part)

    def poll(l, point):
        if alone:
            return
        for layer in range(LAYERS):
            plan = GATHER_PLAN.get((layer, point))
            if plan:

                @pl.when(l == layer)
                def _(plan=plan):
                    with jax.named_scope("gather_" + point):
                        run(plan)

    if not alone:
        staged = []
        for l in range(LAYERS):
            for n, (src, row, count) in enumerate(stage_rows(k.qkv_w, k.out_w, k.up_w, k.down_w, l)):
                dst = k.xs.at[2, pl.ds(l * PACK + row, count), :]
                staged.append(pltpu.make_async_copy(src, dst, k.stage_sem.at[l, n]))
        start(staged)
        place.barrier()
        for l in range(LAYERS):
            wait(staged[9 * l : 9 * l + 9])
            row = l * PACK
            for part in range(PARTS):
                array, first = part_ref(weights, part)
                mine = k.xs[2, row + DEEP * part : row + DEEP * (part + 1), :].astype(LOWER)
                array[l, place.a, place.b, first : first + DEEP, :] = mine
                if ("first", l, part) in GATHER_PLAN[-1, "begin"]:
                    gather.first(l, part)
        k.squares_sum[...] = jnp.zeros_like(k.squares_sum)

    with jax.named_scope("embedding"):
        setup_stage(k)
    start(kept_x(False))
    if not alone:
        with jax.named_scope("gather_setup"):
            run(GATHER_PLAN[-1, "setup"])

    def forward(l, carry):
        if alone:
            pltpu.make_async_copy(k.all_a.at[l], k.wa.at[l], k.load_sem.at[2 * l]).wait()

        @pl.when(l > 0)
        def _():
            wait(kept(KEEP_ATTN, l - 1, False))

        poll(l, "start")
        with jax.named_scope("qkv"):
            forward_qkv(k, l, lambda: poll(l, "qkv_half"))
        poll(l, "qkv")
        with jax.named_scope("attention"):
            forward_windows(k, l, lambda: poll(l, "windows_half"))

        @pl.when(l < LAYERS - 1)
        def _():
            start(kept(KEEP_ATTN, l, False))

        @pl.when(l > 0)
        def _():
            wait(kept(KEEP_FFN, l - 1, False))

        @pl.when(l == 1)
        def _():
            wait(kept_x(False))

        if alone:
            pltpu.make_async_copy(k.all_f.at[l], k.wf.at[l], k.load_sem.at[2 * l + 1]).wait()
        poll(l, "windows")
        with jax.named_scope("ffn_up"):
            forward_up(k, l, lambda: poll(l, "up_half"))
        poll(l, "up")
        with jax.named_scope("ffn_down"):
            forward_down(k, l, (l + 1) % 2 + l // 2)

        @pl.when(l < LAYERS - 1)
        def _():
            start(kept(KEEP_FFN, l, False))

        poll(l, "down")
        return carry

    lax.fori_loop(0, LAYERS, forward, 0)
    if not alone:
        for l, part in parts:
            gather.sent(l, part)
    grad = 2
    with jax.named_scope("head"):
        head_stage(k, grad)

    def backward(n, carry):
        l = LAYERS - 1 - n

        def behind(name, *stages):
            @pl.when(n > 0)
            def _():
                with jax.named_scope(name):
                    for stage, part, *more in stages:
                        stage(l + 1, part, *more)

        @pl.when(n > 0)
        def _():
            wait(kept(KEEP_FFN, l, True))

        def now(name, part):
            if not alone:
                with jax.named_scope("reduce_" + name):
                    getattr(reduce, name)(l, part, *extra.get(name, ()))

        def then(name, part):
            if not alone:

                @pl.when(n > 0)
                def _():
                    with jax.named_scope("reduce_" + name):
                        getattr(reduce, name)(l + 1, part, *extra.get(name, ()))

        def in_ffn():
            then("last", 2)

        def in_windows():
            now("second", 2)
            then("last", 0)

        with jax.named_scope("ffn_back"):
            backward_ffn(k, l, grad, in_ffn)
        then("last", 1)
        then("second", 0)
        with jax.named_scope("down_grads"):
            backward_down_grads(k, l)
        now("start", 2)
        then("third", 0)
        with jax.named_scope("up_grads"):
            backward_up_grads(k, l)

        @pl.when(n < LAYERS - 1)
        def _():
            start(kept(KEEP_FFN, l - 1, True))

        now("start", 1)
        now("first", 2)

        @pl.when(n > 0)
        def _():
            wait(kept(KEEP_ATTN, l, True))

        with jax.named_scope("out_back"):
            backward_out(k, l, grad)
        now("first", 1)
        with jax.named_scope("attention_back"):
            backward_windows(k, l, in_windows)
        now("third", 2)
        with jax.named_scope("qkv_grads"):
            backward_attn_grads(k, l)

        @pl.when(n < LAYERS - 1)
        def _():
            start(kept(KEEP_ATTN, l - 1, True))

        now("start", 0)
        now("second", 1)

        @pl.when(n == LAYERS - 1)
        def _():
            wait(kept_x(True))

        with jax.named_scope("qkv_back"):
            backward_input(k, l, grad)

        @pl.when(n == 0)
        def _():
            start(kept_x(True))

        now("first", 0)
        now("third", 1)
        return carry

    extra = {} if alone else dict(third=(k.shard,), last=(k.shard, k.squares_sum))
    lax.fori_loop(0, LAYERS, backward, 0)
    if alone:
        start(stores)
        small_stage(k, k.small_out, grad)
        wait(stores)
        return
    with jax.named_scope("small_grads"):
        small_stage(k, sums.whole(), grad)
    sums.start()
    with jax.named_scope("reduce_end"):
        reduce.last(0, 2, k.shard, k.squares_sum)
        reduce.second(0, 0)
        sums.step(0)
        reduce.third(0, 0, k.shard)
        sums.step(1)
        reduce.last(0, 1, k.shard, k.squares_sum)
        sums.step(2)
        reduce.last(0, 0, k.shard, k.squares_sum)
    with jax.named_scope("norm"):
        squares = k.squares_sum[...]
        norm.start(sum(squares[:, n * 128 : (n + 1) * 128] for n in range(D // 128)))
        sums.back()
        norm.step()
        sums.last()
        k.small_out[...] = sums.whole()[...]
        k.squares[...] = norm.last()


def train_pass(inputs, weights, alone):
    whole = pl.BlockSpec(memory_space=pltpu.VMEM)
    scalars = pl.BlockSpec(memory_space=pltpu.SMEM)
    anywhere = pl.BlockSpec(memory_space=pl.ANY)
    dma = pltpu.SemaphoreType.DMA
    count = PARTS * LAYERS
    names = ["states", "actions", "returns", "starts", "repeats", "valid"]
    names += ["log_temp", "small", "head_bias"]
    out_shape = {"small_out": ((SMALL, D), WIDE)}
    for name in KEEP:
        shape, dtype = WORK_SHAPES[name]
        out_shape["keep_" + name] = ((LAYERS - 1,) + shape, dtype)
    out_shape["keep_x"] = ((ROWS, D), WIDE)
    scratch = {name: pltpu.VMEM(*shape) for name, shape in WORK_SHAPES.items()}
    scratch["keep_sem"] = dma((len(KEEP) + 1,))
    if alone:
        names += ["all_a", "all_f"]
        out_shape["grad_a"] = ((LAYERS, 4, 8, ATTN, D), LOWER)
        out_shape["grad_f"] = ((LAYERS, 4, 8, FFN, D), LOWER)
        scratch["load_sem"] = dma((count,))
    else:
        names += ["qkv_w", "out_w", "up_w", "down_w"]
        out_shape["shard"] = ((LAYERS, PACK, D), WIDE)
        out_shape["squares"] = ((8, 128), WIDE)
        for part in range(PARTS):
            for n, shape in enumerate(LANDING):
                scratch["land_%d_%d" % (part, n)] = pltpu.VMEM(shape, LOWER)
        scratch["stage_sem"] = dma((LAYERS, 9))
        scratch["squares_sum"] = pltpu.VMEM((8, D), WIDE)
        for name, copies in (("gather", Gather.COPIES), ("reduce", Reduce.COPIES)):
            scratch[name + "_send"] = dma((count, copies))
            scratch[name + "_recv"] = dma((count, copies))
        scratch["credit"] = pltpu.SemaphoreType.REGULAR((PARTS, 8))
        scratch["norm_plane"] = pltpu.VMEM((8, 8, 128), WIDE)
        scratch["norm_column"] = pltpu.VMEM((NZ, 8, 128), WIDE)
        for name, copies in (("sum", Total.COPIES), ("norm", Norm.COPIES)):
            scratch[name + "_send"] = dma((copies,))
            scratch[name + "_recv"] = dma((copies,))
    spaces = dict.fromkeys(("starts", "repeats", "head_bias", "log_temp"), scalars)
    for name in ("all_a", "all_f", "grad_a", "grad_f", "qkv_w", "out_w", "up_w", "down_w"):
        spaces[name] = anywhere
    for name in KEEP + ("x",):
        spaces["keep_" + name] = anywhere
    every = names + list(out_shape) + list(scratch)

    def kernel(*given):
        refs = dict(zip(every, given))
        refs["landing"] = [
            [refs.get("land_%d_%d" % (part, n)) for n in range(len(LANDING))] for part in range(PARTS)
        ]
        train_kernel(refs, alone)

    results = pl.pallas_call(
        kernel,
        name="train_pass",
        out_shape=tuple(jax.ShapeDtypeStruct(*shape) for shape in out_shape.values()),
        in_specs=[spaces.get(name, whole) for name in names],
        out_specs=tuple(spaces.get(name, whole) for name in out_shape),
        scratch_shapes=list(scratch.values()),
        compiler_params=pltpu.CompilerParams(
            vmem_limit_bytes=VMEM_BYTES,
            collective_id=None if alone else 0,
            has_side_effects=not alone,
        ),
        cost_estimate=pl.CostEstimate(
            flops=6 * 10**10, bytes_accessed=4 * 10**7, transcendentals=10**7
        ),
    )(*inputs, *weights)
    return dict(zip(out_shape, results))


def adam_parts(weight, grad, first, second, rate):
    first = BETA_ONE * first + (1.0 - BETA_ONE) * grad
    second = BETA_TWO * second + (1.0 - BETA_TWO) * grad * grad
    fix_one = 1.0 - BETA_ONE**STEP
    fix_two = 1.0 - BETA_TWO**STEP
    fresh = weight - rate * (
        first / fix_one / (jnp.sqrt(second / fix_two) + ADAM_EPS) + DECAY * weight
    )
    return fresh, first, second


def adam_kernel(*refs):
    shard, small_grad, squares, groups, log_temp = refs[:5]
    small, small_first, small_second, bias, bias_first, bias_second = refs[5:11]
    mats, firsts, seconds = refs[11:15], refs[15:19], refs[19:23]
    totals, norm, next_temp, s_next, s_first, s_second, b_next, b_first, b_second = refs[23:32]
    m_next, m_copy, m_first, m_second = refs[32:36], refs[36:40], refs[40:44], refs[44:48]
    l = pl.program_id(0)
    extra = small_grad[NROWS : NROWS + 3, 0:128]
    lane = iota((1, 128), 1)
    bias_mean = jnp.where(lane < A, extra[1:2], 0.0)
    bias_spread = jnp.where(lane < A, extra[2:3], 0.0)

    def all_sum(v):
        return jnp.sum(jnp.sum(v, 0, keepdims=True), 1, keepdims=True)

    grads = small_grad[0:NROWS, :]
    square = (
        all_sum(squares[0:1, :])
        + all_sum(grads * grads)
        + all_sum(bias_mean * bias_mean)
        + all_sum(bias_spread * bias_spread)
    )
    length = jnp.sqrt(square)
    clip = jnp.minimum(1.0, CLIP / (length + 1e-06))

    def rate_of(kind):
        group = jnp.full((1, 1), groups[l, kind], jnp.int32).astype(WIDE)
        return LEARN * jnp.exp2(-group)

    def update(kind, rows, cols, grad):
        at = (0, rows, cols)
        fresh, first, second = adam_parts(
            mats[kind][at], clip * grad, firsts[kind][at], seconds[kind][at], rate_of(kind)
        )
        m_next[kind][at] = fresh
        m_copy[kind][at] = fresh.astype(LOWER)
        m_first[kind][at] = first
        m_second[kind][at] = second

    every = slice(0, 16)
    for j in range(3):
        update(0, every, slice(j * D, (j + 1) * D), shard[0, 16 * j : 16 * j + 16, :])
    update(1, every, slice(0, D), shard[0, 48:64, :])
    for j in range(4):
        update(2, every, slice(j * D, (j + 1) * D), shard[0, 64 + 16 * j : 80 + 16 * j, :])
    update(3, slice(0, 64), slice(0, D), shard[0, 128:192, :])

    @pl.when(l == 0)
    def _():
        s_next[...], s_first[...], s_second[...] = adam_parts(
            small[...], clip * grads, small_first[...], small_second[...], LEARN
        )

        def scalar(v, n):
            return jnp.sum(jnp.where(lane == n, v, 0.0))

        def row(ref):
            v = jnp.zeros((1, 128), WIDE)
            for n in range(2 * A):
                v = jnp.where(lane == n, ref[n], v)
            return v

        grad = bias_mean + pltpu.roll(bias_spread, A, 1)
        results = adam_parts(row(bias), clip * grad, row(bias_first), row(bias_second), LEARN)
        for ref, result in zip((b_next, b_first, b_second), results):
            for n in range(2 * A):
                ref[n] = scalar(result, n)
        sums = extra[0:1]
        for n in range(3):
            totals[n] = scalar(sums, n)
        norm[0] = jnp.sum(length)
        logs = jnp.full((1, 1), log_temp[0], WIDE)
        ratio = jnp.full((1, 1), scalar(sums, 1), WIDE) / jnp.full((1, 1), scalar(sums, 2), WIDE)
        next_temp[0] = jnp.sum(logs - TEMP_RATE * jnp.exp(logs) * (ratio + A))


def adam_all(shard, small_grad, squares, groups, log_temp, smalls, biases, mats, firsts, seconds):
    scalars = pl.BlockSpec(memory_space=pltpu.SMEM)

    def fixed(array):
        return pl.BlockSpec(array.shape, lambda l: (0,) * array.ndim)

    def layer(array):
        return pl.BlockSpec((1,) + array.shape[1:], lambda l: (l, 0, 0))

    def like(array, dtype=WIDE):
        return jax.ShapeDtypeStruct(array.shape, dtype)

    stacks = list(mats) + list(firsts) + list(seconds)
    small, bias = smalls[0], biases[0]
    return pl.pallas_call(
        adam_kernel,
        name="adam",
        grid=(LAYERS,),
        out_shape=(
            (jax.ShapeDtypeStruct((3,), WIDE),)
            + (jax.ShapeDtypeStruct((1,), WIDE),) * 2
            + (like(small),) * 3
            + (like(bias),) * 3
            + tuple(like(m) for m in mats)
            + tuple(like(m, LOWER) for m in mats)
            + tuple(like(m) for m in mats) * 2
        ),
        in_specs=[layer(shard), fixed(small_grad), fixed(squares), scalars, scalars]
        + [fixed(small)] * 3
        + [scalars] * 3
        + [layer(m) for m in stacks],
        out_specs=(scalars,) * 3
        + (fixed(small),) * 3
        + (scalars,) * 3
        + tuple(layer(m) for m in mats) * 4,
        compiler_params=pltpu.CompilerParams(vmem_limit_bytes=VMEM_BYTES),
        cost_estimate=pl.CostEstimate(flops=10**7, bytes_accessed=8 * 10**6, transcendentals=10**6),
    )(shard, small_grad, squares, groups, log_temp, *smalls, *biases, *stacks)


def gather_packed(mats, axes, count):
    group = count // BLOCKS
    pieces = []
    for mat in mats:
        rows, wide = mat.shape[1], mat.shape[2] // D
        piece = mat.astype(LOWER).reshape(LAYERS, rows, wide, D)
        piece = lax.all_gather(piece, axes, axis=1, tiled=True)
        piece = piece.reshape(LAYERS, NZ, NY, NX, NC, group * rows, wide, D)
        piece = piece.transpose(0, 4, 3, 2, 1, 6, 5, 7)
        pieces.append(piece.reshape(LAYERS, 4, 8, wide * group * rows, D))
    return jnp.concatenate(pieces[:2], 3), jnp.concatenate(pieces[2:], 3)


def scatter_packed(grads, mats, axes):
    results, first = [], 0
    for n, mat in enumerate(mats):
        rows, wide = mat.shape[1], mat.shape[2] // D
        total = lax.psum(1, axes) * rows
        deep = total // BLOCKS
        first = 0 if n % 2 == 0 else first
        piece = grads[n // 2][:, :, :, first : first + wide * deep].astype(WIDE)
        first += wide * deep
        piece = piece.reshape(LAYERS, NC, NX, NY, NZ, wide, deep, D)
        piece = piece.transpose(0, 4, 3, 2, 1, 6, 5, 7).reshape(LAYERS, total, wide * D)
        results.append(lax.psum_scatter(piece, axes, scatter_dimension=1, tiled=True))
    return results


def local(
    buf_states,
    buf_actions,
    buf_returns,
    window_starts,
    window_repeats,
    valid_steps,
    matrix_groups,
    log_temp,
    small_rows,
    head_bias,
    qkv_weight,
    out_weight,
    up_weight,
    down_weight,
    small_first,
    bias_first,
    qkv_first,
    out_first,
    up_first,
    down_first,
    small_second,
    bias_second,
    qkv_second,
    out_second,
    up_second,
    down_second,
):
    axes = ("dp", "fsdp")
    mats = (qkv_weight, out_weight, up_weight, down_weight)
    firsts = (qkv_first, out_first, up_first, down_first)
    seconds = (qkv_second, out_second, up_second, down_second)
    pass_inputs = (
        buf_states.T,
        buf_actions.T,
        buf_returns[None],
        window_starts,
        window_repeats,
        valid_steps,
        log_temp,
        small_rows,
        head_bias,
    )
    if FF // down_weight.shape[1] == BLOCKS and lax.psum(1, "fsdp") == NX * NC:
        made = train_pass(pass_inputs, mats, False)
        return adam_all(
            made["shard"],
            made["small_out"],
            made["squares"],
            matrix_groups,
            log_temp,
            (small_rows, small_first, small_second),
            (head_bias, bias_first, bias_second),
            mats,
            firsts,
            seconds,
        )
    packed = gather_packed(mats, axes, FF // down_weight.shape[1])
    made = train_pass(pass_inputs, packed, True)
    big = scatter_packed((made["grad_a"], made["grad_f"]), mats, axes)
    small = made["small_out"]
    small = lax.psum(small, axes)
    small_grad, totals = small[:NROWS], small[NROWS, :3]
    bias_grad = jnp.concatenate([small[NROWS + 1, :A], small[NROWS + 2, :A]])
    square = sum((jnp.sum(piece * piece) for piece in big))
    square = (
        lax.psum(square, axes) + jnp.sum(small_grad * small_grad) + jnp.sum(bias_grad * bias_grad)
    )
    grad_norm = jnp.sqrt(square)
    clip = jnp.minimum(1.0, CLIP / (grad_norm + 1e-06))
    rates = LEARN * jnp.exp2(-matrix_groups.astype(WIDE))
    results = [
        adam_parts(
            mats[kind], clip * big[kind], firsts[kind], seconds[kind], rates[:, kind][:, None, None]
        )
        for kind in range(4)
    ]
    small_new = adam_parts(small_rows, clip * small_grad, small_first, small_second, LEARN)
    bias_new = adam_parts(head_bias, clip * bias_grad, bias_first, bias_second, LEARN)
    next_temp = log_temp - TEMP_RATE * jnp.exp(log_temp) * (totals[1] / totals[2] + A)
    return (
        (totals, grad_norm[None], next_temp)
        + small_new
        + bias_new
        + tuple(r[0] for r in results)
        + tuple(r[0].astype(LOWER) for r in results)
        + tuple(r[1] for r in results)
        + tuple(r[2] for r in results)
    )


def solution(mesh):
    rows = P(("dp", "fsdp"), None)
    vector = P(("dp", "fsdp"))
    stack = P(None, ("dp", "fsdp"), None)
    same = P()
    in_specs = (
        (rows, rows, vector, vector, vector, rows)
        + (same,) * 4
        + (stack,) * 4
        + (same,) * 2
        + (stack,) * 4
        + (same,) * 2
        + (stack,) * 4
    )
    out_specs = (same,) * 9 + (stack,) * 16
    return jax.shard_map(local, mesh=mesh, in_specs=in_specs, out_specs=out_specs, check_vma=False)
```

```python
import math

import jax
import jax.numpy as jnp
from jax import lax
from jax.experimental import pallas as pl
from jax.experimental.pallas import tpu as pltpu
from jax.sharding import PartitionSpec as P

D = 512
H = 8
HD = 64
FF = 2048
S = 11
A = 3
K = 20
STEP = 10

EPS = 1e-05
CLIP = 1.0
LEARN = 0.03
BETA_ONE = 0.5
BETA_TWO = 0.7
DECAY = 0.01
ADAM_EPS = 1e-08
TEMP_RATE = 0.1
MASKED = -1e30
HALF_LOG_TAU = 0.5 * math.log(2.0 * math.pi)
GELU_C = math.sqrt(2.0 / math.pi)
GELU_A = 0.044715
HIGH = lax.Precision.HIGHEST
LOWER = jnp.bfloat16
WIDE = jnp.float32

LAYERS = 3
WINS = 16
BUF_DEV = 64
SLOT = 64
ROWS = WINS * SLOT
CHUNK = 512
CHUNKS = ROWS // CHUNK
BLOCKS = 32
PACK = 192
ATTN, FFN = 64, 128
EMB = S + A + 1 + K + 3
FIN = EMB
HEADW = EMB + 2
BASE = EMB + 2 + 2 * A
PER = 9 + FF // D
NROWS = BASE + LAYERS * PER
SMALL = 96
HEAD_AT = 64
EMB_AT = ROWS - 128
VMEM_BYTES = 64 * 1024 * 1024


def dot(a, b, precision=None):
    return lax.dot_general(
        a, b, (((1,), (0,)), ((), ())), precision=precision, preferred_element_type=WIDE
    )


def dot_nt(a, b, precision=None):
    return lax.dot_general(
        a, b, (((1,), (1,)), ((), ())), precision=precision, preferred_element_type=WIDE
    )


def dot_tn(a, b, precision=None):
    return lax.dot_general(
        a, b, (((0,), (0,)), ((), ())), precision=precision, preferred_element_type=WIDE
    )


def iota(shape, dim):
    return lax.broadcasted_iota(jnp.int32, shape, dim)


def col_sum(v):
    return jnp.sum(v, 0, keepdims=True)


def row_mean(v):
    return jnp.mean(v, -1, keepdims=True)


def norm_parts(x):
    center = x - row_mean(x)
    scale = lax.rsqrt(row_mean(center * center) + EPS)
    return center * scale, scale


def norm_back(xhat, scale, gain, grad):
    scaled = grad * gain
    return scale * (scaled - row_mean(scaled) - xhat * row_mean(scaled * xhat))


def token_rows(at, count):
    row = at + iota((count, 128), 0)
    place = row & (SLOT - 1)
    step = (place * 21846) >> 16
    return row >> 6, step, place - 3 * step, place < 3 * K


def chunk_rows(c):
    return pl.ds(pl.multiple_of(c * CHUNK, CHUNK), CHUNK)


def owner_place(i):
    z, y, x, c = i // 8, (i // 4) % 2, (i // 2) % 2, i % 2
    return 2 * c + x, 4 * y + z


class Kit:
    def __init__(self, **refs):
        self.__dict__.update(refs)

    def row(self, l, k):
        return self.lrows[l, k : k + 1, :]

    def blocks(self, ref, l, first, count, owners):
        places = [owner_place(i) for i in owners]
        return jnp.concatenate([ref[l, a, b, first : first + count, :] for a, b in places], 0)

    def w_qkv(self, l, j):
        return self.blocks(self.wa, l, 16 * j, 16, range(BLOCKS))

    def w_out(self, l):
        return self.blocks(self.wa, l, 48, 16, range(BLOCKS))

    def w_up(self, l, j):
        return self.blocks(self.wf, l, 16 * j, 16, range(BLOCKS))

    def w_down(self, l, j):
        return self.blocks(self.wf, l, 64, 64, range(8 * j, 8 * j + 8))


def slot(l):
    return l % 2


def setup_stage(k):
    k.xs[2, EMB_AT:ROWS, :] = jnp.zeros((128, D), WIDE)
    k.xs[2, EMB_AT : EMB_AT + EMB, :] = k.small[0:EMB, :]
    k.headw[...] = jnp.zeros_like(k.headw)
    k.headw[0, 0:A, :] = k.small[HEADW : HEADW + A, :].astype(LOWER)
    k.headw[1, 0:A, :] = k.small[HEADW + A : HEADW + 2 * A, :].astype(LOWER)
    for l in range(LAYERS):
        k.lrows[l, 0:PER, :] = k.small[BASE + l * PER : BASE + (l + 1) * PER, :]
    k.sgl[...] = jnp.zeros_like(k.sgl)
    k.sgh[...] = jnp.zeros_like(k.sgh)
    k.sgw[...] = jnp.zeros_like(k.sgw)

    lane, sub = iota((WINS, 128), 1), iota((WINS, 128), 0)
    k.meta[...] = jnp.zeros_like(k.meta)
    k.meta[0:WINS, 0:K] = k.valid[...].astype(WIDE)
    meta = k.meta[0:WINS, :]
    for w in range(WINS):
        for n, ref in enumerate((k.starts, k.repeats)):
            meta = jnp.where((sub == w) & (lane == K + n), ref[w].astype(WIDE), meta)
    k.meta[0:WINS, :] = meta
    meta = k.meta[...].astype(LOWER)
    k.buf[...] = jnp.zeros_like(k.buf)
    k.buf[0, 0:S, 0:BUF_DEV] = k.states[...]
    k.buf[0, S + A : S + A + 1, 0:BUF_DEV] = k.returns[...]
    k.buf[1, 0:A, 0:BUF_DEV] = k.actions[...]

    def chunk(c, carry):
        rows = chunk_rows(c)
        win, step, kind, real = token_rows(c * CHUNK, CHUNK)
        lane = iota((CHUNK, 128), 1)
        tok = dot((lane == win).astype(WIDE).astype(LOWER), meta)
        start, repeat = tok[:, K : K + 1], tok[:, K + 1 : K + 2]
        valid = jnp.sum(jnp.where(lane == step, tok, 0.0), -1, keepdims=True)
        key = iota((CHUNK, 128), 0) & (SLOT - 1)
        query = lane & (SLOT - 1)
        allowed = (key <= query) & (((valid > 0.5) & real) | (key == query))
        k.bias[rows, :] = jnp.where(allowed, 0.0, MASKED)
        place = start.astype(jnp.int32) + step
        source = ((lane == place) & real).astype(WIDE)
        raw = dot_nt(source, k.buf[0], HIGH)
        acts = dot_nt(source, k.buf[1], HIGH)
        mine = (
            ((lane < S) & (kind == 1))
            | ((lane >= S) & (lane < S + A) & (kind == 2))
            | ((lane == S + A) & (kind == 0))
        )
        raw = raw + pltpu.roll(acts, S, 1)
        marks = ((lane == S + A + 1 + step) | (lane == S + A + 1 + K + kind)) & real
        feats = jnp.where(mine, raw, 0.0) + marks.astype(WIDE)
        weight = jnp.where((kind == 1) & real, repeat * valid, 0.0)
        acts = pltpu.roll(acts, HEAD_AT, 1)
        ours = (lane >= HEAD_AT) & (lane < HEAD_AT + A)
        feats = jnp.where(ours, acts, jnp.where(lane == HEAD_AT + A, weight, feats))
        k.feats[rows, :] = feats
        k.xs[0, rows, :] = dot(feats, k.xs[2, EMB_AT:ROWS, :], HIGH)
        return carry

    lax.fori_loop(0, CHUNKS, chunk, 0)


def stack_pair(v, first):
    zero = jnp.zeros_like(v)
    return jnp.concatenate([jnp.where(first, v, zero), jnp.where(first, zero, v)], 0)


def join_pair(v, first):
    return jnp.where(first, v[:SLOT], v[SLOT:])


def window_rows(w):
    return pl.ds(pl.multiple_of(w * SLOT, SLOT), SLOT)


def each_chunk(body, between=None):
    def step(c, carry):
        body(c, chunk_rows(c))
        if between is not None:

            @pl.when(c < CHUNKS - 1)
            def _():
                between()

        return carry

    lax.fori_loop(0, CHUNKS, step, 0)


def each_window(body, after=None, between=None):
    def pair(n, carry):
        body(2 * n)
        body(2 * n + 1)
        if between is not None:

            @pl.when(n == WINS // 4 - 1)
            def _():
                between()

        if after is not None:
            after(pl.ds(pl.multiple_of(n * 128, 128), 128))
        return carry

    lax.fori_loop(0, WINS // 2, pair, 0)


def forward_qkv(k, l, between):
    def chunk(c, rows):
        xhat, _ = norm_parts(k.xs[slot(l), rows, :])
        normed = (xhat * k.row(l, 0) + k.row(l, 1)).astype(LOWER)
        k.normed_t[:, rows] = normed.T
        for j in range(3):
            part = dot(normed, k.w_qkv(l, j)) + k.row(l, 4 + j)
            k.qkv[rows, j * D : (j + 1) * D] = part.astype(LOWER)

    each_chunk(chunk, between)


def forward_windows(k, l, between):
    first = iota((SLOT, 128), 1) < HD

    def window(w):
        rows = window_rows(w)
        bias = k.bias[rows, :]
        pairs = [slice(p * 128, (p + 1) * 128) for p in range(H // 2)]

        def qkv(n, at):
            return k.qkv[rows, n * D + at.start : n * D + at.stop]

        scale = jnp.asarray(HD**-0.5, LOWER)
        scores = [dot_nt(qkv(1, at), stack_pair(qkv(0, at) * scale, first)) + bias for at in pairs]
        peaks = [jnp.max(s, 0, keepdims=True) for s in scores]
        expos = [jnp.exp(s - peak) for s, peak in zip(scores, peaks)]
        totals = [jnp.sum(e, 0, keepdims=True) for e in expos]
        probs = [(e * (1.0 / total)).astype(LOWER) for e, total in zip(expos, totals)]
        outs = [dot_tn(p, qkv(2, at)) for p, at in zip(probs, pairs)]
        for p, at in enumerate(pairs):
            k.logs[l, w, p : p + 1, :] = peaks[p] + jnp.log(totals[p])
            k.left[rows, at] = join_pair(outs[p], first).astype(LOWER)

    def turn(rows):
        k.mixed_t[:, rows] = k.left[rows, :].T

    each_window(window, turn, between)


def forward_up(k, l, between):
    def chunk(c, rows):
        mid = k.xs[slot(l), rows, :] + dot(k.left[rows, :], k.w_out(l)) + k.row(l, 7)
        k.mid[rows, :] = mid
        xhat, _ = norm_parts(mid)
        second = (xhat * k.row(l, 2) + k.row(l, 3)).astype(LOWER)
        k.second_t[:, rows] = second.T
        for j in range(4):
            cols = slice(j * D, (j + 1) * D)
            h = dot(second, k.w_up(l, j)) + k.row(l, 8 + j)
            square = h * h
            over = 1.0 + jnp.tanh(h * (GELU_C + GELU_C * GELU_A * square))
            half = 0.5 * h
            acted = (half * over).astype(LOWER)
            slope = over * (0.5 + half * (2.0 - over) * (GELU_C + 3.0 * GELU_A * GELU_C * square))
            k.work[rows, cols] = acted
            k.slope[rows, cols] = slope.astype(LOWER)
            k.act_t[cols, rows] = acted.T

    each_chunk(chunk, between)


def forward_down(k, l, dest):
    def chunk(c, rows):
        w_down = jnp.concatenate([k.w_down(l, j) for j in range(4)], 0)
        k.xs[dest, rows, :] = k.mid[rows, :] + k.row(l, 12) + dot(k.work[rows, :], w_down)

    each_chunk(chunk)


def head_stage(k, at):
    gain, bias = k.small[FIN : FIN + 1, :], k.small[FIN + 1 : FIN + 2, :]
    lane = iota((CHUNK, 128), 1)
    keep = lane < A

    def bias_row(first):
        row = jnp.zeros((1, 128), WIDE)
        at = iota((1, 128), 1)
        for a in range(A):
            row = jnp.where(at == a, k.head_bias[first + a], row)
        return row

    bias_mean, bias_spread = bias_row(0), bias_row(A)
    temp = jnp.exp(jnp.full((1, 128), k.log_temp[0], WIDE))

    def chunk(c, carry):
        rows = chunk_rows(c)
        xhat, scale = norm_parts(k.xs[at, rows, :])
        feats = (xhat * gain + bias).astype(LOWER)
        mean = dot_nt(feats, k.headw[0]) + bias_mean
        spread = jnp.tanh(dot_nt(feats, k.headw[1]) + bias_spread)
        acts = pltpu.roll(k.feats[rows, :], 128 - HEAD_AT, 1)
        weight = acts[:, A : A + 1]
        acts = jnp.where(keep, acts, 0.0)
        target = 0.5 * (jnp.log(1.0 + acts) - jnp.log(1.0 - acts))
        shrink = jnp.exp(-spread)
        zed = (target - mean) * shrink
        terms = 0.5 * zed * zed + spread + HALF_LOG_TAU + jnp.log(1.0 - acts * acts)
        nll = jnp.sum(jnp.where(keep, terms, 0.0), -1, keepdims=True)
        entropy = jnp.sum(jnp.where(keep, spread, 0.0), -1, keepdims=True) + A * (0.5 + HALF_LOG_TAU)
        loss = weight * (nll - temp * entropy)
        sums = jnp.where(lane == 0, loss, jnp.where(lane == 1, weight * entropy, jnp.where(lane == 2, weight, 0.0)))
        d_mean = jnp.where(keep, weight * (-zed * shrink), 0.0).astype(LOWER)
        d_spread = weight * (1.0 - zed * zed - temp) * (1.0 - spread * spread)
        d_spread = jnp.where(keep, d_spread, 0.0).astype(LOWER)
        k.sgh[2:3, 0:128] += col_sum(sums)
        k.sgh[3:4, 0:128] += col_sum(d_mean.astype(WIDE))
        k.sgh[4:5, 0:128] += col_sum(d_spread.astype(WIDE))
        k.sgw[0] += dot_tn(d_mean, feats)[0:8]
        k.sgw[1] += dot_tn(d_spread, feats)[0:8]
        d_feats = dot(d_mean, k.headw[0]) + dot(d_spread, k.headw[1])
        k.sgh[0:1, :] += col_sum(d_feats * xhat)
        k.sgh[1:2, :] += col_sum(d_feats)
        k.xs[at, rows, :] = norm_back(xhat, scale, gain, d_feats)
        return carry

    lax.fori_loop(0, CHUNKS, chunk, 0)


def store_blocks(ref, l, owners, first, count, value):
    value = value.astype(LOWER)
    for n, i in enumerate(owners):
        a, b = owner_place(i)
        ref[l, a, b, first : first + count, :] = value[n * count : (n + 1) * count]


def backward_ffn(k, l, grad, between=None):
    def chunk(c, rows):
        d_down = k.xs[grad, rows, :].astype(LOWER)
        k.dout[rows, :] = d_down
        k.sgl[l, 12:13, :] += col_sum(d_down.astype(WIDE))
        d_second = jnp.zeros((CHUNK, D), WIDE)
        for j in range(4):
            cols = slice(j * D, (j + 1) * D)
            d_acted = dot_nt(d_down, k.w_down(l, j))
            d_hidden = (d_acted * k.slope[rows, cols].astype(WIDE)).astype(LOWER)
            k.work[rows, cols] = d_hidden
            k.sgl[l, 8 + j : 9 + j, :] += col_sum(d_hidden.astype(WIDE))
            d_second = d_second + dot_nt(d_hidden, k.w_up(l, j))
        xhat, scale = norm_parts(k.mid[rows, :])
        k.sgl[l, 2:3, :] += col_sum(d_second * xhat)
        k.sgl[l, 3:4, :] += col_sum(d_second)
        k.xs[grad, rows, :] += norm_back(xhat, scale, k.row(l, 2), d_second)

    each_chunk(chunk, between)


def backward_down_grads(k, l):
    for j in range(4):
        part = dot(k.act_t[j * D : (j + 1) * D, :], k.dout[...])
        store_blocks(k.wf, l, range(8 * j, 8 * j + 8), 64, 64, part)


def backward_up_grads(k, l):
    for j in range(4):
        part = dot(k.second_t[...], k.work[:, j * D : (j + 1) * D])
        store_blocks(k.wf, l, range(BLOCKS), 16 * j, 16, part)


def backward_out(k, l, grad):
    def before(c, rows):
        d_branch = k.xs[grad, rows, :].astype(LOWER)
        k.left[rows, :] = d_branch
        k.sgl[l, 7:8, :] += col_sum(d_branch.astype(WIDE))
        k.dout[rows, :] = dot_nt(d_branch, k.w_out(l)).astype(LOWER)

    each_chunk(before)
    store_blocks(k.wa, l + 1, range(BLOCKS), 48, 16, dot(k.mixed_t[...], k.left[...]))


def backward_windows(k, l, between):
    first = iota((SLOT, 128), 1) < HD
    scale = HD**-0.5

    def window(w):
        rows = window_rows(w)
        bias = k.bias[rows, :]
        pairs = [slice(p * 128, (p + 1) * 128) for p in range(H // 2)]

        def qkv(n, at):
            return k.qkv[rows, n * D + at.start : n * D + at.stop]

        low = jnp.asarray(scale, LOWER)
        query = [stack_pair(qkv(0, at) * low, first) for at in pairs]
        d_mixed = [stack_pair(k.dout[rows, at], first) for at in pairs]
        scores = [dot_nt(qkv(1, at), q) + bias for at, q in zip(pairs, query)]
        d_probs = [dot_nt(qkv(2, at), d) for at, d in zip(pairs, d_mixed)]
        probs = [jnp.exp(s - k.logs[l, w, p : p + 1, :]) for p, s in enumerate(scores)]
        d_values = [dot(p.astype(LOWER), d) for p, d in zip(probs, d_mixed)]
        inner = [p * d for p, d in zip(probs, d_probs)]
        sums = [jnp.sum(i, 0, keepdims=True) for i in inner]
        d_scores = [(i - p * t).astype(LOWER) for i, p, t in zip(inner, probs, sums)]
        d_keyed = [dot(d, q) for d, q in zip(d_scores, query)]
        d_query = [dot_tn(d, qkv(1, at)) for d, at in zip(d_scores, pairs)]
        for p, at in enumerate(pairs):
            values = (join_pair(d_query[p], first) * scale, d_keyed[p], d_values[p])
            for n, value in enumerate(values):
                k.work[rows, n * D + at.start : n * D + at.stop] = value.astype(LOWER)

    each_window(window, None, between)


def backward_attn_grads(k, l):
    for j in range(3):
        part = dot(k.normed_t[...], k.work[:, j * D : (j + 1) * D])
        store_blocks(k.wa, l + 1, range(BLOCKS), 16 * j, 16, part)


def backward_input(k, l, grad):
    def chunk(c, rows):
        d_normed = jnp.zeros((CHUNK, D), WIDE)
        for j in range(3):
            d_part = k.work[rows, j * D : (j + 1) * D]
            k.sgl[l, 4 + j : 5 + j, :] += col_sum(d_part.astype(WIDE))
            d_normed = d_normed + dot_nt(d_part, k.w_qkv(l, j))
        xhat, scale = norm_parts(k.xs[slot(l), rows, :])
        k.sgl[l, 0:1, :] += col_sum(d_normed * xhat)
        k.sgl[l, 1:2, :] += col_sum(d_normed)
        k.xs[grad, rows, :] += norm_back(xhat, scale, k.row(l, 0), d_normed)

    each_chunk(chunk)


def small_stage(k, out, grad):
    out[...] = jnp.zeros_like(out)
    out[0:EMB, :] = dot_tn(k.feats[...], k.xs[grad], HIGH)[0:EMB]
    out[FIN : FIN + 2, :] = k.sgh[0:2, :]
    out[HEADW : HEADW + A, :] = k.sgw[0, 0:A, :]
    out[HEADW + A : HEADW + 2 * A, :] = k.sgw[1, 0:A, :]
    for l in range(LAYERS):
        out[BASE + l * PER : BASE + (l + 1) * PER, :] = k.sgl[l, 0:PER, :]
    out[NROWS : NROWS + 3, :] = k.sgh[2:5, :]


WORK_SHAPES = dict(
    wa=((LAYERS + 1, 4, 8, ATTN, D), LOWER),
    wf=((LAYERS, 4, 8, FFN, D), LOWER),
    xs=((3, ROWS, D), WIDE),
    qkv=((ROWS, 3 * D), LOWER),
    normed_t=((D, ROWS), LOWER),
    mixed_t=((D, ROWS), LOWER),
    slope=((ROWS, FF), LOWER),
    act_t=((FF, ROWS), LOWER),
    second_t=((D, ROWS), LOWER),
    mid=((ROWS, D), WIDE),
    logs=((LAYERS, WINS, 8, 128), WIDE),
    work=((ROWS, FF), LOWER),
    left=((ROWS, D), LOWER),
    dout=((ROWS, D), LOWER),
    feats=((ROWS, 128), WIDE),
    bias=((ROWS, 128), WIDE),
    headw=((2, 128, D), LOWER),
    lrows=((LAYERS, 16, D), WIDE),
    sgl=((LAYERS, 16, D), WIDE),
    sgh=((8, D), WIDE),
    sgw=((2, 8, D), WIDE),
    meta=((128, 128), WIDE),
    buf=((2, 128, 128), WIDE),
)
KEEP_ATTN = ("qkv", "normed_t", "mixed_t")
KEEP_FFN = ("slope", "act_t", "second_t", "mid")
KEEP = KEEP_ATTN + KEEP_FFN


MESH = pl.DeviceIdType.MESH
NZ, NY, NX, NC = 4, 2, 2, 2
NR = NY * NX * NC
SHARD = PACK
PARTS, DEEP = 3, 64
HALF = DEEP // 2


class Place:
    def __init__(self):
        dp, fsdp = lax.axis_index("dp"), lax.axis_index("fsdp")
        self.z, self.y = dp // NY, dp % NY
        self.x, self.c = fsdp // NC, fsdp % NC
        self.a, self.b = 2 * self.c + self.x, 4 * self.y + self.z
        self.r = 4 * self.y + fsdp
        self.to_z = [(((self.z + d) % NZ) * NY + self.y, fsdp) for d in range(1, NZ)]
        self.odd = self.z % 2
        self.to_pair = ((self.z + 1 - 2 * self.odd) * NY + self.y, fsdp)
        self.plane = []
        for d in range(1, 8):
            y, x, c = [
                1 - v if d & bit else v for v, bit in ((self.y, 4), (self.x, 2), (self.c, 1))
            ]
            self.plane.append((self.z * NY + y, x * NC + c))
        self.to_c, self.to_x, self.to_y = self.plane[0], self.plane[1], self.plane[3]

    def barrier(self):
        sem = pltpu.get_barrier_semaphore()
        for partner in self.plane + self.to_z:
            pl.semaphore_signal(sem, inc=1, device_id=partner, device_id_type=MESH)
        pl.semaphore_wait(sem, len(self.plane) + len(self.to_z))


def remote(src, dst, send, recv, to):
    return pltpu.make_async_remote_copy(
        src_ref=src, dst_ref=dst, send_sem=send, recv_sem=recv, device_id=to, device_id_type=MESH
    )


def part_ref(weights, part):
    return weights[min(part, 1)], (0, 0, DEEP)[part]


class Gather:
    COPIES = 13

    def __init__(self, place, weights, send, recv):
        self.at, self.weights, self.send, self.recv = place, weights, send, recv

    def copy(self, l, part, n):
        at = self.at
        array, row = part_ref(self.weights, part)
        a, b, rows, to = at.a, pl.ds(4 * at.y, 4), pl.ds(row, DEEP), at.to_c
        if n < 3:
            b, to = at.b, at.to_z[n]
        elif n < 5:
            to = (at.to_x, at.to_y)[n - 3]
        if n in (6, 8, 10, 11, 12):
            a = 2 * at.c + 1 - at.x
        if n in (7, 9, 10, 11, 12):
            b = pl.ds(4 * (1 - at.y), 4)
        if n in (6, 7):
            first = row + at.odd * HALF + (n - 6) * (HALF // 2)
            rows = pl.ds(pl.multiple_of(first, HALF // 2), HALF // 2)
            to = (at.to_y, at.to_x)[n - 6]
        if n in (10, 11):
            rows = pl.ds(pl.multiple_of(row + at.odd * HALF, HALF), HALF)
        if n == 11:
            to = at.to_pair
        if n == 12:
            rows = pl.ds(pl.multiple_of(row + (1 - at.odd) * HALF, HALF), HALF)
        ref = array.at[l, a, b, rows, :]
        q = PARTS * l + part
        return remote(ref, ref, self.send.at[q, n], self.recv.at[q, n], to)

    def start(self, l, part, *ns):
        for n in ns:
            self.copy(l, part, n).start()

    def wait(self, l, part, *ns):
        for n in ns:
            self.copy(l, part, n).wait_recv()

    def first(self, l, part):
        self.start(l, part, 0, 1, 2)

    def second(self, l, part):
        self.wait(l, part, 0, 1, 2)
        self.start(l, part, 3, 4, 5)

    def third(self, l, part):
        self.wait(l, part, 3)
        self.start(l, part, 6, 8)
        self.wait(l, part, 4)
        self.start(l, part, 7, 9)

    def fourth(self, l, part):
        self.wait(l, part, 6, 7)
        self.start(l, part, 11, 10)

    def fifth(self, l, part):
        self.wait(l, part, 11)
        self.start(l, part, 12)

    def last(self, l, part):
        self.wait(l, part, 5, 8, 9, 10, 12)

    def sent(self, l, part):
        for n in range(self.COPIES):
            self.copy(l, part, n).wait_send()


class Reduce:
    COPIES = 8

    def __init__(self, place, grads, landing, send, recv, credit):
        self.at, self.grads, self.landing = place, grads, landing
        self.send, self.recv, self.credit = send, recv, credit

    def refs(self, l, part):
        array, row = part_ref(self.grads, part)
        grads = array.at[l + 1 - min(part, 1), :, :, pl.ds(row, DEEP), :]
        return (grads, *self.landing[part])

    def copy(self, l, part, n):
        at, half = self.at, HALF
        g, r0, r1a, r1b, r2, r3 = self.refs(l, part)
        top, low, other = pl.ds(0, half), pl.ds(half, half), pl.ds(4 * (1 - at.y), 4)
        if n == 0:
            src, dst, to = g.at[pl.ds(2 * (1 - at.c), 2)], r0, at.to_c
        elif n == 1:
            src, dst, to = r0.at[1 - at.x, :, top, :], r1a, at.to_x
        elif n == 2:
            src, dst, to = r0.at[:, other, low, :], r1b, at.to_y
        elif n == 3:
            src, dst, to = r1a.at[other], r2.at[:, top, :], at.to_y
        elif n == 4:
            src, dst, to = r1b.at[1 - at.x], r2.at[:, low, :], at.to_x
        else:
            src, dst, to = r2.at[(at.z + n - 4) % NZ], r3.at[n - 5], at.to_z[n - 5]
        q = PARTS * l + part
        return remote(src, dst, self.send.at[q, n], self.recv.at[q, n], to)

    def may_send(self, l, part, *partners):
        @pl.when(l < LAYERS - 1)
        def _():
            for n in partners:
                pl.semaphore_wait(self.credit.at[part, n], 1)

    def allow(self, l, part, *credits):
        at = self.at

        @pl.when(l > 0)
        def _():
            for n, to in credits:
                pl.semaphore_signal(
                    self.credit.at[part, n], inc=1, device_id=to, device_id_type=MESH
                )

    def start(self, l, part):
        self.may_send(l, part, 0)
        self.copy(l, part, 0).start()

    def first(self, l, part):
        at, half = self.at, HALF
        g, r0, _, _, _, _ = self.refs(l, part)
        top, low = pl.ds(0, half), pl.ds(half, half)
        self.copy(l, part, 0).wait_recv()

        def along_x(n, carry):
            x = 1 - at.x
            total = g[2 * at.c + x, n, top].astype(WIDE) + r0[x, n, top].astype(WIDE)
            r0[x, n, top] = total.astype(LOWER)
            return carry

        def along_y(n, carry):
            x, b = n // 4, 4 * (1 - at.y) + n % 4
            total = g[2 * at.c + x, b, low].astype(WIDE) + r0[x, b, low].astype(WIDE)
            r0[x, b, low] = total.astype(LOWER)
            return carry

        lax.fori_loop(0, 8, along_x, 0)
        self.may_send(l, part, 1, 2)
        self.copy(l, part, 1).start()
        lax.fori_loop(0, 8, along_y, 0)
        self.copy(l, part, 2).start()

    def second(self, l, part):
        at, half = self.at, HALF
        g, r0, r1a, r1b, _, _ = self.refs(l, part)
        top, low = pl.ds(0, half), pl.ds(half, half)

        def along_y(n, carry):
            b = 4 * (1 - at.y) + n
            total = g[at.a, b, top].astype(WIDE) + r0[at.x, b, top].astype(WIDE)
            r1a[b] = (total + r1a[b].astype(WIDE)).astype(LOWER)
            return carry

        def along_x(n, carry):
            x, b = 1 - at.x, 4 * at.y + n
            total = g[2 * at.c + x, b, low].astype(WIDE) + r0[x, b, low].astype(WIDE)
            r1b[x, n] = (total + r1b[x, n].astype(WIDE)).astype(LOWER)
            return carry

        self.copy(l, part, 1).wait_recv()
        lax.fori_loop(0, NZ, along_y, 0)
        self.may_send(l, part, 6, 7)
        self.copy(l, part, 3).start()
        self.copy(l, part, 2).wait_recv()
        lax.fori_loop(0, NZ, along_x, 0)
        self.copy(l, part, 4).start()

    def chip_sums(self, l, part, z):
        at, half = self.at, HALF
        g, r0, r1a, r1b, r2, _ = self.refs(l, part)
        top, low, b = pl.ds(0, half), pl.ds(half, half), 4 * at.y + z
        upper = g[at.a, b, top].astype(WIDE) + r0[at.x, b, top].astype(WIDE)
        lower = g[at.a, b, low].astype(WIDE) + r0[at.x, b, low].astype(WIDE)
        return (
            upper + r1a[b].astype(WIDE) + r2[z, top].astype(WIDE),
            lower + r1b[at.x, z].astype(WIDE) + r2[z, low].astype(WIDE),
        )

    def third(self, l, part, out):
        at, half, row = self.at, HALF, DEEP * part
        r2 = self.landing[part][3]
        for n in (3, 4):
            self.copy(l, part, n).wait_recv()
        self.may_send(l, part, 3, 4, 5)
        for n in range(3):
            z = (at.z + n + 1) % NZ
            upper, lower = self.chip_sums(l, part, z)
            r2[z, pl.ds(0, half)] = upper.astype(LOWER)
            r2[z, pl.ds(half, half)] = lower.astype(LOWER)
            self.copy(l, part, 5 + n).start()
        upper, lower = self.chip_sums(l, part, at.z)
        out[l, row : row + half, :] = upper
        out[l, row + half : row + 2 * half, :] = lower
        for n in range(5):
            self.copy(l, part, n).wait_send()
        self.allow(l, part, (0, at.to_c), (1, at.to_x), (2, at.to_y))

    def last(self, l, part, out, squares):
        at, row = self.at, DEEP * part
        r3 = self.landing[part][4]
        rows = slice(row, row + DEEP)
        total = out[l, rows, :]
        for n in range(3):
            self.copy(l, part, 5 + n).wait_recv()
            total = total + r3[n].astype(WIDE)
        out[l, rows, :] = total
        squares[0:1, :] += col_sum(total * total)
        for n in range(5, self.COPIES):
            self.copy(l, part, n).wait_send()
        late = [(6, at.to_x), (7, at.to_y)] + [(5 - n, at.to_z[n]) for n in range(3)]
        self.allow(l, part, *late)


class Total:
    COPIES = 7

    def __init__(self, place, ref, rows, send, recv):
        self.at, self.ref, self.rows = place, ref, rows // 2
        self.send, self.recv = send, recv

    def half(self, n):
        return self.ref.at[pl.ds(pl.multiple_of(n * self.rows, 8), self.rows), :]

    def whole(self):
        return self.ref.at[pl.ds(0, 2 * self.rows), :]

    def copy(self, n):
        at = self.at
        mine, other = self.half(at.c), self.half(1 - at.c)
        src, dst, to = (
            (other, self.half(2), at.to_c),
            (self.half(8), self.half(3), at.to_x),
            (self.half(9), self.half(4), at.to_y),
            (self.half(10), self.half(5), at.to_z[0]),
            (self.half(10), self.half(6), at.to_z[1]),
            (self.half(10), self.half(7), at.to_z[2]),
            (mine, self.half(11), at.to_c),
        )[n]
        return remote(src, dst, self.send.at[n], self.recv.at[n], to)

    def start(self):
        self.copy(0).start()

    def step(self, n):
        self.copy(n).wait_recv()
        own = self.half(self.at.c) if n == 0 else self.half(7 + n)
        self.half(8 + n)[...] = own[...] + self.half(2 + n)[...]
        for m in ((1,), (2,), (3, 4, 5))[n]:
            self.copy(m).start()

    def back(self):
        for m in (3, 4, 5):
            self.copy(m).wait_recv()
        self.copy(0).wait_send()
        total = None
        for z in range(NZ):
            term = self.half(10)[...]
            for n in range(3):
                from_z = (self.at.z + NZ - 1 - n) % NZ
                term = jnp.where(from_z == z, self.half(5 + n)[...], term)
            total = term if total is None else total + term
        self.half(self.at.c)[...] = total
        self.copy(6).start()

    def last(self):
        self.copy(6).wait_recv()
        self.half(1 - self.at.c)[...] = self.half(11)[...]
        for n in range(1, self.COPIES):
            self.copy(n).wait_send()


class Norm:
    COPIES = 10

    def __init__(self, place, plane, column, send, recv):
        self.at, self.plane, self.column = place, plane, column
        self.send, self.recv = send, recv

    def copy(self, n):
        at = self.at
        if n < 7:
            ref, to = self.plane.at[at.r], at.plane[n]
        else:
            ref, to = self.column.at[at.z], at.to_z[n - 7]
        return remote(ref, ref, self.send.at[n], self.recv.at[n], to)

    def start(self, tile):
        self.plane[self.at.r] = tile
        for n in range(7):
            self.copy(n).start()

    def total(self, ref, ns):
        for n in ns:
            self.copy(n).wait_recv()
        total = ref[0]
        for n in range(1, ref.shape[0]):
            total = total + ref[n]
        return total

    def step(self):
        self.column[self.at.z] = self.total(self.plane, range(7))
        for n in range(7, self.COPIES):
            self.copy(n).start()

    def last(self):
        total = self.total(self.column, range(7, self.COPIES))
        for n in range(self.COPIES):
            self.copy(n).wait_send()
        return total


LANDING = (
    (NX, 8, DEEP, D),
    (8, HALF, D),
    (NX, NZ, HALF, D),
    (NZ, DEEP, D),
    (3, DEEP, D),
)


def stage_rows(qkv, out, up, down, l):
    return (
        [(qkv.at[l, :, pl.ds(j * D, D)], 16 * j, 16) for j in range(3)]
        + [(out.at[l], 48, 16)]
        + [(up.at[l, :, pl.ds(j * D, D)], 64 + 16 * j, 16) for j in range(4)]
        + [(down.at[l], 128, 64)]
    )


BEGIN, SETUP, START, QKV_HALF, QKV, WINDOWS_HALF, WINDOWS, UP_HALF, UP, DOWN = range(10)
FIRST, SECOND, THIRD, FOURTH, FIFTH, LAST, SEND = range(7)
GATHER_PLAN = {
    (-1, BEGIN): [(FIRST, 0, 0), (FIRST, 0, 1), (FIRST, 0, 2)],
    (-1, SETUP): [(FIRST, 1, 0), (FIRST, 1, 1), (SECOND, 0, 0)],
    (0, START): [(FIRST, 1, 2), (SECOND, 0, 1), (THIRD, 0, 0), (FOURTH, 0, 0), (SECOND, 0, 2), (THIRD, 0, 1), (FIFTH, 0, 0), (LAST, 0, 0), (SECOND, 1, 0), (FOURTH, 0, 1)],
    (0, QKV): [(FIRST, 2, 0), (THIRD, 0, 2), (FIFTH, 0, 1)],
    (0, WINDOWS_HALF): [(SECOND, 1, 1), (LAST, 0, 1)],
    (0, WINDOWS): [(FIRST, 2, 1), (FOURTH, 0, 2)],
    (0, UP_HALF): [(THIRD, 1, 0), (FIFTH, 0, 2), (SECOND, 1, 2)],
    (0, UP): [(FIRST, 2, 2), (LAST, 0, 2), (FOURTH, 1, 0), (SECOND, 2, 0)],
    (0, DOWN): [(THIRD, 1, 1), (FIFTH, 1, 0)],
    (1, START): [(LAST, 1, 0), (FOURTH, 1, 1)],
    (1, QKV_HALF): [(SECOND, 2, 1)],
    (1, QKV): [(THIRD, 1, 2), (FIFTH, 1, 1)],
    (1, WINDOWS_HALF): [(LAST, 1, 1)],
    (1, WINDOWS): [(SECOND, 2, 2), (FOURTH, 1, 2)],
    (1, UP_HALF): [(THIRD, 2, 0), (FIFTH, 1, 2), (LAST, 1, 2)],
    (1, UP): [(FOURTH, 2, 0)],
    (1, DOWN): [(THIRD, 2, 1), (FIFTH, 2, 0)],
    (2, START): [(LAST, 2, 0), (FOURTH, 2, 1)],
    (2, QKV): [(THIRD, 2, 2), (FIFTH, 2, 1)],
    (2, WINDOWS_HALF): [(LAST, 2, 1)],
    (2, WINDOWS): [(FOURTH, 2, 2)],
    (2, UP_HALF): [(FIFTH, 2, 2), (LAST, 2, 2)],
}


def train_kernel(refs, alone):
    k = Kit(**refs)

    def kept(names, l, back):
        copies = []
        for name in names:
            here, there = refs[name], refs["keep_" + name].at[l]
            src, dst = (there, here) if back else (here, there)
            copies.append(pltpu.make_async_copy(src, dst, k.keep_sem.at[KEEP.index(name)]))
        return copies

    def start(copies):
        for copy in copies:
            copy.start()

    def wait(copies):
        for copy in copies:
            copy.wait()

    def kept_x(back):
        here, there = k.xs.at[0], k.keep_x
        src, dst = (there, here) if back else (here, there)
        return [pltpu.make_async_copy(src, dst, k.keep_sem.at[len(KEEP)])]

    arrays = [(l, n) for l in range(LAYERS) for n in (0, 1)]
    parts = [(l, part) for l in range(LAYERS) for part in range(PARTS)]
    weights = (k.wa, k.wf)
    if alone:
        loads = [
            pltpu.make_async_copy((k.all_a, k.all_f)[n].at[l], weights[n].at[l], k.load_sem.at[2 * l + n])
            for l, n in arrays
        ]
        stores = [
            pltpu.make_async_copy(
                weights[n].at[l + 1 - n], (k.grad_a, k.grad_f)[n].at[l], k.load_sem.at[2 * l + n]
            )
            for l, n in arrays
        ]
        start(loads)
    else:
        place = Place()
        gather = Gather(place, weights, k.gather_send, k.gather_recv)
        reduce = Reduce(
            place, weights, k.landing, k.reduce_send, k.reduce_recv, k.credit
        )
        sums = Total(place, k.mid, SMALL, k.sum_send, k.sum_recv)
        norm = Norm(place, k.norm_plane, k.norm_column, k.norm_send, k.norm_recv)

    def run(plan):
        stages = (
            gather.first,
            gather.second,
            gather.third,
            gather.fourth,
            gather.fifth,
            gather.last,
        )
        for stage, l, part in plan:
            stages[stage](l, part)

    def poll(l, point):
        if alone:
            return
        for layer in range(LAYERS):
            plan = GATHER_PLAN.get((layer, point))
            if plan:

                @pl.when(l == layer)
                def _(plan=plan):
                    run(plan)

    if not alone:
        staged = []
        for l in range(LAYERS):
            for n, (src, row, count) in enumerate(stage_rows(k.qkv_w, k.out_w, k.up_w, k.down_w, l)):
                dst = k.xs.at[2, pl.ds(l * PACK + row, count), :]
                staged.append(pltpu.make_async_copy(src, dst, k.stage_sem.at[l, n]))
        start(staged)
        place.barrier()
        for l in range(LAYERS):
            wait(staged[9 * l : 9 * l + 9])
            row = l * PACK
            for part in range(PARTS):
                array, first = part_ref(weights, part)
                mine = k.xs[2, row + DEEP * part : row + DEEP * (part + 1), :].astype(LOWER)
                array[l, place.a, place.b, first : first + DEEP, :] = mine
                if (FIRST, l, part) in GATHER_PLAN[-1, BEGIN]:
                    gather.first(l, part)
        k.squares_sum[...] = jnp.zeros_like(k.squares_sum)

    setup_stage(k)
    start(kept_x(False))
    if not alone:
        run(GATHER_PLAN[-1, SETUP])

    def forward(l, carry):
        if alone:
            pltpu.make_async_copy(k.all_a.at[l], k.wa.at[l], k.load_sem.at[2 * l]).wait()

        @pl.when(l > 0)
        def _():
            wait(kept(KEEP_ATTN, l - 1, False))

        poll(l, START)
        forward_qkv(k, l, lambda: poll(l, QKV_HALF))
        poll(l, QKV)
        forward_windows(k, l, lambda: poll(l, WINDOWS_HALF))

        @pl.when(l < LAYERS - 1)
        def _():
            start(kept(KEEP_ATTN, l, False))

        @pl.when(l > 0)
        def _():
            wait(kept(KEEP_FFN, l - 1, False))

        @pl.when(l == 1)
        def _():
            wait(kept_x(False))

        if alone:
            pltpu.make_async_copy(k.all_f.at[l], k.wf.at[l], k.load_sem.at[2 * l + 1]).wait()
        poll(l, WINDOWS)
        forward_up(k, l, lambda: poll(l, UP_HALF))
        poll(l, UP)
        forward_down(k, l, (l + 1) % 2 + l // 2)

        @pl.when(l < LAYERS - 1)
        def _():
            start(kept(KEEP_FFN, l, False))

        poll(l, DOWN)
        return carry

    lax.fori_loop(0, LAYERS, forward, 0)
    if not alone:
        for l, part in parts:
            gather.sent(l, part)
    grad = 2
    head_stage(k, grad)

    def run_reduce(stage, l, part):
        if stage == THIRD:
            reduce.third(l, part, k.shard)
        elif stage == LAST:
            reduce.last(l, part, k.shard, k.squares_sum)
        else:
            {SEND: reduce.start, FIRST: reduce.first, SECOND: reduce.second}[stage](l, part)

    def backward(n, carry):
        l = LAYERS - 1 - n

        def behind(name, *stages):
            @pl.when(n > 0)
            def _():
                for stage, part, *more in stages:
                    stage(l + 1, part, *more)

        @pl.when(n > 0)
        def _():
            wait(kept(KEEP_FFN, l, True))

        def now(stage, part):
            if not alone:
                run_reduce(stage, l, part)

        def then(stage, part):
            if not alone:

                @pl.when(n > 0)
                def _():
                    run_reduce(stage, l + 1, part)

        def in_ffn():
            then(LAST, 2)

        def in_windows():
            now(SECOND, 2)
            then(LAST, 0)

        backward_ffn(k, l, grad, in_ffn)
        then(LAST, 1)
        then(SECOND, 0)
        backward_down_grads(k, l)
        now(SEND, 2)
        then(THIRD, 0)
        backward_up_grads(k, l)

        @pl.when(n < LAYERS - 1)
        def _():
            start(kept(KEEP_FFN, l - 1, True))

        now(SEND, 1)
        now(FIRST, 2)

        @pl.when(n > 0)
        def _():
            wait(kept(KEEP_ATTN, l, True))

        backward_out(k, l, grad)
        now(FIRST, 1)
        backward_windows(k, l, in_windows)
        now(THIRD, 2)
        backward_attn_grads(k, l)

        @pl.when(n < LAYERS - 1)
        def _():
            start(kept(KEEP_ATTN, l - 1, True))

        now(SEND, 0)
        now(SECOND, 1)

        @pl.when(n == LAYERS - 1)
        def _():
            wait(kept_x(True))

        backward_input(k, l, grad)

        @pl.when(n == 0)
        def _():
            start(kept_x(True))

        now(FIRST, 0)
        now(THIRD, 1)
        return carry

    lax.fori_loop(0, LAYERS, backward, 0)
    if alone:
        start(stores)
        small_stage(k, k.small_out, grad)
        wait(stores)
        return
    small_stage(k, sums.whole(), grad)
    sums.start()
    reduce.last(0, 2, k.shard, k.squares_sum)
    reduce.second(0, 0)
    sums.step(0)
    reduce.third(0, 0, k.shard)
    sums.step(1)
    reduce.last(0, 1, k.shard, k.squares_sum)
    sums.step(2)
    reduce.last(0, 0, k.shard, k.squares_sum)
    squares = k.squares_sum[...]
    norm.start(sum(squares[:, n * 128 : (n + 1) * 128] for n in range(D // 128)))
    sums.back()
    norm.step()
    sums.last()
    k.small_out[...] = sums.whole()[...]
    k.squares[...] = norm.last()


def train_pass(inputs, weights, alone):
    whole = pl.BlockSpec(memory_space=pltpu.VMEM)
    scalars = pl.BlockSpec(memory_space=pltpu.SMEM)
    anywhere = pl.BlockSpec(memory_space=pl.ANY)
    dma = pltpu.SemaphoreType.DMA
    count = PARTS * LAYERS
    names = ["states", "actions", "returns", "starts", "repeats", "valid"]
    names += ["log_temp", "small", "head_bias"]
    out_shape = {"small_out": ((SMALL, D), WIDE)}
    for name in KEEP:
        shape, dtype = WORK_SHAPES[name]
        out_shape["keep_" + name] = ((LAYERS - 1,) + shape, dtype)
    out_shape["keep_x"] = ((ROWS, D), WIDE)
    scratch = {name: pltpu.VMEM(*shape) for name, shape in WORK_SHAPES.items()}
    scratch["keep_sem"] = dma((len(KEEP) + 1,))
    if alone:
        names += ["all_a", "all_f"]
        out_shape["grad_a"] = ((LAYERS, 4, 8, ATTN, D), LOWER)
        out_shape["grad_f"] = ((LAYERS, 4, 8, FFN, D), LOWER)
        scratch["load_sem"] = dma((count,))
    else:
        names += ["qkv_w", "out_w", "up_w", "down_w"]
        out_shape["shard"] = ((LAYERS, PACK, D), WIDE)
        out_shape["squares"] = ((8, 128), WIDE)
        for part in range(PARTS):
            for n, shape in enumerate(LANDING):
                scratch["land_%d_%d" % (part, n)] = pltpu.VMEM(shape, LOWER)
        scratch["stage_sem"] = dma((LAYERS, 9))
        scratch["squares_sum"] = pltpu.VMEM((8, D), WIDE)
        for name, copies in (("gather", Gather.COPIES), ("reduce", Reduce.COPIES)):
            scratch[name + "_send"] = dma((count, copies))
            scratch[name + "_recv"] = dma((count, copies))
        scratch["credit"] = pltpu.SemaphoreType.REGULAR((PARTS, 8))
        scratch["norm_plane"] = pltpu.VMEM((8, 8, 128), WIDE)
        scratch["norm_column"] = pltpu.VMEM((NZ, 8, 128), WIDE)
        for name, copies in (("sum", Total.COPIES), ("norm", Norm.COPIES)):
            scratch[name + "_send"] = dma((copies,))
            scratch[name + "_recv"] = dma((copies,))
    spaces = dict.fromkeys(("starts", "repeats", "head_bias", "log_temp"), scalars)
    for name in ("all_a", "all_f", "grad_a", "grad_f", "qkv_w", "out_w", "up_w", "down_w"):
        spaces[name] = anywhere
    for name in KEEP + ("x",):
        spaces["keep_" + name] = anywhere
    every = names + list(out_shape) + list(scratch)

    def kernel(*given):
        refs = dict(zip(every, given))
        refs["landing"] = [
            [refs.get("land_%d_%d" % (part, n)) for n in range(len(LANDING))] for part in range(PARTS)
        ]
        train_kernel(refs, alone)

    results = pl.pallas_call(
        kernel,
        name="train_pass",
        out_shape=tuple(jax.ShapeDtypeStruct(*shape) for shape in out_shape.values()),
        in_specs=[spaces.get(name, whole) for name in names],
        out_specs=tuple(spaces.get(name, whole) for name in out_shape),
        scratch_shapes=list(scratch.values()),
        compiler_params=pltpu.CompilerParams(
            vmem_limit_bytes=VMEM_BYTES,
            collective_id=None if alone else 0,
            has_side_effects=not alone,
        ),
        cost_estimate=pl.CostEstimate(
            flops=6 * 10**10, bytes_accessed=4 * 10**7, transcendentals=10**7
        ),
    )(*inputs, *weights)
    return dict(zip(out_shape, results))


def adam_parts(weight, grad, first, second, rate):
    first = BETA_ONE * first + (1.0 - BETA_ONE) * grad
    second = BETA_TWO * second + (1.0 - BETA_TWO) * grad * grad
    fix_one = 1.0 - BETA_ONE**STEP
    fix_two = 1.0 - BETA_TWO**STEP
    fresh = weight - rate * (
        first * (1.0 / fix_one) / (jnp.sqrt(second * (1.0 / fix_two)) + ADAM_EPS) + DECAY * weight
    )
    return fresh, first, second


def adam_kernel(*refs):
    shard, small_grad, squares, groups, log_temp = refs[:5]
    small, small_first, small_second, bias, bias_first, bias_second = refs[5:11]
    mats, firsts, seconds = refs[11:15], refs[15:19], refs[19:23]
    totals, norm, next_temp, s_next, s_first, s_second, b_next, b_first, b_second = refs[23:32]
    m_next, m_copy, m_first, m_second = refs[32:36], refs[36:40], refs[40:44], refs[44:48]
    extra = small_grad[NROWS : NROWS + 3, 0:128]
    lane = iota((1, 128), 1)
    bias_mean = jnp.where(lane < A, extra[1:2], 0.0)
    bias_spread = jnp.where(lane < A, extra[2:3], 0.0)

    def all_sum(v):
        return jnp.sum(jnp.sum(v, 0, keepdims=True), 1, keepdims=True)

    grads = small_grad[0:NROWS, :]
    square = (
        all_sum(squares[0:1, :])
        + all_sum(grads * grads)
        + all_sum(bias_mean * bias_mean)
        + all_sum(bias_spread * bias_spread)
    )
    length = jnp.sqrt(square)
    clip = jnp.minimum(1.0, CLIP / (length + 1e-06))

    def rate_of(l, kind):
        group = jnp.full((1, 1), groups[l, kind], jnp.int32).astype(WIDE)
        return LEARN * jnp.exp2(-group)

    def update(l, kind, rows, cols, grad):
        at = (l, rows, cols)
        fresh, first, second = adam_parts(
            mats[kind][at], clip * grad, firsts[kind][at], seconds[kind][at], rate_of(l, kind)
        )
        m_next[kind][at] = fresh
        m_copy[kind][at] = fresh.astype(LOWER)
        m_first[kind][at] = first
        m_second[kind][at] = second

    every = slice(0, 16)
    for l in range(LAYERS):
        for j in range(3):
            update(l, 0, every, slice(j * D, (j + 1) * D), shard[l, 16 * j : 16 * j + 16, :])
        update(l, 1, every, slice(0, D), shard[l, 48:64, :])
        for j in range(4):
            rows = slice(64 + 16 * j, 80 + 16 * j)
            update(l, 2, every, slice(j * D, (j + 1) * D), shard[l, rows, :])
        update(l, 3, slice(0, 64), slice(0, D), shard[l, 128:192, :])

    s_next[...], s_first[...], s_second[...] = adam_parts(
        small[...], clip * grads, small_first[...], small_second[...], LEARN
    )

    def scalar(v, n):
        return jnp.sum(jnp.where(lane == n, v, 0.0))

    def row(ref):
        v = jnp.zeros((1, 128), WIDE)
        for n in range(2 * A):
            v = jnp.where(lane == n, ref[n], v)
        return v

    grad = bias_mean + pltpu.roll(bias_spread, A, 1)
    results = adam_parts(row(bias), clip * grad, row(bias_first), row(bias_second), LEARN)
    for ref, result in zip((b_next, b_first, b_second), results):
        for n in range(2 * A):
            ref[n] = scalar(result, n)
    sums = extra[0:1]
    for n in range(3):
        totals[n] = scalar(sums, n)
    norm[0] = jnp.sum(length)
    logs = jnp.full((1, 1), log_temp[0], WIDE)
    ratio = jnp.full((1, 1), scalar(sums, 1), WIDE) / jnp.full((1, 1), scalar(sums, 2), WIDE)
    next_temp[0] = jnp.sum(logs - TEMP_RATE * jnp.exp(logs) * (ratio + A))


def adam_all(shard, small_grad, squares, groups, log_temp, smalls, biases, mats, firsts, seconds):
    scalars = pl.BlockSpec(memory_space=pltpu.SMEM)

    whole = pl.BlockSpec(memory_space=pltpu.VMEM)

    def like(array, dtype=WIDE):
        return jax.ShapeDtypeStruct(array.shape, dtype)

    stacks = list(mats) + list(firsts) + list(seconds)
    small, bias = smalls[0], biases[0]
    return pl.pallas_call(
        adam_kernel,
        name="adam",
        out_shape=(
            (jax.ShapeDtypeStruct((3,), WIDE),)
            + (jax.ShapeDtypeStruct((1,), WIDE),) * 2
            + (like(small),) * 3
            + (like(bias),) * 3
            + tuple(like(m) for m in mats)
            + tuple(like(m, LOWER) for m in mats)
            + tuple(like(m) for m in mats) * 2
        ),
        in_specs=[whole] * 3 + [scalars] * 2 + [whole] * 3 + [scalars] * 3 + [whole] * 12,
        out_specs=(scalars,) * 3 + (whole,) * 3 + (scalars,) * 3 + (whole,) * 16,
        compiler_params=pltpu.CompilerParams(vmem_limit_bytes=VMEM_BYTES),
        cost_estimate=pl.CostEstimate(flops=10**7, bytes_accessed=8 * 10**6, transcendentals=10**6),
    )(shard, small_grad, squares, groups, log_temp, *smalls, *biases, *stacks)


def gather_packed(mats, axes, count):
    group = count // BLOCKS
    pieces = []
    for mat in mats:
        rows, wide = mat.shape[1], mat.shape[2] // D
        piece = mat.astype(LOWER).reshape(LAYERS, rows, wide, D)
        piece = lax.all_gather(piece, axes, axis=1, tiled=True)
        piece = piece.reshape(LAYERS, NZ, NY, NX, NC, group * rows, wide, D)
        piece = piece.transpose(0, 4, 3, 2, 1, 6, 5, 7)
        pieces.append(piece.reshape(LAYERS, 4, 8, wide * group * rows, D))
    return jnp.concatenate(pieces[:2], 3), jnp.concatenate(pieces[2:], 3)


def scatter_packed(grads, mats, axes):
    results, first = [], 0
    for n, mat in enumerate(mats):
        rows, wide = mat.shape[1], mat.shape[2] // D
        total = lax.psum(1, axes) * rows
        deep = total // BLOCKS
        first = 0 if n % 2 == 0 else first
        piece = grads[n // 2][:, :, :, first : first + wide * deep].astype(WIDE)
        first += wide * deep
        piece = piece.reshape(LAYERS, NC, NX, NY, NZ, wide, deep, D)
        piece = piece.transpose(0, 4, 3, 2, 1, 6, 5, 7).reshape(LAYERS, total, wide * D)
        results.append(lax.psum_scatter(piece, axes, scatter_dimension=1, tiled=True))
    return results


def local(
    buf_states,
    buf_actions,
    buf_returns,
    window_starts,
    window_repeats,
    valid_steps,
    matrix_groups,
    log_temp,
    small_rows,
    head_bias,
    qkv_weight,
    out_weight,
    up_weight,
    down_weight,
    small_first,
    bias_first,
    qkv_first,
    out_first,
    up_first,
    down_first,
    small_second,
    bias_second,
    qkv_second,
    out_second,
    up_second,
    down_second,
):
    axes = ("dp", "fsdp")
    mats = (qkv_weight, out_weight, up_weight, down_weight)
    firsts = (qkv_first, out_first, up_first, down_first)
    seconds = (qkv_second, out_second, up_second, down_second)
    pass_inputs = (
        buf_states.T,
        buf_actions.T,
        buf_returns[None],
        window_starts,
        window_repeats,
        valid_steps,
        log_temp,
        small_rows,
        head_bias,
    )
    if FF // down_weight.shape[1] == BLOCKS and lax.psum(1, "fsdp") == NX * NC:
        made = train_pass(pass_inputs, mats, False)
        return adam_all(
            made["shard"],
            made["small_out"],
            made["squares"],
            matrix_groups,
            log_temp,
            (small_rows, small_first, small_second),
            (head_bias, bias_first, bias_second),
            mats,
            firsts,
            seconds,
        )
    packed = gather_packed(mats, axes, FF // down_weight.shape[1])
    made = train_pass(pass_inputs, packed, True)
    big = scatter_packed((made["grad_a"], made["grad_f"]), mats, axes)
    small = made["small_out"]
    small = lax.psum(small, axes)
    small_grad, totals = small[:NROWS], small[NROWS, :3]
    bias_grad = jnp.concatenate([small[NROWS + 1, :A], small[NROWS + 2, :A]])
    square = sum((jnp.sum(piece * piece) for piece in big))
    square = (
        lax.psum(square, axes) + jnp.sum(small_grad * small_grad) + jnp.sum(bias_grad * bias_grad)
    )
    grad_norm = jnp.sqrt(square)
    clip = jnp.minimum(1.0, CLIP / (grad_norm + 1e-06))
    rates = LEARN * jnp.exp2(-matrix_groups.astype(WIDE))
    results = [
        adam_parts(
            mats[kind], clip * big[kind], firsts[kind], seconds[kind], rates[:, kind][:, None, None]
        )
        for kind in range(4)
    ]
    small_new = adam_parts(small_rows, clip * small_grad, small_first, small_second, LEARN)
    bias_new = adam_parts(head_bias, clip * bias_grad, bias_first, bias_second, LEARN)
    next_temp = log_temp - TEMP_RATE * jnp.exp(log_temp) * (totals[1] / totals[2] + A)
    return (
        (totals, grad_norm[None], next_temp)
        + small_new
        + bias_new
        + tuple(r[0] for r in results)
        + tuple(r[0].astype(LOWER) for r in results)
        + tuple(r[1] for r in results)
        + tuple(r[2] for r in results)
    )


def solution(mesh):
    rows = P(("dp", "fsdp"), None)
    vector = P(("dp", "fsdp"))
    stack = P(None, ("dp", "fsdp"), None)
    same = P()
    in_specs = (
        (rows, rows, vector, vector, vector, rows)
        + (same,) * 4
        + (stack,) * 4
        + (same,) * 2
        + (stack,) * 4
        + (same,) * 2
        + (stack,) * 4
    )
    out_specs = (same,) * 9 + (stack,) * 16
    return jax.shard_map(local, mesh=mesh, in_specs=in_specs, out_specs=out_specs, check_vma=False)
```

```python
import math

import jax
import jax.numpy as jnp
from jax import lax
from jax.experimental import pallas as pl
from jax.experimental.pallas import tpu as pltpu
from jax.sharding import PartitionSpec as P

D = 512
H = 8
HD = 64
FF = 2048
S = 11
A = 3
K = 20
STEP = 10

EPS = 1e-05
CLIP = 1.0
LEARN = 0.03
BETA_ONE = 0.5
BETA_TWO = 0.7
DECAY = 0.01
ADAM_EPS = 1e-08
TEMP_RATE = 0.1
MASKED = -1e30
HALF_LOG_TAU = 0.5 * math.log(2.0 * math.pi)
GELU_C = math.sqrt(2.0 / math.pi)
GELU_A = 0.044715
HIGH = lax.Precision.HIGHEST
LOWER = jnp.bfloat16
WIDE = jnp.float32

LAYERS = 3
WINS = 16
BUF_DEV = 64
SLOT = 64
ROWS = WINS * SLOT
CHUNK = 512
CHUNKS = ROWS // CHUNK
BLOCKS = 32
PACK = 192
ATTN, FFN = 64, 128
EMB = S + A + 1 + K + 3
FIN = EMB
HEADW = EMB + 2
BASE = EMB + 2 + 2 * A
PER = 9 + FF // D
NROWS = BASE + LAYERS * PER
SMALL = 96
HEAD_AT = 64
EMB_AT = ROWS - 128
VMEM_BYTES = 64 * 1024 * 1024


def dot(a, b, precision=None):
    return lax.dot_general(
        a, b, (((1,), (0,)), ((), ())), precision=precision, preferred_element_type=WIDE
    )


def dot_nt(a, b, precision=None):
    return lax.dot_general(
        a, b, (((1,), (1,)), ((), ())), precision=precision, preferred_element_type=WIDE
    )


def dot_tn(a, b, precision=None):
    return lax.dot_general(
        a, b, (((0,), (0,)), ((), ())), precision=precision, preferred_element_type=WIDE
    )


def iota(shape, dim):
    return lax.broadcasted_iota(jnp.int32, shape, dim)


def col_sum(v):
    return jnp.sum(v, 0, keepdims=True)


def row_mean(v):
    return jnp.mean(v, -1, keepdims=True)


def norm_parts(x):
    center = x - row_mean(x)
    scale = lax.rsqrt(row_mean(center * center) + EPS)
    return center * scale, scale


def norm_back(xhat, scale, gain, grad):
    scaled = grad * gain
    return scale * (scaled - row_mean(scaled) - xhat * row_mean(scaled * xhat))


def token_rows(at, count):
    row = at + iota((count, 128), 0)
    place = row & (SLOT - 1)
    step = (place * 21846) >> 16
    return row >> 6, step, place - 3 * step, place < 3 * K


def chunk_rows(c):
    return pl.ds(pl.multiple_of(c * CHUNK, CHUNK), CHUNK)


def owner_place(i):
    z, y, x, c = i // 8, (i // 4) % 2, (i // 2) % 2, i % 2
    return 2 * c + x, 4 * y + z


class Kit:
    def __init__(self, **refs):
        self.__dict__.update(refs)

    def row(self, l, k):
        return self.lrows[l, k : k + 1, :]

    def blocks(self, ref, l, first, count, owners):
        places = [owner_place(i) for i in owners]
        return jnp.concatenate([ref[l, a, b, first : first + count, :] for a, b in places], 0)

    def w_qkv(self, l, j):
        return self.blocks(self.wa, l, 16 * j, 16, range(BLOCKS))

    def w_out(self, l):
        return self.blocks(self.wa, l, 48, 16, range(BLOCKS))

    def w_up(self, l, j):
        return self.blocks(self.wf, l, 16 * j, 16, range(BLOCKS))

    def w_down(self, l, j):
        return self.blocks(self.wf, l, 64, 64, range(8 * j, 8 * j + 8))


def slot(l):
    return l % 2


def setup_stage(k):
    k.xs[2, EMB_AT:ROWS, :] = jnp.zeros((128, D), WIDE)
    k.xs[2, EMB_AT : EMB_AT + EMB, :] = k.small[0:EMB, :]
    k.headw[...] = jnp.zeros_like(k.headw)
    k.headw[0, 0:A, :] = k.small[HEADW : HEADW + A, :].astype(LOWER)
    k.headw[1, 0:A, :] = k.small[HEADW + A : HEADW + 2 * A, :].astype(LOWER)
    for l in range(LAYERS):
        k.lrows[l, 0:PER, :] = k.small[BASE + l * PER : BASE + (l + 1) * PER, :]
    k.sgl[...] = jnp.zeros_like(k.sgl)
    k.sgh[...] = jnp.zeros_like(k.sgh)
    k.sgw[...] = jnp.zeros_like(k.sgw)

    lane, sub = iota((WINS, 128), 1), iota((WINS, 128), 0)
    k.meta[...] = jnp.zeros_like(k.meta)
    k.meta[0:WINS, 0:K] = k.valid[...].astype(WIDE)
    meta = k.meta[0:WINS, :]
    for w in range(WINS):
        for n, ref in enumerate((k.starts, k.repeats)):
            meta = jnp.where((sub == w) & (lane == K + n), ref[w].astype(WIDE), meta)
    k.meta[0:WINS, :] = meta
    meta = k.meta[...].astype(LOWER)
    k.buf[...] = jnp.zeros_like(k.buf)
    k.buf[0, 0:S, 0:BUF_DEV] = k.states[...]
    k.buf[0, S + A : S + A + 1, 0:BUF_DEV] = k.returns[...]
    k.buf[1, 0:A, 0:BUF_DEV] = k.actions[...]

    def chunk(c, carry):
        rows = chunk_rows(c)
        win, step, kind, real = token_rows(c * CHUNK, CHUNK)
        lane = iota((CHUNK, 128), 1)
        tok = dot((lane == win).astype(WIDE).astype(LOWER), meta)
        start, repeat = tok[:, K : K + 1], tok[:, K + 1 : K + 2]
        valid = jnp.sum(jnp.where(lane == step, tok, 0.0), -1, keepdims=True)
        key = iota((CHUNK, 128), 0) & (SLOT - 1)
        query = lane & (SLOT - 1)
        allowed = (key <= query) & (((valid > 0.5) & real) | (key == query))
        k.bias[rows, :] = jnp.where(allowed, 0.0, MASKED)
        place = start.astype(jnp.int32) + step
        source = ((lane == place) & real).astype(WIDE)
        raw = dot_nt(source, k.buf[0], HIGH)
        acts = dot_nt(source, k.buf[1], HIGH)
        mine = (
            ((lane < S) & (kind == 1))
            | ((lane >= S) & (lane < S + A) & (kind == 2))
            | ((lane == S + A) & (kind == 0))
        )
        raw = raw + pltpu.roll(acts, S, 1)
        marks = ((lane == S + A + 1 + step) | (lane == S + A + 1 + K + kind)) & real
        feats = jnp.where(mine, raw, 0.0) + marks.astype(WIDE)
        weight = jnp.where((kind == 1) & real, repeat * valid, 0.0)
        acts = pltpu.roll(acts, HEAD_AT, 1)
        ours = (lane >= HEAD_AT) & (lane < HEAD_AT + A)
        feats = jnp.where(ours, acts, jnp.where(lane == HEAD_AT + A, weight, feats))
        k.feats[rows, :] = feats
        k.xs[0, rows, :] = dot(feats, k.xs[2, EMB_AT:ROWS, :], HIGH)
        return carry

    lax.fori_loop(0, CHUNKS, chunk, 0)


def stack_pair(v, first):
    zero = jnp.zeros_like(v)
    return jnp.concatenate([jnp.where(first, v, zero), jnp.where(first, zero, v)], 0)


def join_pair(v, first):
    return jnp.where(first, v[:SLOT], v[SLOT:])


def window_rows(w):
    return pl.ds(pl.multiple_of(w * SLOT, SLOT), SLOT)


def each_chunk(body, between=None):
    def step(c, carry):
        body(c, chunk_rows(c))
        if between is not None:

            @pl.when(c < CHUNKS - 1)
            def _():
                between()

        return carry

    lax.fori_loop(0, CHUNKS, step, 0)


def each_pair(body, between=None):
    def pair(n, carry):
        chains = [
            (2 * n + w, window_rows(2 * n + w), slice(p * 128, (p + 1) * 128))
            for w in range(2)
            for p in range(H // 2)
        ]
        body(pl.ds(pl.multiple_of(n * 128, 128), 128), chains)
        if between is not None:

            @pl.when(n == WINS // 4 - 1)
            def _():
                between()

        return carry

    lax.fori_loop(0, WINS // 2, pair, 0)


def forward_qkv(k, l, between):
    def chunk(c, rows):
        xhat, _ = norm_parts(k.xs[slot(l), rows, :])
        normed = (xhat * k.row(l, 0) + k.row(l, 1)).astype(LOWER)
        k.normed_t[:, rows] = normed.T
        for j in range(3):
            part = dot(normed, k.w_qkv(l, j)) + k.row(l, 4 + j)
            k.qkv[rows, j * D : (j + 1) * D] = part.astype(LOWER)

    each_chunk(chunk, between)


def qkv_part(k, n, rows, at):
    return k.qkv[rows, n * D + at.start : n * D + at.stop]


def forward_windows(k, l, between):
    first = iota((SLOT, 128), 1) < HD
    scale = jnp.asarray(HD**-0.5, LOWER)

    def pair(both, chains):
        query = [stack_pair(qkv_part(k, 0, rows, at) * scale, first) for _, rows, at in chains]
        scores = [
            dot_nt(qkv_part(k, 1, rows, at), q) + k.bias[rows, :]
            for q, (_, rows, at) in zip(query, chains)
        ]
        peaks = [jnp.max(s, 0, keepdims=True) for s in scores]
        expos = [jnp.exp(s - peak) for s, peak in zip(scores, peaks)]
        totals = [jnp.sum(e, 0, keepdims=True) for e in expos]
        probs = [(e * (1.0 / total)).astype(LOWER) for e, total in zip(expos, totals)]
        outs = [dot_tn(p, qkv_part(k, 2, rows, at)) for p, (_, rows, at) in zip(probs, chains)]
        for peak, total, out, (w, rows, at) in zip(peaks, totals, outs, chains):
            p = at.start // 128
            k.logs[l, w, p : p + 1, :] = peak + jnp.log(total)
            k.left[rows, at] = join_pair(out, first).astype(LOWER)
        k.mixed_t[:, both] = k.left[both, :].T

    each_pair(pair, between)


def forward_up(k, l, between):
    def chunk(c, rows):
        mid = k.xs[slot(l), rows, :] + dot(k.left[rows, :], k.w_out(l)) + k.row(l, 7)
        k.mid[rows, :] = mid
        xhat, _ = norm_parts(mid)
        second = (xhat * k.row(l, 2) + k.row(l, 3)).astype(LOWER)
        k.second_t[:, rows] = second.T
        ahead = dot(second, k.w_up(l, 0))
        for j in range(4):
            cols = slice(j * D, (j + 1) * D)
            h = ahead + k.row(l, 8 + j)
            if j < 3:
                ahead = dot(second, k.w_up(l, j + 1))
            square = h * h
            over = 1.0 + jnp.tanh(h * (GELU_C + GELU_C * GELU_A * square))
            half = 0.5 * h
            acted = (half * over).astype(LOWER)
            slope = over * (0.5 + half * (2.0 - over) * (GELU_C + 3.0 * GELU_A * GELU_C * square))
            k.work[rows, cols] = acted
            k.slope[rows, cols] = slope.astype(LOWER)
            k.act_t[cols, rows] = acted.T

    each_chunk(chunk, between)


def forward_down(k, l, dest):
    def chunk(c, rows):
        w_down = jnp.concatenate([k.w_down(l, j) for j in range(4)], 0)
        k.xs[dest, rows, :] = k.mid[rows, :] + k.row(l, 12) + dot(k.work[rows, :], w_down)

    each_chunk(chunk)


def head_stage(k, at):
    gain, bias = k.small[FIN : FIN + 1, :], k.small[FIN + 1 : FIN + 2, :]
    lane = iota((CHUNK, 128), 1)
    keep = lane < A

    def bias_row(first):
        row = jnp.zeros((1, 128), WIDE)
        at = iota((1, 128), 1)
        for a in range(A):
            row = jnp.where(at == a, k.head_bias[first + a], row)
        return row

    bias_mean, bias_spread = bias_row(0), bias_row(A)
    temp = jnp.exp(jnp.full((1, 128), k.log_temp[0], WIDE))

    def chunk(c, carry):
        rows = chunk_rows(c)
        xhat, scale = norm_parts(k.xs[at, rows, :])
        feats = (xhat * gain + bias).astype(LOWER)
        mean = dot_nt(feats, k.headw[0]) + bias_mean
        spread = jnp.tanh(dot_nt(feats, k.headw[1]) + bias_spread)
        acts = pltpu.roll(k.feats[rows, :], 128 - HEAD_AT, 1)
        weight = acts[:, A : A + 1]
        acts = jnp.where(keep, acts, 0.0)
        target = 0.5 * (jnp.log(1.0 + acts) - jnp.log(1.0 - acts))
        shrink = jnp.exp(-spread)
        zed = (target - mean) * shrink
        terms = 0.5 * zed * zed + spread + HALF_LOG_TAU + jnp.log(1.0 - acts * acts)
        nll = jnp.sum(jnp.where(keep, terms, 0.0), -1, keepdims=True)
        entropy = jnp.sum(jnp.where(keep, spread, 0.0), -1, keepdims=True) + A * (0.5 + HALF_LOG_TAU)
        loss = weight * (nll - temp * entropy)
        sums = jnp.where(lane == 0, loss, jnp.where(lane == 1, weight * entropy, jnp.where(lane == 2, weight, 0.0)))
        d_mean = jnp.where(keep, weight * (-zed * shrink), 0.0).astype(LOWER)
        d_spread = weight * (1.0 - zed * zed - temp) * (1.0 - spread * spread)
        d_spread = jnp.where(keep, d_spread, 0.0).astype(LOWER)
        k.sgh[2:3, 0:128] += col_sum(sums)
        k.sgh[3:4, 0:128] += col_sum(d_mean.astype(WIDE))
        k.sgh[4:5, 0:128] += col_sum(d_spread.astype(WIDE))
        k.sgw[0] += dot_tn(d_mean, feats)[0:8]
        k.sgw[1] += dot_tn(d_spread, feats)[0:8]
        d_feats = dot(d_mean, k.headw[0]) + dot(d_spread, k.headw[1])
        k.sgh[0:1, :] += col_sum(d_feats * xhat)
        k.sgh[1:2, :] += col_sum(d_feats)
        k.xs[at, rows, :] = norm_back(xhat, scale, gain, d_feats)
        return carry

    lax.fori_loop(0, CHUNKS, chunk, 0)


def store_blocks(ref, l, owners, first, count, value):
    value = value.astype(LOWER)
    for n, i in enumerate(owners):
        a, b = owner_place(i)
        ref[l, a, b, first : first + count, :] = value[n * count : (n + 1) * count]


def backward_ffn(k, l, grad, between=None):
    def chunk(c, rows):
        d_down = k.xs[grad, rows, :].astype(LOWER)
        k.dout[rows, :] = d_down
        k.sgl[l, 12:13, :] += col_sum(d_down.astype(WIDE))
        d_second = jnp.zeros((CHUNK, D), WIDE)
        ahead = dot_nt(d_down, k.w_down(l, 0))
        for j in range(4):
            cols = slice(j * D, (j + 1) * D)
            d_acted = ahead
            if j < 3:
                ahead = dot_nt(d_down, k.w_down(l, j + 1))
            d_hidden = (d_acted * k.slope[rows, cols].astype(WIDE)).astype(LOWER)
            k.work[rows, cols] = d_hidden
            k.sgl[l, 8 + j : 9 + j, :] += col_sum(d_hidden.astype(WIDE))
            d_second = d_second + dot_nt(d_hidden, k.w_up(l, j))
        xhat, scale = norm_parts(k.mid[rows, :])
        k.sgl[l, 2:3, :] += col_sum(d_second * xhat)
        k.sgl[l, 3:4, :] += col_sum(d_second)
        k.xs[grad, rows, :] += norm_back(xhat, scale, k.row(l, 2), d_second)

    each_chunk(chunk, between)


def backward_down_grads(k, l):
    for j in range(4):
        part = dot(k.act_t[j * D : (j + 1) * D, :], k.dout[...])
        store_blocks(k.wf, l, range(8 * j, 8 * j + 8), 64, 64, part)


def backward_up_grads(k, l):
    for j in range(4):
        part = dot(k.second_t[...], k.work[:, j * D : (j + 1) * D])
        store_blocks(k.wf, l, range(BLOCKS), 16 * j, 16, part)


def backward_out(k, l, grad):
    def before(c, rows):
        d_branch = k.xs[grad, rows, :].astype(LOWER)
        k.left[rows, :] = d_branch
        k.sgl[l, 7:8, :] += col_sum(d_branch.astype(WIDE))
        k.dout[rows, :] = dot_nt(d_branch, k.w_out(l)).astype(LOWER)

    each_chunk(before)
    store_blocks(k.wa, l + 1, range(BLOCKS), 48, 16, dot(k.mixed_t[...], k.left[...]))


def backward_windows(k, l, between):
    first = iota((SLOT, 128), 1) < HD
    scale = HD**-0.5
    low = jnp.asarray(scale, LOWER)

    def pair(both, chains):
        query = [stack_pair(qkv_part(k, 0, rows, at) * low, first) for _, rows, at in chains]
        d_mixed = [stack_pair(k.dout[rows, at], first) for _, rows, at in chains]
        shift = [
            k.bias[rows, :] - k.logs[l, w, at.start // 128 : at.start // 128 + 1, :]
            for w, rows, at in chains
        ]
        scores = [dot_nt(qkv_part(k, 1, rows, at), q) for q, (_, rows, at) in zip(query, chains)]
        d_probs = [dot_nt(qkv_part(k, 2, rows, at), d) for d, (_, rows, at) in zip(d_mixed, chains)]
        probs = [jnp.exp(s + more) for s, more in zip(scores, shift)]
        d_values = [dot(p.astype(LOWER), d) for p, d in zip(probs, d_mixed)]
        inner = [p * d for p, d in zip(probs, d_probs)]
        sums = [jnp.sum(i, 0, keepdims=True) for i in inner]
        d_scores = [(i - p * t).astype(LOWER) for i, p, t in zip(inner, probs, sums)]
        d_keyed = [dot(d, q) for d, q in zip(d_scores, query)]
        d_query = [dot_tn(d, qkv_part(k, 1, rows, at)) for d, (_, rows, at) in zip(d_scores, chains)]
        for n, (_, rows, at) in enumerate(chains):
            values = (join_pair(d_query[n], first) * scale, d_keyed[n], d_values[n])
            for m, value in enumerate(values):
                k.work[rows, m * D + at.start : m * D + at.stop] = value.astype(LOWER)

    each_pair(pair, between)


def backward_attn_grads(k, l):
    for j in range(3):
        part = dot(k.normed_t[...], k.work[:, j * D : (j + 1) * D])
        store_blocks(k.wa, l + 1, range(BLOCKS), 16 * j, 16, part)


def backward_input(k, l, grad):
    def chunk(c, rows):
        d_normed = jnp.zeros((CHUNK, D), WIDE)
        for j in range(3):
            d_part = k.work[rows, j * D : (j + 1) * D]
            k.sgl[l, 4 + j : 5 + j, :] += col_sum(d_part.astype(WIDE))
            d_normed = d_normed + dot_nt(d_part, k.w_qkv(l, j))
        xhat, scale = norm_parts(k.xs[slot(l), rows, :])
        k.sgl[l, 0:1, :] += col_sum(d_normed * xhat)
        k.sgl[l, 1:2, :] += col_sum(d_normed)
        k.xs[grad, rows, :] += norm_back(xhat, scale, k.row(l, 0), d_normed)

    each_chunk(chunk)


def small_stage(k, out, grad):
    out[...] = jnp.zeros_like(out)
    out[0:EMB, :] = dot_tn(k.feats[...], k.xs[grad], HIGH)[0:EMB]
    out[FIN : FIN + 2, :] = k.sgh[0:2, :]
    out[HEADW : HEADW + A, :] = k.sgw[0, 0:A, :]
    out[HEADW + A : HEADW + 2 * A, :] = k.sgw[1, 0:A, :]
    for l in range(LAYERS):
        out[BASE + l * PER : BASE + (l + 1) * PER, :] = k.sgl[l, 0:PER, :]
    out[NROWS : NROWS + 3, :] = k.sgh[2:5, :]


WORK_SHAPES = dict(
    wa=((LAYERS + 1, 4, 8, ATTN, D), LOWER),
    wf=((LAYERS, 4, 8, FFN, D), LOWER),
    xs=((3, ROWS, D), WIDE),
    qkv=((ROWS, 3 * D), LOWER),
    normed_t=((D, ROWS), LOWER),
    mixed_t=((D, ROWS), LOWER),
    slope=((ROWS, FF), LOWER),
    act_t=((FF, ROWS), LOWER),
    second_t=((D, ROWS), LOWER),
    mid=((ROWS, D), WIDE),
    logs=((LAYERS, WINS, 8, 128), WIDE),
    work=((ROWS, FF), LOWER),
    left=((ROWS, D), LOWER),
    dout=((ROWS, D), LOWER),
    feats=((ROWS, 128), WIDE),
    bias=((ROWS, 128), WIDE),
    headw=((2, 128, D), LOWER),
    lrows=((LAYERS, 16, D), WIDE),
    sgl=((LAYERS, 16, D), WIDE),
    sgh=((8, D), WIDE),
    sgw=((2, 8, D), WIDE),
    meta=((128, 128), WIDE),
    buf=((2, 128, 128), WIDE),
)
KEEP_ATTN = ("qkv", "normed_t", "mixed_t")
KEEP_FFN = ("slope", "act_t", "second_t", "mid")
KEEP = KEEP_ATTN + KEEP_FFN


MESH = pl.DeviceIdType.MESH
NZ, NY, NX, NC = 4, 2, 2, 2
NR = NY * NX * NC
SHARD = PACK
PARTS, DEEP = 3, 64
HALF = DEEP // 2


class Place:
    def __init__(self):
        dp, fsdp = lax.axis_index("dp"), lax.axis_index("fsdp")
        self.z, self.y = dp // NY, dp % NY
        self.x, self.c = fsdp // NC, fsdp % NC
        self.a, self.b = 2 * self.c + self.x, 4 * self.y + self.z
        self.r = 4 * self.y + fsdp
        self.to_z = [(((self.z + d) % NZ) * NY + self.y, fsdp) for d in range(1, NZ)]
        self.odd = self.z % 2
        self.to_pair = ((self.z + 1 - 2 * self.odd) * NY + self.y, fsdp)
        self.plane = []
        for d in range(1, 8):
            y, x, c = [
                1 - v if d & bit else v for v, bit in ((self.y, 4), (self.x, 2), (self.c, 1))
            ]
            self.plane.append((self.z * NY + y, x * NC + c))
        self.to_c, self.to_x, self.to_y = self.plane[0], self.plane[1], self.plane[3]

    def barrier(self):
        sem = pltpu.get_barrier_semaphore()
        for partner in self.plane + self.to_z:
            pl.semaphore_signal(sem, inc=1, device_id=partner, device_id_type=MESH)
        pl.semaphore_wait(sem, len(self.plane) + len(self.to_z))


def remote(src, dst, send, recv, to):
    return pltpu.make_async_remote_copy(
        src_ref=src, dst_ref=dst, send_sem=send, recv_sem=recv, device_id=to, device_id_type=MESH
    )


def part_ref(weights, part):
    return weights[min(part, 1)], (0, 0, DEEP)[part]


class Gather:
    COPIES = 13

    def __init__(self, place, weights, send, recv):
        self.at, self.weights, self.send, self.recv = place, weights, send, recv

    def copy(self, l, part, n):
        at = self.at
        array, row = part_ref(self.weights, part)
        a, b, rows, to = at.a, pl.ds(4 * at.y, 4), pl.ds(row, DEEP), at.to_c
        if n < 3:
            b, to = at.b, at.to_z[n]
        elif n < 5:
            to = (at.to_x, at.to_y)[n - 3]
        if n in (6, 8, 10, 11, 12):
            a = 2 * at.c + 1 - at.x
        if n in (7, 9, 10, 11, 12):
            b = pl.ds(4 * (1 - at.y), 4)
        if n in (6, 7):
            first = row + at.odd * HALF + (n - 6) * (HALF // 2)
            rows = pl.ds(pl.multiple_of(first, HALF // 2), HALF // 2)
            to = (at.to_y, at.to_x)[n - 6]
        if n in (10, 11):
            rows = pl.ds(pl.multiple_of(row + at.odd * HALF, HALF), HALF)
        if n == 11:
            to = at.to_pair
        if n == 12:
            rows = pl.ds(pl.multiple_of(row + (1 - at.odd) * HALF, HALF), HALF)
        ref = array.at[l, a, b, rows, :]
        q = PARTS * l + part
        return remote(ref, ref, self.send.at[q, n], self.recv.at[q, n], to)

    def start(self, l, part, *ns):
        for n in ns:
            self.copy(l, part, n).start()

    def wait(self, l, part, *ns):
        for n in ns:
            self.copy(l, part, n).wait_recv()

    def first(self, l, part):
        self.start(l, part, 0, 1, 2)

    def second(self, l, part):
        self.wait(l, part, 0, 1, 2)
        self.start(l, part, 3, 4, 5)

    def third(self, l, part):
        self.wait(l, part, 3)
        self.start(l, part, 6, 8)
        self.wait(l, part, 4)
        self.start(l, part, 7, 9)

    def fourth(self, l, part):
        self.wait(l, part, 6, 7)
        self.start(l, part, 11, 10)

    def fifth(self, l, part):
        self.wait(l, part, 11)
        self.start(l, part, 12)

    def last(self, l, part):
        self.wait(l, part, 5, 8, 9, 10, 12)

    def sent(self, l, part):
        for n in range(self.COPIES):
            self.copy(l, part, n).wait_send()


class Reduce:
    COPIES = 8

    def __init__(self, place, grads, landing, send, recv, credit):
        self.at, self.grads, self.landing = place, grads, landing
        self.send, self.recv, self.credit = send, recv, credit

    def refs(self, l, part):
        array, row = part_ref(self.grads, part)
        grads = array.at[l + 1 - min(part, 1), :, :, pl.ds(row, DEEP), :]
        return (grads, *self.landing[part])

    def copy(self, l, part, n):
        at, half = self.at, HALF
        g, r0, r1a, r1b, r2, r3 = self.refs(l, part)
        top, low, other = pl.ds(0, half), pl.ds(half, half), pl.ds(4 * (1 - at.y), 4)
        if n == 0:
            src, dst, to = g.at[pl.ds(2 * (1 - at.c), 2)], r0, at.to_c
        elif n == 1:
            src, dst, to = r0.at[1 - at.x, :, top, :], r1a, at.to_x
        elif n == 2:
            src, dst, to = r0.at[:, other, low, :], r1b, at.to_y
        elif n == 3:
            src, dst, to = r1a.at[other], r2.at[:, top, :], at.to_y
        elif n == 4:
            src, dst, to = r1b.at[1 - at.x], r2.at[:, low, :], at.to_x
        else:
            src, dst, to = r2.at[(at.z + n - 4) % NZ], r3.at[n - 5], at.to_z[n - 5]
        q = PARTS * l + part
        return remote(src, dst, self.send.at[q, n], self.recv.at[q, n], to)

    def may_send(self, l, part, *partners):
        @pl.when(l < LAYERS - 1)
        def _():
            for n in partners:
                pl.semaphore_wait(self.credit.at[part, n], 1)

    def allow(self, l, part, *credits):
        at = self.at

        @pl.when(l > 0)
        def _():
            for n, to in credits:
                pl.semaphore_signal(
                    self.credit.at[part, n], inc=1, device_id=to, device_id_type=MESH
                )

    def start(self, l, part):
        self.may_send(l, part, 0)
        self.copy(l, part, 0).start()

    def first(self, l, part):
        at, half = self.at, HALF
        g, r0, _, _, _, _ = self.refs(l, part)
        top, low = pl.ds(0, half), pl.ds(half, half)
        self.copy(l, part, 0).wait_recv()

        def along_x(n, carry):
            x = 1 - at.x
            total = g[2 * at.c + x, n, top].astype(WIDE) + r0[x, n, top].astype(WIDE)
            r0[x, n, top] = total.astype(LOWER)
            return carry

        def along_y(n, carry):
            x, b = n // 4, 4 * (1 - at.y) + n % 4
            total = g[2 * at.c + x, b, low].astype(WIDE) + r0[x, b, low].astype(WIDE)
            r0[x, b, low] = total.astype(LOWER)
            return carry

        lax.fori_loop(0, 8, along_x, 0)
        self.may_send(l, part, 1, 2)
        self.copy(l, part, 1).start()
        lax.fori_loop(0, 8, along_y, 0)
        self.copy(l, part, 2).start()

    def second(self, l, part):
        at, half = self.at, HALF
        g, r0, r1a, r1b, _, _ = self.refs(l, part)
        top, low = pl.ds(0, half), pl.ds(half, half)

        def along_y(n, carry):
            b = 4 * (1 - at.y) + n
            total = g[at.a, b, top].astype(WIDE) + r0[at.x, b, top].astype(WIDE)
            r1a[b] = (total + r1a[b].astype(WIDE)).astype(LOWER)
            return carry

        def along_x(n, carry):
            x, b = 1 - at.x, 4 * at.y + n
            total = g[2 * at.c + x, b, low].astype(WIDE) + r0[x, b, low].astype(WIDE)
            r1b[x, n] = (total + r1b[x, n].astype(WIDE)).astype(LOWER)
            return carry

        self.copy(l, part, 1).wait_recv()
        lax.fori_loop(0, NZ, along_y, 0)
        self.may_send(l, part, 6, 7)
        self.copy(l, part, 3).start()
        self.copy(l, part, 2).wait_recv()
        lax.fori_loop(0, NZ, along_x, 0)
        self.copy(l, part, 4).start()

    def chip_sums(self, l, part, z):
        at, half = self.at, HALF
        g, r0, r1a, r1b, r2, _ = self.refs(l, part)
        top, low, b = pl.ds(0, half), pl.ds(half, half), 4 * at.y + z
        upper = g[at.a, b, top].astype(WIDE) + r0[at.x, b, top].astype(WIDE)
        lower = g[at.a, b, low].astype(WIDE) + r0[at.x, b, low].astype(WIDE)
        return (
            upper + r1a[b].astype(WIDE) + r2[z, top].astype(WIDE),
            lower + r1b[at.x, z].astype(WIDE) + r2[z, low].astype(WIDE),
        )

    def third(self, l, part, out):
        at, half, row = self.at, HALF, DEEP * part
        r2 = self.landing[part][3]
        for n in (3, 4):
            self.copy(l, part, n).wait_recv()
        self.may_send(l, part, 3, 4, 5)
        for n in range(3):
            z = (at.z + n + 1) % NZ
            upper, lower = self.chip_sums(l, part, z)
            r2[z, pl.ds(0, half)] = upper.astype(LOWER)
            r2[z, pl.ds(half, half)] = lower.astype(LOWER)
            self.copy(l, part, 5 + n).start()
        upper, lower = self.chip_sums(l, part, at.z)
        out[l, row : row + half, :] = upper
        out[l, row + half : row + 2 * half, :] = lower
        for n in range(5):
            self.copy(l, part, n).wait_send()
        self.allow(l, part, (0, at.to_c), (1, at.to_x), (2, at.to_y))

    def last(self, l, part, out, squares):
        at, row = self.at, DEEP * part
        r3 = self.landing[part][4]
        rows = slice(row, row + DEEP)
        total = out[l, rows, :]
        for n in range(3):
            self.copy(l, part, 5 + n).wait_recv()
            total = total + r3[n].astype(WIDE)
        out[l, rows, :] = total
        squares[0:1, :] += col_sum(total * total)
        for n in range(5, self.COPIES):
            self.copy(l, part, n).wait_send()
        late = [(6, at.to_x), (7, at.to_y)] + [(5 - n, at.to_z[n]) for n in range(3)]
        self.allow(l, part, *late)


class Total:
    COPIES = 7

    def __init__(self, place, ref, rows, send, recv):
        self.at, self.ref, self.rows = place, ref, rows // 2
        self.send, self.recv = send, recv

    def half(self, n):
        return self.ref.at[pl.ds(pl.multiple_of(n * self.rows, 8), self.rows), :]

    def whole(self):
        return self.ref.at[pl.ds(0, 2 * self.rows), :]

    def copy(self, n):
        at = self.at
        mine, other = self.half(at.c), self.half(1 - at.c)
        src, dst, to = (
            (other, self.half(2), at.to_c),
            (self.half(8), self.half(3), at.to_x),
            (self.half(9), self.half(4), at.to_y),
            (self.half(10), self.half(5), at.to_z[0]),
            (self.half(10), self.half(6), at.to_z[1]),
            (self.half(10), self.half(7), at.to_z[2]),
            (mine, self.half(11), at.to_c),
        )[n]
        return remote(src, dst, self.send.at[n], self.recv.at[n], to)

    def start(self):
        self.copy(0).start()

    def step(self, n):
        self.copy(n).wait_recv()
        own = self.half(self.at.c) if n == 0 else self.half(7 + n)
        self.half(8 + n)[...] = own[...] + self.half(2 + n)[...]
        for m in ((1,), (2,), (3, 4, 5))[n]:
            self.copy(m).start()

    def back(self):
        for m in (3, 4, 5):
            self.copy(m).wait_recv()
        self.copy(0).wait_send()
        total = None
        for z in range(NZ):
            term = self.half(10)[...]
            for n in range(3):
                from_z = (self.at.z + NZ - 1 - n) % NZ
                term = jnp.where(from_z == z, self.half(5 + n)[...], term)
            total = term if total is None else total + term
        self.half(self.at.c)[...] = total
        self.copy(6).start()

    def last(self):
        self.copy(6).wait_recv()
        self.half(1 - self.at.c)[...] = self.half(11)[...]
        for n in range(1, self.COPIES):
            self.copy(n).wait_send()


class Norm:
    COPIES = 10

    def __init__(self, place, plane, column, send, recv):
        self.at, self.plane, self.column = place, plane, column
        self.send, self.recv = send, recv

    def copy(self, n):
        at = self.at
        if n < 7:
            ref, to = self.plane.at[at.r], at.plane[n]
        else:
            ref, to = self.column.at[at.z], at.to_z[n - 7]
        return remote(ref, ref, self.send.at[n], self.recv.at[n], to)

    def start(self, tile):
        self.plane[self.at.r] = tile
        for n in range(7):
            self.copy(n).start()

    def total(self, ref, ns):
        for n in ns:
            self.copy(n).wait_recv()
        total = ref[0]
        for n in range(1, ref.shape[0]):
            total = total + ref[n]
        return total

    def step(self):
        self.column[self.at.z] = self.total(self.plane, range(7))
        for n in range(7, self.COPIES):
            self.copy(n).start()

    def last(self):
        total = self.total(self.column, range(7, self.COPIES))
        for n in range(self.COPIES):
            self.copy(n).wait_send()
        return total


LANDING = (
    (NX, 8, DEEP, D),
    (8, HALF, D),
    (NX, NZ, HALF, D),
    (NZ, DEEP, D),
    (3, DEEP, D),
)


def stage_rows(qkv, out, up, down, l):
    return (
        [(qkv.at[l, :, pl.ds(j * D, D)], 16 * j, 16) for j in range(3)]
        + [(out.at[l], 48, 16)]
        + [(up.at[l, :, pl.ds(j * D, D)], 64 + 16 * j, 16) for j in range(4)]
        + [(down.at[l], 128, 64)]
    )


BEGIN, SETUP, START, QKV_HALF, QKV, WINDOWS_HALF, WINDOWS, UP_HALF, UP, DOWN = range(10)
FIRST, SECOND, THIRD, FOURTH, FIFTH, LAST, SEND = range(7)
GATHER_PLAN = {
    (-1, BEGIN): [(FIRST, 0, 0), (FIRST, 0, 1), (FIRST, 0, 2)],
    (-1, SETUP): [(FIRST, 1, 0), (FIRST, 1, 1), (SECOND, 0, 0)],
    (0, START): [(FIRST, 1, 2), (SECOND, 0, 1), (THIRD, 0, 0), (FOURTH, 0, 0), (SECOND, 0, 2), (THIRD, 0, 1), (FIFTH, 0, 0), (LAST, 0, 0), (SECOND, 1, 0), (FOURTH, 0, 1)],
    (0, QKV): [(FIRST, 2, 0), (THIRD, 0, 2), (FIFTH, 0, 1)],
    (0, WINDOWS_HALF): [(SECOND, 1, 1), (LAST, 0, 1)],
    (0, WINDOWS): [(FIRST, 2, 1), (FOURTH, 0, 2)],
    (0, UP_HALF): [(THIRD, 1, 0), (FIFTH, 0, 2), (SECOND, 1, 2)],
    (0, UP): [(FIRST, 2, 2), (LAST, 0, 2), (FOURTH, 1, 0), (SECOND, 2, 0)],
    (0, DOWN): [(THIRD, 1, 1), (FIFTH, 1, 0)],
    (1, START): [(LAST, 1, 0), (FOURTH, 1, 1)],
    (1, QKV_HALF): [(SECOND, 2, 1)],
    (1, QKV): [(THIRD, 1, 2), (FIFTH, 1, 1)],
    (1, WINDOWS_HALF): [(LAST, 1, 1)],
    (1, WINDOWS): [(SECOND, 2, 2), (FOURTH, 1, 2)],
    (1, UP_HALF): [(THIRD, 2, 0), (FIFTH, 1, 2), (LAST, 1, 2)],
    (1, UP): [(FOURTH, 2, 0)],
    (1, DOWN): [(THIRD, 2, 1), (FIFTH, 2, 0)],
    (2, START): [(LAST, 2, 0), (FOURTH, 2, 1)],
    (2, QKV): [(THIRD, 2, 2), (FIFTH, 2, 1)],
    (2, WINDOWS_HALF): [(LAST, 2, 1)],
    (2, WINDOWS): [(FOURTH, 2, 2)],
    (2, UP_HALF): [(FIFTH, 2, 2), (LAST, 2, 2)],
}


def train_kernel(refs, alone):
    k = Kit(**refs)

    def kept(names, l, back):
        copies = []
        for name in names:
            here, there = refs[name], refs["keep_" + name].at[l]
            src, dst = (there, here) if back else (here, there)
            copies.append(pltpu.make_async_copy(src, dst, k.keep_sem.at[KEEP.index(name)]))
        return copies

    def start(copies):
        for copy in copies:
            copy.start()

    def wait(copies):
        for copy in copies:
            copy.wait()

    def kept_x(back):
        here, there = k.xs.at[0], k.keep_x
        src, dst = (there, here) if back else (here, there)
        return [pltpu.make_async_copy(src, dst, k.keep_sem.at[len(KEEP)])]

    arrays = [(l, n) for l in range(LAYERS) for n in (0, 1)]
    parts = [(l, part) for l in range(LAYERS) for part in range(PARTS)]
    weights = (k.wa, k.wf)
    if alone:
        loads = [
            pltpu.make_async_copy((k.all_a, k.all_f)[n].at[l], weights[n].at[l], k.load_sem.at[2 * l + n])
            for l, n in arrays
        ]
        stores = [
            pltpu.make_async_copy(
                weights[n].at[l + 1 - n], (k.grad_a, k.grad_f)[n].at[l], k.load_sem.at[2 * l + n]
            )
            for l, n in arrays
        ]
        start(loads)
    else:
        place = Place()
        gather = Gather(place, weights, k.gather_send, k.gather_recv)
        reduce = Reduce(
            place, weights, k.landing, k.reduce_send, k.reduce_recv, k.credit
        )
        sums = Total(place, k.mid, SMALL, k.sum_send, k.sum_recv)
        norm = Norm(place, k.norm_plane, k.norm_column, k.norm_send, k.norm_recv)

    def run(plan):
        stages = (
            gather.first,
            gather.second,
            gather.third,
            gather.fourth,
            gather.fifth,
            gather.last,
        )
        for stage, l, part in plan:
            stages[stage](l, part)

    def poll(l, point):
        if alone:
            return
        for layer in range(LAYERS):
            plan = GATHER_PLAN.get((layer, point))
            if plan:

                @pl.when(l == layer)
                def _(plan=plan):
                    run(plan)

    if not alone:
        staged = []
        for l in range(LAYERS):
            for n, (src, row, count) in enumerate(stage_rows(k.qkv_w, k.out_w, k.up_w, k.down_w, l)):
                dst = k.xs.at[2, pl.ds(l * PACK + row, count), :]
                staged.append(pltpu.make_async_copy(src, dst, k.stage_sem.at[l, n]))
        start(staged)
        place.barrier()
        for l in range(LAYERS):
            wait(staged[9 * l : 9 * l + 9])
            row = l * PACK
            for part in range(PARTS):
                array, first = part_ref(weights, part)
                mine = k.xs[2, row + DEEP * part : row + DEEP * (part + 1), :].astype(LOWER)
                array[l, place.a, place.b, first : first + DEEP, :] = mine
                if (FIRST, l, part) in GATHER_PLAN[-1, BEGIN]:
                    gather.first(l, part)
        k.squares_sum[...] = jnp.zeros_like(k.squares_sum)

    setup_stage(k)
    start(kept_x(False))
    if not alone:
        run(GATHER_PLAN[-1, SETUP])

    def forward(l, carry):
        if alone:
            pltpu.make_async_copy(k.all_a.at[l], k.wa.at[l], k.load_sem.at[2 * l]).wait()

        @pl.when(l > 0)
        def _():
            wait(kept(KEEP_ATTN, l - 1, False))

        poll(l, START)
        forward_qkv(k, l, lambda: poll(l, QKV_HALF))
        poll(l, QKV)
        forward_windows(k, l, lambda: poll(l, WINDOWS_HALF))

        @pl.when(l < LAYERS - 1)
        def _():
            start(kept(KEEP_ATTN, l, False))

        @pl.when(l > 0)
        def _():
            wait(kept(KEEP_FFN, l - 1, False))

        @pl.when(l == 1)
        def _():
            wait(kept_x(False))

        if alone:
            pltpu.make_async_copy(k.all_f.at[l], k.wf.at[l], k.load_sem.at[2 * l + 1]).wait()
        poll(l, WINDOWS)
        forward_up(k, l, lambda: poll(l, UP_HALF))
        poll(l, UP)
        forward_down(k, l, (l + 1) % 2 + l // 2)

        @pl.when(l < LAYERS - 1)
        def _():
            start(kept(KEEP_FFN, l, False))

        poll(l, DOWN)
        return carry

    lax.fori_loop(0, LAYERS, forward, 0)
    if not alone:
        for l, part in parts:
            gather.sent(l, part)
    grad = 2
    head_stage(k, grad)

    def run_reduce(stage, l, part):
        if stage == THIRD:
            reduce.third(l, part, k.shard)
        elif stage == LAST:
            reduce.last(l, part, k.shard, k.squares_sum)
        else:
            {SEND: reduce.start, FIRST: reduce.first, SECOND: reduce.second}[stage](l, part)

    def backward(n, carry):
        l = LAYERS - 1 - n

        def behind(name, *stages):
            @pl.when(n > 0)
            def _():
                for stage, part, *more in stages:
                    stage(l + 1, part, *more)

        @pl.when(n > 0)
        def _():
            wait(kept(KEEP_FFN, l, True))

        def now(stage, part):
            if not alone:
                run_reduce(stage, l, part)

        def then(stage, part):
            if not alone:

                @pl.when(n > 0)
                def _():
                    run_reduce(stage, l + 1, part)

        def in_ffn():
            then(LAST, 2)

        def in_windows():
            now(SECOND, 2)
            then(LAST, 0)

        backward_ffn(k, l, grad, in_ffn)
        then(LAST, 1)
        then(SECOND, 0)
        backward_down_grads(k, l)
        now(SEND, 2)
        then(THIRD, 0)
        backward_up_grads(k, l)

        @pl.when(n < LAYERS - 1)
        def _():
            start(kept(KEEP_FFN, l - 1, True))

        now(SEND, 1)
        now(FIRST, 2)

        @pl.when(n > 0)
        def _():
            wait(kept(KEEP_ATTN, l, True))

        backward_out(k, l, grad)
        now(FIRST, 1)
        backward_windows(k, l, in_windows)
        now(THIRD, 2)
        backward_attn_grads(k, l)

        @pl.when(n < LAYERS - 1)
        def _():
            start(kept(KEEP_ATTN, l - 1, True))

        now(SEND, 0)
        now(SECOND, 1)

        @pl.when(n == LAYERS - 1)
        def _():
            wait(kept_x(True))

        backward_input(k, l, grad)

        @pl.when(n == 0)
        def _():
            start(kept_x(True))

        now(FIRST, 0)
        now(THIRD, 1)
        return carry

    lax.fori_loop(0, LAYERS, backward, 0)
    if alone:
        start(stores)
        small_stage(k, k.small_out, grad)
        wait(stores)
        return
    small_stage(k, sums.whole(), grad)
    sums.start()
    reduce.last(0, 2, k.shard, k.squares_sum)
    reduce.second(0, 0)
    sums.step(0)
    reduce.third(0, 0, k.shard)
    sums.step(1)
    reduce.last(0, 1, k.shard, k.squares_sum)
    sums.step(2)
    reduce.last(0, 0, k.shard, k.squares_sum)
    squares = k.squares_sum[...]
    norm.start(sum(squares[:, n * 128 : (n + 1) * 128] for n in range(D // 128)))
    sums.back()
    norm.step()
    sums.last()
    k.small_out[...] = sums.whole()[...]
    k.squares[...] = norm.last()


def train_pass(inputs, weights, alone):
    whole = pl.BlockSpec(memory_space=pltpu.VMEM)
    scalars = pl.BlockSpec(memory_space=pltpu.SMEM)
    anywhere = pl.BlockSpec(memory_space=pl.ANY)
    dma = pltpu.SemaphoreType.DMA
    count = PARTS * LAYERS
    names = ["states", "actions", "returns", "starts", "repeats", "valid"]
    names += ["log_temp", "small", "head_bias"]
    out_shape = {"small_out": ((SMALL, D), WIDE)}
    for name in KEEP:
        shape, dtype = WORK_SHAPES[name]
        out_shape["keep_" + name] = ((LAYERS - 1,) + shape, dtype)
    out_shape["keep_x"] = ((ROWS, D), WIDE)
    scratch = {name: pltpu.VMEM(*shape) for name, shape in WORK_SHAPES.items()}
    scratch["keep_sem"] = dma((len(KEEP) + 1,))
    if alone:
        names += ["all_a", "all_f"]
        out_shape["grad_a"] = ((LAYERS, 4, 8, ATTN, D), LOWER)
        out_shape["grad_f"] = ((LAYERS, 4, 8, FFN, D), LOWER)
        scratch["load_sem"] = dma((count,))
    else:
        names += ["qkv_w", "out_w", "up_w", "down_w"]
        out_shape["shard"] = ((LAYERS, PACK, D), WIDE)
        out_shape["squares"] = ((8, 128), WIDE)
        for part in range(PARTS):
            for n, shape in enumerate(LANDING):
                scratch["land_%d_%d" % (part, n)] = pltpu.VMEM(shape, LOWER)
        scratch["stage_sem"] = dma((LAYERS, 9))
        scratch["squares_sum"] = pltpu.VMEM((8, D), WIDE)
        for name, copies in (("gather", Gather.COPIES), ("reduce", Reduce.COPIES)):
            scratch[name + "_send"] = dma((count, copies))
            scratch[name + "_recv"] = dma((count, copies))
        scratch["credit"] = pltpu.SemaphoreType.REGULAR((PARTS, 8))
        scratch["norm_plane"] = pltpu.VMEM((8, 8, 128), WIDE)
        scratch["norm_column"] = pltpu.VMEM((NZ, 8, 128), WIDE)
        for name, copies in (("sum", Total.COPIES), ("norm", Norm.COPIES)):
            scratch[name + "_send"] = dma((copies,))
            scratch[name + "_recv"] = dma((copies,))
    spaces = dict.fromkeys(("starts", "repeats", "head_bias", "log_temp"), scalars)
    for name in ("all_a", "all_f", "grad_a", "grad_f", "qkv_w", "out_w", "up_w", "down_w"):
        spaces[name] = anywhere
    for name in KEEP + ("x",):
        spaces["keep_" + name] = anywhere
    every = names + list(out_shape) + list(scratch)

    def kernel(*given):
        refs = dict(zip(every, given))
        refs["landing"] = [
            [refs.get("land_%d_%d" % (part, n)) for n in range(len(LANDING))] for part in range(PARTS)
        ]
        train_kernel(refs, alone)

    results = pl.pallas_call(
        kernel,
        name="train_pass",
        out_shape=tuple(jax.ShapeDtypeStruct(*shape) for shape in out_shape.values()),
        in_specs=[spaces.get(name, whole) for name in names],
        out_specs=tuple(spaces.get(name, whole) for name in out_shape),
        scratch_shapes=list(scratch.values()),
        compiler_params=pltpu.CompilerParams(
            vmem_limit_bytes=VMEM_BYTES,
            collective_id=None if alone else 0,
            has_side_effects=not alone,
        ),
        cost_estimate=pl.CostEstimate(
            flops=6 * 10**10, bytes_accessed=4 * 10**7, transcendentals=10**7
        ),
    )(*inputs, *weights)
    return dict(zip(out_shape, results))


def adam_parts(weight, grad, first, second, rate):
    first = BETA_ONE * first + (1.0 - BETA_ONE) * grad
    second = BETA_TWO * second + (1.0 - BETA_TWO) * grad * grad
    fix_one = 1.0 - BETA_ONE**STEP
    fix_two = 1.0 - BETA_TWO**STEP
    fresh = weight - rate * (
        first * (1.0 / fix_one) / (jnp.sqrt(second * (1.0 / fix_two)) + ADAM_EPS) + DECAY * weight
    )
    return fresh, first, second


def adam_kernel(*refs):
    shard, small_grad, squares, groups, log_temp = refs[:5]
    small, small_first, small_second, bias, bias_first, bias_second = refs[5:11]
    mats, firsts, seconds = refs[11:15], refs[15:19], refs[19:23]
    totals, norm, next_temp, s_next, s_first, s_second, b_next, b_first, b_second = refs[23:32]
    m_next, m_copy, m_first, m_second = refs[32:36], refs[36:40], refs[40:44], refs[44:48]
    extra = small_grad[NROWS : NROWS + 3, 0:128]
    lane = iota((1, 128), 1)
    bias_mean = jnp.where(lane < A, extra[1:2], 0.0)
    bias_spread = jnp.where(lane < A, extra[2:3], 0.0)

    def all_sum(v):
        return jnp.sum(jnp.sum(v, 0, keepdims=True), 1, keepdims=True)

    grads = small_grad[0:NROWS, :]
    square = (
        all_sum(squares[0:1, :])
        + all_sum(grads * grads)
        + all_sum(bias_mean * bias_mean)
        + all_sum(bias_spread * bias_spread)
    )
    length = jnp.sqrt(square)
    clip = jnp.minimum(1.0, CLIP / (length + 1e-06))

    def rate_of(l, kind):
        group = jnp.full((1, 1), groups[l, kind], jnp.int32).astype(WIDE)
        return LEARN * jnp.exp2(-group)

    def update(l, kind, rows, cols, grad):
        at = (l, rows, cols)
        fresh, first, second = adam_parts(
            mats[kind][at], clip * grad, firsts[kind][at], seconds[kind][at], rate_of(l, kind)
        )
        m_next[kind][at] = fresh
        m_copy[kind][at] = fresh.astype(LOWER)
        m_first[kind][at] = first
        m_second[kind][at] = second

    every = slice(0, 16)
    for l in range(LAYERS):
        for j in range(3):
            update(l, 0, every, slice(j * D, (j + 1) * D), shard[l, 16 * j : 16 * j + 16, :])
        update(l, 1, every, slice(0, D), shard[l, 48:64, :])
        for j in range(4):
            rows = slice(64 + 16 * j, 80 + 16 * j)
            update(l, 2, every, slice(j * D, (j + 1) * D), shard[l, rows, :])
        update(l, 3, slice(0, 64), slice(0, D), shard[l, 128:192, :])

    s_next[...], s_first[...], s_second[...] = adam_parts(
        small[...], clip * grads, small_first[...], small_second[...], LEARN
    )

    def scalar(v, n):
        return jnp.sum(jnp.where(lane == n, v, 0.0))

    def row(ref):
        v = jnp.zeros((1, 128), WIDE)
        for n in range(2 * A):
            v = jnp.where(lane == n, ref[n], v)
        return v

    grad = bias_mean + pltpu.roll(bias_spread, A, 1)
    results = adam_parts(row(bias), clip * grad, row(bias_first), row(bias_second), LEARN)
    for ref, result in zip((b_next, b_first, b_second), results):
        for n in range(2 * A):
            ref[n] = scalar(result, n)
    sums = extra[0:1]
    for n in range(3):
        totals[n] = scalar(sums, n)
    norm[0] = jnp.sum(length)
    logs = jnp.full((1, 1), log_temp[0], WIDE)
    ratio = jnp.full((1, 1), scalar(sums, 1), WIDE) / jnp.full((1, 1), scalar(sums, 2), WIDE)
    next_temp[0] = jnp.sum(logs - TEMP_RATE * jnp.exp(logs) * (ratio + A))


def adam_all(shard, small_grad, squares, groups, log_temp, smalls, biases, mats, firsts, seconds):
    scalars = pl.BlockSpec(memory_space=pltpu.SMEM)

    whole = pl.BlockSpec(memory_space=pltpu.VMEM)

    def like(array, dtype=WIDE):
        return jax.ShapeDtypeStruct(array.shape, dtype)

    stacks = list(mats) + list(firsts) + list(seconds)
    small, bias = smalls[0], biases[0]
    return pl.pallas_call(
        adam_kernel,
        name="adam",
        out_shape=(
            (jax.ShapeDtypeStruct((3,), WIDE),)
            + (jax.ShapeDtypeStruct((1,), WIDE),) * 2
            + (like(small),) * 3
            + (like(bias),) * 3
            + tuple(like(m) for m in mats)
            + tuple(like(m, LOWER) for m in mats)
            + tuple(like(m) for m in mats) * 2
        ),
        in_specs=[whole] * 3 + [scalars] * 2 + [whole] * 3 + [scalars] * 3 + [whole] * 12,
        out_specs=(scalars,) * 3 + (whole,) * 3 + (scalars,) * 3 + (whole,) * 16,
        compiler_params=pltpu.CompilerParams(vmem_limit_bytes=VMEM_BYTES),
        cost_estimate=pl.CostEstimate(flops=10**7, bytes_accessed=8 * 10**6, transcendentals=10**6),
    )(shard, small_grad, squares, groups, log_temp, *smalls, *biases, *stacks)


def gather_packed(mats, axes, count):
    group = count // BLOCKS
    pieces = []
    for mat in mats:
        rows, wide = mat.shape[1], mat.shape[2] // D
        piece = mat.astype(LOWER).reshape(LAYERS, rows, wide, D)
        piece = lax.all_gather(piece, axes, axis=1, tiled=True)
        piece = piece.reshape(LAYERS, NZ, NY, NX, NC, group * rows, wide, D)
        piece = piece.transpose(0, 4, 3, 2, 1, 6, 5, 7)
        pieces.append(piece.reshape(LAYERS, 4, 8, wide * group * rows, D))
    return jnp.concatenate(pieces[:2], 3), jnp.concatenate(pieces[2:], 3)


def scatter_packed(grads, mats, axes):
    results, first = [], 0
    for n, mat in enumerate(mats):
        rows, wide = mat.shape[1], mat.shape[2] // D
        total = lax.psum(1, axes) * rows
        deep = total // BLOCKS
        first = 0 if n % 2 == 0 else first
        piece = grads[n // 2][:, :, :, first : first + wide * deep].astype(WIDE)
        first += wide * deep
        piece = piece.reshape(LAYERS, NC, NX, NY, NZ, wide, deep, D)
        piece = piece.transpose(0, 4, 3, 2, 1, 6, 5, 7).reshape(LAYERS, total, wide * D)
        results.append(lax.psum_scatter(piece, axes, scatter_dimension=1, tiled=True))
    return results


def local(
    buf_states,
    buf_actions,
    buf_returns,
    window_starts,
    window_repeats,
    valid_steps,
    matrix_groups,
    log_temp,
    small_rows,
    head_bias,
    qkv_weight,
    out_weight,
    up_weight,
    down_weight,
    small_first,
    bias_first,
    qkv_first,
    out_first,
    up_first,
    down_first,
    small_second,
    bias_second,
    qkv_second,
    out_second,
    up_second,
    down_second,
):
    axes = ("dp", "fsdp")
    mats = (qkv_weight, out_weight, up_weight, down_weight)
    firsts = (qkv_first, out_first, up_first, down_first)
    seconds = (qkv_second, out_second, up_second, down_second)
    pass_inputs = (
        buf_states.T,
        buf_actions.T,
        buf_returns[None],
        window_starts,
        window_repeats,
        valid_steps,
        log_temp,
        small_rows,
        head_bias,
    )
    if FF // down_weight.shape[1] == BLOCKS and lax.psum(1, "fsdp") == NX * NC:
        made = train_pass(pass_inputs, mats, False)
        return adam_all(
            made["shard"],
            made["small_out"],
            made["squares"],
            matrix_groups,
            log_temp,
            (small_rows, small_first, small_second),
            (head_bias, bias_first, bias_second),
            mats,
            firsts,
            seconds,
        )
    packed = gather_packed(mats, axes, FF // down_weight.shape[1])
    made = train_pass(pass_inputs, packed, True)
    big = scatter_packed((made["grad_a"], made["grad_f"]), mats, axes)
    small = made["small_out"]
    small = lax.psum(small, axes)
    small_grad, totals = small[:NROWS], small[NROWS, :3]
    bias_grad = jnp.concatenate([small[NROWS + 1, :A], small[NROWS + 2, :A]])
    square = sum((jnp.sum(piece * piece) for piece in big))
    square = (
        lax.psum(square, axes) + jnp.sum(small_grad * small_grad) + jnp.sum(bias_grad * bias_grad)
    )
    grad_norm = jnp.sqrt(square)
    clip = jnp.minimum(1.0, CLIP / (grad_norm + 1e-06))
    rates = LEARN * jnp.exp2(-matrix_groups.astype(WIDE))
    results = [
        adam_parts(
            mats[kind], clip * big[kind], firsts[kind], seconds[kind], rates[:, kind][:, None, None]
        )
        for kind in range(4)
    ]
    small_new = adam_parts(small_rows, clip * small_grad, small_first, small_second, LEARN)
    bias_new = adam_parts(head_bias, clip * bias_grad, bias_first, bias_second, LEARN)
    next_temp = log_temp - TEMP_RATE * jnp.exp(log_temp) * (totals[1] / totals[2] + A)
    return (
        (totals, grad_norm[None], next_temp)
        + small_new
        + bias_new
        + tuple(r[0] for r in results)
        + tuple(r[0].astype(LOWER) for r in results)
        + tuple(r[1] for r in results)
        + tuple(r[2] for r in results)
    )


def solution(mesh):
    rows = P(("dp", "fsdp"), None)
    vector = P(("dp", "fsdp"))
    stack = P(None, ("dp", "fsdp"), None)
    same = P()
    in_specs = (
        (rows, rows, vector, vector, vector, rows)
        + (same,) * 4
        + (stack,) * 4
        + (same,) * 2
        + (stack,) * 4
        + (same,) * 2
        + (stack,) * 4
    )
    out_specs = (same,) * 9 + (stack,) * 16
    return jax.shard_map(local, mesh=mesh, in_specs=in_specs, out_specs=out_specs, check_vma=False)
```

```python
import math

import jax
import jax.numpy as jnp
from jax import lax
from jax.experimental import pallas as pl
from jax.experimental.pallas import tpu as pltpu
from jax.sharding import PartitionSpec as P

D = 512
H = 8
HD = 64
FF = 2048
S = 11
A = 3
K = 20
STEP = 10

EPS = 1e-05
CLIP = 1.0
LEARN = 0.03
BETA_ONE = 0.5
BETA_TWO = 0.7
DECAY = 0.01
ADAM_EPS = 1e-08
TEMP_RATE = 0.1
MASKED = -1e30
HALF_LOG_TAU = 0.5 * math.log(2.0 * math.pi)
GELU_C = math.sqrt(2.0 / math.pi)
GELU_A = 0.044715
HIGH = lax.Precision.HIGHEST
LOWER = jnp.bfloat16
WIDE = jnp.float32

LAYERS = 3
WINS = 16
BUF_DEV = 64
SLOT = 64
ROWS = WINS * SLOT
CHUNK = 512
CHUNKS = ROWS // CHUNK
BLOCKS = 32
PACK = 192
ATTN, FFN = 64, 128
EMB = S + A + 1 + K + 3
FIN = EMB
HEADW = EMB + 2
BASE = EMB + 2 + 2 * A
PER = 9 + FF // D
NROWS = BASE + LAYERS * PER
SMALL = 96
HEAD_AT = 64
EMB_AT = ROWS - 128
VMEM_BYTES = 64 * 1024 * 1024


def dot(a, b, precision=None):
    return lax.dot_general(
        a, b, (((1,), (0,)), ((), ())), precision=precision, preferred_element_type=WIDE
    )


def dot_nt(a, b, precision=None):
    return lax.dot_general(
        a, b, (((1,), (1,)), ((), ())), precision=precision, preferred_element_type=WIDE
    )


def dot_tn(a, b, precision=None):
    return lax.dot_general(
        a, b, (((0,), (0,)), ((), ())), precision=precision, preferred_element_type=WIDE
    )


def iota(shape, dim):
    return lax.broadcasted_iota(jnp.int32, shape, dim)


def col_sum(v):
    return jnp.sum(v, 0, keepdims=True)


def row_mean(v):
    return jnp.mean(v, -1, keepdims=True)


def norm_parts(x):
    center = x - row_mean(x)
    scale = lax.rsqrt(row_mean(center * center) + EPS)
    return center * scale, scale


def norm_back(xhat, scale, gain, grad):
    scaled = grad * gain
    return scale * (scaled - row_mean(scaled) - xhat * row_mean(scaled * xhat))


def token_rows(at, count):
    row = at + iota((count, 128), 0)
    place = row & (SLOT - 1)
    step = (place * 21846) >> 16
    return row >> 6, step, place - 3 * step, place < 3 * K


def chunk_rows(c):
    return pl.ds(pl.multiple_of(c * CHUNK, CHUNK), CHUNK)


def owner_place(i):
    z, y, x, c = i // 8, (i // 4) % 2, (i // 2) % 2, i % 2
    return 2 * c + x, 4 * y + z


class Kit:
    def __init__(self, **refs):
        self.__dict__.update(refs)

    def row(self, l, k):
        return self.lrows[l, k : k + 1, :]

    def blocks(self, ref, l, first, count, owners):
        places = [owner_place(i) for i in owners]
        return jnp.concatenate([ref[l, a, b, first : first + count, :] for a, b in places], 0)

    def w_qkv(self, l, j):
        return self.blocks(self.wa, l, 16 * j, 16, range(BLOCKS))

    def w_out(self, l):
        return self.blocks(self.wa, l, 48, 16, range(BLOCKS))

    def w_up(self, l, j):
        return self.blocks(self.wf, l, 16 * j, 16, range(BLOCKS))

    def w_down(self, l, j):
        return self.blocks(self.wf, l, 64, 64, range(8 * j, 8 * j + 8))


def slot(l):
    return l % 2


def setup_stage(k):
    k.xs[2, EMB_AT:ROWS, :] = jnp.zeros((128, D), WIDE)
    k.xs[2, EMB_AT : EMB_AT + EMB, :] = k.small[0:EMB, :]
    k.headw[...] = jnp.zeros_like(k.headw)
    k.headw[0, 0:A, :] = k.small[HEADW : HEADW + A, :].astype(LOWER)
    k.headw[1, 0:A, :] = k.small[HEADW + A : HEADW + 2 * A, :].astype(LOWER)
    for l in range(LAYERS):
        k.lrows[l, 0:PER, :] = k.small[BASE + l * PER : BASE + (l + 1) * PER, :]
    k.sgl[...] = jnp.zeros_like(k.sgl)
    k.sgh[...] = jnp.zeros_like(k.sgh)
    k.sgw[...] = jnp.zeros_like(k.sgw)

    lane, sub = iota((WINS, 128), 1), iota((WINS, 128), 0)
    k.meta[...] = jnp.zeros_like(k.meta)
    k.meta[0:WINS, 0:K] = k.valid[...].astype(WIDE)
    meta = k.meta[0:WINS, :]
    for w in range(WINS):
        for n, ref in enumerate((k.starts, k.repeats)):
            meta = jnp.where((sub == w) & (lane == K + n), ref[w].astype(WIDE), meta)
    k.meta[0:WINS, :] = meta
    meta = k.meta[...].astype(LOWER)
    k.buf[...] = jnp.zeros_like(k.buf)
    k.buf[0, 0:S, 0:BUF_DEV] = k.states[...]
    k.buf[0, S + A : S + A + 1, 0:BUF_DEV] = k.returns[...]
    k.buf[1, 0:A, 0:BUF_DEV] = k.actions[...]

    def chunk(c, carry):
        rows = chunk_rows(c)
        win, step, kind, real = token_rows(c * CHUNK, CHUNK)
        lane = iota((CHUNK, 128), 1)
        tok = dot((lane == win).astype(WIDE).astype(LOWER), meta)
        start, repeat = tok[:, K : K + 1], tok[:, K + 1 : K + 2]
        valid = jnp.sum(jnp.where(lane == step, tok, 0.0), -1, keepdims=True)
        key = iota((CHUNK, 128), 0) & (SLOT - 1)
        query = lane & (SLOT - 1)
        allowed = (key <= query) & (((valid > 0.5) & real) | (key == query))
        k.bias[rows, :] = jnp.where(allowed, 0.0, MASKED)
        place = start.astype(jnp.int32) + step
        source = ((lane == place) & real).astype(WIDE)
        raw = dot_nt(source, k.buf[0], HIGH)
        acts = dot_nt(source, k.buf[1], HIGH)
        mine = (
            ((lane < S) & (kind == 1))
            | ((lane >= S) & (lane < S + A) & (kind == 2))
            | ((lane == S + A) & (kind == 0))
        )
        raw = raw + pltpu.roll(acts, S, 1)
        marks = ((lane == S + A + 1 + step) | (lane == S + A + 1 + K + kind)) & real
        feats = jnp.where(mine, raw, 0.0) + marks.astype(WIDE)
        weight = jnp.where((kind == 1) & real, repeat * valid, 0.0)
        acts = pltpu.roll(acts, HEAD_AT, 1)
        ours = (lane >= HEAD_AT) & (lane < HEAD_AT + A)
        feats = jnp.where(ours, acts, jnp.where(lane == HEAD_AT + A, weight, feats))
        k.feats[rows, :] = feats
        k.xs[0, rows, :] = dot(feats, k.xs[2, EMB_AT:ROWS, :], HIGH)
        return carry

    lax.fori_loop(0, CHUNKS, chunk, 0)


def stack_pair(v, first):
    zero = jnp.zeros_like(v)
    return jnp.concatenate([jnp.where(first, v, zero), jnp.where(first, zero, v)], 0)


def join_pair(v, first):
    return jnp.where(first, v[:SLOT], v[SLOT:])


def window_rows(w):
    return pl.ds(pl.multiple_of(w * SLOT, SLOT), SLOT)


def each_chunk(body, between=None):
    def step(c, carry):
        body(c, chunk_rows(c))
        if between is not None:

            @pl.when(c < CHUNKS - 1)
            def _():
                between()

        return carry

    lax.fori_loop(0, CHUNKS, step, 0)


def each_pair(body, between=None):
    def pair(n, carry):
        chains = [
            (2 * n + w, window_rows(2 * n + w), slice(p * 128, (p + 1) * 128))
            for w in range(2)
            for p in range(H // 2)
        ]
        body(pl.ds(pl.multiple_of(n * 128, 128), 128), chains)
        if between is not None:

            @pl.when(n == WINS // 4 - 1)
            def _():
                between()

        return carry

    lax.fori_loop(0, WINS // 2, pair, 0)


def forward_qkv(k, l, between):
    def chunk(c, rows):
        xhat, _ = norm_parts(k.xs[slot(l), rows, :])
        normed = (xhat * k.row(l, 0) + k.row(l, 1)).astype(LOWER)
        k.normed_t[:, rows] = normed.T
        for j in range(3):
            part = dot(normed, k.w_qkv(l, j)) + k.row(l, 4 + j)
            k.qkv[rows, j * D : (j + 1) * D] = part.astype(LOWER)

    each_chunk(chunk, between)


def qkv_part(k, n, rows, at):
    return k.qkv[rows, n * D + at.start : n * D + at.stop]


def forward_windows(k, l, between):
    first = iota((SLOT, 128), 1) < HD
    scale = jnp.asarray(HD**-0.5, LOWER)

    def pair(both, chains):
        query = [stack_pair(qkv_part(k, 0, rows, at) * scale, first) for _, rows, at in chains]
        scores = [
            dot_nt(qkv_part(k, 1, rows, at), q) + k.bias[rows, :]
            for q, (_, rows, at) in zip(query, chains)
        ]
        peaks = [jnp.max(s, 0, keepdims=True) for s in scores]
        expos = [jnp.exp(s - peak) for s, peak in zip(scores, peaks)]
        totals = [jnp.sum(e, 0, keepdims=True) for e in expos]
        probs = [(e * (1.0 / total)).astype(LOWER) for e, total in zip(expos, totals)]
        outs = [dot_tn(p, qkv_part(k, 2, rows, at)) for p, (_, rows, at) in zip(probs, chains)]
        for peak, total, out, (w, rows, at) in zip(peaks, totals, outs, chains):
            p = at.start // 128
            k.logs[l, w, p : p + 1, :] = peak + jnp.log(total)
            k.left[rows, at] = join_pair(out, first).astype(LOWER)
        k.mixed_t[:, both] = k.left[both, :].T

    each_pair(pair, between)


def forward_up(k, l, between):
    def chunk(c, rows):
        mid = k.xs[slot(l), rows, :] + dot(k.left[rows, :], k.w_out(l)) + k.row(l, 7)
        k.mid[rows, :] = mid
        xhat, _ = norm_parts(mid)
        second = (xhat * k.row(l, 2) + k.row(l, 3)).astype(LOWER)
        k.second_t[:, rows] = second.T
        ahead = dot(second, k.w_up(l, 0))
        for j in range(4):
            cols = slice(j * D, (j + 1) * D)
            h = ahead + k.row(l, 8 + j)
            if j < 3:
                ahead = dot(second, k.w_up(l, j + 1))
            square = h * h
            over = 1.0 + jnp.tanh(h * (GELU_C + GELU_C * GELU_A * square))
            half = 0.5 * h
            acted = (half * over).astype(LOWER)
            slope = over * (0.5 + half * (2.0 - over) * (GELU_C + 3.0 * GELU_A * GELU_C * square))
            k.work[rows, cols] = acted
            k.slope[rows, cols] = slope.astype(LOWER)
            k.act_t[cols, rows] = acted.T

    each_chunk(chunk, between)


def forward_down(k, l, dest):
    def chunk(c, rows):
        w_down = jnp.concatenate([k.w_down(l, j) for j in range(4)], 0)
        k.xs[dest, rows, :] = k.mid[rows, :] + k.row(l, 12) + dot(k.work[rows, :], w_down)

    each_chunk(chunk)


def head_stage(k, at):
    gain, bias = k.small[FIN : FIN + 1, :], k.small[FIN + 1 : FIN + 2, :]
    lane = iota((CHUNK, 128), 1)
    keep = lane < A

    def bias_row(first):
        row = jnp.zeros((1, 128), WIDE)
        at = iota((1, 128), 1)
        for a in range(A):
            row = jnp.where(at == a, k.head_bias[first + a], row)
        return row

    bias_mean, bias_spread = bias_row(0), bias_row(A)
    temp = jnp.exp(jnp.full((1, 128), k.log_temp[0], WIDE))

    def chunk(c, carry):
        rows = chunk_rows(c)
        xhat, scale = norm_parts(k.xs[at, rows, :])
        feats = (xhat * gain + bias).astype(LOWER)
        mean = dot_nt(feats, k.headw[0]) + bias_mean
        spread = jnp.tanh(dot_nt(feats, k.headw[1]) + bias_spread)
        acts = pltpu.roll(k.feats[rows, :], 128 - HEAD_AT, 1)
        weight = acts[:, A : A + 1]
        acts = jnp.where(keep, acts, 0.0)
        target = 0.5 * (jnp.log(1.0 + acts) - jnp.log(1.0 - acts))
        shrink = jnp.exp(-spread)
        zed = (target - mean) * shrink
        terms = 0.5 * zed * zed + spread + HALF_LOG_TAU + jnp.log(1.0 - acts * acts)
        nll = jnp.sum(jnp.where(keep, terms, 0.0), -1, keepdims=True)
        entropy = jnp.sum(jnp.where(keep, spread, 0.0), -1, keepdims=True) + A * (0.5 + HALF_LOG_TAU)
        loss = weight * (nll - temp * entropy)
        sums = jnp.where(lane == 0, loss, jnp.where(lane == 1, weight * entropy, jnp.where(lane == 2, weight, 0.0)))
        d_mean = jnp.where(keep, weight * (-zed * shrink), 0.0).astype(LOWER)
        d_spread = weight * (1.0 - zed * zed - temp) * (1.0 - spread * spread)
        d_spread = jnp.where(keep, d_spread, 0.0).astype(LOWER)
        k.sgh[2:3, 0:128] += col_sum(sums)
        k.sgh[3:4, 0:128] += col_sum(d_mean.astype(WIDE))
        k.sgh[4:5, 0:128] += col_sum(d_spread.astype(WIDE))
        k.sgw[0] += dot_tn(d_mean, feats)[0:8]
        k.sgw[1] += dot_tn(d_spread, feats)[0:8]
        d_feats = dot(d_mean, k.headw[0]) + dot(d_spread, k.headw[1])
        k.sgh[0:1, :] += col_sum(d_feats * xhat)
        k.sgh[1:2, :] += col_sum(d_feats)
        k.xs[at, rows, :] = norm_back(xhat, scale, gain, d_feats)
        return carry

    lax.fori_loop(0, CHUNKS, chunk, 0)


def store_blocks(ref, l, owners, first, count, value):
    value = value.astype(LOWER)
    for n, i in enumerate(owners):
        a, b = owner_place(i)
        ref[l, a, b, first : first + count, :] = value[n * count : (n + 1) * count]


def backward_ffn(k, l, grad, between=None):
    def chunk(c, rows):
        d_down = k.xs[grad, rows, :].astype(LOWER)
        k.dout[rows, :] = d_down
        k.sgl[l, 12:13, :] += col_sum(d_down.astype(WIDE))
        d_second = jnp.zeros((CHUNK, D), WIDE)
        ahead = dot_nt(d_down, k.w_down(l, 0))
        for j in range(4):
            cols = slice(j * D, (j + 1) * D)
            d_acted = ahead
            if j < 3:
                ahead = dot_nt(d_down, k.w_down(l, j + 1))
            d_hidden = (d_acted * k.slope[rows, cols].astype(WIDE)).astype(LOWER)
            k.work[rows, cols] = d_hidden
            k.sgl[l, 8 + j : 9 + j, :] += col_sum(d_hidden.astype(WIDE))
            d_second = d_second + dot_nt(d_hidden, k.w_up(l, j))
        xhat, scale = norm_parts(k.mid[rows, :])
        k.sgl[l, 2:3, :] += col_sum(d_second * xhat)
        k.sgl[l, 3:4, :] += col_sum(d_second)
        k.xs[grad, rows, :] += norm_back(xhat, scale, k.row(l, 2), d_second)

    each_chunk(chunk, between)


def backward_down_grads(k, l):
    for j in range(4):
        part = dot(k.act_t[j * D : (j + 1) * D, :], k.dout[...])
        store_blocks(k.wf, l, range(8 * j, 8 * j + 8), 64, 64, part)


def backward_up_grads(k, l):
    for j in range(4):
        part = dot(k.second_t[...], k.work[:, j * D : (j + 1) * D])
        store_blocks(k.wf, l, range(BLOCKS), 16 * j, 16, part)


def backward_out(k, l, grad):
    def before(c, rows):
        d_branch = k.xs[grad, rows, :].astype(LOWER)
        k.left[rows, :] = d_branch
        k.sgl[l, 7:8, :] += col_sum(d_branch.astype(WIDE))
        k.dout[rows, :] = dot_nt(d_branch, k.w_out(l)).astype(LOWER)

    each_chunk(before)
    store_blocks(k.wa, l + 1, range(BLOCKS), 48, 16, dot(k.mixed_t[...], k.left[...]))


def backward_windows(k, l, between):
    first = iota((SLOT, 128), 1) < HD
    scale = HD**-0.5
    low = jnp.asarray(scale, LOWER)

    def pair(both, chains):
        query = [stack_pair(qkv_part(k, 0, rows, at) * low, first) for _, rows, at in chains]
        d_mixed = [stack_pair(k.dout[rows, at], first) for _, rows, at in chains]
        shift = [
            k.bias[rows, :] - k.logs[l, w, at.start // 128 : at.start // 128 + 1, :]
            for w, rows, at in chains
        ]
        scores = [dot_nt(qkv_part(k, 1, rows, at), q) for q, (_, rows, at) in zip(query, chains)]
        d_probs = [dot_nt(qkv_part(k, 2, rows, at), d) for d, (_, rows, at) in zip(d_mixed, chains)]
        probs = [jnp.exp(s + more) for s, more in zip(scores, shift)]
        d_values = [dot(p.astype(LOWER), d) for p, d in zip(probs, d_mixed)]
        inner = [p * d for p, d in zip(probs, d_probs)]
        sums = [jnp.sum(i, 0, keepdims=True) for i in inner]
        d_scores = [(i - p * t).astype(LOWER) for i, p, t in zip(inner, probs, sums)]
        d_keyed = [dot(d, q) for d, q in zip(d_scores, query)]
        d_query = [dot_tn(d, qkv_part(k, 1, rows, at)) for d, (_, rows, at) in zip(d_scores, chains)]
        for n, (_, rows, at) in enumerate(chains):
            values = (join_pair(d_query[n], first) * scale, d_keyed[n], d_values[n])
            for m, value in enumerate(values):
                k.work[rows, m * D + at.start : m * D + at.stop] = value.astype(LOWER)

    each_pair(pair, between)


def backward_attn_grads(k, l):
    for j in range(3):
        part = dot(k.normed_t[...], k.work[:, j * D : (j + 1) * D])
        store_blocks(k.wa, l + 1, range(BLOCKS), 16 * j, 16, part)


def backward_input(k, l, grad):
    def chunk(c, rows):
        d_normed = jnp.zeros((CHUNK, D), WIDE)
        for j in range(3):
            d_part = k.work[rows, j * D : (j + 1) * D]
            k.sgl[l, 4 + j : 5 + j, :] += col_sum(d_part.astype(WIDE))
            d_normed = d_normed + dot_nt(d_part, k.w_qkv(l, j))
        xhat, scale = norm_parts(k.xs[slot(l), rows, :])
        k.sgl[l, 0:1, :] += col_sum(d_normed * xhat)
        k.sgl[l, 1:2, :] += col_sum(d_normed)
        k.xs[grad, rows, :] += norm_back(xhat, scale, k.row(l, 0), d_normed)

    each_chunk(chunk)


def small_stage(k, out, grad):
    out[...] = jnp.zeros_like(out)
    out[0:EMB, :] = dot_tn(k.feats[...], k.xs[grad], HIGH)[0:EMB]
    out[FIN : FIN + 2, :] = k.sgh[0:2, :]
    out[HEADW : HEADW + A, :] = k.sgw[0, 0:A, :]
    out[HEADW + A : HEADW + 2 * A, :] = k.sgw[1, 0:A, :]
    for l in range(LAYERS):
        out[BASE + l * PER : BASE + (l + 1) * PER, :] = k.sgl[l, 0:PER, :]
    out[NROWS : NROWS + 3, :] = k.sgh[2:5, :]


WORK_SHAPES = dict(
    wa=((LAYERS + 1, 4, 8, ATTN, D), LOWER),
    wf=((LAYERS, 4, 8, FFN, D), LOWER),
    xs=((3, ROWS, D), WIDE),
    qkv=((ROWS, 3 * D), LOWER),
    normed_t=((D, ROWS), LOWER),
    mixed_t=((D, ROWS), LOWER),
    slope=((ROWS, FF), LOWER),
    act_t=((FF, ROWS), LOWER),
    second_t=((D, ROWS), LOWER),
    mid=((ROWS, D), WIDE),
    logs=((LAYERS, WINS, 8, 128), WIDE),
    work=((ROWS, FF), LOWER),
    left=((ROWS, D), LOWER),
    dout=((ROWS, D), LOWER),
    feats=((ROWS, 128), WIDE),
    bias=((ROWS, 128), WIDE),
    headw=((2, 128, D), LOWER),
    lrows=((LAYERS, 16, D), WIDE),
    sgl=((LAYERS, 16, D), WIDE),
    sgh=((8, D), WIDE),
    sgw=((2, 8, D), WIDE),
    meta=((128, 128), WIDE),
    buf=((2, 128, 128), WIDE),
)
KEEP_ATTN = ("qkv", "normed_t", "mixed_t")
KEEP_FFN = ("slope", "act_t", "second_t", "mid")
KEEP = KEEP_ATTN + KEEP_FFN


MESH = pl.DeviceIdType.MESH
NZ, NY, NX, NC = 4, 2, 2, 2
NR = NY * NX * NC
SHARD = PACK
PARTS, DEEP = 3, 64
HALF = DEEP // 2


class Place:
    def __init__(self):
        dp, fsdp = lax.axis_index("dp"), lax.axis_index("fsdp")
        self.z, self.y = dp // NY, dp % NY
        self.x, self.c = fsdp // NC, fsdp % NC
        self.a, self.b = 2 * self.c + self.x, 4 * self.y + self.z
        self.r = 4 * self.y + fsdp
        self.to_z = [(((self.z + d) % NZ) * NY + self.y, fsdp) for d in range(1, NZ)]
        self.odd = self.z % 2
        self.to_pair = ((self.z + 1 - 2 * self.odd) * NY + self.y, fsdp)
        self.plane = []
        for d in range(1, 8):
            y, x, c = [
                1 - v if d & bit else v for v, bit in ((self.y, 4), (self.x, 2), (self.c, 1))
            ]
            self.plane.append((self.z * NY + y, x * NC + c))
        self.to_c, self.to_x, self.to_y = self.plane[0], self.plane[1], self.plane[3]

    def barrier(self):
        sem = pltpu.get_barrier_semaphore()
        for partner in self.plane + self.to_z:
            pl.semaphore_signal(sem, inc=1, device_id=partner, device_id_type=MESH)
        pl.semaphore_wait(sem, len(self.plane) + len(self.to_z))


def remote(src, dst, send, recv, to):
    return pltpu.make_async_remote_copy(
        src_ref=src, dst_ref=dst, send_sem=send, recv_sem=recv, device_id=to, device_id_type=MESH
    )


def part_ref(weights, part):
    return weights[min(part, 1)], (0, 0, DEEP)[part]


class Gather:
    COPIES = 13

    def __init__(self, place, weights, send, recv):
        self.at, self.weights, self.send, self.recv = place, weights, send, recv

    def copy(self, l, part, n):
        at = self.at
        array, row = part_ref(self.weights, part)
        a, b, rows, to = at.a, pl.ds(4 * at.y, 4), pl.ds(row, DEEP), at.to_c
        if n < 3:
            b, to = at.b, at.to_z[n]
        elif n < 5:
            to = (at.to_x, at.to_y)[n - 3]
        if n in (6, 8, 10, 11, 12):
            a = 2 * at.c + 1 - at.x
        if n in (7, 9, 10, 11, 12):
            b = pl.ds(4 * (1 - at.y), 4)
        if n in (6, 7):
            first = row + at.odd * HALF + (n - 6) * (HALF // 2)
            rows = pl.ds(pl.multiple_of(first, HALF // 2), HALF // 2)
            to = (at.to_y, at.to_x)[n - 6]
        if n in (10, 11):
            rows = pl.ds(pl.multiple_of(row + at.odd * HALF, HALF), HALF)
        if n == 11:
            to = at.to_pair
        if n == 12:
            rows = pl.ds(pl.multiple_of(row + (1 - at.odd) * HALF, HALF), HALF)
        ref = array.at[l, a, b, rows, :]
        q = PARTS * l + part
        return remote(ref, ref, self.send.at[q, n], self.recv.at[q, n], to)

    def start(self, l, part, *ns):
        for n in ns:
            self.copy(l, part, n).start()

    def wait(self, l, part, *ns):
        for n in ns:
            self.copy(l, part, n).wait_recv()

    def first(self, l, part):
        self.start(l, part, 0, 1, 2)

    def second(self, l, part):
        self.wait(l, part, 0, 1, 2)
        self.start(l, part, 3, 4, 5)

    def third(self, l, part):
        self.wait(l, part, 3)
        self.start(l, part, 6, 8)
        self.wait(l, part, 4)
        self.start(l, part, 7, 9)

    def fourth(self, l, part):
        self.wait(l, part, 6, 7)
        self.start(l, part, 11, 10)

    def fifth(self, l, part):
        self.wait(l, part, 11)
        self.start(l, part, 12)

    def last(self, l, part):
        self.wait(l, part, 5, 8, 9, 10, 12)

    def sent(self, l, part):
        for n in range(self.COPIES):
            self.copy(l, part, n).wait_send()


class Reduce:
    COPIES = 8

    def __init__(self, place, grads, landing, send, recv, credit):
        self.at, self.grads, self.landing = place, grads, landing
        self.send, self.recv, self.credit = send, recv, credit

    def refs(self, l, part):
        array, row = part_ref(self.grads, part)
        grads = array.at[l + 1 - min(part, 1), :, :, pl.ds(row, DEEP), :]
        return (grads, *self.landing[part])

    def copy(self, l, part, n):
        at, half = self.at, HALF
        g, r0, r1a, r1b, r2, r3 = self.refs(l, part)
        top, low, other = pl.ds(0, half), pl.ds(half, half), pl.ds(4 * (1 - at.y), 4)
        if n == 0:
            src, dst, to = g.at[pl.ds(2 * (1 - at.c), 2)], r0, at.to_c
        elif n == 1:
            src, dst, to = r0.at[1 - at.x, :, top, :], r1a, at.to_x
        elif n == 2:
            src, dst, to = r0.at[:, other, low, :], r1b, at.to_y
        elif n == 3:
            src, dst, to = r1a.at[other], r2.at[:, top, :], at.to_y
        elif n == 4:
            src, dst, to = r1b.at[1 - at.x], r2.at[:, low, :], at.to_x
        else:
            src, dst, to = r2.at[(at.z + n - 4) % NZ], r3.at[n - 5], at.to_z[n - 5]
        q = PARTS * l + part
        return remote(src, dst, self.send.at[q, n], self.recv.at[q, n], to)

    def may_send(self, l, part, *partners):
        @pl.when(l < LAYERS - 1)
        def _():
            for n in partners:
                pl.semaphore_wait(self.credit.at[part, n], 1)

    def allow(self, l, part, *credits):
        at = self.at

        @pl.when(l > 0)
        def _():
            for n, to in credits:
                pl.semaphore_signal(
                    self.credit.at[part, n], inc=1, device_id=to, device_id_type=MESH
                )

    def start(self, l, part):
        self.may_send(l, part, 0)
        self.copy(l, part, 0).start()

    def first(self, l, part):
        at, half = self.at, HALF
        g, r0, _, _, _, _ = self.refs(l, part)
        top, low = pl.ds(0, half), pl.ds(half, half)
        self.copy(l, part, 0).wait_recv()

        x = 1 - at.x
        total = g[2 * at.c + x, :, top].astype(WIDE) + r0[x, :, top].astype(WIDE)
        r0[x, :, top] = total.astype(LOWER)
        self.may_send(l, part, 1, 2)
        self.copy(l, part, 1).start()
        other = pl.ds(4 * (1 - at.y), 4)
        for x in range(NX):
            total = g[2 * at.c + x, other, low].astype(WIDE) + r0[x, other, low].astype(WIDE)
            r0[x, other, low] = total.astype(LOWER)
        self.copy(l, part, 2).start()

    def second(self, l, part):
        at, half = self.at, HALF
        g, r0, r1a, r1b, _, _ = self.refs(l, part)
        top, low = pl.ds(0, half), pl.ds(half, half)

        x, other, column = 1 - at.x, pl.ds(4 * (1 - at.y), 4), pl.ds(4 * at.y, 4)
        self.copy(l, part, 1).wait_recv()
        total = g[at.a, other, top].astype(WIDE) + r0[at.x, other, top].astype(WIDE)
        r1a[other] = (total + r1a[other].astype(WIDE)).astype(LOWER)
        self.may_send(l, part, 6, 7)
        self.copy(l, part, 3).start()
        self.copy(l, part, 2).wait_recv()
        total = g[2 * at.c + x, column, low].astype(WIDE) + r0[x, column, low].astype(WIDE)
        r1b[x] = (total + r1b[x].astype(WIDE)).astype(LOWER)
        self.copy(l, part, 4).start()

    def chip_sums(self, l, part, z):
        at, half = self.at, HALF
        g, r0, r1a, r1b, r2, _ = self.refs(l, part)
        top, low, b = pl.ds(0, half), pl.ds(half, half), 4 * at.y + z
        upper = g[at.a, b, top].astype(WIDE) + r0[at.x, b, top].astype(WIDE)
        lower = g[at.a, b, low].astype(WIDE) + r0[at.x, b, low].astype(WIDE)
        return (
            upper + r1a[b].astype(WIDE) + r2[z, top].astype(WIDE),
            lower + r1b[at.x, z].astype(WIDE) + r2[z, low].astype(WIDE),
        )

    def third(self, l, part, out):
        at, half, row = self.at, HALF, DEEP * part
        r2 = self.landing[part][3]
        for n in (3, 4):
            self.copy(l, part, n).wait_recv()
        self.may_send(l, part, 3, 4, 5)
        for n in range(3):
            z = (at.z + n + 1) % NZ
            upper, lower = self.chip_sums(l, part, z)
            r2[z, pl.ds(0, half)] = upper.astype(LOWER)
            r2[z, pl.ds(half, half)] = lower.astype(LOWER)
            self.copy(l, part, 5 + n).start()
        upper, lower = self.chip_sums(l, part, at.z)
        out[l, row : row + half, :] = upper
        out[l, row + half : row + 2 * half, :] = lower
        for n in range(5):
            self.copy(l, part, n).wait_send()
        self.allow(l, part, (0, at.to_c), (1, at.to_x), (2, at.to_y))

    def last(self, l, part, out, squares):
        at, row = self.at, DEEP * part
        r3 = self.landing[part][4]
        rows = slice(row, row + DEEP)
        total = out[l, rows, :]
        for n in range(3):
            self.copy(l, part, 5 + n).wait_recv()
            total = total + r3[n].astype(WIDE)
        out[l, rows, :] = total
        squares[0:1, :] += col_sum(total * total)
        for n in range(5, self.COPIES):
            self.copy(l, part, n).wait_send()
        late = [(6, at.to_x), (7, at.to_y)] + [(5 - n, at.to_z[n]) for n in range(3)]
        self.allow(l, part, *late)


class Total:
    COPIES = 7

    def __init__(self, place, ref, rows, send, recv):
        self.at, self.ref, self.rows = place, ref, rows // 2
        self.send, self.recv = send, recv

    def half(self, n):
        return self.ref.at[pl.ds(pl.multiple_of(n * self.rows, 8), self.rows), :]

    def whole(self):
        return self.ref.at[pl.ds(0, 2 * self.rows), :]

    def copy(self, n):
        at = self.at
        mine, other = self.half(at.c), self.half(1 - at.c)
        src, dst, to = (
            (other, self.half(2), at.to_c),
            (self.half(8), self.half(3), at.to_x),
            (self.half(9), self.half(4), at.to_y),
            (self.half(10), self.half(5), at.to_z[0]),
            (self.half(10), self.half(6), at.to_z[1]),
            (self.half(10), self.half(7), at.to_z[2]),
            (mine, self.half(11), at.to_c),
        )[n]
        return remote(src, dst, self.send.at[n], self.recv.at[n], to)

    def start(self):
        self.copy(0).start()

    def step(self, n):
        self.copy(n).wait_recv()
        own = self.half(self.at.c) if n == 0 else self.half(7 + n)
        self.half(8 + n)[...] = own[...] + self.half(2 + n)[...]
        for m in ((1,), (2,), (3, 4, 5))[n]:
            self.copy(m).start()

    def back(self):
        for m in (3, 4, 5):
            self.copy(m).wait_recv()
        self.copy(0).wait_send()
        total = None
        for z in range(NZ):
            term = self.half(10)[...]
            for n in range(3):
                from_z = (self.at.z + NZ - 1 - n) % NZ
                term = jnp.where(from_z == z, self.half(5 + n)[...], term)
            total = term if total is None else total + term
        self.half(self.at.c)[...] = total
        self.copy(6).start()

    def last(self):
        self.copy(6).wait_recv()
        self.half(1 - self.at.c)[...] = self.half(11)[...]
        for n in range(1, self.COPIES):
            self.copy(n).wait_send()


class Norm:
    COPIES = 10

    def __init__(self, place, plane, column, send, recv):
        self.at, self.plane, self.column = place, plane, column
        self.send, self.recv = send, recv

    def copy(self, n):
        at = self.at
        if n < 7:
            ref, to = self.plane.at[at.r], at.plane[n]
        else:
            ref, to = self.column.at[at.z], at.to_z[n - 7]
        return remote(ref, ref, self.send.at[n], self.recv.at[n], to)

    def start(self, tile):
        self.plane[self.at.r] = tile
        for n in range(7):
            self.copy(n).start()

    def total(self, ref, ns):
        for n in ns:
            self.copy(n).wait_recv()
        total = ref[0]
        for n in range(1, ref.shape[0]):
            total = total + ref[n]
        return total

    def step(self):
        self.column[self.at.z] = self.total(self.plane, range(7))
        for n in range(7, self.COPIES):
            self.copy(n).start()

    def last(self):
        total = self.total(self.column, range(7, self.COPIES))
        for n in range(self.COPIES):
            self.copy(n).wait_send()
        return total


LANDING = (
    (NX, 8, DEEP, D),
    (8, HALF, D),
    (NX, NZ, HALF, D),
    (NZ, DEEP, D),
    (3, DEEP, D),
)


def stage_rows(qkv, out, up, down, l):
    return (
        [(qkv.at[l, :, pl.ds(j * D, D)], 16 * j, 16) for j in range(3)]
        + [(out.at[l], 48, 16)]
        + [(up.at[l, :, pl.ds(j * D, D)], 64 + 16 * j, 16) for j in range(4)]
        + [(down.at[l], 128, 64)]
    )


BEGIN, SETUP, START, QKV_HALF, QKV, WINDOWS_HALF, WINDOWS, UP_HALF, UP, DOWN = range(10)
FIRST, SECOND, THIRD, FOURTH, FIFTH, LAST, SEND = range(7)
GATHER_PLAN = {
    (-1, BEGIN): [(FIRST, 0, 0), (FIRST, 0, 1), (FIRST, 0, 2)],
    (-1, SETUP): [(FIRST, 1, 0), (FIRST, 1, 1), (SECOND, 0, 0)],
    (0, START): [(FIRST, 1, 2), (SECOND, 0, 1), (THIRD, 0, 0), (FOURTH, 0, 0), (SECOND, 0, 2), (THIRD, 0, 1), (FIFTH, 0, 0), (LAST, 0, 0)],
    (0, QKV_HALF): [(SECOND, 1, 0), (FOURTH, 0, 1)],
    (0, QKV): [(FIRST, 2, 0), (THIRD, 0, 2), (FIFTH, 0, 1)],
    (0, WINDOWS_HALF): [(SECOND, 1, 1), (LAST, 0, 1)],
    (0, WINDOWS): [(FIRST, 2, 1), (FOURTH, 0, 2)],
    (0, UP_HALF): [(THIRD, 1, 0), (FIFTH, 0, 2), (SECOND, 1, 2)],
    (0, UP): [(FIRST, 2, 2), (LAST, 0, 2), (FOURTH, 1, 0), (SECOND, 2, 0)],
    (0, DOWN): [(THIRD, 1, 1), (FIFTH, 1, 0)],
    (1, START): [(LAST, 1, 0), (FOURTH, 1, 1)],
    (1, QKV_HALF): [(SECOND, 2, 1)],
    (1, QKV): [(THIRD, 1, 2), (FIFTH, 1, 1)],
    (1, WINDOWS_HALF): [(LAST, 1, 1)],
    (1, WINDOWS): [(SECOND, 2, 2), (FOURTH, 1, 2)],
    (1, UP_HALF): [(THIRD, 2, 0), (FIFTH, 1, 2), (LAST, 1, 2)],
    (1, UP): [(FOURTH, 2, 0)],
    (1, DOWN): [(THIRD, 2, 1), (FIFTH, 2, 0)],
    (2, START): [(LAST, 2, 0), (FOURTH, 2, 1)],
    (2, QKV): [(THIRD, 2, 2), (FIFTH, 2, 1)],
    (2, WINDOWS_HALF): [(LAST, 2, 1)],
    (2, WINDOWS): [(FOURTH, 2, 2)],
    (2, UP_HALF): [(FIFTH, 2, 2), (LAST, 2, 2)],
}


def train_kernel(refs, alone):
    k = Kit(**refs)

    def kept(names, l, back):
        copies = []
        for name in names:
            here, there = refs[name], refs["keep_" + name].at[l]
            src, dst = (there, here) if back else (here, there)
            copies.append(pltpu.make_async_copy(src, dst, k.keep_sem.at[KEEP.index(name)]))
        return copies

    def start(copies):
        for copy in copies:
            copy.start()

    def wait(copies):
        for copy in copies:
            copy.wait()

    def kept_x(back):
        here, there = k.xs.at[0], k.keep_x
        src, dst = (there, here) if back else (here, there)
        return [pltpu.make_async_copy(src, dst, k.keep_sem.at[len(KEEP)])]

    arrays = [(l, n) for l in range(LAYERS) for n in (0, 1)]
    parts = [(l, part) for l in range(LAYERS) for part in range(PARTS)]
    weights = (k.wa, k.wf)
    if alone:
        loads = [
            pltpu.make_async_copy((k.all_a, k.all_f)[n].at[l], weights[n].at[l], k.load_sem.at[2 * l + n])
            for l, n in arrays
        ]
        stores = [
            pltpu.make_async_copy(
                weights[n].at[l + 1 - n], (k.grad_a, k.grad_f)[n].at[l], k.load_sem.at[2 * l + n]
            )
            for l, n in arrays
        ]
        start(loads)
    else:
        place = Place()
        gather = Gather(place, weights, k.gather_send, k.gather_recv)
        reduce = Reduce(
            place, weights, k.landing, k.reduce_send, k.reduce_recv, k.credit
        )
        sums = Total(place, k.mid, SMALL, k.sum_send, k.sum_recv)
        norm = Norm(place, k.norm_plane, k.norm_column, k.norm_send, k.norm_recv)

    def run(plan):
        stages = (
            gather.first,
            gather.second,
            gather.third,
            gather.fourth,
            gather.fifth,
            gather.last,
        )
        for stage, l, part in plan:
            stages[stage](l, part)

    def poll(l, point):
        if alone:
            return
        for layer in range(LAYERS):
            plan = GATHER_PLAN.get((layer, point))
            if plan:

                @pl.when(l == layer)
                def _(plan=plan):
                    run(plan)

    if not alone:
        staged = []
        for l in range(LAYERS):
            for n, (src, row, count) in enumerate(stage_rows(k.qkv_w, k.out_w, k.up_w, k.down_w, l)):
                dst = k.xs.at[2, pl.ds(l * PACK + row, count), :]
                staged.append(pltpu.make_async_copy(src, dst, k.stage_sem.at[l, n]))
        start(staged)
        place.barrier()
        for l in range(LAYERS):
            wait(staged[9 * l : 9 * l + 9])
            row = l * PACK
            for part in range(PARTS):
                array, first = part_ref(weights, part)
                mine = k.xs[2, row + DEEP * part : row + DEEP * (part + 1), :].astype(LOWER)
                array[l, place.a, place.b, first : first + DEEP, :] = mine
                if (FIRST, l, part) in GATHER_PLAN[-1, BEGIN]:
                    gather.first(l, part)
        k.squares_sum[...] = jnp.zeros_like(k.squares_sum)

    setup_stage(k)
    start(kept_x(False))
    if not alone:
        run(GATHER_PLAN[-1, SETUP])

    def forward(l, carry):
        if alone:
            pltpu.make_async_copy(k.all_a.at[l], k.wa.at[l], k.load_sem.at[2 * l]).wait()

        @pl.when(l > 0)
        def _():
            wait(kept(KEEP_ATTN, l - 1, False))

        poll(l, START)
        forward_qkv(k, l, lambda: poll(l, QKV_HALF))
        poll(l, QKV)
        forward_windows(k, l, lambda: poll(l, WINDOWS_HALF))

        @pl.when(l < LAYERS - 1)
        def _():
            start(kept(KEEP_ATTN, l, False))

        @pl.when(l > 0)
        def _():
            wait(kept(KEEP_FFN, l - 1, False))

        @pl.when(l == 1)
        def _():
            wait(kept_x(False))

        if alone:
            pltpu.make_async_copy(k.all_f.at[l], k.wf.at[l], k.load_sem.at[2 * l + 1]).wait()
        poll(l, WINDOWS)
        forward_up(k, l, lambda: poll(l, UP_HALF))
        poll(l, UP)
        forward_down(k, l, (l + 1) % 2 + l // 2)

        @pl.when(l < LAYERS - 1)
        def _():
            start(kept(KEEP_FFN, l, False))

        poll(l, DOWN)
        return carry

    lax.fori_loop(0, LAYERS, forward, 0)
    if not alone:
        for l, part in parts:
            gather.sent(l, part)
    grad = 2
    head_stage(k, grad)

    def run_reduce(stage, l, part):
        if stage == THIRD:
            reduce.third(l, part, k.shard)
        elif stage == LAST:
            reduce.last(l, part, k.shard, k.squares_sum)
        else:
            {SEND: reduce.start, FIRST: reduce.first, SECOND: reduce.second}[stage](l, part)

    def backward(n, carry):
        l = LAYERS - 1 - n

        def behind(name, *stages):
            @pl.when(n > 0)
            def _():
                for stage, part, *more in stages:
                    stage(l + 1, part, *more)

        @pl.when(n > 0)
        def _():
            wait(kept(KEEP_FFN, l, True))

        def now(stage, part, early=None):
            if alone:
                return
            if early is None:
                run_reduce(stage, l, part)
                return

            @pl.when((n == LAYERS - 1) if early else (n < LAYERS - 1))
            def _():
                run_reduce(stage, l, part)

        def then(stage, part):
            if not alone:

                @pl.when(n > 0)
                def _():
                    run_reduce(stage, l + 1, part)

        def in_ffn():
            then(LAST, 2)
            then(THIRD, 1)
            then(FIRST, 0)

        def in_windows():
            now(FIRST, 1, False)
            now(SECOND, 2, True)

        backward_ffn(k, l, grad, in_ffn)
        backward_down_grads(k, l)
        now(SEND, 2)
        then(LAST, 1)
        then(SECOND, 0)
        backward_up_grads(k, l)

        @pl.when(n < LAYERS - 1)
        def _():
            start(kept(KEEP_FFN, l - 1, True))

        now(SEND, 1)
        now(FIRST, 2, True)

        @pl.when(n > 0)
        def _():
            wait(kept(KEEP_ATTN, l, True))

        backward_out(k, l, grad)
        now(FIRST, 2, False)
        now(FIRST, 1, True)
        then(THIRD, 0)
        backward_windows(k, l, in_windows)
        now(SECOND, 2, False)
        now(THIRD, 2, True)
        then(LAST, 0)
        backward_attn_grads(k, l)

        @pl.when(n < LAYERS - 1)
        def _():
            start(kept(KEEP_ATTN, l - 1, True))

        now(SEND, 0)
        now(THIRD, 2, False)
        now(SECOND, 1, True)

        @pl.when(n == LAYERS - 1)
        def _():
            wait(kept_x(True))

        backward_input(k, l, grad)

        @pl.when(n == 0)
        def _():
            start(kept_x(True))

        now(SECOND, 1, False)
        now(FIRST, 0, True)
        now(THIRD, 1, True)
        return carry

    lax.fori_loop(0, LAYERS, backward, 0)
    if alone:
        start(stores)
        small_stage(k, k.small_out, grad)
        wait(stores)
        return
    small_stage(k, sums.whole(), grad)
    sums.start()
    reduce.last(0, 2, k.shard, k.squares_sum)
    reduce.second(0, 0)
    sums.step(0)
    reduce.third(0, 0, k.shard)
    sums.step(1)
    reduce.last(0, 1, k.shard, k.squares_sum)
    sums.step(2)
    reduce.last(0, 0, k.shard, k.squares_sum)
    squares = k.squares_sum[...]
    norm.start(sum(squares[:, n * 128 : (n + 1) * 128] for n in range(D // 128)))
    sums.back()
    norm.step()
    sums.last()
    k.small_out[...] = sums.whole()[...]
    k.squares[...] = norm.last()


def train_pass(inputs, weights, alone):
    whole = pl.BlockSpec(memory_space=pltpu.VMEM)
    scalars = pl.BlockSpec(memory_space=pltpu.SMEM)
    anywhere = pl.BlockSpec(memory_space=pl.ANY)
    dma = pltpu.SemaphoreType.DMA
    count = PARTS * LAYERS
    names = ["states", "actions", "returns", "starts", "repeats", "valid"]
    names += ["log_temp", "small", "head_bias"]
    out_shape = {"small_out": ((SMALL, D), WIDE)}
    for name in KEEP:
        shape, dtype = WORK_SHAPES[name]
        out_shape["keep_" + name] = ((LAYERS - 1,) + shape, dtype)
    out_shape["keep_x"] = ((ROWS, D), WIDE)
    scratch = {name: pltpu.VMEM(*shape) for name, shape in WORK_SHAPES.items()}
    scratch["keep_sem"] = dma((len(KEEP) + 1,))
    if alone:
        names += ["all_a", "all_f"]
        out_shape["grad_a"] = ((LAYERS, 4, 8, ATTN, D), LOWER)
        out_shape["grad_f"] = ((LAYERS, 4, 8, FFN, D), LOWER)
        scratch["load_sem"] = dma((count,))
    else:
        names += ["qkv_w", "out_w", "up_w", "down_w"]
        out_shape["shard"] = ((LAYERS, PACK, D), WIDE)
        out_shape["squares"] = ((8, 128), WIDE)
        for part in range(PARTS):
            for n, shape in enumerate(LANDING):
                scratch["land_%d_%d" % (part, n)] = pltpu.VMEM(shape, LOWER)
        scratch["stage_sem"] = dma((LAYERS, 9))
        scratch["squares_sum"] = pltpu.VMEM((8, D), WIDE)
        for name, copies in (("gather", Gather.COPIES), ("reduce", Reduce.COPIES)):
            scratch[name + "_send"] = dma((count, copies))
            scratch[name + "_recv"] = dma((count, copies))
        scratch["credit"] = pltpu.SemaphoreType.REGULAR((PARTS, 8))
        scratch["norm_plane"] = pltpu.VMEM((8, 8, 128), WIDE)
        scratch["norm_column"] = pltpu.VMEM((NZ, 8, 128), WIDE)
        for name, copies in (("sum", Total.COPIES), ("norm", Norm.COPIES)):
            scratch[name + "_send"] = dma((copies,))
            scratch[name + "_recv"] = dma((copies,))
    spaces = dict.fromkeys(("starts", "repeats", "head_bias", "log_temp"), scalars)
    for name in ("all_a", "all_f", "grad_a", "grad_f", "qkv_w", "out_w", "up_w", "down_w"):
        spaces[name] = anywhere
    for name in KEEP + ("x",):
        spaces["keep_" + name] = anywhere
    every = names + list(out_shape) + list(scratch)

    def kernel(*given):
        refs = dict(zip(every, given))
        refs["landing"] = [
            [refs.get("land_%d_%d" % (part, n)) for n in range(len(LANDING))] for part in range(PARTS)
        ]
        train_kernel(refs, alone)

    results = pl.pallas_call(
        kernel,
        name="train_pass",
        out_shape=tuple(jax.ShapeDtypeStruct(*shape) for shape in out_shape.values()),
        in_specs=[spaces.get(name, whole) for name in names],
        out_specs=tuple(spaces.get(name, whole) for name in out_shape),
        scratch_shapes=list(scratch.values()),
        compiler_params=pltpu.CompilerParams(
            vmem_limit_bytes=VMEM_BYTES,
            collective_id=None if alone else 0,
            has_side_effects=not alone,
        ),
        cost_estimate=pl.CostEstimate(
            flops=6 * 10**10, bytes_accessed=4 * 10**7, transcendentals=10**7
        ),
    )(*inputs, *weights)
    return dict(zip(out_shape, results))


def adam_parts(weight, grad, first, second, rate):
    first = BETA_ONE * first + (1.0 - BETA_ONE) * grad
    second = BETA_TWO * second + (1.0 - BETA_TWO) * grad * grad
    fix_one = 1.0 - BETA_ONE**STEP
    fix_two = 1.0 - BETA_TWO**STEP
    fresh = weight - rate * (
        first * (1.0 / fix_one) / (jnp.sqrt(second * (1.0 / fix_two)) + ADAM_EPS) + DECAY * weight
    )
    return fresh, first, second


def adam_kernel(*refs):
    shard, small_grad, squares, groups, log_temp = refs[:5]
    small, small_first, small_second, bias, bias_first, bias_second = refs[5:11]
    mats, firsts, seconds = refs[11:15], refs[15:19], refs[19:23]
    totals, norm, next_temp, s_next, s_first, s_second, b_next, b_first, b_second = refs[23:32]
    m_next, m_copy, m_first, m_second = refs[32:36], refs[36:40], refs[40:44], refs[44:48]
    extra = small_grad[NROWS : NROWS + 3, 0:128]
    lane = iota((1, 128), 1)
    bias_mean = jnp.where(lane < A, extra[1:2], 0.0)
    bias_spread = jnp.where(lane < A, extra[2:3], 0.0)

    def all_sum(v):
        return jnp.sum(jnp.sum(v, 0, keepdims=True), 1, keepdims=True)

    grads = small_grad[0:NROWS, :]
    square = (
        all_sum(squares[0:1, :])
        + all_sum(grads * grads)
        + all_sum(bias_mean * bias_mean)
        + all_sum(bias_spread * bias_spread)
    )
    length = jnp.sqrt(square)
    clip = jnp.minimum(1.0, CLIP / (length + 1e-06))

    def rate_of(l, kind):
        group = jnp.full((1, 1), groups[l, kind], jnp.int32).astype(WIDE)
        return LEARN * jnp.exp2(-group)

    def update(l, kind, rows, cols, grad):
        at = (l, rows, cols)
        fresh, first, second = adam_parts(
            mats[kind][at], clip * grad, firsts[kind][at], seconds[kind][at], rate_of(l, kind)
        )
        m_next[kind][at] = fresh
        m_copy[kind][at] = fresh.astype(LOWER)
        m_first[kind][at] = first
        m_second[kind][at] = second

    every = slice(0, 16)
    for l in range(LAYERS):
        for j in range(3):
            update(l, 0, every, slice(j * D, (j + 1) * D), shard[l, 16 * j : 16 * j + 16, :])
        update(l, 1, every, slice(0, D), shard[l, 48:64, :])
        for j in range(4):
            rows = slice(64 + 16 * j, 80 + 16 * j)
            update(l, 2, every, slice(j * D, (j + 1) * D), shard[l, rows, :])
        update(l, 3, slice(0, 64), slice(0, D), shard[l, 128:192, :])

    s_next[...], s_first[...], s_second[...] = adam_parts(
        small[...], clip * grads, small_first[...], small_second[...], LEARN
    )

    def scalar(v, n):
        return jnp.sum(jnp.where(lane == n, v, 0.0))

    def row(ref):
        v = jnp.zeros((1, 128), WIDE)
        for n in range(2 * A):
            v = jnp.where(lane == n, ref[n], v)
        return v

    grad = bias_mean + pltpu.roll(bias_spread, A, 1)
    results = adam_parts(row(bias), clip * grad, row(bias_first), row(bias_second), LEARN)
    for ref, result in zip((b_next, b_first, b_second), results):
        for n in range(2 * A):
            ref[n] = scalar(result, n)
    sums = extra[0:1]
    for n in range(3):
        totals[n] = scalar(sums, n)
    norm[0] = jnp.sum(length)
    logs = jnp.full((1, 1), log_temp[0], WIDE)
    ratio = jnp.full((1, 1), scalar(sums, 1), WIDE) / jnp.full((1, 1), scalar(sums, 2), WIDE)
    next_temp[0] = jnp.sum(logs - TEMP_RATE * jnp.exp(logs) * (ratio + A))


def adam_all(shard, small_grad, squares, groups, log_temp, smalls, biases, mats, firsts, seconds):
    scalars = pl.BlockSpec(memory_space=pltpu.SMEM)

    whole = pl.BlockSpec(memory_space=pltpu.VMEM)

    def like(array, dtype=WIDE):
        return jax.ShapeDtypeStruct(array.shape, dtype)

    stacks = list(mats) + list(firsts) + list(seconds)
    small, bias = smalls[0], biases[0]
    return pl.pallas_call(
        adam_kernel,
        name="adam",
        out_shape=(
            (jax.ShapeDtypeStruct((3,), WIDE),)
            + (jax.ShapeDtypeStruct((1,), WIDE),) * 2
            + (like(small),) * 3
            + (like(bias),) * 3
            + tuple(like(m) for m in mats)
            + tuple(like(m, LOWER) for m in mats)
            + tuple(like(m) for m in mats) * 2
        ),
        in_specs=[whole] * 3 + [scalars] * 2 + [whole] * 3 + [scalars] * 3 + [whole] * 12,
        out_specs=(scalars,) * 3 + (whole,) * 3 + (scalars,) * 3 + (whole,) * 16,
        compiler_params=pltpu.CompilerParams(vmem_limit_bytes=VMEM_BYTES),
        cost_estimate=pl.CostEstimate(flops=10**7, bytes_accessed=8 * 10**6, transcendentals=10**6),
    )(shard, small_grad, squares, groups, log_temp, *smalls, *biases, *stacks)


def gather_packed(mats, axes, count):
    group = count // BLOCKS
    pieces = []
    for mat in mats:
        rows, wide = mat.shape[1], mat.shape[2] // D
        piece = mat.astype(LOWER).reshape(LAYERS, rows, wide, D)
        piece = lax.all_gather(piece, axes, axis=1, tiled=True)
        piece = piece.reshape(LAYERS, NZ, NY, NX, NC, group * rows, wide, D)
        piece = piece.transpose(0, 4, 3, 2, 1, 6, 5, 7)
        pieces.append(piece.reshape(LAYERS, 4, 8, wide * group * rows, D))
    return jnp.concatenate(pieces[:2], 3), jnp.concatenate(pieces[2:], 3)


def scatter_packed(grads, mats, axes):
    results, first = [], 0
    for n, mat in enumerate(mats):
        rows, wide = mat.shape[1], mat.shape[2] // D
        total = lax.psum(1, axes) * rows
        deep = total // BLOCKS
        first = 0 if n % 2 == 0 else first
        piece = grads[n // 2][:, :, :, first : first + wide * deep].astype(WIDE)
        first += wide * deep
        piece = piece.reshape(LAYERS, NC, NX, NY, NZ, wide, deep, D)
        piece = piece.transpose(0, 4, 3, 2, 1, 6, 5, 7).reshape(LAYERS, total, wide * D)
        results.append(lax.psum_scatter(piece, axes, scatter_dimension=1, tiled=True))
    return results


def local(
    buf_states,
    buf_actions,
    buf_returns,
    window_starts,
    window_repeats,
    valid_steps,
    matrix_groups,
    log_temp,
    small_rows,
    head_bias,
    qkv_weight,
    out_weight,
    up_weight,
    down_weight,
    small_first,
    bias_first,
    qkv_first,
    out_first,
    up_first,
    down_first,
    small_second,
    bias_second,
    qkv_second,
    out_second,
    up_second,
    down_second,
):
    axes = ("dp", "fsdp")
    mats = (qkv_weight, out_weight, up_weight, down_weight)
    firsts = (qkv_first, out_first, up_first, down_first)
    seconds = (qkv_second, out_second, up_second, down_second)
    pass_inputs = (
        buf_states.T,
        buf_actions.T,
        buf_returns[None],
        window_starts,
        window_repeats,
        valid_steps,
        log_temp,
        small_rows,
        head_bias,
    )
    if FF // down_weight.shape[1] == BLOCKS and lax.psum(1, "fsdp") == NX * NC:
        made = train_pass(pass_inputs, mats, False)
        return adam_all(
            made["shard"],
            made["small_out"],
            made["squares"],
            matrix_groups,
            log_temp,
            (small_rows, small_first, small_second),
            (head_bias, bias_first, bias_second),
            mats,
            firsts,
            seconds,
        )
    packed = gather_packed(mats, axes, FF // down_weight.shape[1])
    made = train_pass(pass_inputs, packed, True)
    big = scatter_packed((made["grad_a"], made["grad_f"]), mats, axes)
    small = made["small_out"]
    small = lax.psum(small, axes)
    small_grad, totals = small[:NROWS], small[NROWS, :3]
    bias_grad = jnp.concatenate([small[NROWS + 1, :A], small[NROWS + 2, :A]])
    square = sum((jnp.sum(piece * piece) for piece in big))
    square = (
        lax.psum(square, axes) + jnp.sum(small_grad * small_grad) + jnp.sum(bias_grad * bias_grad)
    )
    grad_norm = jnp.sqrt(square)
    clip = jnp.minimum(1.0, CLIP / (grad_norm + 1e-06))
    rates = LEARN * jnp.exp2(-matrix_groups.astype(WIDE))
    results = [
        adam_parts(
            mats[kind], clip * big[kind], firsts[kind], seconds[kind], rates[:, kind][:, None, None]
        )
        for kind in range(4)
    ]
    small_new = adam_parts(small_rows, clip * small_grad, small_first, small_second, LEARN)
    bias_new = adam_parts(head_bias, clip * bias_grad, bias_first, bias_second, LEARN)
    next_temp = log_temp - TEMP_RATE * jnp.exp(log_temp) * (totals[1] / totals[2] + A)
    return (
        (totals, grad_norm[None], next_temp)
        + small_new
        + bias_new
        + tuple(r[0] for r in results)
        + tuple(r[0].astype(LOWER) for r in results)
        + tuple(r[1] for r in results)
        + tuple(r[2] for r in results)
    )


def solution(mesh):
    rows = P(("dp", "fsdp"), None)
    vector = P(("dp", "fsdp"))
    stack = P(None, ("dp", "fsdp"), None)
    same = P()
    in_specs = (
        (rows, rows, vector, vector, vector, rows)
        + (same,) * 4
        + (stack,) * 4
        + (same,) * 2
        + (stack,) * 4
        + (same,) * 2
        + (stack,) * 4
    )
    out_specs = (same,) * 9 + (stack,) * 16
    return jax.shard_map(local, mesh=mesh, in_specs=in_specs, out_specs=out_specs, check_vma=False)
```

```python
import math

import jax
import jax.numpy as jnp
from jax import lax
from jax.experimental import pallas as pl
from jax.experimental.pallas import tpu as pltpu
from jax.sharding import PartitionSpec as P

D = 512
H = 8
HD = 64
FF = 2048
S = 11
A = 3
K = 20
STEP = 10

EPS = 1e-05
CLIP = 1.0
LEARN = 0.03
BETA_ONE = 0.5
BETA_TWO = 0.7
DECAY = 0.01
ADAM_EPS = 1e-08
TEMP_RATE = 0.1
MASKED = -1e30
HALF_LOG_TAU = 0.5 * math.log(2.0 * math.pi)
GELU_C = math.sqrt(2.0 / math.pi)
GELU_A = 0.044715
HIGH = lax.Precision.HIGHEST
LOWER = jnp.bfloat16
WIDE = jnp.float32

LAYERS = 3
WINS = 16
BUF_DEV = 64
SLOT = 64
ROWS = WINS * SLOT
CHUNK = 512
CHUNKS = ROWS // CHUNK
STATE_SLOT = 24
STATES = WINS * STATE_SLOT
BLOCKS = 32
PACK = 192
ATTN, FFN = 64, 128
EMB = S + A + 1 + K + 3
FIN = EMB
HEADW = EMB + 2
BASE = EMB + 2 + 2 * A
PER = 9 + FF // D
NROWS = BASE + LAYERS * PER
SMALL = 96
HEAD_AT = 64
EMB_AT = ROWS - 128
VMEM_BYTES = 64 * 1024 * 1024


def dot(a, b, precision=None):
    return lax.dot_general(
        a, b, (((1,), (0,)), ((), ())), precision=precision, preferred_element_type=WIDE
    )


def dot_nt(a, b, precision=None):
    return lax.dot_general(
        a, b, (((1,), (1,)), ((), ())), precision=precision, preferred_element_type=WIDE
    )


def dot_tn(a, b, precision=None):
    return lax.dot_general(
        a, b, (((0,), (0,)), ((), ())), precision=precision, preferred_element_type=WIDE
    )


def iota(shape, dim):
    return lax.broadcasted_iota(jnp.int32, shape, dim)


def col_sum(v):
    return jnp.sum(v, 0, keepdims=True)


def row_mean(v):
    return jnp.mean(v, -1, keepdims=True)


def norm_parts(x):
    center = x - row_mean(x)
    scale = lax.rsqrt(row_mean(center * center) + EPS)
    return center * scale, scale


def norm_back(xhat, scale, gain, grad):
    scaled = grad * gain
    return scale * (scaled - row_mean(scaled) - xhat * row_mean(scaled * xhat))


def token_rows(at, count):
    row = at + iota((count, 128), 0)
    place = row & (SLOT - 1)
    step = (place * 21846) >> 16
    return row >> 6, step, place - 3 * step, place < 3 * K


def chunk_rows(c):
    return pl.ds(pl.multiple_of(c * CHUNK, CHUNK), CHUNK)


def owner_place(i):
    z, y, x, c = i // 8, (i // 4) % 2, (i // 2) % 2, i % 2
    return 2 * c + x, 4 * y + z


class Kit:
    def __init__(self, **refs):
        self.__dict__.update(refs)

    def row(self, l, k):
        return self.lrows[l, k : k + 1, :]

    def blocks(self, ref, l, first, count, owners):
        places = [owner_place(i) for i in owners]
        return jnp.concatenate([ref[l, a, b, first : first + count, :] for a, b in places], 0)

    def w_qkv(self, l, j):
        return self.blocks(self.wa, l, 16 * j, 16, range(BLOCKS))

    def w_out(self, l):
        return self.blocks(self.wa, l, 48, 16, range(BLOCKS))

    def w_up(self, l, j):
        return self.blocks(self.wf, l, 16 * j, 16, range(BLOCKS))

    def w_down(self, l, j):
        return self.blocks(self.wf, l, 64, 64, range(8 * j, 8 * j + 8))


def slot(l):
    return l % 2


def setup_stage(k):
    k.xs[2, EMB_AT:ROWS, :] = jnp.zeros((128, D), WIDE)
    k.xs[2, EMB_AT : EMB_AT + EMB, :] = k.small[0:EMB, :]
    k.headw[...] = jnp.zeros_like(k.headw)
    k.headw[0, 0:A, :] = k.small[HEADW : HEADW + A, :].astype(LOWER)
    k.headw[1, 0:A, :] = k.small[HEADW + A : HEADW + 2 * A, :].astype(LOWER)
    for l in range(LAYERS):
        k.lrows[l, 0:PER, :] = k.small[BASE + l * PER : BASE + (l + 1) * PER, :]
    k.sgl[...] = jnp.zeros_like(k.sgl)
    k.sgh[...] = jnp.zeros_like(k.sgh)
    k.sgw[...] = jnp.zeros_like(k.sgw)

    lane, sub = iota((WINS, 128), 1), iota((WINS, 128), 0)
    k.meta[...] = jnp.zeros_like(k.meta)
    k.meta[0:WINS, 0:K] = k.valid[...].astype(WIDE)
    meta = k.meta[0:WINS, :]
    for w in range(WINS):
        for n, ref in enumerate((k.starts, k.repeats)):
            meta = jnp.where((sub == w) & (lane == K + n), ref[w].astype(WIDE), meta)
    k.meta[0:WINS, :] = meta
    meta = k.meta[...].astype(LOWER)
    k.buf[...] = jnp.zeros_like(k.buf)
    k.buf[0, 0:S, 0:BUF_DEV] = k.states[...]
    k.buf[0, S + A : S + A + 1, 0:BUF_DEV] = k.returns[...]
    k.buf[1, 0:A, 0:BUF_DEV] = k.actions[...]

    def chunk(c, carry):
        rows = chunk_rows(c)
        win, step, kind, real = token_rows(c * CHUNK, CHUNK)
        lane = iota((CHUNK, 128), 1)
        tok = dot((lane == win).astype(WIDE).astype(LOWER), meta)
        start, repeat = tok[:, K : K + 1], tok[:, K + 1 : K + 2]
        valid = jnp.sum(jnp.where(lane == step, tok, 0.0), -1, keepdims=True)
        key = iota((CHUNK, 128), 0) & (SLOT - 1)
        query = lane & (SLOT - 1)
        allowed = (key <= query) & (((valid > 0.5) & real) | (key == query))
        k.bias[rows, :] = jnp.where(allowed, 0.0, MASKED)
        place = start.astype(jnp.int32) + step
        source = ((lane == place) & real).astype(WIDE)
        raw = dot_nt(source, k.buf[0], HIGH)
        acts = dot_nt(source, k.buf[1], HIGH)
        mine = (
            ((lane < S) & (kind == 1))
            | ((lane >= S) & (lane < S + A) & (kind == 2))
            | ((lane == S + A) & (kind == 0))
        )
        raw = raw + pltpu.roll(acts, S, 1)
        marks = ((lane == S + A + 1 + step) | (lane == S + A + 1 + K + kind)) & real
        feats = jnp.where(mine, raw, 0.0) + marks.astype(WIDE)
        weight = jnp.where((kind == 1) & real, repeat * valid, 0.0)
        acts = pltpu.roll(acts, HEAD_AT, 1)
        ours = (lane >= HEAD_AT) & (lane < HEAD_AT + A)
        feats = jnp.where(ours, acts, jnp.where(lane == HEAD_AT + A, weight, feats))
        k.feats[rows, :] = feats
        k.xs[0, rows, :] = dot(feats, k.xs[2, EMB_AT:ROWS, :], HIGH)
        return carry

    lax.fori_loop(0, CHUNKS, chunk, 0)


def stack_pair(v, first):
    zero = jnp.zeros_like(v)
    return jnp.concatenate([jnp.where(first, v, zero), jnp.where(first, zero, v)], 0)


def join_pair(v, first):
    return jnp.where(first, v[:SLOT], v[SLOT:])


def window_rows(w):
    return pl.ds(pl.multiple_of(w * SLOT, SLOT), SLOT)


def each_chunk(body, between=None):
    def step(c, carry):
        body(c, chunk_rows(c))
        if between is not None:

            @pl.when(c < CHUNKS - 1)
            def _():
                between()

        return carry

    lax.fori_loop(0, CHUNKS, step, 0)


def each_pair(body, between=None):
    def pair(n, carry):
        chains = [
            (2 * n + w, window_rows(2 * n + w), slice(p * 128, (p + 1) * 128))
            for w in range(2)
            for p in range(H // 2)
        ]
        body(pl.ds(pl.multiple_of(n * 128, 128), 128), chains)
        if between is not None:

            @pl.when(n == WINS // 4 - 1)
            def _():
                between()

        return carry

    lax.fori_loop(0, WINS // 2, pair, 0)


def forward_qkv(k, l, between):
    def chunk(c, rows):
        xhat, _ = norm_parts(k.xs[slot(l), rows, :])
        normed = (xhat * k.row(l, 0) + k.row(l, 1)).astype(LOWER)
        k.normed_t[:, rows] = normed.T
        for j in range(3):
            part = dot(normed, k.w_qkv(l, j)) + k.row(l, 4 + j)
            k.qkv[rows, j * D : (j + 1) * D] = part.astype(LOWER)

    each_chunk(chunk, between)


def qkv_part(k, n, rows, at):
    return k.qkv[rows, n * D + at.start : n * D + at.stop]


def forward_windows(k, l, between):
    first = iota((SLOT, 128), 1) < HD
    scale = jnp.asarray(HD**-0.5, LOWER)

    def pair(both, chains):
        query = [stack_pair(qkv_part(k, 0, rows, at) * scale, first) for _, rows, at in chains]
        scores = [
            dot_nt(qkv_part(k, 1, rows, at), q) + k.bias[rows, :]
            for q, (_, rows, at) in zip(query, chains)
        ]
        peaks = [jnp.max(s, 0, keepdims=True) for s in scores]
        expos = [jnp.exp(s - peak) for s, peak in zip(scores, peaks)]
        totals = [jnp.sum(e, 0, keepdims=True) for e in expos]
        probs = [(e * (1.0 / total)).astype(LOWER) for e, total in zip(expos, totals)]
        outs = [dot_tn(p, qkv_part(k, 2, rows, at)) for p, (_, rows, at) in zip(probs, chains)]
        for peak, total, out, (w, rows, at) in zip(peaks, totals, outs, chains):
            p = at.start // 128
            k.logs[l, w, p : p + 1, :] = peak + jnp.log(total)
            k.left[rows, at] = join_pair(out, first).astype(LOWER)
        k.mixed_t[:, both] = k.left[both, :].T

    each_pair(pair, between)


def state_places(compact, full):
    win = (compact * 2731) >> 16
    step = compact - STATE_SLOT * win
    return ((full == win * SLOT + 3 * step + 1) & (step < K)).astype(WIDE).astype(LOWER)


def take_states(c):
    shape = (STATES, CHUNK)
    return state_places(iota(shape, 0), c * CHUNK + iota(shape, 1))


def put_states(c):
    shape = (CHUNK, STATES)
    return state_places(iota(shape, 1), c * CHUNK + iota(shape, 0))


def three_parts(v):
    high = v.astype(LOWER)
    rest = v - high.astype(WIDE)
    mid = rest.astype(LOWER)
    return high, mid, (rest - mid.astype(WIDE)).astype(LOWER)


def states_of(ref):
    total = None
    for c in range(CHUNKS):
        pick = take_states(c)
        for part in three_parts(ref[c * CHUNK : (c + 1) * CHUNK, :]):
            term = dot(pick, part)
            total = term if total is None else total + term
    return total


def forward_up(k, l, between):
    each_chunk(lambda c, rows: up_rows(k, l, rows, k.xs[slot(l), rows, :], k.left[rows, :]), between)


def up_rows(k, l, rows, x, mixed):
    mid = x + dot(mixed, k.w_out(l)) + k.row(l, 7)
    k.mid[rows, :] = mid
    xhat, _ = norm_parts(mid)
    second = (xhat * k.row(l, 2) + k.row(l, 3)).astype(LOWER)
    k.second_t[:, rows] = second.T
    ahead = dot(second, k.w_up(l, 0))
    for j in range(4):
        cols = slice(j * D, (j + 1) * D)
        h = ahead + k.row(l, 8 + j)
        if j < 3:
            ahead = dot(second, k.w_up(l, j + 1))
        square = h * h
        over = 1.0 + jnp.tanh(h * (GELU_C + GELU_C * GELU_A * square))
        half = 0.5 * h
        acted = (half * over).astype(LOWER)
        slope = over * (0.5 + half * (2.0 - over) * (GELU_C + 3.0 * GELU_A * GELU_C * square))
        k.work[rows, cols] = acted
        k.slope[rows, cols] = slope.astype(LOWER)
        k.act_t[cols, rows] = acted.T


def forward_down(k, l, dest):
    each_chunk(lambda c, rows: down_rows(k, l, rows, dest))


def down_rows(k, l, rows, dest):
    w_down = jnp.concatenate([k.w_down(l, j) for j in range(4)], 0)
    k.xs[dest, rows, :] = k.mid[rows, :] + k.row(l, 12) + dot(k.work[rows, :], w_down)


def forward_up_states(k, l):
    rows = slice(0, STATES)
    mixed = None
    for c in range(CHUNKS):
        term = dot(take_states(c), k.left[c * CHUNK : (c + 1) * CHUNK, :])
        mixed = term if mixed is None else mixed + term
    mixed = mixed.astype(LOWER)
    k.mixed_t[:, rows] = mixed.T
    up_rows(k, l, rows, states_of(k.xs.at[slot(l)]), mixed)


def head_stage(k, at):
    gain, bias = k.small[FIN : FIN + 1, :], k.small[FIN + 1 : FIN + 2, :]
    lane = iota((STATES, 128), 1)
    keep = lane < A

    def bias_row(first):
        row = jnp.zeros((1, 128), WIDE)
        at = iota((1, 128), 1)
        for a in range(A):
            row = jnp.where(at == a, k.head_bias[first + a], row)
        return row

    bias_mean, bias_spread = bias_row(0), bias_row(A)
    temp = jnp.exp(jnp.full((1, 128), k.log_temp[0], WIDE))

    rows = slice(0, STATES)
    xhat, scale = norm_parts(k.xs[at, rows, :])
    feats = (xhat * gain + bias).astype(LOWER)
    mean = dot_nt(feats, k.headw[0]) + bias_mean
    spread = jnp.tanh(dot_nt(feats, k.headw[1]) + bias_spread)
    acts = pltpu.roll(states_of(k.feats), 128 - HEAD_AT, 1)
    weight = acts[:, A : A + 1]
    acts = jnp.where(keep, acts, 0.0)
    target = 0.5 * (jnp.log(1.0 + acts) - jnp.log(1.0 - acts))
    shrink = jnp.exp(-spread)
    zed = (target - mean) * shrink
    terms = 0.5 * zed * zed + spread + HALF_LOG_TAU + jnp.log(1.0 - acts * acts)
    nll = jnp.sum(jnp.where(keep, terms, 0.0), -1, keepdims=True)
    entropy = jnp.sum(jnp.where(keep, spread, 0.0), -1, keepdims=True) + A * (0.5 + HALF_LOG_TAU)
    loss = weight * (nll - temp * entropy)
    sums = jnp.where(lane == 0, loss, jnp.where(lane == 1, weight * entropy, jnp.where(lane == 2, weight, 0.0)))
    d_mean = jnp.where(keep, weight * (-zed * shrink), 0.0).astype(LOWER)
    d_spread = weight * (1.0 - zed * zed - temp) * (1.0 - spread * spread)
    d_spread = jnp.where(keep, d_spread, 0.0).astype(LOWER)
    k.sgh[2:3, 0:128] += col_sum(sums)
    k.sgh[3:4, 0:128] += col_sum(d_mean.astype(WIDE))
    k.sgh[4:5, 0:128] += col_sum(d_spread.astype(WIDE))
    k.sgw[0] += dot_tn(d_mean, feats)[0:8]
    k.sgw[1] += dot_tn(d_spread, feats)[0:8]
    d_feats = dot(d_mean, k.headw[0]) + dot(d_spread, k.headw[1])
    k.sgh[0:1, :] += col_sum(d_feats * xhat)
    k.sgh[1:2, :] += col_sum(d_feats)
    k.xs[at, rows, :] = norm_back(xhat, scale, gain, d_feats)


def store_blocks(ref, l, owners, first, count, value):
    value = value.astype(LOWER)
    for n, i in enumerate(owners):
        a, b = owner_place(i)
        ref[l, a, b, first : first + count, :] = value[n * count : (n + 1) * count]


def backward_ffn(k, l, grad, between=None):
    each_chunk(lambda c, rows: ffn_back_rows(k, l, rows, grad), between)


def ffn_back_rows(k, l, rows, grad):
    d_down = k.xs[grad, rows, :].astype(LOWER)
    k.dout[rows, :] = d_down
    k.sgl[l, 12:13, :] += col_sum(d_down.astype(WIDE))
    d_second = jnp.zeros(d_down.shape, WIDE)
    ahead = dot_nt(d_down, k.w_down(l, 0))
    for j in range(4):
        cols = slice(j * D, (j + 1) * D)
        d_acted = ahead
        if j < 3:
            ahead = dot_nt(d_down, k.w_down(l, j + 1))
        d_hidden = (d_acted * k.slope[rows, cols].astype(WIDE)).astype(LOWER)
        k.work[rows, cols] = d_hidden
        k.sgl[l, 8 + j : 9 + j, :] += col_sum(d_hidden.astype(WIDE))
        d_second = d_second + dot_nt(d_hidden, k.w_up(l, j))
    xhat, scale = norm_parts(k.mid[rows, :])
    k.sgl[l, 2:3, :] += col_sum(d_second * xhat)
    k.sgl[l, 3:4, :] += col_sum(d_second)
    k.xs[grad, rows, :] += norm_back(xhat, scale, k.row(l, 2), d_second)


def backward_down_grads(k, l, rows=slice(0, ROWS)):
    for j in range(4):
        part = dot(k.act_t[j * D : (j + 1) * D, rows], k.dout[rows, :])
        store_blocks(k.wf, l, range(8 * j, 8 * j + 8), 64, 64, part)


def backward_up_grads(k, l, rows=slice(0, ROWS)):
    for j in range(4):
        part = dot(k.second_t[:, rows], k.work[rows, j * D : (j + 1) * D])
        store_blocks(k.wf, l, range(BLOCKS), 16 * j, 16, part)


def backward_out(k, l, grad):
    def before(c, rows):
        d_branch = k.xs[grad, rows, :].astype(LOWER)
        k.left[rows, :] = d_branch
        k.sgl[l, 7:8, :] += col_sum(d_branch.astype(WIDE))
        k.dout[rows, :] = dot_nt(d_branch, k.w_out(l)).astype(LOWER)

    each_chunk(before)
    store_blocks(k.wa, l + 1, range(BLOCKS), 48, 16, dot(k.mixed_t[...], k.left[...]))


def backward_out_states(k, l, grad):
    rows = slice(0, STATES)
    d_mid = k.xs[grad, rows, :]
    d_branch = d_mid.astype(LOWER)
    k.sgl[l, 7:8, :] += col_sum(d_branch.astype(WIDE))
    d_mixed = dot_nt(d_branch, k.w_out(l)).astype(LOWER)
    store_blocks(k.wa, l + 1, range(BLOCKS), 48, 16, dot(k.mixed_t[:, rows], d_branch))
    parts = three_parts(d_mid)
    for c in range(CHUNKS):
        where = slice(c * CHUNK, (c + 1) * CHUNK)
        put = put_states(c)
        k.dout[where, :] = dot(put, d_mixed).astype(LOWER)
        k.xs[grad, where, :] = dot(put, parts[0]) + dot(put, parts[1]) + dot(put, parts[2])


def backward_windows(k, l, between):
    first = iota((SLOT, 128), 1) < HD
    scale = HD**-0.5
    low = jnp.asarray(scale, LOWER)

    def pair(both, chains):
        query = [stack_pair(qkv_part(k, 0, rows, at) * low, first) for _, rows, at in chains]
        d_mixed = [stack_pair(k.dout[rows, at], first) for _, rows, at in chains]
        shift = [
            k.bias[rows, :] - k.logs[l, w, at.start // 128 : at.start // 128 + 1, :]
            for w, rows, at in chains
        ]
        scores = [dot_nt(qkv_part(k, 1, rows, at), q) for q, (_, rows, at) in zip(query, chains)]
        d_probs = [dot_nt(qkv_part(k, 2, rows, at), d) for d, (_, rows, at) in zip(d_mixed, chains)]
        probs = [jnp.exp(s + more) for s, more in zip(scores, shift)]
        d_values = [dot(p.astype(LOWER), d) for p, d in zip(probs, d_mixed)]
        inner = [p * d for p, d in zip(probs, d_probs)]
        sums = [jnp.sum(i, 0, keepdims=True) for i in inner]
        d_scores = [(i - p * t).astype(LOWER) for i, p, t in zip(inner, probs, sums)]
        d_keyed = [dot(d, q) for d, q in zip(d_scores, query)]
        d_query = [dot_tn(d, qkv_part(k, 1, rows, at)) for d, (_, rows, at) in zip(d_scores, chains)]
        for n, (_, rows, at) in enumerate(chains):
            values = (join_pair(d_query[n], first) * scale, d_keyed[n], d_values[n])
            for m, value in enumerate(values):
                k.work[rows, m * D + at.start : m * D + at.stop] = value.astype(LOWER)

    each_pair(pair, between)


def backward_attn_grads(k, l):
    for j in range(3):
        part = dot(k.normed_t[...], k.work[:, j * D : (j + 1) * D])
        store_blocks(k.wa, l + 1, range(BLOCKS), 16 * j, 16, part)


def backward_input(k, l, grad):
    def chunk(c, rows):
        d_normed = jnp.zeros((CHUNK, D), WIDE)
        for j in range(3):
            d_part = k.work[rows, j * D : (j + 1) * D]
            k.sgl[l, 4 + j : 5 + j, :] += col_sum(d_part.astype(WIDE))
            d_normed = d_normed + dot_nt(d_part, k.w_qkv(l, j))
        xhat, scale = norm_parts(k.xs[slot(l), rows, :])
        k.sgl[l, 0:1, :] += col_sum(d_normed * xhat)
        k.sgl[l, 1:2, :] += col_sum(d_normed)
        k.xs[grad, rows, :] += norm_back(xhat, scale, k.row(l, 0), d_normed)

    each_chunk(chunk)


def small_stage(k, out, grad):
    out[...] = jnp.zeros_like(out)
    out[0:EMB, :] = dot_tn(k.feats[...], k.xs[grad], HIGH)[0:EMB]
    out[FIN : FIN + 2, :] = k.sgh[0:2, :]
    out[HEADW : HEADW + A, :] = k.sgw[0, 0:A, :]
    out[HEADW + A : HEADW + 2 * A, :] = k.sgw[1, 0:A, :]
    for l in range(LAYERS):
        out[BASE + l * PER : BASE + (l + 1) * PER, :] = k.sgl[l, 0:PER, :]
    out[NROWS : NROWS + 3, :] = k.sgh[2:5, :]


WORK_SHAPES = dict(
    wa=((LAYERS + 1, 4, 8, ATTN, D), LOWER),
    wf=((LAYERS, 4, 8, FFN, D), LOWER),
    xs=((3, ROWS, D), WIDE),
    qkv=((ROWS, 3 * D), LOWER),
    normed_t=((D, ROWS), LOWER),
    mixed_t=((D, ROWS), LOWER),
    slope=((ROWS, FF), LOWER),
    act_t=((FF, ROWS), LOWER),
    second_t=((D, ROWS), LOWER),
    mid=((ROWS, D), WIDE),
    logs=((LAYERS, WINS, 8, 128), WIDE),
    work=((ROWS, FF), LOWER),
    left=((ROWS, D), LOWER),
    dout=((ROWS, D), LOWER),
    feats=((ROWS, 128), WIDE),
    bias=((ROWS, 128), WIDE),
    headw=((2, 128, D), LOWER),
    lrows=((LAYERS, 16, D), WIDE),
    sgl=((LAYERS, 16, D), WIDE),
    sgh=((8, D), WIDE),
    sgw=((2, 8, D), WIDE),
    meta=((128, 128), WIDE),
    buf=((2, 128, 128), WIDE),
)
KEEP_ATTN = ("qkv", "normed_t", "mixed_t")
KEEP_FFN = ("slope", "act_t", "second_t", "mid")
KEEP = KEEP_ATTN + KEEP_FFN


MESH = pl.DeviceIdType.MESH
NZ, NY, NX, NC = 4, 2, 2, 2
NR = NY * NX * NC
SHARD = PACK
PARTS, DEEP = 3, 64
HALF = DEEP // 2


class Place:
    def __init__(self):
        dp, fsdp = lax.axis_index("dp"), lax.axis_index("fsdp")
        self.z, self.y = dp // NY, dp % NY
        self.x, self.c = fsdp // NC, fsdp % NC
        self.a, self.b = 2 * self.c + self.x, 4 * self.y + self.z
        self.r = 4 * self.y + fsdp
        self.to_z = [(((self.z + d) % NZ) * NY + self.y, fsdp) for d in range(1, NZ)]
        self.odd = self.z % 2
        self.to_pair = ((self.z + 1 - 2 * self.odd) * NY + self.y, fsdp)
        self.plane = []
        for d in range(1, 8):
            y, x, c = [
                1 - v if d & bit else v for v, bit in ((self.y, 4), (self.x, 2), (self.c, 1))
            ]
            self.plane.append((self.z * NY + y, x * NC + c))
        self.to_c, self.to_x, self.to_y = self.plane[0], self.plane[1], self.plane[3]

    def barrier(self):
        sem = pltpu.get_barrier_semaphore()
        for partner in self.plane + self.to_z:
            pl.semaphore_signal(sem, inc=1, device_id=partner, device_id_type=MESH)
        pl.semaphore_wait(sem, len(self.plane) + len(self.to_z))


def remote(src, dst, send, recv, to):
    return pltpu.make_async_remote_copy(
        src_ref=src, dst_ref=dst, send_sem=send, recv_sem=recv, device_id=to, device_id_type=MESH
    )


def part_ref(weights, part):
    return weights[min(part, 1)], (0, 0, DEEP)[part]


class Gather:
    COPIES = 13

    def __init__(self, place, weights, send, recv):
        self.at, self.weights, self.send, self.recv = place, weights, send, recv

    def copy(self, l, part, n):
        at = self.at
        array, row = part_ref(self.weights, part)
        a, b, rows, to = at.a, pl.ds(4 * at.y, 4), pl.ds(row, DEEP), at.to_c
        if n < 3:
            b, to = at.b, at.to_z[n]
        elif n < 5:
            to = (at.to_x, at.to_y)[n - 3]
        if n in (6, 8, 10, 11, 12):
            a = 2 * at.c + 1 - at.x
        if n in (7, 9, 10, 11, 12):
            b = pl.ds(4 * (1 - at.y), 4)
        if n in (6, 7):
            first = row + at.odd * HALF + (n - 6) * (HALF // 2)
            rows = pl.ds(pl.multiple_of(first, HALF // 2), HALF // 2)
            to = (at.to_y, at.to_x)[n - 6]
        if n in (10, 11):
            rows = pl.ds(pl.multiple_of(row + at.odd * HALF, HALF), HALF)
        if n == 11:
            to = at.to_pair
        if n == 12:
            rows = pl.ds(pl.multiple_of(row + (1 - at.odd) * HALF, HALF), HALF)
        ref = array.at[l, a, b, rows, :]
        q = PARTS * l + part
        return remote(ref, ref, self.send.at[q, n], self.recv.at[q, n], to)

    def start(self, l, part, *ns):
        for n in ns:
            self.copy(l, part, n).start()

    def wait(self, l, part, *ns):
        for n in ns:
            self.copy(l, part, n).wait_recv()

    def first(self, l, part):
        self.start(l, part, 0, 1, 2)

    def second(self, l, part):
        self.wait(l, part, 0, 1, 2)
        self.start(l, part, 3, 4, 5)

    def third(self, l, part):
        self.wait(l, part, 3)
        self.start(l, part, 6, 8)
        self.wait(l, part, 4)
        self.start(l, part, 7, 9)

    def fourth(self, l, part):
        self.wait(l, part, 6, 7)
        self.start(l, part, 11, 10)

    def fifth(self, l, part):
        self.wait(l, part, 11)
        self.start(l, part, 12)

    def last(self, l, part):
        self.wait(l, part, 5, 8, 9, 10, 12)

    def sent(self, l, part):
        for n in range(self.COPIES):
            self.copy(l, part, n).wait_send()


class Reduce:
    COPIES = 8

    def __init__(self, place, grads, landing, send, recv, credit):
        self.at, self.grads, self.landing = place, grads, landing
        self.send, self.recv, self.credit = send, recv, credit

    def refs(self, l, part):
        array, row = part_ref(self.grads, part)
        grads = array.at[l + 1 - min(part, 1), :, :, pl.ds(row, DEEP), :]
        return (grads, *self.landing[part])

    def copy(self, l, part, n):
        at, half = self.at, HALF
        g, r0, r1a, r1b, r2, r3 = self.refs(l, part)
        top, low, other = pl.ds(0, half), pl.ds(half, half), pl.ds(4 * (1 - at.y), 4)
        if n == 0:
            src, dst, to = g.at[pl.ds(2 * (1 - at.c), 2)], r0, at.to_c
        elif n == 1:
            src, dst, to = r0.at[1 - at.x, :, top, :], r1a, at.to_x
        elif n == 2:
            src, dst, to = r0.at[:, other, low, :], r1b, at.to_y
        elif n == 3:
            src, dst, to = r1a.at[other], r2.at[:, top, :], at.to_y
        elif n == 4:
            src, dst, to = r1b.at[1 - at.x], r2.at[:, low, :], at.to_x
        else:
            src, dst, to = r2.at[(at.z + n - 4) % NZ], r3.at[n - 5], at.to_z[n - 5]
        q = PARTS * l + part
        return remote(src, dst, self.send.at[q, n], self.recv.at[q, n], to)

    def may_send(self, l, part, *partners):
        @pl.when(l < LAYERS - 1)
        def _():
            for n in partners:
                pl.semaphore_wait(self.credit.at[part, n], 1)

    def allow(self, l, part, *credits):
        at = self.at

        @pl.when(l > 0)
        def _():
            for n, to in credits:
                pl.semaphore_signal(
                    self.credit.at[part, n], inc=1, device_id=to, device_id_type=MESH
                )

    def start(self, l, part):
        self.may_send(l, part, 0)
        self.copy(l, part, 0).start()

    def first(self, l, part):
        at, half = self.at, HALF
        g, r0, _, _, _, _ = self.refs(l, part)
        top, low = pl.ds(0, half), pl.ds(half, half)
        self.copy(l, part, 0).wait_recv()

        x = 1 - at.x
        total = g[2 * at.c + x, :, top].astype(WIDE) + r0[x, :, top].astype(WIDE)
        r0[x, :, top] = total.astype(LOWER)
        self.may_send(l, part, 1, 2)
        self.copy(l, part, 1).start()
        other = pl.ds(4 * (1 - at.y), 4)
        for x in range(NX):
            total = g[2 * at.c + x, other, low].astype(WIDE) + r0[x, other, low].astype(WIDE)
            r0[x, other, low] = total.astype(LOWER)
        self.copy(l, part, 2).start()

    def second(self, l, part):
        at, half = self.at, HALF
        g, r0, r1a, r1b, _, _ = self.refs(l, part)
        top, low = pl.ds(0, half), pl.ds(half, half)

        x, other, column = 1 - at.x, pl.ds(4 * (1 - at.y), 4), pl.ds(4 * at.y, 4)
        self.copy(l, part, 1).wait_recv()
        total = g[at.a, other, top].astype(WIDE) + r0[at.x, other, top].astype(WIDE)
        r1a[other] = (total + r1a[other].astype(WIDE)).astype(LOWER)
        self.may_send(l, part, 6, 7)
        self.copy(l, part, 3).start()
        self.copy(l, part, 2).wait_recv()
        total = g[2 * at.c + x, column, low].astype(WIDE) + r0[x, column, low].astype(WIDE)
        r1b[x] = (total + r1b[x].astype(WIDE)).astype(LOWER)
        self.copy(l, part, 4).start()

    def chip_sums(self, l, part, z):
        at, half = self.at, HALF
        g, r0, r1a, r1b, r2, _ = self.refs(l, part)
        top, low, b = pl.ds(0, half), pl.ds(half, half), 4 * at.y + z
        upper = g[at.a, b, top].astype(WIDE) + r0[at.x, b, top].astype(WIDE)
        lower = g[at.a, b, low].astype(WIDE) + r0[at.x, b, low].astype(WIDE)
        return (
            upper + r1a[b].astype(WIDE) + r2[z, top].astype(WIDE),
            lower + r1b[at.x, z].astype(WIDE) + r2[z, low].astype(WIDE),
        )

    def third(self, l, part, out):
        at, half, row = self.at, HALF, DEEP * part
        r2 = self.landing[part][3]
        for n in (3, 4):
            self.copy(l, part, n).wait_recv()
        self.may_send(l, part, 3, 4, 5)
        for n in range(3):
            z = (at.z + n + 1) % NZ
            upper, lower = self.chip_sums(l, part, z)
            r2[z, pl.ds(0, half)] = upper.astype(LOWER)
            r2[z, pl.ds(half, half)] = lower.astype(LOWER)
            self.copy(l, part, 5 + n).start()
        upper, lower = self.chip_sums(l, part, at.z)
        out[l, row : row + half, :] = upper
        out[l, row + half : row + 2 * half, :] = lower
        for n in range(5):
            self.copy(l, part, n).wait_send()
        self.allow(l, part, (0, at.to_c), (1, at.to_x), (2, at.to_y))

    def last(self, l, part, out, squares):
        at, row = self.at, DEEP * part
        r3 = self.landing[part][4]
        rows = slice(row, row + DEEP)
        total = out[l, rows, :]
        for n in range(3):
            self.copy(l, part, 5 + n).wait_recv()
            total = total + r3[n].astype(WIDE)
        out[l, rows, :] = total
        squares[0:1, :] += col_sum(total * total)
        for n in range(5, self.COPIES):
            self.copy(l, part, n).wait_send()
        late = [(6, at.to_x), (7, at.to_y)] + [(5 - n, at.to_z[n]) for n in range(3)]
        self.allow(l, part, *late)


class Total:
    COPIES = 7

    def __init__(self, place, ref, rows, send, recv):
        self.at, self.ref, self.rows = place, ref, rows // 2
        self.send, self.recv = send, recv

    def half(self, n):
        return self.ref.at[pl.ds(pl.multiple_of(n * self.rows, 8), self.rows), :]

    def whole(self):
        return self.ref.at[pl.ds(0, 2 * self.rows), :]

    def copy(self, n):
        at = self.at
        mine, other = self.half(at.c), self.half(1 - at.c)
        src, dst, to = (
            (other, self.half(2), at.to_c),
            (self.half(8), self.half(3), at.to_x),
            (self.half(9), self.half(4), at.to_y),
            (self.half(10), self.half(5), at.to_z[0]),
            (self.half(10), self.half(6), at.to_z[1]),
            (self.half(10), self.half(7), at.to_z[2]),
            (mine, self.half(11), at.to_c),
        )[n]
        return remote(src, dst, self.send.at[n], self.recv.at[n], to)

    def start(self):
        self.copy(0).start()

    def step(self, n):
        self.copy(n).wait_recv()
        own = self.half(self.at.c) if n == 0 else self.half(7 + n)
        self.half(8 + n)[...] = own[...] + self.half(2 + n)[...]
        for m in ((1,), (2,), (3, 4, 5))[n]:
            self.copy(m).start()

    def back(self):
        for m in (3, 4, 5):
            self.copy(m).wait_recv()
        self.copy(0).wait_send()
        total = None
        for z in range(NZ):
            term = self.half(10)[...]
            for n in range(3):
                from_z = (self.at.z + NZ - 1 - n) % NZ
                term = jnp.where(from_z == z, self.half(5 + n)[...], term)
            total = term if total is None else total + term
        self.half(self.at.c)[...] = total
        self.copy(6).start()

    def last(self):
        self.copy(6).wait_recv()
        self.half(1 - self.at.c)[...] = self.half(11)[...]
        for n in range(1, self.COPIES):
            self.copy(n).wait_send()


class Norm:
    COPIES = 10

    def __init__(self, place, plane, column, send, recv):
        self.at, self.plane, self.column = place, plane, column
        self.send, self.recv = send, recv

    def copy(self, n):
        at = self.at
        if n < 7:
            ref, to = self.plane.at[at.r], at.plane[n]
        else:
            ref, to = self.column.at[at.z], at.to_z[n - 7]
        return remote(ref, ref, self.send.at[n], self.recv.at[n], to)

    def start(self, tile):
        self.plane[self.at.r] = tile
        for n in range(7):
            self.copy(n).start()

    def total(self, ref, ns):
        for n in ns:
            self.copy(n).wait_recv()
        total = ref[0]
        for n in range(1, ref.shape[0]):
            total = total + ref[n]
        return total

    def step(self):
        self.column[self.at.z] = self.total(self.plane, range(7))
        for n in range(7, self.COPIES):
            self.copy(n).start()

    def last(self):
        total = self.total(self.column, range(7, self.COPIES))
        for n in range(self.COPIES):
            self.copy(n).wait_send()
        return total


LANDING = (
    (NX, 8, DEEP, D),
    (8, HALF, D),
    (NX, NZ, HALF, D),
    (NZ, DEEP, D),
    (3, DEEP, D),
)


def stage_rows(qkv, out, up, down, l):
    return (
        [(qkv.at[l, :, pl.ds(j * D, D)], 16 * j, 16) for j in range(3)]
        + [(out.at[l], 48, 16)]
        + [(up.at[l, :, pl.ds(j * D, D)], 64 + 16 * j, 16) for j in range(4)]
        + [(down.at[l], 128, 64)]
    )


BEGIN, SETUP, START, QKV_HALF, QKV, WINDOWS_HALF, WINDOWS, UP_HALF, UP, DOWN = range(10)
FIRST, SECOND, THIRD, FOURTH, FIFTH, LAST, SEND = range(7)
GATHER_PLAN = {
    (-1, BEGIN): [(FIRST, 0, 0), (FIRST, 0, 1), (FIRST, 0, 2)],
    (-1, SETUP): [(FIRST, 1, 0), (FIRST, 1, 1), (SECOND, 0, 0)],
    (0, START): [(FIRST, 1, 2), (SECOND, 0, 1), (THIRD, 0, 0), (FOURTH, 0, 0), (SECOND, 0, 2), (THIRD, 0, 1), (FIFTH, 0, 0), (LAST, 0, 0)],
    (0, QKV_HALF): [(SECOND, 1, 0), (FOURTH, 0, 1)],
    (0, QKV): [(FIRST, 2, 0), (THIRD, 0, 2), (FIFTH, 0, 1)],
    (0, WINDOWS_HALF): [(SECOND, 1, 1), (LAST, 0, 1)],
    (0, WINDOWS): [(FIRST, 2, 1), (FOURTH, 0, 2)],
    (0, UP_HALF): [(THIRD, 1, 0), (FIFTH, 0, 2), (SECOND, 1, 2)],
    (0, UP): [(FIRST, 2, 2), (LAST, 0, 2), (FOURTH, 1, 0), (SECOND, 2, 0)],
    (0, DOWN): [(THIRD, 1, 1), (FIFTH, 1, 0)],
    (1, START): [(LAST, 1, 0), (FOURTH, 1, 1)],
    (1, QKV_HALF): [(SECOND, 2, 1)],
    (1, QKV): [(THIRD, 1, 2), (FIFTH, 1, 1)],
    (1, WINDOWS_HALF): [(LAST, 1, 1)],
    (1, WINDOWS): [(SECOND, 2, 2), (FOURTH, 1, 2)],
    (1, UP_HALF): [(THIRD, 2, 0), (FIFTH, 1, 2), (LAST, 1, 2)],
    (1, UP): [(FOURTH, 2, 0)],
    (1, DOWN): [(THIRD, 2, 1), (FIFTH, 2, 0)],
    (2, START): [(LAST, 2, 0), (FOURTH, 2, 1)],
    (2, QKV): [(THIRD, 2, 2), (FIFTH, 2, 1)],
    (2, WINDOWS_HALF): [(LAST, 2, 1)],
    (2, WINDOWS): [(FOURTH, 2, 2)],
    (2, UP): [(FIFTH, 2, 2), (LAST, 2, 2)],
}


def train_kernel(refs, alone):
    k = Kit(**refs)

    def kept(names, l, back):
        copies = []
        for name in names:
            here, there = refs[name], refs["keep_" + name].at[l]
            src, dst = (there, here) if back else (here, there)
            copies.append(pltpu.make_async_copy(src, dst, k.keep_sem.at[KEEP.index(name)]))
        return copies

    def start(copies):
        for copy in copies:
            copy.start()

    def wait(copies):
        for copy in copies:
            copy.wait()

    def kept_x(back):
        here, there = k.xs.at[0], k.keep_x
        src, dst = (there, here) if back else (here, there)
        return [pltpu.make_async_copy(src, dst, k.keep_sem.at[len(KEEP)])]

    arrays = [(l, n) for l in range(LAYERS) for n in (0, 1)]
    parts = [(l, part) for l in range(LAYERS) for part in range(PARTS)]
    weights = (k.wa, k.wf)
    if alone:
        loads = [
            pltpu.make_async_copy((k.all_a, k.all_f)[n].at[l], weights[n].at[l], k.load_sem.at[2 * l + n])
            for l, n in arrays
        ]
        stores = [
            pltpu.make_async_copy(
                weights[n].at[l + 1 - n], (k.grad_a, k.grad_f)[n].at[l], k.load_sem.at[2 * l + n]
            )
            for l, n in arrays
        ]
        start(loads)
    else:
        place = Place()
        gather = Gather(place, weights, k.gather_send, k.gather_recv)
        reduce = Reduce(
            place, weights, k.landing, k.reduce_send, k.reduce_recv, k.credit
        )
        sums = Total(place, k.mid, SMALL, k.sum_send, k.sum_recv)
        norm = Norm(place, k.norm_plane, k.norm_column, k.norm_send, k.norm_recv)

    def run(plan):
        stages = (
            gather.first,
            gather.second,
            gather.third,
            gather.fourth,
            gather.fifth,
            gather.last,
        )
        for stage, l, part in plan:
            stages[stage](l, part)

    def poll(l, point):
        if alone:
            return
        for layer in range(LAYERS):
            plan = GATHER_PLAN.get((layer, point))
            if plan:

                @pl.when(l == layer)
                def _(plan=plan):
                    run(plan)

    if not alone:
        staged = []
        for l in range(LAYERS):
            for n, (src, row, count) in enumerate(stage_rows(k.qkv_w, k.out_w, k.up_w, k.down_w, l)):
                dst = k.xs.at[2, pl.ds(l * PACK + row, count), :]
                staged.append(pltpu.make_async_copy(src, dst, k.stage_sem.at[l, n]))
        start(staged)
        place.barrier()
        for l in range(LAYERS):
            wait(staged[9 * l : 9 * l + 9])
            row = l * PACK
            for part in range(PARTS):
                array, first = part_ref(weights, part)
                mine = k.xs[2, row + DEEP * part : row + DEEP * (part + 1), :].astype(LOWER)
                array[l, place.a, place.b, first : first + DEEP, :] = mine
                if (FIRST, l, part) in GATHER_PLAN[-1, BEGIN]:
                    gather.first(l, part)
        k.squares_sum[...] = jnp.zeros_like(k.squares_sum)

    setup_stage(k)
    start(kept_x(False))
    if not alone:
        run(GATHER_PLAN[-1, SETUP])

    grad = 2

    def forward(l, carry):
        if alone:
            pltpu.make_async_copy(k.all_a.at[l], k.wa.at[l], k.load_sem.at[2 * l]).wait()

        @pl.when(l > 0)
        def _():
            wait(kept(KEEP_ATTN, l - 1, False))

        poll(l, START)
        forward_qkv(k, l, lambda: poll(l, QKV_HALF))
        poll(l, QKV)
        forward_windows(k, l, lambda: poll(l, WINDOWS_HALF))

        @pl.when(l < LAYERS - 1)
        def _():
            start(kept(KEEP_ATTN, l, False))

        @pl.when(l > 0)
        def _():
            wait(kept(KEEP_FFN, l - 1, False))

        @pl.when(l == 1)
        def _():
            wait(kept_x(False))

        if alone:
            pltpu.make_async_copy(k.all_f.at[l], k.wf.at[l], k.load_sem.at[2 * l + 1]).wait()
        poll(l, WINDOWS)

        @pl.when(l < LAYERS - 1)
        def _():
            forward_up(k, l, lambda: poll(l, UP_HALF))

        @pl.when(l == LAYERS - 1)
        def _():
            forward_up_states(k, l)

        poll(l, UP)

        @pl.when(l < LAYERS - 1)
        def _():
            forward_down(k, l, (l + 1) % 2)

        @pl.when(l == LAYERS - 1)
        def _():
            down_rows(k, l, slice(0, STATES), grad)

        @pl.when(l < LAYERS - 1)
        def _():
            start(kept(KEEP_FFN, l, False))

        poll(l, DOWN)
        return carry

    lax.fori_loop(0, LAYERS, forward, 0)
    if not alone:
        for l, part in parts:
            gather.sent(l, part)
    head_stage(k, grad)

    def run_reduce(stage, l, part):
        if stage == THIRD:
            reduce.third(l, part, k.shard)
        elif stage == LAST:
            reduce.last(l, part, k.shard, k.squares_sum)
        else:
            {SEND: reduce.start, FIRST: reduce.first, SECOND: reduce.second}[stage](l, part)

    def backward(n, carry):
        l = LAYERS - 1 - n

        def behind(name, *stages):
            @pl.when(n > 0)
            def _():
                for stage, part, *more in stages:
                    stage(l + 1, part, *more)

        @pl.when(n > 0)
        def _():
            wait(kept(KEEP_FFN, l, True))

        def now(stage, part, early=None):
            if alone:
                return
            if early is None:
                run_reduce(stage, l, part)
                return

            @pl.when((n == LAYERS - 1) if early else (n < LAYERS - 1))
            def _():
                run_reduce(stage, l, part)

        def then(stage, part):
            if not alone:

                @pl.when(n > 0)
                def _():
                    run_reduce(stage, l + 1, part)

        def in_ffn():
            then(LAST, 2)
            then(THIRD, 1)
            then(FIRST, 0)

        def in_windows():
            now(FIRST, 1, False)
            now(SECOND, 2, True)

        states = slice(0, STATES)

        @pl.when(n > 0)
        def _():
            backward_ffn(k, l, grad, in_ffn)
            backward_down_grads(k, l)

        @pl.when(n == 0)
        def _():
            ffn_back_rows(k, l, states, grad)
            backward_down_grads(k, l, states)

        now(SEND, 2)
        then(LAST, 1)
        then(SECOND, 0)

        @pl.when(n > 0)
        def _():
            backward_up_grads(k, l)

        @pl.when(n == 0)
        def _():
            backward_up_grads(k, l, states)

        @pl.when(n < LAYERS - 1)
        def _():
            start(kept(KEEP_FFN, l - 1, True))

        now(SEND, 1)
        now(FIRST, 2, True)

        @pl.when(n > 0)
        def _():
            wait(kept(KEEP_ATTN, l, True))

        @pl.when(n > 0)
        def _():
            backward_out(k, l, grad)

        @pl.when(n == 0)
        def _():
            backward_out_states(k, l, grad)

        now(FIRST, 2, False)
        now(FIRST, 1, True)
        then(THIRD, 0)
        backward_windows(k, l, in_windows)
        now(SECOND, 2, False)
        now(THIRD, 2, True)
        then(LAST, 0)
        backward_attn_grads(k, l)

        @pl.when(n < LAYERS - 1)
        def _():
            start(kept(KEEP_ATTN, l - 1, True))

        now(SEND, 0)
        now(THIRD, 2, False)
        now(SECOND, 1, True)

        @pl.when(n == LAYERS - 1)
        def _():
            wait(kept_x(True))

        backward_input(k, l, grad)

        @pl.when(n == 0)
        def _():
            start(kept_x(True))

        now(SECOND, 1, False)
        now(FIRST, 0, True)
        now(THIRD, 1, True)
        return carry

    lax.fori_loop(0, LAYERS, backward, 0)
    if alone:
        start(stores)
        small_stage(k, k.small_out, grad)
        wait(stores)
        return
    small_stage(k, sums.whole(), grad)
    sums.start()
    reduce.last(0, 2, k.shard, k.squares_sum)
    reduce.second(0, 0)
    sums.step(0)
    reduce.third(0, 0, k.shard)
    sums.step(1)
    reduce.last(0, 1, k.shard, k.squares_sum)
    sums.step(2)
    reduce.last(0, 0, k.shard, k.squares_sum)
    squares = k.squares_sum[...]
    norm.start(sum(squares[:, n * 128 : (n + 1) * 128] for n in range(D // 128)))
    sums.back()
    norm.step()
    sums.last()
    k.small_out[...] = sums.whole()[...]
    k.squares[...] = norm.last()


def train_pass(inputs, weights, alone):
    whole = pl.BlockSpec(memory_space=pltpu.VMEM)
    scalars = pl.BlockSpec(memory_space=pltpu.SMEM)
    anywhere = pl.BlockSpec(memory_space=pl.ANY)
    dma = pltpu.SemaphoreType.DMA
    count = PARTS * LAYERS
    names = ["states", "actions", "returns", "starts", "repeats", "valid"]
    names += ["log_temp", "small", "head_bias"]
    out_shape = {"small_out": ((SMALL, D), WIDE)}
    for name in KEEP:
        shape, dtype = WORK_SHAPES[name]
        out_shape["keep_" + name] = ((LAYERS - 1,) + shape, dtype)
    out_shape["keep_x"] = ((ROWS, D), WIDE)
    scratch = {name: pltpu.VMEM(*shape) for name, shape in WORK_SHAPES.items()}
    scratch["keep_sem"] = dma((len(KEEP) + 1,))
    if alone:
        names += ["all_a", "all_f"]
        out_shape["grad_a"] = ((LAYERS, 4, 8, ATTN, D), LOWER)
        out_shape["grad_f"] = ((LAYERS, 4, 8, FFN, D), LOWER)
        scratch["load_sem"] = dma((count,))
    else:
        names += ["qkv_w", "out_w", "up_w", "down_w"]
        out_shape["shard"] = ((LAYERS, PACK, D), WIDE)
        out_shape["squares"] = ((8, 128), WIDE)
        for part in range(PARTS):
            for n, shape in enumerate(LANDING):
                scratch["land_%d_%d" % (part, n)] = pltpu.VMEM(shape, LOWER)
        scratch["stage_sem"] = dma((LAYERS, 9))
        scratch["squares_sum"] = pltpu.VMEM((8, D), WIDE)
        for name, copies in (("gather", Gather.COPIES), ("reduce", Reduce.COPIES)):
            scratch[name + "_send"] = dma((count, copies))
            scratch[name + "_recv"] = dma((count, copies))
        scratch["credit"] = pltpu.SemaphoreType.REGULAR((PARTS, 8))
        scratch["norm_plane"] = pltpu.VMEM((8, 8, 128), WIDE)
        scratch["norm_column"] = pltpu.VMEM((NZ, 8, 128), WIDE)
        for name, copies in (("sum", Total.COPIES), ("norm", Norm.COPIES)):
            scratch[name + "_send"] = dma((copies,))
            scratch[name + "_recv"] = dma((copies,))
    spaces = dict.fromkeys(("starts", "repeats", "head_bias", "log_temp"), scalars)
    for name in ("all_a", "all_f", "grad_a", "grad_f", "qkv_w", "out_w", "up_w", "down_w"):
        spaces[name] = anywhere
    for name in KEEP + ("x",):
        spaces["keep_" + name] = anywhere
    every = names + list(out_shape) + list(scratch)

    def kernel(*given):
        refs = dict(zip(every, given))
        refs["landing"] = [
            [refs.get("land_%d_%d" % (part, n)) for n in range(len(LANDING))] for part in range(PARTS)
        ]
        train_kernel(refs, alone)

    results = pl.pallas_call(
        kernel,
        name="train_pass",
        out_shape=tuple(jax.ShapeDtypeStruct(*shape) for shape in out_shape.values()),
        in_specs=[spaces.get(name, whole) for name in names],
        out_specs=tuple(spaces.get(name, whole) for name in out_shape),
        scratch_shapes=list(scratch.values()),
        compiler_params=pltpu.CompilerParams(
            vmem_limit_bytes=VMEM_BYTES,
            collective_id=None if alone else 0,
            has_side_effects=not alone,
        ),
        cost_estimate=pl.CostEstimate(
            flops=6 * 10**10, bytes_accessed=4 * 10**7, transcendentals=10**7
        ),
    )(*inputs, *weights)
    return dict(zip(out_shape, results))


def adam_parts(weight, grad, first, second, rate):
    first = BETA_ONE * first + (1.0 - BETA_ONE) * grad
    second = BETA_TWO * second + (1.0 - BETA_TWO) * grad * grad
    fix_one = 1.0 - BETA_ONE**STEP
    fix_two = 1.0 - BETA_TWO**STEP
    fresh = weight - rate * (
        first * (1.0 / fix_one) / (jnp.sqrt(second * (1.0 / fix_two)) + ADAM_EPS) + DECAY * weight
    )
    return fresh, first, second


def adam_kernel(*refs):
    shard, small_grad, squares, groups, log_temp = refs[:5]
    small, small_first, small_second, bias, bias_first, bias_second = refs[5:11]
    mats, firsts, seconds = refs[11:15], refs[15:19], refs[19:23]
    totals, norm, next_temp, s_next, s_first, s_second, b_next, b_first, b_second = refs[23:32]
    m_next, m_copy, m_first, m_second = refs[32:36], refs[36:40], refs[40:44], refs[44:48]
    extra = small_grad[NROWS : NROWS + 3, 0:128]
    lane = iota((1, 128), 1)
    bias_mean = jnp.where(lane < A, extra[1:2], 0.0)
    bias_spread = jnp.where(lane < A, extra[2:3], 0.0)

    def all_sum(v):
        return jnp.sum(jnp.sum(v, 0, keepdims=True), 1, keepdims=True)

    grads = small_grad[0:NROWS, :]
    square = (
        all_sum(squares[0:1, :])
        + all_sum(grads * grads)
        + all_sum(bias_mean * bias_mean)
        + all_sum(bias_spread * bias_spread)
    )
    length = jnp.sqrt(square)
    clip = jnp.minimum(1.0, CLIP / (length + 1e-06))

    def rate_of(l, kind):
        group = jnp.full((1, 1), groups[l, kind], jnp.int32).astype(WIDE)
        return LEARN * jnp.exp2(-group)

    def update(l, kind, rows, cols, grad):
        at = (l, rows, cols)
        fresh, first, second = adam_parts(
            mats[kind][at], clip * grad, firsts[kind][at], seconds[kind][at], rate_of(l, kind)
        )
        m_next[kind][at] = fresh
        m_copy[kind][at] = fresh.astype(LOWER)
        m_first[kind][at] = first
        m_second[kind][at] = second

    every = slice(0, 16)
    for l in range(LAYERS):
        for j in range(3):
            update(l, 0, every, slice(j * D, (j + 1) * D), shard[l, 16 * j : 16 * j + 16, :])
        update(l, 1, every, slice(0, D), shard[l, 48:64, :])
        for j in range(4):
            rows = slice(64 + 16 * j, 80 + 16 * j)
            update(l, 2, every, slice(j * D, (j + 1) * D), shard[l, rows, :])
        update(l, 3, slice(0, 64), slice(0, D), shard[l, 128:192, :])

    s_next[...], s_first[...], s_second[...] = adam_parts(
        small[...], clip * grads, small_first[...], small_second[...], LEARN
    )

    def scalar(v, n):
        return jnp.sum(jnp.where(lane == n, v, 0.0))

    def row(ref):
        v = jnp.zeros((1, 128), WIDE)
        for n in range(2 * A):
            v = jnp.where(lane == n, ref[n], v)
        return v

    grad = bias_mean + pltpu.roll(bias_spread, A, 1)
    results = adam_parts(row(bias), clip * grad, row(bias_first), row(bias_second), LEARN)
    for ref, result in zip((b_next, b_first, b_second), results):
        for n in range(2 * A):
            ref[n] = scalar(result, n)
    sums = extra[0:1]
    for n in range(3):
        totals[n] = scalar(sums, n)
    norm[0] = jnp.sum(length)
    logs = jnp.full((1, 1), log_temp[0], WIDE)
    ratio = jnp.full((1, 1), scalar(sums, 1), WIDE) / jnp.full((1, 1), scalar(sums, 2), WIDE)
    next_temp[0] = jnp.sum(logs - TEMP_RATE * jnp.exp(logs) * (ratio + A))


def adam_all(shard, small_grad, squares, groups, log_temp, smalls, biases, mats, firsts, seconds):
    scalars = pl.BlockSpec(memory_space=pltpu.SMEM)

    whole = pl.BlockSpec(memory_space=pltpu.VMEM)

    def like(array, dtype=WIDE):
        return jax.ShapeDtypeStruct(array.shape, dtype)

    stacks = list(mats) + list(firsts) + list(seconds)
    small, bias = smalls[0], biases[0]
    return pl.pallas_call(
        adam_kernel,
        name="adam",
        out_shape=(
            (jax.ShapeDtypeStruct((3,), WIDE),)
            + (jax.ShapeDtypeStruct((1,), WIDE),) * 2
            + (like(small),) * 3
            + (like(bias),) * 3
            + tuple(like(m) for m in mats)
            + tuple(like(m, LOWER) for m in mats)
            + tuple(like(m) for m in mats) * 2
        ),
        in_specs=[whole] * 3 + [scalars] * 2 + [whole] * 3 + [scalars] * 3 + [whole] * 12,
        out_specs=(scalars,) * 3 + (whole,) * 3 + (scalars,) * 3 + (whole,) * 16,
        compiler_params=pltpu.CompilerParams(vmem_limit_bytes=VMEM_BYTES),
        cost_estimate=pl.CostEstimate(flops=10**7, bytes_accessed=8 * 10**6, transcendentals=10**6),
    )(shard, small_grad, squares, groups, log_temp, *smalls, *biases, *stacks)


def gather_packed(mats, axes, count):
    group = count // BLOCKS
    pieces = []
    for mat in mats:
        rows, wide = mat.shape[1], mat.shape[2] // D
        piece = mat.astype(LOWER).reshape(LAYERS, rows, wide, D)
        piece = lax.all_gather(piece, axes, axis=1, tiled=True)
        piece = piece.reshape(LAYERS, NZ, NY, NX, NC, group * rows, wide, D)
        piece = piece.transpose(0, 4, 3, 2, 1, 6, 5, 7)
        pieces.append(piece.reshape(LAYERS, 4, 8, wide * group * rows, D))
    return jnp.concatenate(pieces[:2], 3), jnp.concatenate(pieces[2:], 3)


def scatter_packed(grads, mats, axes):
    results, first = [], 0
    for n, mat in enumerate(mats):
        rows, wide = mat.shape[1], mat.shape[2] // D
        total = lax.psum(1, axes) * rows
        deep = total // BLOCKS
        first = 0 if n % 2 == 0 else first
        piece = grads[n // 2][:, :, :, first : first + wide * deep].astype(WIDE)
        first += wide * deep
        piece = piece.reshape(LAYERS, NC, NX, NY, NZ, wide, deep, D)
        piece = piece.transpose(0, 4, 3, 2, 1, 6, 5, 7).reshape(LAYERS, total, wide * D)
        results.append(lax.psum_scatter(piece, axes, scatter_dimension=1, tiled=True))
    return results


def local(
    buf_states,
    buf_actions,
    buf_returns,
    window_starts,
    window_repeats,
    valid_steps,
    matrix_groups,
    log_temp,
    small_rows,
    head_bias,
    qkv_weight,
    out_weight,
    up_weight,
    down_weight,
    small_first,
    bias_first,
    qkv_first,
    out_first,
    up_first,
    down_first,
    small_second,
    bias_second,
    qkv_second,
    out_second,
    up_second,
    down_second,
):
    axes = ("dp", "fsdp")
    mats = (qkv_weight, out_weight, up_weight, down_weight)
    firsts = (qkv_first, out_first, up_first, down_first)
    seconds = (qkv_second, out_second, up_second, down_second)
    pass_inputs = (
        buf_states.T,
        buf_actions.T,
        buf_returns[None],
        window_starts,
        window_repeats,
        valid_steps,
        log_temp,
        small_rows,
        head_bias,
    )
    if FF // down_weight.shape[1] == BLOCKS and lax.psum(1, "fsdp") == NX * NC:
        made = train_pass(pass_inputs, mats, False)
        return adam_all(
            made["shard"],
            made["small_out"],
            made["squares"],
            matrix_groups,
            log_temp,
            (small_rows, small_first, small_second),
            (head_bias, bias_first, bias_second),
            mats,
            firsts,
            seconds,
        )
    packed = gather_packed(mats, axes, FF // down_weight.shape[1])
    made = train_pass(pass_inputs, packed, True)
    big = scatter_packed((made["grad_a"], made["grad_f"]), mats, axes)
    small = made["small_out"]
    small = lax.psum(small, axes)
    small_grad, totals = small[:NROWS], small[NROWS, :3]
    bias_grad = jnp.concatenate([small[NROWS + 1, :A], small[NROWS + 2, :A]])
    square = sum((jnp.sum(piece * piece) for piece in big))
    square = (
        lax.psum(square, axes) + jnp.sum(small_grad * small_grad) + jnp.sum(bias_grad * bias_grad)
    )
    grad_norm = jnp.sqrt(square)
    clip = jnp.minimum(1.0, CLIP / (grad_norm + 1e-06))
    rates = LEARN * jnp.exp2(-matrix_groups.astype(WIDE))
    results = [
        adam_parts(
            mats[kind], clip * big[kind], firsts[kind], seconds[kind], rates[:, kind][:, None, None]
        )
        for kind in range(4)
    ]
    small_new = adam_parts(small_rows, clip * small_grad, small_first, small_second, LEARN)
    bias_new = adam_parts(head_bias, clip * bias_grad, bias_first, bias_second, LEARN)
    next_temp = log_temp - TEMP_RATE * jnp.exp(log_temp) * (totals[1] / totals[2] + A)
    return (
        (totals, grad_norm[None], next_temp)
        + small_new
        + bias_new
        + tuple(r[0] for r in results)
        + tuple(r[0].astype(LOWER) for r in results)
        + tuple(r[1] for r in results)
        + tuple(r[2] for r in results)
    )


def solution(mesh):
    rows = P(("dp", "fsdp"), None)
    vector = P(("dp", "fsdp"))
    stack = P(None, ("dp", "fsdp"), None)
    same = P()
    in_specs = (
        (rows, rows, vector, vector, vector, rows)
        + (same,) * 4
        + (stack,) * 4
        + (same,) * 2
        + (stack,) * 4
        + (same,) * 2
        + (stack,) * 4
    )
    out_specs = (same,) * 9 + (stack,) * 16
    return jax.shard_map(local, mesh=mesh, in_specs=in_specs, out_specs=out_specs, check_vma=False)
```

```python
import math

import jax
import jax.numpy as jnp
from jax import lax
from jax.experimental import pallas as pl
from jax.experimental.pallas import tpu as pltpu
from jax.sharding import PartitionSpec as P

D = 512
H = 8
HD = 64
FF = 2048
S = 11
A = 3
K = 20
STEP = 10

EPS = 1e-05
CLIP = 1.0
LEARN = 0.03
BETA_ONE = 0.5
BETA_TWO = 0.7
DECAY = 0.01
ADAM_EPS = 1e-08
TEMP_RATE = 0.1
MASKED = -1e30
HALF_LOG_TAU = 0.5 * math.log(2.0 * math.pi)
GELU_C = math.sqrt(2.0 / math.pi)
GELU_A = 0.044715
HIGH = lax.Precision.HIGHEST
LOWER = jnp.bfloat16
WIDE = jnp.float32

LAYERS = 3
WINS = 16
BUF_DEV = 64
SLOT = 64
ROWS = WINS * SLOT
CHUNK = 512
CHUNKS = ROWS // CHUNK
STATE_SLOT = 24
STATES = WINS * STATE_SLOT
BLOCKS = 32
PACK = 192
ATTN, FFN = 64, 128
EMB = S + A + 1 + K + 3
FIN = EMB
HEADW = EMB + 2
BASE = EMB + 2 + 2 * A
PER = 9 + FF // D
NROWS = BASE + LAYERS * PER
SMALL = 96
HEAD_AT = 64
EMB_AT = ROWS - 128
VMEM_BYTES = 64 * 1024 * 1024


def dot(a, b, precision=None):
    return lax.dot_general(
        a, b, (((1,), (0,)), ((), ())), precision=precision, preferred_element_type=WIDE
    )


def dot_nt(a, b, precision=None):
    return lax.dot_general(
        a, b, (((1,), (1,)), ((), ())), precision=precision, preferred_element_type=WIDE
    )


def dot_tn(a, b, precision=None):
    return lax.dot_general(
        a, b, (((0,), (0,)), ((), ())), precision=precision, preferred_element_type=WIDE
    )


def iota(shape, dim):
    return lax.broadcasted_iota(jnp.int32, shape, dim)


def col_sum(v):
    return jnp.sum(v, 0, keepdims=True)


def row_mean(v):
    return jnp.mean(v, -1, keepdims=True)


def norm_parts(x):
    center = x - row_mean(x)
    scale = lax.rsqrt(row_mean(center * center) + EPS)
    return center * scale, scale


def norm_back(xhat, scale, gain, grad):
    scaled = grad * gain
    return scale * (scaled - row_mean(scaled) - xhat * row_mean(scaled * xhat))


def token_rows(at, count):
    row = at + iota((count, 128), 0)
    place = row & (SLOT - 1)
    step = (place * 21846) >> 16
    return row >> 6, step, place - 3 * step, place < 3 * K


def chunk_rows(c):
    return pl.ds(pl.multiple_of(c * CHUNK, CHUNK), CHUNK)


def owner_place(i):
    z, y, x, c = i // 8, (i // 4) % 2, (i // 2) % 2, i % 2
    return 2 * c + x, 4 * y + z


class Kit:
    def __init__(self, **refs):
        self.__dict__.update(refs)

    def row(self, l, k):
        return self.lrows[l, k : k + 1, :]

    def blocks(self, ref, l, first, count, owners):
        places = [owner_place(i) for i in owners]
        return jnp.concatenate([ref[l, a, b, first : first + count, :] for a, b in places], 0)

    def w_qkv(self, l, j):
        return self.blocks(self.wa, l, 16 * j, 16, range(BLOCKS))

    def w_out(self, l):
        return self.blocks(self.wa, l, 48, 16, range(BLOCKS))

    def w_up(self, l, j):
        return self.blocks(self.wf, l, 16 * j, 16, range(BLOCKS))

    def w_down(self, l, j):
        return self.blocks(self.wf, l, 64, 64, range(8 * j, 8 * j + 8))


def slot(l):
    return l % 2


def setup_stage(k):
    k.xs[2, EMB_AT:ROWS, :] = jnp.zeros((128, D), WIDE)
    k.xs[2, EMB_AT : EMB_AT + EMB, :] = k.small[0:EMB, :]
    k.headw[...] = jnp.zeros_like(k.headw)
    k.headw[0, 0:A, :] = k.small[HEADW : HEADW + A, :].astype(LOWER)
    k.headw[1, 0:A, :] = k.small[HEADW + A : HEADW + 2 * A, :].astype(LOWER)
    for l in range(LAYERS):
        k.lrows[l, 0:PER, :] = k.small[BASE + l * PER : BASE + (l + 1) * PER, :]
    k.sgl[...] = jnp.zeros_like(k.sgl)
    k.sgh[...] = jnp.zeros_like(k.sgh)
    k.sgw[...] = jnp.zeros_like(k.sgw)

    lane, sub = iota((WINS, 128), 1), iota((WINS, 128), 0)
    k.meta[...] = jnp.zeros_like(k.meta)
    k.meta[0:WINS, 0:K] = k.valid[...].astype(WIDE)
    meta = k.meta[0:WINS, :]
    for w in range(WINS):
        for n, ref in enumerate((k.starts, k.repeats)):
            meta = jnp.where((sub == w) & (lane == K + n), ref[w].astype(WIDE), meta)
    k.meta[0:WINS, :] = meta
    meta = k.meta[...].astype(LOWER)
    k.buf[...] = jnp.zeros_like(k.buf)
    k.buf[0, 0:S, 0:BUF_DEV] = k.states[...]
    k.buf[0, S + A : S + A + 1, 0:BUF_DEV] = k.returns[...]
    k.buf[1, 0:A, 0:BUF_DEV] = k.actions[...]

    def chunk(c, carry):
        rows = chunk_rows(c)
        win, step, kind, real = token_rows(c * CHUNK, CHUNK)
        lane = iota((CHUNK, 128), 1)
        tok = dot((lane == win).astype(WIDE).astype(LOWER), meta)
        start, repeat = tok[:, K : K + 1], tok[:, K + 1 : K + 2]
        valid = jnp.sum(jnp.where(lane == step, tok, 0.0), -1, keepdims=True)
        key = iota((CHUNK, 128), 0) & (SLOT - 1)
        query = lane & (SLOT - 1)
        allowed = (key <= query) & (((valid > 0.5) & real) | (key == query))
        k.bias[rows, :] = jnp.where(allowed, 0.0, MASKED)
        place = start.astype(jnp.int32) + step
        source = ((lane == place) & real).astype(WIDE)
        raw = dot_nt(source, k.buf[0], HIGH)
        acts = dot_nt(source, k.buf[1], HIGH)
        mine = (
            ((lane < S) & (kind == 1))
            | ((lane >= S) & (lane < S + A) & (kind == 2))
            | ((lane == S + A) & (kind == 0))
        )
        raw = raw + pltpu.roll(acts, S, 1)
        marks = ((lane == S + A + 1 + step) | (lane == S + A + 1 + K + kind)) & real
        feats = jnp.where(mine, raw, 0.0) + marks.astype(WIDE)
        weight = jnp.where((kind == 1) & real, repeat * valid, 0.0)
        acts = pltpu.roll(acts, HEAD_AT, 1)
        ours = (lane >= HEAD_AT) & (lane < HEAD_AT + A)
        feats = jnp.where(ours, acts, jnp.where(lane == HEAD_AT + A, weight, feats))
        k.feats[rows, :] = feats
        k.xs[0, rows, :] = dot(feats, k.xs[2, EMB_AT:ROWS, :], HIGH)
        return carry

    lax.fori_loop(0, CHUNKS, chunk, 0)


def stack_pair(v, first):
    zero = jnp.zeros_like(v)
    return jnp.concatenate([jnp.where(first, v, zero), jnp.where(first, zero, v)], 0)


def join_pair(v, first):
    return jnp.where(first, v[:SLOT], v[SLOT:])


def window_rows(w):
    return pl.ds(pl.multiple_of(w * SLOT, SLOT), SLOT)


def each_chunk(body, between=None):
    def step(c, carry):
        body(c, chunk_rows(c))
        if between is not None:

            @pl.when(c < CHUNKS - 1)
            def _():
                between()

        return carry

    lax.fori_loop(0, CHUNKS, step, 0)


def each_pair(body, between=None):
    def pair(n, carry):
        chains = [
            (2 * n + w, window_rows(2 * n + w), slice(p * 128, (p + 1) * 128))
            for w in range(2)
            for p in range(H // 2)
        ]
        body(pl.ds(pl.multiple_of(n * 128, 128), 128), chains)
        if between is not None:

            @pl.when(n == WINS // 4 - 1)
            def _():
                between()

        return carry

    lax.fori_loop(0, WINS // 2, pair, 0)


def forward_qkv(k, l, between):
    def chunk(c, rows):
        xhat, _ = norm_parts(k.xs[slot(l), rows, :])
        normed = (xhat * k.row(l, 0) + k.row(l, 1)).astype(LOWER)
        k.normed_t[:, rows] = normed.T
        for j in range(3):
            part = dot(normed, k.w_qkv(l, j)) + k.row(l, 4 + j)
            k.qkv[rows, j * D : (j + 1) * D] = part.astype(LOWER)

    each_chunk(chunk, between)


def qkv_part(k, n, rows, at):
    return k.qkv[rows, n * D + at.start : n * D + at.stop]


def forward_windows(k, l, between):
    first = iota((SLOT, 128), 1) < HD
    scale = jnp.asarray(HD**-0.5, LOWER)

    def pair(both, chains):
        query = [stack_pair(qkv_part(k, 0, rows, at) * scale, first) for _, rows, at in chains]
        scores = [
            dot_nt(qkv_part(k, 1, rows, at), q) + k.bias[rows, :]
            for q, (_, rows, at) in zip(query, chains)
        ]
        peaks = [jnp.max(s, 0, keepdims=True) for s in scores]
        expos = [jnp.exp(s - peak) for s, peak in zip(scores, peaks)]
        totals = [jnp.sum(e, 0, keepdims=True) for e in expos]
        probs = [(e * (1.0 / total)).astype(LOWER) for e, total in zip(expos, totals)]
        outs = [dot_tn(p, qkv_part(k, 2, rows, at)) for p, (_, rows, at) in zip(probs, chains)]
        for peak, total, out, (w, rows, at) in zip(peaks, totals, outs, chains):
            p = at.start // 128
            k.logs[l, w, p : p + 1, :] = peak + jnp.log(total)
            k.left[rows, at] = join_pair(out, first).astype(LOWER)
        k.mixed_t[:, both] = k.left[both, :].T

    each_pair(pair, between)


TILES = [slice(n * 128, (n + 1) * 128) for n in range(D // 128)]


def load_mid(k, rows):
    return jnp.concatenate([k.mid[n, rows, :] for n in range(len(TILES))], 1)


def store_mid(k, rows, value):
    for n, tile in enumerate(TILES):
        k.mid[n, rows, :] = value[:, tile]


def take_states(src, dst, cols):
    dst[0:STATES, cols] = jnp.zeros((STATES, 128), WIDE)
    for w in range(WINS):
        rows = slice(w * STATE_SLOT, w * STATE_SLOT + K)
        dst[rows, cols] = src[pl.ds(w * SLOT + 1, K, stride=3), :]


def put_states(k, value):
    for n, tile in enumerate(TILES):
        dst = k.mid.at[n]
        dst[...] = jnp.zeros((ROWS, 128), WIDE)
        for w in range(WINS):
            rows = slice(w * STATE_SLOT, w * STATE_SLOT + K)
            dst[pl.ds(w * SLOT + 1, K, stride=3), :] = value[rows, tile]


def forward_up(k, l, between):
    each_chunk(lambda c, rows: up_rows(k, l, rows, k.xs[slot(l), rows, :], k.left[rows, :]), between)


def up_rows(k, l, rows, x, mixed):
    mid = x + dot(mixed, k.w_out(l)) + k.row(l, 7)
    store_mid(k, rows, mid)
    xhat, _ = norm_parts(mid)
    second = (xhat * k.row(l, 2) + k.row(l, 3)).astype(LOWER)
    k.second_t[:, rows] = second.T
    ahead = dot(second, k.w_up(l, 0))
    for j in range(4):
        cols = slice(j * D, (j + 1) * D)
        h = ahead + k.row(l, 8 + j)
        if j < 3:
            ahead = dot(second, k.w_up(l, j + 1))
        square = h * h
        over = 1.0 + jnp.tanh(h * (GELU_C + GELU_C * GELU_A * square))
        half = 0.5 * h
        acted = (half * over).astype(LOWER)
        slope = over * (0.5 + half * (2.0 - over) * (GELU_C + 3.0 * GELU_A * GELU_C * square))
        k.work[rows, cols] = acted
        k.slope[rows, cols] = slope.astype(LOWER)
        k.act_t[cols, rows] = acted.T


def forward_down(k, l, dest):
    each_chunk(lambda c, rows: down_rows(k, l, rows, dest))


def down_rows(k, l, rows, dest):
    w_down = jnp.concatenate([k.w_down(l, j) for j in range(4)], 0)
    k.xs[dest, rows, :] = load_mid(k, rows) + k.row(l, 12) + dot(k.work[rows, :], w_down)


def forward_up_states(k, l, spare):
    every, rows = slice(0, ROWS), slice(0, STATES)
    store_mid(k, every, k.left[...].astype(WIDE))
    for n, tile in enumerate(TILES):
        take_states(k.mid.at[n], k.xs.at[spare], tile)
    mixed = k.xs[spare, rows, :].astype(LOWER)
    k.mixed_t[:, rows] = mixed.T
    store_mid(k, every, k.xs[slot(l)])
    for n, tile in enumerate(TILES):
        take_states(k.mid.at[n], k.xs.at[spare], tile)
    up_rows(k, l, rows, k.xs[spare, rows, :], mixed)


def head_stage(k, at):
    gain, bias = k.small[FIN : FIN + 1, :], k.small[FIN + 1 : FIN + 2, :]
    lane = iota((STATES, 128), 1)
    keep = lane < A

    def bias_row(first):
        row = jnp.zeros((1, 128), WIDE)
        at = iota((1, 128), 1)
        for a in range(A):
            row = jnp.where(at == a, k.head_bias[first + a], row)
        return row

    bias_mean, bias_spread = bias_row(0), bias_row(A)
    temp = jnp.exp(jnp.full((1, 128), k.log_temp[0], WIDE))

    rows = slice(0, STATES)
    xhat, scale = norm_parts(k.xs[at, rows, :])
    feats = (xhat * gain + bias).astype(LOWER)
    mean = dot_nt(feats, k.headw[0]) + bias_mean
    spread = jnp.tanh(dot_nt(feats, k.headw[1]) + bias_spread)
    take_states(k.feats, k.heads, slice(0, 128))
    acts = pltpu.roll(k.heads[...], 128 - HEAD_AT, 1)
    weight = acts[:, A : A + 1]
    acts = jnp.where(keep, acts, 0.0)
    target = 0.5 * (jnp.log(1.0 + acts) - jnp.log(1.0 - acts))
    shrink = jnp.exp(-spread)
    zed = (target - mean) * shrink
    terms = 0.5 * zed * zed + spread + HALF_LOG_TAU + jnp.log(1.0 - acts * acts)
    nll = jnp.sum(jnp.where(keep, terms, 0.0), -1, keepdims=True)
    entropy = jnp.sum(jnp.where(keep, spread, 0.0), -1, keepdims=True) + A * (0.5 + HALF_LOG_TAU)
    loss = weight * (nll - temp * entropy)
    sums = jnp.where(lane == 0, loss, jnp.where(lane == 1, weight * entropy, jnp.where(lane == 2, weight, 0.0)))
    d_mean = jnp.where(keep, weight * (-zed * shrink), 0.0).astype(LOWER)
    d_spread = weight * (1.0 - zed * zed - temp) * (1.0 - spread * spread)
    d_spread = jnp.where(keep, d_spread, 0.0).astype(LOWER)
    k.sgh[2:3, 0:128] += col_sum(sums)
    k.sgh[3:4, 0:128] += col_sum(d_mean.astype(WIDE))
    k.sgh[4:5, 0:128] += col_sum(d_spread.astype(WIDE))
    k.sgw[0] += dot_tn(d_mean, feats)[0:8]
    k.sgw[1] += dot_tn(d_spread, feats)[0:8]
    d_feats = dot(d_mean, k.headw[0]) + dot(d_spread, k.headw[1])
    k.sgh[0:1, :] += col_sum(d_feats * xhat)
    k.sgh[1:2, :] += col_sum(d_feats)
    k.xs[at, rows, :] = norm_back(xhat, scale, gain, d_feats)


def store_blocks(ref, l, owners, first, count, value):
    value = value.astype(LOWER)
    for n, i in enumerate(owners):
        a, b = owner_place(i)
        ref[l, a, b, first : first + count, :] = value[n * count : (n + 1) * count]


def backward_ffn(k, l, grad, between=None):
    each_chunk(lambda c, rows: ffn_back_rows(k, l, rows, grad), between)


def ffn_back_rows(k, l, rows, grad):
    d_down = k.xs[grad, rows, :].astype(LOWER)
    k.dout[rows, :] = d_down
    k.sgl[l, 12:13, :] += col_sum(d_down.astype(WIDE))
    d_second = jnp.zeros(d_down.shape, WIDE)
    ahead = dot_nt(d_down, k.w_down(l, 0))
    for j in range(4):
        cols = slice(j * D, (j + 1) * D)
        d_acted = ahead
        if j < 3:
            ahead = dot_nt(d_down, k.w_down(l, j + 1))
        d_hidden = (d_acted * k.slope[rows, cols].astype(WIDE)).astype(LOWER)
        k.work[rows, cols] = d_hidden
        k.sgl[l, 8 + j : 9 + j, :] += col_sum(d_hidden.astype(WIDE))
        d_second = d_second + dot_nt(d_hidden, k.w_up(l, j))
    xhat, scale = norm_parts(load_mid(k, rows))
    k.sgl[l, 2:3, :] += col_sum(d_second * xhat)
    k.sgl[l, 3:4, :] += col_sum(d_second)
    k.xs[grad, rows, :] += norm_back(xhat, scale, k.row(l, 2), d_second)


def backward_down_grads(k, l, rows=slice(0, ROWS)):
    for j in range(4):
        part = dot(k.act_t[j * D : (j + 1) * D, rows], k.dout[rows, :])
        store_blocks(k.wf, l, range(8 * j, 8 * j + 8), 64, 64, part)


def backward_up_grads(k, l, rows=slice(0, ROWS)):
    for j in range(4):
        part = dot(k.second_t[:, rows], k.work[rows, j * D : (j + 1) * D])
        store_blocks(k.wf, l, range(BLOCKS), 16 * j, 16, part)


def backward_out(k, l, grad):
    def before(c, rows):
        d_branch = k.xs[grad, rows, :].astype(LOWER)
        k.left[rows, :] = d_branch
        k.sgl[l, 7:8, :] += col_sum(d_branch.astype(WIDE))
        k.dout[rows, :] = dot_nt(d_branch, k.w_out(l)).astype(LOWER)

    each_chunk(before)
    store_blocks(k.wa, l + 1, range(BLOCKS), 48, 16, dot(k.mixed_t[...], k.left[...]))


def backward_out_states(k, l, grad):
    rows = slice(0, STATES)
    d_mid = k.xs[grad, rows, :]
    d_branch = d_mid.astype(LOWER)
    k.sgl[l, 7:8, :] += col_sum(d_branch.astype(WIDE))
    d_mixed = dot_nt(d_branch, k.w_out(l)).astype(LOWER)
    store_blocks(k.wa, l + 1, range(BLOCKS), 48, 16, dot(k.mixed_t[:, rows], d_branch))
    put_states(k, d_mixed.astype(WIDE))
    k.dout[...] = load_mid(k, slice(0, ROWS)).astype(LOWER)
    put_states(k, d_mid)
    k.xs[grad] = load_mid(k, slice(0, ROWS))


def backward_windows(k, l, between):
    first = iota((SLOT, 128), 1) < HD
    scale = HD**-0.5
    low = jnp.asarray(scale, LOWER)

    def pair(both, chains):
        query = [stack_pair(qkv_part(k, 0, rows, at) * low, first) for _, rows, at in chains]
        d_mixed = [stack_pair(k.dout[rows, at], first) for _, rows, at in chains]
        shift = [
            k.bias[rows, :] - k.logs[l, w, at.start // 128 : at.start // 128 + 1, :]
            for w, rows, at in chains
        ]
        scores = [dot_nt(qkv_part(k, 1, rows, at), q) for q, (_, rows, at) in zip(query, chains)]
        d_probs = [dot_nt(qkv_part(k, 2, rows, at), d) for d, (_, rows, at) in zip(d_mixed, chains)]
        probs = [jnp.exp(s + more) for s, more in zip(scores, shift)]
        d_values = [dot(p.astype(LOWER), d) for p, d in zip(probs, d_mixed)]
        inner = [p * d for p, d in zip(probs, d_probs)]
        sums = [jnp.sum(i, 0, keepdims=True) for i in inner]
        d_scores = [(i - p * t).astype(LOWER) for i, p, t in zip(inner, probs, sums)]
        d_keyed = [dot(d, q) for d, q in zip(d_scores, query)]
        d_query = [dot_tn(d, qkv_part(k, 1, rows, at)) for d, (_, rows, at) in zip(d_scores, chains)]
        for n, (_, rows, at) in enumerate(chains):
            values = (join_pair(d_query[n], first) * scale, d_keyed[n], d_values[n])
            for m, value in enumerate(values):
                k.work[rows, m * D + at.start : m * D + at.stop] = value.astype(LOWER)

    each_pair(pair, between)


def backward_attn_grads(k, l):
    for j in range(3):
        part = dot(k.normed_t[...], k.work[:, j * D : (j + 1) * D])
        store_blocks(k.wa, l + 1, range(BLOCKS), 16 * j, 16, part)


def backward_input(k, l, grad):
    def chunk(c, rows):
        d_normed = jnp.zeros((CHUNK, D), WIDE)
        for j in range(3):
            d_part = k.work[rows, j * D : (j + 1) * D]
            k.sgl[l, 4 + j : 5 + j, :] += col_sum(d_part.astype(WIDE))
            d_normed = d_normed + dot_nt(d_part, k.w_qkv(l, j))
        xhat, scale = norm_parts(k.xs[slot(l), rows, :])
        k.sgl[l, 0:1, :] += col_sum(d_normed * xhat)
        k.sgl[l, 1:2, :] += col_sum(d_normed)
        k.xs[grad, rows, :] += norm_back(xhat, scale, k.row(l, 0), d_normed)

    each_chunk(chunk)


def small_stage(k, out, grad):
    out[...] = jnp.zeros_like(out)
    out[0:EMB, :] = dot_tn(k.feats[...], k.xs[grad], HIGH)[0:EMB]
    out[FIN : FIN + 2, :] = k.sgh[0:2, :]
    out[HEADW : HEADW + A, :] = k.sgw[0, 0:A, :]
    out[HEADW + A : HEADW + 2 * A, :] = k.sgw[1, 0:A, :]
    for l in range(LAYERS):
        out[BASE + l * PER : BASE + (l + 1) * PER, :] = k.sgl[l, 0:PER, :]
    out[NROWS : NROWS + 3, :] = k.sgh[2:5, :]


WORK_SHAPES = dict(
    wa=((LAYERS + 1, 4, 8, ATTN, D), LOWER),
    wf=((LAYERS, 4, 8, FFN, D), LOWER),
    xs=((3, ROWS, D), WIDE),
    qkv=((ROWS, 3 * D), LOWER),
    normed_t=((D, ROWS), LOWER),
    mixed_t=((D, ROWS), LOWER),
    slope=((ROWS, FF), LOWER),
    act_t=((FF, ROWS), LOWER),
    second_t=((D, ROWS), LOWER),
    mid=((D // 128, ROWS, 128), WIDE),
    logs=((LAYERS, WINS, 8, 128), WIDE),
    work=((ROWS, FF), LOWER),
    left=((ROWS, D), LOWER),
    dout=((ROWS, D), LOWER),
    feats=((ROWS, 128), WIDE),
    heads=((STATES, 128), WIDE),
    bias=((ROWS, 128), WIDE),
    headw=((2, 128, D), LOWER),
    lrows=((LAYERS, 16, D), WIDE),
    sgl=((LAYERS, 16, D), WIDE),
    sgh=((8, D), WIDE),
    sgw=((2, 8, D), WIDE),
    meta=((128, 128), WIDE),
    buf=((2, 128, 128), WIDE),
)
KEEP_ATTN = ("qkv", "normed_t", "mixed_t")
KEEP_FFN = ("slope", "act_t", "second_t", "mid")
KEEP = KEEP_ATTN + KEEP_FFN


MESH = pl.DeviceIdType.MESH
NZ, NY, NX, NC = 4, 2, 2, 2
NR = NY * NX * NC
SHARD = PACK
PARTS, DEEP = 3, 64
HALF = DEEP // 2


class Place:
    def __init__(self):
        dp, fsdp = lax.axis_index("dp"), lax.axis_index("fsdp")
        self.z, self.y = dp // NY, dp % NY
        self.x, self.c = fsdp // NC, fsdp % NC
        self.a, self.b = 2 * self.c + self.x, 4 * self.y + self.z
        self.r = 4 * self.y + fsdp
        self.to_z = [(((self.z + d) % NZ) * NY + self.y, fsdp) for d in range(1, NZ)]
        self.odd = self.z % 2
        self.to_pair = ((self.z + 1 - 2 * self.odd) * NY + self.y, fsdp)
        self.plane = []
        for d in range(1, 8):
            y, x, c = [
                1 - v if d & bit else v for v, bit in ((self.y, 4), (self.x, 2), (self.c, 1))
            ]
            self.plane.append((self.z * NY + y, x * NC + c))
        self.to_c, self.to_x, self.to_y = self.plane[0], self.plane[1], self.plane[3]

    def barrier(self):
        sem = pltpu.get_barrier_semaphore()
        for partner in self.plane + self.to_z:
            pl.semaphore_signal(sem, inc=1, device_id=partner, device_id_type=MESH)
        pl.semaphore_wait(sem, len(self.plane) + len(self.to_z))


def remote(src, dst, send, recv, to):
    return pltpu.make_async_remote_copy(
        src_ref=src, dst_ref=dst, send_sem=send, recv_sem=recv, device_id=to, device_id_type=MESH
    )


def part_ref(weights, part):
    return weights[min(part, 1)], (0, 0, DEEP)[part]


class Gather:
    COPIES = 13

    def __init__(self, place, weights, send, recv):
        self.at, self.weights, self.send, self.recv = place, weights, send, recv

    def copy(self, l, part, n):
        at = self.at
        array, row = part_ref(self.weights, part)
        a, b, rows, to = at.a, pl.ds(4 * at.y, 4), pl.ds(row, DEEP), at.to_c
        if n < 3:
            b, to = at.b, at.to_z[n]
        elif n < 5:
            to = (at.to_x, at.to_y)[n - 3]
        if n in (6, 8, 10, 11, 12):
            a = 2 * at.c + 1 - at.x
        if n in (7, 9, 10, 11, 12):
            b = pl.ds(4 * (1 - at.y), 4)
        if n in (6, 7):
            first = row + at.odd * HALF + (n - 6) * (HALF // 2)
            rows = pl.ds(pl.multiple_of(first, HALF // 2), HALF // 2)
            to = (at.to_y, at.to_x)[n - 6]
        if n in (10, 11):
            rows = pl.ds(pl.multiple_of(row + at.odd * HALF, HALF), HALF)
        if n == 11:
            to = at.to_pair
        if n == 12:
            rows = pl.ds(pl.multiple_of(row + (1 - at.odd) * HALF, HALF), HALF)
        ref = array.at[l, a, b, rows, :]
        q = PARTS * l + part
        return remote(ref, ref, self.send.at[q, n], self.recv.at[q, n], to)

    def start(self, l, part, *ns):
        for n in ns:
            self.copy(l, part, n).start()

    def wait(self, l, part, *ns):
        for n in ns:
            self.copy(l, part, n).wait_recv()

    def first(self, l, part):
        self.start(l, part, 0, 1, 2)

    def second(self, l, part):
        self.wait(l, part, 0, 1, 2)
        self.start(l, part, 3, 4, 5)

    def third(self, l, part):
        self.wait(l, part, 3)
        self.start(l, part, 6, 8)
        self.wait(l, part, 4)
        self.start(l, part, 7, 9)

    def fourth(self, l, part):
        self.wait(l, part, 6, 7)
        self.start(l, part, 11, 10)

    def fifth(self, l, part):
        self.wait(l, part, 11)
        self.start(l, part, 12)

    def last(self, l, part):
        self.wait(l, part, 5, 8, 9, 10, 12)

    def sent(self, l, part):
        for n in range(self.COPIES):
            self.copy(l, part, n).wait_send()


class Reduce:
    COPIES = 8

    def __init__(self, place, grads, landing, send, recv, credit):
        self.at, self.grads, self.landing = place, grads, landing
        self.send, self.recv, self.credit = send, recv, credit

    def refs(self, l, part):
        array, row = part_ref(self.grads, part)
        grads = array.at[l + 1 - min(part, 1), :, :, pl.ds(row, DEEP), :]
        return (grads, *self.landing[part])

    def copy(self, l, part, n):
        at, half = self.at, HALF
        g, r0, r1a, r1b, r2, r3 = self.refs(l, part)
        top, low, other = pl.ds(0, half), pl.ds(half, half), pl.ds(4 * (1 - at.y), 4)
        if n == 0:
            src, dst, to = g.at[pl.ds(2 * (1 - at.c), 2)], r0, at.to_c
        elif n == 1:
            src, dst, to = r0.at[1 - at.x, :, top, :], r1a, at.to_x
        elif n == 2:
            src, dst, to = r0.at[:, other, low, :], r1b, at.to_y
        elif n == 3:
            src, dst, to = r1a.at[other], r2.at[:, top, :], at.to_y
        elif n == 4:
            src, dst, to = r1b.at[1 - at.x], r2.at[:, low, :], at.to_x
        else:
            src, dst, to = r2.at[(at.z + n - 4) % NZ], r3.at[n - 5], at.to_z[n - 5]
        q = PARTS * l + part
        return remote(src, dst, self.send.at[q, n], self.recv.at[q, n], to)

    def may_send(self, l, part, *partners):
        @pl.when(l < LAYERS - 1)
        def _():
            for n in partners:
                pl.semaphore_wait(self.credit.at[part, n], 1)

    def allow(self, l, part, *credits):
        at = self.at

        @pl.when(l > 0)
        def _():
            for n, to in credits:
                pl.semaphore_signal(
                    self.credit.at[part, n], inc=1, device_id=to, device_id_type=MESH
                )

    def start(self, l, part):
        self.may_send(l, part, 0)
        self.copy(l, part, 0).start()

    def first(self, l, part):
        at, half = self.at, HALF
        g, r0, _, _, _, _ = self.refs(l, part)
        top, low = pl.ds(0, half), pl.ds(half, half)
        self.copy(l, part, 0).wait_recv()

        x = 1 - at.x
        total = g[2 * at.c + x, :, top].astype(WIDE) + r0[x, :, top].astype(WIDE)
        r0[x, :, top] = total.astype(LOWER)
        self.may_send(l, part, 1, 2)
        self.copy(l, part, 1).start()
        other = pl.ds(4 * (1 - at.y), 4)
        for x in range(NX):
            total = g[2 * at.c + x, other, low].astype(WIDE) + r0[x, other, low].astype(WIDE)
            r0[x, other, low] = total.astype(LOWER)
        self.copy(l, part, 2).start()

    def second(self, l, part):
        at, half = self.at, HALF
        g, r0, r1a, r1b, _, _ = self.refs(l, part)
        top, low = pl.ds(0, half), pl.ds(half, half)

        x, other, column = 1 - at.x, pl.ds(4 * (1 - at.y), 4), pl.ds(4 * at.y, 4)
        self.copy(l, part, 1).wait_recv()
        total = g[at.a, other, top].astype(WIDE) + r0[at.x, other, top].astype(WIDE)
        r1a[other] = (total + r1a[other].astype(WIDE)).astype(LOWER)
        self.may_send(l, part, 6, 7)
        self.copy(l, part, 3).start()
        self.copy(l, part, 2).wait_recv()
        total = g[2 * at.c + x, column, low].astype(WIDE) + r0[x, column, low].astype(WIDE)
        r1b[x] = (total + r1b[x].astype(WIDE)).astype(LOWER)
        self.copy(l, part, 4).start()

    def chip_sums(self, l, part, z):
        at, half = self.at, HALF
        g, r0, r1a, r1b, r2, _ = self.refs(l, part)
        top, low, b = pl.ds(0, half), pl.ds(half, half), 4 * at.y + z
        upper = g[at.a, b, top].astype(WIDE) + r0[at.x, b, top].astype(WIDE)
        lower = g[at.a, b, low].astype(WIDE) + r0[at.x, b, low].astype(WIDE)
        return (
            upper + r1a[b].astype(WIDE) + r2[z, top].astype(WIDE),
            lower + r1b[at.x, z].astype(WIDE) + r2[z, low].astype(WIDE),
        )

    def third(self, l, part, out):
        at, half, row = self.at, HALF, DEEP * part
        r2 = self.landing[part][3]
        for n in (3, 4):
            self.copy(l, part, n).wait_recv()
        self.may_send(l, part, 3, 4, 5)
        for n in range(3):
            z = (at.z + n + 1) % NZ
            upper, lower = self.chip_sums(l, part, z)
            r2[z, pl.ds(0, half)] = upper.astype(LOWER)
            r2[z, pl.ds(half, half)] = lower.astype(LOWER)
            self.copy(l, part, 5 + n).start()
        upper, lower = self.chip_sums(l, part, at.z)
        out[l, row : row + half, :] = upper
        out[l, row + half : row + 2 * half, :] = lower
        for n in range(5):
            self.copy(l, part, n).wait_send()
        self.allow(l, part, (0, at.to_c), (1, at.to_x), (2, at.to_y))

    def last(self, l, part, out, squares):
        at, row = self.at, DEEP * part
        r3 = self.landing[part][4]
        rows = slice(row, row + DEEP)
        total = out[l, rows, :]
        for n in range(3):
            self.copy(l, part, 5 + n).wait_recv()
            total = total + r3[n].astype(WIDE)
        out[l, rows, :] = total
        squares[0:1, :] += col_sum(total * total)
        for n in range(5, self.COPIES):
            self.copy(l, part, n).wait_send()
        late = [(6, at.to_x), (7, at.to_y)] + [(5 - n, at.to_z[n]) for n in range(3)]
        self.allow(l, part, *late)


class Total:
    COPIES = 7

    def __init__(self, place, ref, rows, send, recv):
        self.at, self.ref, self.rows = place, ref, rows // 2
        self.send, self.recv = send, recv

    def half(self, n):
        return self.ref.at[pl.ds(pl.multiple_of(n * self.rows, 8), self.rows), :]

    def whole(self):
        return self.ref.at[pl.ds(0, 2 * self.rows), :]

    def copy(self, n):
        at = self.at
        mine, other = self.half(at.c), self.half(1 - at.c)
        src, dst, to = (
            (other, self.half(2), at.to_c),
            (self.half(8), self.half(3), at.to_x),
            (self.half(9), self.half(4), at.to_y),
            (self.half(10), self.half(5), at.to_z[0]),
            (self.half(10), self.half(6), at.to_z[1]),
            (self.half(10), self.half(7), at.to_z[2]),
            (mine, self.half(11), at.to_c),
        )[n]
        return remote(src, dst, self.send.at[n], self.recv.at[n], to)

    def start(self):
        self.copy(0).start()

    def step(self, n):
        self.copy(n).wait_recv()
        own = self.half(self.at.c) if n == 0 else self.half(7 + n)
        self.half(8 + n)[...] = own[...] + self.half(2 + n)[...]
        for m in ((1,), (2,), (3, 4, 5))[n]:
            self.copy(m).start()

    def back(self):
        for m in (3, 4, 5):
            self.copy(m).wait_recv()
        self.copy(0).wait_send()
        total = None
        for z in range(NZ):
            term = self.half(10)[...]
            for n in range(3):
                from_z = (self.at.z + NZ - 1 - n) % NZ
                term = jnp.where(from_z == z, self.half(5 + n)[...], term)
            total = term if total is None else total + term
        self.half(self.at.c)[...] = total
        self.copy(6).start()

    def last(self):
        self.copy(6).wait_recv()
        self.half(1 - self.at.c)[...] = self.half(11)[...]
        for n in range(1, self.COPIES):
            self.copy(n).wait_send()


class Norm:
    COPIES = 10

    def __init__(self, place, plane, column, send, recv):
        self.at, self.plane, self.column = place, plane, column
        self.send, self.recv = send, recv

    def copy(self, n):
        at = self.at
        if n < 7:
            ref, to = self.plane.at[at.r], at.plane[n]
        else:
            ref, to = self.column.at[at.z], at.to_z[n - 7]
        return remote(ref, ref, self.send.at[n], self.recv.at[n], to)

    def start(self, tile):
        self.plane[self.at.r] = tile
        for n in range(7):
            self.copy(n).start()

    def total(self, ref, ns):
        for n in ns:
            self.copy(n).wait_recv()
        total = ref[0]
        for n in range(1, ref.shape[0]):
            total = total + ref[n]
        return total

    def step(self):
        self.column[self.at.z] = self.total(self.plane, range(7))
        for n in range(7, self.COPIES):
            self.copy(n).start()

    def last(self):
        total = self.total(self.column, range(7, self.COPIES))
        for n in range(self.COPIES):
            self.copy(n).wait_send()
        return total


LANDING = (
    (NX, 8, DEEP, D),
    (8, HALF, D),
    (NX, NZ, HALF, D),
    (NZ, DEEP, D),
    (3, DEEP, D),
)


def stage_rows(qkv, out, up, down, l):
    return (
        [(qkv.at[l, :, pl.ds(j * D, D)], 16 * j, 16) for j in range(3)]
        + [(out.at[l], 48, 16)]
        + [(up.at[l, :, pl.ds(j * D, D)], 64 + 16 * j, 16) for j in range(4)]
        + [(down.at[l], 128, 64)]
    )


BEGIN, SETUP, START, QKV_HALF, QKV, WINDOWS_HALF, WINDOWS, UP_HALF, UP, DOWN = range(10)
FIRST, SECOND, THIRD, FOURTH, FIFTH, LAST, SEND = range(7)
GATHER_PLAN = {
    (-1, BEGIN): [(FIRST, 0, 0), (FIRST, 0, 1), (FIRST, 0, 2)],
    (-1, SETUP): [(FIRST, 1, 0), (FIRST, 1, 1), (SECOND, 0, 0)],
    (0, START): [(FIRST, 1, 2), (SECOND, 0, 1), (THIRD, 0, 0), (FOURTH, 0, 0), (SECOND, 0, 2), (THIRD, 0, 1), (FIFTH, 0, 0), (LAST, 0, 0)],
    (0, QKV_HALF): [(SECOND, 1, 0), (FOURTH, 0, 1)],
    (0, QKV): [(FIRST, 2, 0), (THIRD, 0, 2), (FIFTH, 0, 1)],
    (0, WINDOWS_HALF): [(SECOND, 1, 1), (LAST, 0, 1)],
    (0, WINDOWS): [(FIRST, 2, 1), (FOURTH, 0, 2)],
    (0, UP_HALF): [(THIRD, 1, 0), (FIFTH, 0, 2), (SECOND, 1, 2)],
    (0, UP): [(FIRST, 2, 2), (LAST, 0, 2), (FOURTH, 1, 0), (SECOND, 2, 0)],
    (0, DOWN): [(THIRD, 1, 1), (FIFTH, 1, 0)],
    (1, START): [(LAST, 1, 0), (FOURTH, 1, 1)],
    (1, QKV_HALF): [(SECOND, 2, 1)],
    (1, QKV): [(THIRD, 1, 2), (FIFTH, 1, 1)],
    (1, WINDOWS_HALF): [(LAST, 1, 1)],
    (1, WINDOWS): [(SECOND, 2, 2), (FOURTH, 1, 2)],
    (1, UP_HALF): [(THIRD, 2, 0), (FIFTH, 1, 2), (LAST, 1, 2)],
    (1, UP): [(FOURTH, 2, 0)],
    (1, DOWN): [(THIRD, 2, 1), (FIFTH, 2, 0)],
    (2, START): [(LAST, 2, 0), (FOURTH, 2, 1)],
    (2, QKV): [(THIRD, 2, 2), (FIFTH, 2, 1)],
    (2, WINDOWS_HALF): [(LAST, 2, 1)],
    (2, WINDOWS): [(FOURTH, 2, 2)],
    (2, UP): [(FIFTH, 2, 2), (LAST, 2, 2)],
}


def train_kernel(refs, alone):
    k = Kit(**refs)

    def kept(names, l, back):
        copies = []
        for name in names:
            here, there = refs[name], refs["keep_" + name].at[l]
            src, dst = (there, here) if back else (here, there)
            copies.append(pltpu.make_async_copy(src, dst, k.keep_sem.at[KEEP.index(name)]))
        return copies

    def start(copies):
        for copy in copies:
            copy.start()

    def wait(copies):
        for copy in copies:
            copy.wait()

    def kept_x(back):
        here, there = k.xs.at[0], k.keep_x
        src, dst = (there, here) if back else (here, there)
        return [pltpu.make_async_copy(src, dst, k.keep_sem.at[len(KEEP)])]

    arrays = [(l, n) for l in range(LAYERS) for n in (0, 1)]
    parts = [(l, part) for l in range(LAYERS) for part in range(PARTS)]
    weights = (k.wa, k.wf)
    if alone:
        loads = [
            pltpu.make_async_copy((k.all_a, k.all_f)[n].at[l], weights[n].at[l], k.load_sem.at[2 * l + n])
            for l, n in arrays
        ]
        stores = [
            pltpu.make_async_copy(
                weights[n].at[l + 1 - n], (k.grad_a, k.grad_f)[n].at[l], k.load_sem.at[2 * l + n]
            )
            for l, n in arrays
        ]
        start(loads)
    else:
        place = Place()
        gather = Gather(place, weights, k.gather_send, k.gather_recv)
        reduce = Reduce(
            place, weights, k.landing, k.reduce_send, k.reduce_recv, k.credit
        )
        sums = Total(place, k.xs.at[1], SMALL, k.sum_send, k.sum_recv)
        norm = Norm(place, k.norm_plane, k.norm_column, k.norm_send, k.norm_recv)

    def run(plan):
        stages = (
            gather.first,
            gather.second,
            gather.third,
            gather.fourth,
            gather.fifth,
            gather.last,
        )
        for stage, l, part in plan:
            stages[stage](l, part)

    def poll(l, point):
        if alone:
            return
        for layer in range(LAYERS):
            plan = GATHER_PLAN.get((layer, point))
            if plan:

                @pl.when(l == layer)
                def _(plan=plan):
                    run(plan)

    if not alone:
        staged = []
        for l in range(LAYERS):
            for n, (src, row, count) in enumerate(stage_rows(k.qkv_w, k.out_w, k.up_w, k.down_w, l)):
                dst = k.xs.at[2, pl.ds(l * PACK + row, count), :]
                staged.append(pltpu.make_async_copy(src, dst, k.stage_sem.at[l, n]))
        start(staged)
        place.barrier()
        for l in range(LAYERS):
            wait(staged[9 * l : 9 * l + 9])
            row = l * PACK
            for part in range(PARTS):
                array, first = part_ref(weights, part)
                mine = k.xs[2, row + DEEP * part : row + DEEP * (part + 1), :].astype(LOWER)
                array[l, place.a, place.b, first : first + DEEP, :] = mine
                if (FIRST, l, part) in GATHER_PLAN[-1, BEGIN]:
                    gather.first(l, part)
        k.squares_sum[...] = jnp.zeros_like(k.squares_sum)

    setup_stage(k)
    start(kept_x(False))
    if not alone:
        run(GATHER_PLAN[-1, SETUP])

    grad = 2

    def forward(l, carry):
        if alone:
            pltpu.make_async_copy(k.all_a.at[l], k.wa.at[l], k.load_sem.at[2 * l]).wait()

        @pl.when(l > 0)
        def _():
            wait(kept(KEEP_ATTN, l - 1, False))

        poll(l, START)
        forward_qkv(k, l, lambda: poll(l, QKV_HALF))
        poll(l, QKV)
        forward_windows(k, l, lambda: poll(l, WINDOWS_HALF))

        @pl.when(l < LAYERS - 1)
        def _():
            start(kept(KEEP_ATTN, l, False))

        @pl.when(l > 0)
        def _():
            wait(kept(KEEP_FFN, l - 1, False))

        @pl.when(l == 1)
        def _():
            wait(kept_x(False))

        if alone:
            pltpu.make_async_copy(k.all_f.at[l], k.wf.at[l], k.load_sem.at[2 * l + 1]).wait()
        poll(l, WINDOWS)

        @pl.when(l < LAYERS - 1)
        def _():
            forward_up(k, l, lambda: poll(l, UP_HALF))

        @pl.when(l == LAYERS - 1)
        def _():
            forward_up_states(k, l, grad)

        poll(l, UP)

        @pl.when(l < LAYERS - 1)
        def _():
            forward_down(k, l, (l + 1) % 2)

        @pl.when(l == LAYERS - 1)
        def _():
            down_rows(k, l, slice(0, STATES), grad)

        @pl.when(l < LAYERS - 1)
        def _():
            start(kept(KEEP_FFN, l, False))

        poll(l, DOWN)
        return carry

    lax.fori_loop(0, LAYERS, forward, 0)
    if not alone:
        for l, part in parts:
            gather.sent(l, part)
    head_stage(k, grad)

    def run_reduce(stage, l, part):
        if stage == THIRD:
            reduce.third(l, part, k.shard)
        elif stage == LAST:
            reduce.last(l, part, k.shard, k.squares_sum)
        else:
            {SEND: reduce.start, FIRST: reduce.first, SECOND: reduce.second}[stage](l, part)

    def backward(n, carry):
        l = LAYERS - 1 - n

        def behind(name, *stages):
            @pl.when(n > 0)
            def _():
                for stage, part, *more in stages:
                    stage(l + 1, part, *more)

        @pl.when(n > 0)
        def _():
            wait(kept(KEEP_FFN, l, True))

        def now(stage, part, early=None):
            if alone:
                return
            if early is None:
                run_reduce(stage, l, part)
                return

            @pl.when((n == LAYERS - 1) if early else (n < LAYERS - 1))
            def _():
                run_reduce(stage, l, part)

        def then(stage, part):
            if not alone:

                @pl.when(n > 0)
                def _():
                    run_reduce(stage, l + 1, part)

        def in_ffn():
            then(LAST, 2)
            then(THIRD, 1)
            then(FIRST, 0)

        def in_windows():
            now(FIRST, 1, False)
            now(SECOND, 2, True)

        states = slice(0, STATES)

        @pl.when(n > 0)
        def _():
            backward_ffn(k, l, grad, in_ffn)
            backward_down_grads(k, l)

        @pl.when(n == 0)
        def _():
            ffn_back_rows(k, l, states, grad)
            backward_down_grads(k, l, states)

        now(SEND, 2)
        then(LAST, 1)
        then(SECOND, 0)

        @pl.when(n > 0)
        def _():
            backward_up_grads(k, l)

        @pl.when(n == 0)
        def _():
            backward_up_grads(k, l, states)

        @pl.when((n > 0) & (n < LAYERS - 1))
        def _():
            start(kept(KEEP_FFN, l - 1, True))

        now(SEND, 1)
        now(FIRST, 2, True)

        @pl.when(n > 0)
        def _():
            wait(kept(KEEP_ATTN, l, True))

        @pl.when(n > 0)
        def _():
            backward_out(k, l, grad)

        @pl.when(n == 0)
        def _():
            backward_out_states(k, l, grad)
            start(kept(KEEP_FFN, l - 1, True))

        now(FIRST, 2, False)
        now(FIRST, 1, True)
        then(THIRD, 0)
        backward_windows(k, l, in_windows)
        now(SECOND, 2, False)
        now(THIRD, 2, True)
        then(LAST, 0)
        backward_attn_grads(k, l)

        @pl.when(n < LAYERS - 1)
        def _():
            start(kept(KEEP_ATTN, l - 1, True))

        now(SEND, 0)
        now(THIRD, 2, False)
        now(SECOND, 1, True)

        @pl.when(n == LAYERS - 1)
        def _():
            wait(kept_x(True))

        backward_input(k, l, grad)

        @pl.when(n == 0)
        def _():
            start(kept_x(True))

        now(SECOND, 1, False)
        now(FIRST, 0, True)
        now(THIRD, 1, True)
        return carry

    lax.fori_loop(0, LAYERS, backward, 0)
    if alone:
        start(stores)
        small_stage(k, k.small_out, grad)
        wait(stores)
        return
    small_stage(k, sums.whole(), grad)
    sums.start()
    reduce.last(0, 2, k.shard, k.squares_sum)
    reduce.second(0, 0)
    sums.step(0)
    reduce.third(0, 0, k.shard)
    sums.step(1)
    reduce.last(0, 1, k.shard, k.squares_sum)
    sums.step(2)
    reduce.last(0, 0, k.shard, k.squares_sum)
    squares = k.squares_sum[...]
    norm.start(sum(squares[:, n * 128 : (n + 1) * 128] for n in range(D // 128)))
    sums.back()
    norm.step()
    sums.last()
    k.small_out[...] = sums.whole()[...]
    k.squares[...] = norm.last()


def train_pass(inputs, weights, alone):
    whole = pl.BlockSpec(memory_space=pltpu.VMEM)
    scalars = pl.BlockSpec(memory_space=pltpu.SMEM)
    anywhere = pl.BlockSpec(memory_space=pl.ANY)
    dma = pltpu.SemaphoreType.DMA
    count = PARTS * LAYERS
    names = ["states", "actions", "returns", "starts", "repeats", "valid"]
    names += ["log_temp", "small", "head_bias"]
    out_shape = {"small_out": ((SMALL, D), WIDE)}
    for name in KEEP:
        shape, dtype = WORK_SHAPES[name]
        out_shape["keep_" + name] = ((LAYERS - 1,) + shape, dtype)
    out_shape["keep_x"] = ((ROWS, D), WIDE)
    scratch = {name: pltpu.VMEM(*shape) for name, shape in WORK_SHAPES.items()}
    scratch["keep_sem"] = dma((len(KEEP) + 1,))
    if alone:
        names += ["all_a", "all_f"]
        out_shape["grad_a"] = ((LAYERS, 4, 8, ATTN, D), LOWER)
        out_shape["grad_f"] = ((LAYERS, 4, 8, FFN, D), LOWER)
        scratch["load_sem"] = dma((count,))
    else:
        names += ["qkv_w", "out_w", "up_w", "down_w"]
        out_shape["shard"] = ((LAYERS, PACK, D), WIDE)
        out_shape["squares"] = ((8, 128), WIDE)
        for part in range(PARTS):
            for n, shape in enumerate(LANDING):
                scratch["land_%d_%d" % (part, n)] = pltpu.VMEM(shape, LOWER)
        scratch["stage_sem"] = dma((LAYERS, 9))
        scratch["squares_sum"] = pltpu.VMEM((8, D), WIDE)
        for name, copies in (("gather", Gather.COPIES), ("reduce", Reduce.COPIES)):
            scratch[name + "_send"] = dma((count, copies))
            scratch[name + "_recv"] = dma((count, copies))
        scratch["credit"] = pltpu.SemaphoreType.REGULAR((PARTS, 8))
        scratch["norm_plane"] = pltpu.VMEM((8, 8, 128), WIDE)
        scratch["norm_column"] = pltpu.VMEM((NZ, 8, 128), WIDE)
        for name, copies in (("sum", Total.COPIES), ("norm", Norm.COPIES)):
            scratch[name + "_send"] = dma((copies,))
            scratch[name + "_recv"] = dma((copies,))
    spaces = dict.fromkeys(("starts", "repeats", "head_bias", "log_temp"), scalars)
    for name in ("all_a", "all_f", "grad_a", "grad_f", "qkv_w", "out_w", "up_w", "down_w"):
        spaces[name] = anywhere
    for name in KEEP + ("x",):
        spaces["keep_" + name] = anywhere
    every = names + list(out_shape) + list(scratch)

    def kernel(*given):
        refs = dict(zip(every, given))
        refs["landing"] = [
            [refs.get("land_%d_%d" % (part, n)) for n in range(len(LANDING))] for part in range(PARTS)
        ]
        train_kernel(refs, alone)

    results = pl.pallas_call(
        kernel,
        name="train_pass",
        out_shape=tuple(jax.ShapeDtypeStruct(*shape) for shape in out_shape.values()),
        in_specs=[spaces.get(name, whole) for name in names],
        out_specs=tuple(spaces.get(name, whole) for name in out_shape),
        scratch_shapes=list(scratch.values()),
        compiler_params=pltpu.CompilerParams(
            vmem_limit_bytes=VMEM_BYTES,
            collective_id=None if alone else 0,
            has_side_effects=not alone,
        ),
        cost_estimate=pl.CostEstimate(
            flops=6 * 10**10, bytes_accessed=4 * 10**7, transcendentals=10**7
        ),
    )(*inputs, *weights)
    return dict(zip(out_shape, results))


def adam_parts(weight, grad, first, second, rate):
    first = BETA_ONE * first + (1.0 - BETA_ONE) * grad
    second = BETA_TWO * second + (1.0 - BETA_TWO) * grad * grad
    fix_one = 1.0 - BETA_ONE**STEP
    fix_two = 1.0 - BETA_TWO**STEP
    fresh = weight - rate * (
        first * (1.0 / fix_one) / (jnp.sqrt(second * (1.0 / fix_two)) + ADAM_EPS) + DECAY * weight
    )
    return fresh, first, second


def adam_kernel(*refs):
    shard, small_grad, squares, groups, log_temp = refs[:5]
    small, small_first, small_second, bias, bias_first, bias_second = refs[5:11]
    mats, firsts, seconds = refs[11:15], refs[15:19], refs[19:23]
    totals, norm, next_temp, s_next, s_first, s_second, b_next, b_first, b_second = refs[23:32]
    m_next, m_copy, m_first, m_second = refs[32:36], refs[36:40], refs[40:44], refs[44:48]
    extra = small_grad[NROWS : NROWS + 3, 0:128]
    lane = iota((1, 128), 1)
    bias_mean = jnp.where(lane < A, extra[1:2], 0.0)
    bias_spread = jnp.where(lane < A, extra[2:3], 0.0)

    def all_sum(v):
        return jnp.sum(jnp.sum(v, 0, keepdims=True), 1, keepdims=True)

    grads = small_grad[0:NROWS, :]
    square = (
        all_sum(squares[0:1, :])
        + all_sum(grads * grads)
        + all_sum(bias_mean * bias_mean)
        + all_sum(bias_spread * bias_spread)
    )
    length = jnp.sqrt(square)
    clip = jnp.minimum(1.0, CLIP / (length + 1e-06))

    def rate_of(l, kind):
        group = jnp.full((1, 1), groups[l, kind], jnp.int32).astype(WIDE)
        return LEARN * jnp.exp2(-group)

    def update(l, kind, rows, cols, grad):
        at = (l, rows, cols)
        fresh, first, second = adam_parts(
            mats[kind][at], clip * grad, firsts[kind][at], seconds[kind][at], rate_of(l, kind)
        )
        m_next[kind][at] = fresh
        m_copy[kind][at] = fresh.astype(LOWER)
        m_first[kind][at] = first
        m_second[kind][at] = second

    every = slice(0, 16)
    for l in range(LAYERS):
        for j in range(3):
            update(l, 0, every, slice(j * D, (j + 1) * D), shard[l, 16 * j : 16 * j + 16, :])
        update(l, 1, every, slice(0, D), shard[l, 48:64, :])
        for j in range(4):
            rows = slice(64 + 16 * j, 80 + 16 * j)
            update(l, 2, every, slice(j * D, (j + 1) * D), shard[l, rows, :])
        update(l, 3, slice(0, 64), slice(0, D), shard[l, 128:192, :])

    s_next[...], s_first[...], s_second[...] = adam_parts(
        small[...], clip * grads, small_first[...], small_second[...], LEARN
    )

    def scalar(v, n):
        return jnp.sum(jnp.where(lane == n, v, 0.0))

    def row(ref):
        v = jnp.zeros((1, 128), WIDE)
        for n in range(2 * A):
            v = jnp.where(lane == n, ref[n], v)
        return v

    grad = bias_mean + pltpu.roll(bias_spread, A, 1)
    results = adam_parts(row(bias), clip * grad, row(bias_first), row(bias_second), LEARN)
    for ref, result in zip((b_next, b_first, b_second), results):
        for n in range(2 * A):
            ref[n] = scalar(result, n)
    sums = extra[0:1]
    for n in range(3):
        totals[n] = scalar(sums, n)
    norm[0] = jnp.sum(length)
    logs = jnp.full((1, 1), log_temp[0], WIDE)
    ratio = jnp.full((1, 1), scalar(sums, 1), WIDE) / jnp.full((1, 1), scalar(sums, 2), WIDE)
    next_temp[0] = jnp.sum(logs - TEMP_RATE * jnp.exp(logs) * (ratio + A))


def adam_all(shard, small_grad, squares, groups, log_temp, smalls, biases, mats, firsts, seconds):
    scalars = pl.BlockSpec(memory_space=pltpu.SMEM)

    whole = pl.BlockSpec(memory_space=pltpu.VMEM)

    def like(array, dtype=WIDE):
        return jax.ShapeDtypeStruct(array.shape, dtype)

    stacks = list(mats) + list(firsts) + list(seconds)
    small, bias = smalls[0], biases[0]
    return pl.pallas_call(
        adam_kernel,
        name="adam",
        out_shape=(
            (jax.ShapeDtypeStruct((3,), WIDE),)
            + (jax.ShapeDtypeStruct((1,), WIDE),) * 2
            + (like(small),) * 3
            + (like(bias),) * 3
            + tuple(like(m) for m in mats)
            + tuple(like(m, LOWER) for m in mats)
            + tuple(like(m) for m in mats) * 2
        ),
        in_specs=[whole] * 3 + [scalars] * 2 + [whole] * 3 + [scalars] * 3 + [whole] * 12,
        out_specs=(scalars,) * 3 + (whole,) * 3 + (scalars,) * 3 + (whole,) * 16,
        compiler_params=pltpu.CompilerParams(vmem_limit_bytes=VMEM_BYTES),
        cost_estimate=pl.CostEstimate(flops=10**7, bytes_accessed=8 * 10**6, transcendentals=10**6),
    )(shard, small_grad, squares, groups, log_temp, *smalls, *biases, *stacks)


def gather_packed(mats, axes, count):
    group = count // BLOCKS
    pieces = []
    for mat in mats:
        rows, wide = mat.shape[1], mat.shape[2] // D
        piece = mat.astype(LOWER).reshape(LAYERS, rows, wide, D)
        piece = lax.all_gather(piece, axes, axis=1, tiled=True)
        piece = piece.reshape(LAYERS, NZ, NY, NX, NC, group * rows, wide, D)
        piece = piece.transpose(0, 4, 3, 2, 1, 6, 5, 7)
        pieces.append(piece.reshape(LAYERS, 4, 8, wide * group * rows, D))
    return jnp.concatenate(pieces[:2], 3), jnp.concatenate(pieces[2:], 3)


def scatter_packed(grads, mats, axes):
    results, first = [], 0
    for n, mat in enumerate(mats):
        rows, wide = mat.shape[1], mat.shape[2] // D
        total = lax.psum(1, axes) * rows
        deep = total // BLOCKS
        first = 0 if n % 2 == 0 else first
        piece = grads[n // 2][:, :, :, first : first + wide * deep].astype(WIDE)
        first += wide * deep
        piece = piece.reshape(LAYERS, NC, NX, NY, NZ, wide, deep, D)
        piece = piece.transpose(0, 4, 3, 2, 1, 6, 5, 7).reshape(LAYERS, total, wide * D)
        results.append(lax.psum_scatter(piece, axes, scatter_dimension=1, tiled=True))
    return results


def local(
    buf_states,
    buf_actions,
    buf_returns,
    window_starts,
    window_repeats,
    valid_steps,
    matrix_groups,
    log_temp,
    small_rows,
    head_bias,
    qkv_weight,
    out_weight,
    up_weight,
    down_weight,
    small_first,
    bias_first,
    qkv_first,
    out_first,
    up_first,
    down_first,
    small_second,
    bias_second,
    qkv_second,
    out_second,
    up_second,
    down_second,
):
    axes = ("dp", "fsdp")
    mats = (qkv_weight, out_weight, up_weight, down_weight)
    firsts = (qkv_first, out_first, up_first, down_first)
    seconds = (qkv_second, out_second, up_second, down_second)
    pass_inputs = (
        buf_states.T,
        buf_actions.T,
        buf_returns[None],
        window_starts,
        window_repeats,
        valid_steps,
        log_temp,
        small_rows,
        head_bias,
    )
    if FF // down_weight.shape[1] == BLOCKS and lax.psum(1, "fsdp") == NX * NC:
        made = train_pass(pass_inputs, mats, False)
        return adam_all(
            made["shard"],
            made["small_out"],
            made["squares"],
            matrix_groups,
            log_temp,
            (small_rows, small_first, small_second),
            (head_bias, bias_first, bias_second),
            mats,
            firsts,
            seconds,
        )
    packed = gather_packed(mats, axes, FF // down_weight.shape[1])
    made = train_pass(pass_inputs, packed, True)
    big = scatter_packed((made["grad_a"], made["grad_f"]), mats, axes)
    small = made["small_out"]
    small = lax.psum(small, axes)
    small_grad, totals = small[:NROWS], small[NROWS, :3]
    bias_grad = jnp.concatenate([small[NROWS + 1, :A], small[NROWS + 2, :A]])
    square = sum((jnp.sum(piece * piece) for piece in big))
    square = (
        lax.psum(square, axes) + jnp.sum(small_grad * small_grad) + jnp.sum(bias_grad * bias_grad)
    )
    grad_norm = jnp.sqrt(square)
    clip = jnp.minimum(1.0, CLIP / (grad_norm + 1e-06))
    rates = LEARN * jnp.exp2(-matrix_groups.astype(WIDE))
    results = [
        adam_parts(
            mats[kind], clip * big[kind], firsts[kind], seconds[kind], rates[:, kind][:, None, None]
        )
        for kind in range(4)
    ]
    small_new = adam_parts(small_rows, clip * small_grad, small_first, small_second, LEARN)
    bias_new = adam_parts(head_bias, clip * bias_grad, bias_first, bias_second, LEARN)
    next_temp = log_temp - TEMP_RATE * jnp.exp(log_temp) * (totals[1] / totals[2] + A)
    return (
        (totals, grad_norm[None], next_temp)
        + small_new
        + bias_new
        + tuple(r[0] for r in results)
        + tuple(r[0].astype(LOWER) for r in results)
        + tuple(r[1] for r in results)
        + tuple(r[2] for r in results)
    )


def solution(mesh):
    rows = P(("dp", "fsdp"), None)
    vector = P(("dp", "fsdp"))
    stack = P(None, ("dp", "fsdp"), None)
    same = P()
    in_specs = (
        (rows, rows, vector, vector, vector, rows)
        + (same,) * 4
        + (stack,) * 4
        + (same,) * 2
        + (stack,) * 4
        + (same,) * 2
        + (stack,) * 4
    )
    out_specs = (same,) * 9 + (stack,) * 16
    return jax.shard_map(local, mesh=mesh, in_specs=in_specs, out_specs=out_specs, check_vma=False)
```

```python
import math

import jax
import jax.numpy as jnp
from jax import lax
from jax.experimental import pallas as pl
from jax.experimental.pallas import tpu as pltpu
from jax.sharding import PartitionSpec as P

D = 512
H = 8
HD = 64
FF = 2048
S = 11
A = 3
K = 20
STEP = 10

EPS = 1e-05
CLIP = 1.0
LEARN = 0.03
BETA_ONE = 0.5
BETA_TWO = 0.7
DECAY = 0.01
ADAM_EPS = 1e-08
TEMP_RATE = 0.1
MASKED = -1e30
HALF_LOG_TAU = 0.5 * math.log(2.0 * math.pi)
GELU_C = math.sqrt(2.0 / math.pi)
GELU_A = 0.044715
HIGH = lax.Precision.HIGHEST
LOWER = jnp.bfloat16
WIDE = jnp.float32

LAYERS = 3
WINS = 16
BUF_DEV = 64
SLOT = 64
ROWS = WINS * SLOT
CHUNK = 512
CHUNKS = ROWS // CHUNK
STATE_SLOT = 24
STATES = WINS * STATE_SLOT
BLOCKS = 32
PACK = 192
ATTN, FFN = 64, 128
EMB = S + A + 1 + K + 3
FIN = EMB
HEADW = EMB + 2
BASE = EMB + 2 + 2 * A
PER = 9 + FF // D
NROWS = BASE + LAYERS * PER
SMALL = 96
HEAD_AT = 64
EMB_AT = ROWS - 128
VMEM_BYTES = 64 * 1024 * 1024


def dot(a, b, precision=None):
    return lax.dot_general(
        a, b, (((1,), (0,)), ((), ())), precision=precision, preferred_element_type=WIDE
    )


def dot_nt(a, b, precision=None):
    return lax.dot_general(
        a, b, (((1,), (1,)), ((), ())), precision=precision, preferred_element_type=WIDE
    )


def dot_tn(a, b, precision=None):
    return lax.dot_general(
        a, b, (((0,), (0,)), ((), ())), precision=precision, preferred_element_type=WIDE
    )


def iota(shape, dim):
    return lax.broadcasted_iota(jnp.int32, shape, dim)


def col_sum(v):
    return jnp.sum(v, 0, keepdims=True)


def row_mean(v):
    return jnp.mean(v, -1, keepdims=True)


def norm_parts(x):
    center = x - row_mean(x)
    scale = lax.rsqrt(row_mean(center * center) + EPS)
    return center * scale, scale


def norm_back(xhat, scale, gain, grad):
    scaled = grad * gain
    return scale * (scaled - row_mean(scaled) - xhat * row_mean(scaled * xhat))


def token_rows(at, count):
    row = at + iota((count, 128), 0)
    place = row & (SLOT - 1)
    step = (place * 21846) >> 16
    return row >> 6, step, place - 3 * step, place < 3 * K


def chunk_rows(c):
    return pl.ds(pl.multiple_of(c * CHUNK, CHUNK), CHUNK)


def owner_place(i):
    z, y, x, c = i // 8, (i // 4) % 2, (i // 2) % 2, i % 2
    return 2 * c + x, 4 * y + z


class Kit:
    def __init__(self, **refs):
        self.__dict__.update(refs)

    def row(self, l, k):
        return self.lrows[l, k : k + 1, :]

    def blocks(self, ref, l, first, count, owners):
        places = [owner_place(i) for i in owners]
        return jnp.concatenate([ref[l, a, b, first : first + count, :] for a, b in places], 0)

    def w_qkv(self, l, j):
        return self.blocks(self.wa, l, 16 * j, 16, range(BLOCKS))

    def w_out(self, l):
        return self.blocks(self.wa, l, 48, 16, range(BLOCKS))

    def w_up(self, l, j):
        return self.blocks(self.wf, l, 16 * j, 16, range(BLOCKS))

    def w_down(self, l, j):
        return self.blocks(self.wf, l, 64, 64, range(8 * j, 8 * j + 8))


def slot(l):
    return l % 2


def setup_stage(k):
    k.xs[2, EMB_AT:ROWS, :] = jnp.zeros((128, D), WIDE)
    k.xs[2, EMB_AT : EMB_AT + EMB, :] = k.small[0:EMB, :]
    k.headw[...] = jnp.zeros_like(k.headw)
    k.headw[0, 0:A, :] = k.small[HEADW : HEADW + A, :].astype(LOWER)
    k.headw[1, 0:A, :] = k.small[HEADW + A : HEADW + 2 * A, :].astype(LOWER)
    for l in range(LAYERS):
        k.lrows[l, 0:PER, :] = k.small[BASE + l * PER : BASE + (l + 1) * PER, :]
    k.sgl[...] = jnp.zeros_like(k.sgl)
    k.sgh[...] = jnp.zeros_like(k.sgh)
    k.sgw[...] = jnp.zeros_like(k.sgw)

    lane, sub = iota((WINS, 128), 1), iota((WINS, 128), 0)
    k.meta[...] = jnp.zeros_like(k.meta)
    k.meta[0:WINS, 0:K] = k.valid[...].astype(WIDE)
    meta = k.meta[0:WINS, :]
    for w in range(WINS):
        for n, ref in enumerate((k.starts, k.repeats)):
            meta = jnp.where((sub == w) & (lane == K + n), ref[w].astype(WIDE), meta)
    k.meta[0:WINS, :] = meta
    meta = k.meta[...].astype(LOWER)
    k.buf[...] = jnp.zeros_like(k.buf)
    k.buf[0, 0:S, 0:BUF_DEV] = k.states[...]
    k.buf[0, S + A : S + A + 1, 0:BUF_DEV] = k.returns[...]
    k.buf[1, 0:A, 0:BUF_DEV] = k.actions[...]

    def chunk(c, carry):
        rows = chunk_rows(c)
        win, step, kind, real = token_rows(c * CHUNK, CHUNK)
        lane = iota((CHUNK, 128), 1)
        tok = dot((lane == win).astype(WIDE).astype(LOWER), meta)
        start, repeat = tok[:, K : K + 1], tok[:, K + 1 : K + 2]
        valid = jnp.sum(jnp.where(lane == step, tok, 0.0), -1, keepdims=True)
        key = iota((CHUNK, 128), 0) & (SLOT - 1)
        query = lane & (SLOT - 1)
        allowed = (key <= query) & (((valid > 0.5) & real) | (key == query))
        k.bias[rows, :] = jnp.where(allowed, 0.0, MASKED)
        place = start.astype(jnp.int32) + step
        source = ((lane == place) & real).astype(WIDE)
        raw = dot_nt(source, k.buf[0], HIGH)
        acts = dot_nt(source, k.buf[1], HIGH)
        mine = (
            ((lane < S) & (kind == 1))
            | ((lane >= S) & (lane < S + A) & (kind == 2))
            | ((lane == S + A) & (kind == 0))
        )
        raw = raw + pltpu.roll(acts, S, 1)
        marks = ((lane == S + A + 1 + step) | (lane == S + A + 1 + K + kind)) & real
        feats = jnp.where(mine, raw, 0.0) + marks.astype(WIDE)
        weight = jnp.where((kind == 1) & real, repeat * valid, 0.0)
        acts = pltpu.roll(acts, HEAD_AT, 1)
        ours = (lane >= HEAD_AT) & (lane < HEAD_AT + A)
        feats = jnp.where(ours, acts, jnp.where(lane == HEAD_AT + A, weight, feats))
        k.feats[rows, :] = feats
        k.xs[0, rows, :] = dot(feats, k.xs[2, EMB_AT:ROWS, :], HIGH)
        return carry

    lax.fori_loop(0, CHUNKS, chunk, 0)


def stack_pair(v, first):
    zero = jnp.zeros_like(v)
    return jnp.concatenate([jnp.where(first, v, zero), jnp.where(first, zero, v)], 0)


def join_pair(v, first):
    return jnp.where(first, v[:SLOT], v[SLOT:])


def window_rows(w):
    return pl.ds(pl.multiple_of(w * SLOT, SLOT), SLOT)


def each_chunk(body, between=None):
    def step(c, carry):
        body(c, chunk_rows(c))
        if between is not None:

            @pl.when(c < CHUNKS - 1)
            def _():
                between()

        return carry

    lax.fori_loop(0, CHUNKS, step, 0)


def each_pair(body, between=None):
    def pair(n, carry):
        chains = [
            (2 * n + w, window_rows(2 * n + w), slice(p * 128, (p + 1) * 128))
            for w in range(2)
            for p in range(H // 2)
        ]
        body(pl.ds(pl.multiple_of(n * 128, 128), 128), chains)
        if between is not None:

            @pl.when(n == WINS // 4 - 1)
            def _():
                between()

        return carry

    lax.fori_loop(0, WINS // 2, pair, 0)


def forward_qkv(k, l, between):
    def chunk(c, rows):
        xhat, _ = norm_parts(k.xs[slot(l), rows, :])
        normed = (xhat * k.row(l, 0) + k.row(l, 1)).astype(LOWER)
        k.normed_t[:, rows] = normed.T
        for j in range(3):
            part = dot(normed, k.w_qkv(l, j)) + k.row(l, 4 + j)
            k.qkv[rows, j * D : (j + 1) * D] = part.astype(LOWER)

    each_chunk(chunk, between)


def qkv_part(k, n, rows, at):
    return k.qkv[rows, n * D + at.start : n * D + at.stop]


def forward_windows(k, l, between):
    first = iota((SLOT, 128), 1) < HD
    scale = jnp.asarray(HD**-0.5, LOWER)

    def pair(both, chains):
        query = [stack_pair(qkv_part(k, 0, rows, at) * scale, first) for _, rows, at in chains]
        scores = [
            dot_nt(qkv_part(k, 1, rows, at), q) + k.bias[rows, :]
            for q, (_, rows, at) in zip(query, chains)
        ]
        peaks = [jnp.max(s, 0, keepdims=True) for s in scores]
        expos = [jnp.exp(s - peak) for s, peak in zip(scores, peaks)]
        totals = [jnp.sum(e, 0, keepdims=True) for e in expos]
        probs = [(e * (1.0 / total)).astype(LOWER) for e, total in zip(expos, totals)]
        outs = [dot_tn(p, qkv_part(k, 2, rows, at)) for p, (_, rows, at) in zip(probs, chains)]
        for peak, total, out, (w, rows, at) in zip(peaks, totals, outs, chains):
            p = at.start // 128
            k.logs[l, w, p : p + 1, :] = peak + jnp.log(total)
            k.left[rows, at] = join_pair(out, first).astype(LOWER)
        k.mixed_t[:, both] = k.left[both, :].T

    each_pair(pair, between)


TILES = [slice(n * 128, (n + 1) * 128) for n in range(D // 128)]


def load_mid(k, rows):
    return jnp.concatenate([k.mid[n, rows, :] for n in range(len(TILES))], 1)


def store_mid(k, rows, value):
    for n, tile in enumerate(TILES):
        k.mid[n, rows, :] = value[:, tile]


def take_states(src, dst, cols):
    dst[0:STATES, cols] = jnp.zeros((STATES, 128), WIDE)
    for w in range(WINS):
        rows = slice(w * STATE_SLOT, w * STATE_SLOT + K)
        dst[rows, cols] = src[pl.ds(w * SLOT + 1, K, stride=3), :]


def put_states(k, value):
    for n, tile in enumerate(TILES):
        dst = k.mid.at[n]
        dst[...] = jnp.zeros((ROWS, 128), WIDE)
        for w in range(WINS):
            rows = slice(w * STATE_SLOT, w * STATE_SLOT + K)
            dst[pl.ds(w * SLOT + 1, K, stride=3), :] = value[rows, tile]


def forward_up(k, l, between):
    each_chunk(lambda c, rows: up_rows(k, l, rows, k.xs[slot(l), rows, :], k.left[rows, :]), between)


def up_rows(k, l, rows, x, mixed):
    mid = x + dot(mixed, k.w_out(l)) + k.row(l, 7)
    store_mid(k, rows, mid)
    xhat, _ = norm_parts(mid)
    second = (xhat * k.row(l, 2) + k.row(l, 3)).astype(LOWER)
    k.second_t[:, rows] = second.T
    ahead = dot(second, k.w_up(l, 0))
    for j in range(4):
        cols = slice(j * D, (j + 1) * D)
        h = ahead + k.row(l, 8 + j)
        if j < 3:
            ahead = dot(second, k.w_up(l, j + 1))
        square = h * h
        over = 1.0 + jnp.tanh(h * (GELU_C + GELU_C * GELU_A * square))
        half = 0.5 * h
        acted = (half * over).astype(LOWER)
        slope = over * (0.5 + half * (2.0 - over) * (GELU_C + 3.0 * GELU_A * GELU_C * square))
        k.work[rows, cols] = acted
        k.slope[rows, cols] = slope.astype(LOWER)
        k.act_t[cols, rows] = acted.T


def forward_down(k, l, dest):
    each_chunk(lambda c, rows: down_rows(k, l, rows, dest))


def down_rows(k, l, rows, dest):
    w_down = jnp.concatenate([k.w_down(l, j) for j in range(4)], 0)
    k.xs[dest, rows, :] = load_mid(k, rows) + k.row(l, 12) + dot(k.work[rows, :], w_down)


def forward_up_states(k, l, spare):
    every, rows = slice(0, ROWS), slice(0, STATES)
    store_mid(k, every, k.left[...].astype(WIDE))
    for n, tile in enumerate(TILES):
        take_states(k.mid.at[n], k.xs.at[spare], tile)
    mixed = k.xs[spare, rows, :].astype(LOWER)
    k.mixed_t[:, rows] = mixed.T
    store_mid(k, every, k.xs[slot(l)])
    for n, tile in enumerate(TILES):
        take_states(k.mid.at[n], k.xs.at[spare], tile)
    up_rows(k, l, rows, k.xs[spare, rows, :], mixed)


def head_stage(k, at):
    gain, bias = k.small[FIN : FIN + 1, :], k.small[FIN + 1 : FIN + 2, :]
    lane = iota((STATES, 128), 1)
    keep = lane < A

    def bias_row(first):
        row = jnp.zeros((1, 128), WIDE)
        at = iota((1, 128), 1)
        for a in range(A):
            row = jnp.where(at == a, k.head_bias[first + a], row)
        return row

    bias_mean, bias_spread = bias_row(0), bias_row(A)
    temp = jnp.exp(jnp.full((1, 128), k.log_temp[0], WIDE))

    rows = slice(0, STATES)
    xhat, scale = norm_parts(k.xs[at, rows, :])
    feats = (xhat * gain + bias).astype(LOWER)
    mean = dot_nt(feats, k.headw[0]) + bias_mean
    spread = jnp.tanh(dot_nt(feats, k.headw[1]) + bias_spread)
    take_states(k.feats, k.heads, slice(0, 128))
    acts = pltpu.roll(k.heads[...], 128 - HEAD_AT, 1)
    weight = acts[:, A : A + 1]
    acts = jnp.where(keep, acts, 0.0)
    target = 0.5 * (jnp.log(1.0 + acts) - jnp.log(1.0 - acts))
    shrink = jnp.exp(-spread)
    zed = (target - mean) * shrink
    terms = 0.5 * zed * zed + spread + HALF_LOG_TAU + jnp.log(1.0 - acts * acts)
    nll = jnp.sum(jnp.where(keep, terms, 0.0), -1, keepdims=True)
    entropy = jnp.sum(jnp.where(keep, spread, 0.0), -1, keepdims=True) + A * (0.5 + HALF_LOG_TAU)
    loss = weight * (nll - temp * entropy)
    sums = jnp.where(lane == 0, loss, jnp.where(lane == 1, weight * entropy, jnp.where(lane == 2, weight, 0.0)))
    d_mean = jnp.where(keep, weight * (-zed * shrink), 0.0).astype(LOWER)
    d_spread = weight * (1.0 - zed * zed - temp) * (1.0 - spread * spread)
    d_spread = jnp.where(keep, d_spread, 0.0).astype(LOWER)
    k.sgh[2:3, 0:128] += col_sum(sums)
    k.sgh[3:4, 0:128] += col_sum(d_mean.astype(WIDE))
    k.sgh[4:5, 0:128] += col_sum(d_spread.astype(WIDE))
    k.sgw[0] += dot_tn(d_mean, feats)[0:8]
    k.sgw[1] += dot_tn(d_spread, feats)[0:8]
    d_feats = dot(d_mean, k.headw[0]) + dot(d_spread, k.headw[1])
    k.sgh[0:1, :] += col_sum(d_feats * xhat)
    k.sgh[1:2, :] += col_sum(d_feats)
    k.xs[at, rows, :] = norm_back(xhat, scale, gain, d_feats)


def store_blocks(ref, l, owners, first, count, value):
    value = value.astype(LOWER)
    for n, i in enumerate(owners):
        a, b = owner_place(i)
        ref[l, a, b, first : first + count, :] = value[n * count : (n + 1) * count]


def backward_ffn(k, l, grad, between=None):
    each_chunk(lambda c, rows: ffn_back_rows(k, l, rows, grad), between)


def ffn_back_rows(k, l, rows, grad):
    d_down = k.xs[grad, rows, :].astype(LOWER)
    k.dout[rows, :] = d_down
    k.sgl[l, 12:13, :] += col_sum(d_down.astype(WIDE))
    d_second = jnp.zeros(d_down.shape, WIDE)
    ahead = dot_nt(d_down, k.w_down(l, 0))
    for j in range(4):
        cols = slice(j * D, (j + 1) * D)
        d_acted = ahead
        if j < 3:
            ahead = dot_nt(d_down, k.w_down(l, j + 1))
        d_hidden = (d_acted * k.slope[rows, cols].astype(WIDE)).astype(LOWER)
        k.work[rows, cols] = d_hidden
        k.sgl[l, 8 + j : 9 + j, :] += col_sum(d_hidden.astype(WIDE))
        d_second = d_second + dot_nt(d_hidden, k.w_up(l, j))
    xhat, scale = norm_parts(load_mid(k, rows))
    k.sgl[l, 2:3, :] += col_sum(d_second * xhat)
    k.sgl[l, 3:4, :] += col_sum(d_second)
    k.xs[grad, rows, :] += norm_back(xhat, scale, k.row(l, 2), d_second)


def backward_down_grads(k, l, rows=slice(0, ROWS)):
    for j in range(4):
        part = dot(k.act_t[j * D : (j + 1) * D, rows], k.dout[rows, :])
        store_blocks(k.wf, l, range(8 * j, 8 * j + 8), 64, 64, part)


def backward_up_grads(k, l, rows=slice(0, ROWS)):
    for j in range(4):
        part = dot(k.second_t[:, rows], k.work[rows, j * D : (j + 1) * D])
        store_blocks(k.wf, l, range(BLOCKS), 16 * j, 16, part)


def backward_out(k, l, grad):
    def before(c, rows):
        d_branch = k.xs[grad, rows, :].astype(LOWER)
        k.left[rows, :] = d_branch
        k.sgl[l, 7:8, :] += col_sum(d_branch.astype(WIDE))
        k.dout[rows, :] = dot_nt(d_branch, k.w_out(l)).astype(LOWER)

    each_chunk(before)
    store_blocks(k.wa, l + 1, range(BLOCKS), 48, 16, dot(k.mixed_t[...], k.left[...]))


def backward_out_states(k, l, grad):
    rows = slice(0, STATES)
    d_mid = k.xs[grad, rows, :]
    d_branch = d_mid.astype(LOWER)
    k.sgl[l, 7:8, :] += col_sum(d_branch.astype(WIDE))
    d_mixed = dot_nt(d_branch, k.w_out(l)).astype(LOWER)
    store_blocks(k.wa, l + 1, range(BLOCKS), 48, 16, dot(k.mixed_t[:, rows], d_branch))
    put_states(k, d_mixed.astype(WIDE))
    k.dout[...] = load_mid(k, slice(0, ROWS)).astype(LOWER)
    put_states(k, d_mid)
    k.xs[grad] = load_mid(k, slice(0, ROWS))


def backward_windows(k, l, between):
    first = iota((SLOT, 128), 1) < HD
    scale = HD**-0.5
    low = jnp.asarray(scale, LOWER)

    def pair(both, chains):
        query = [stack_pair(qkv_part(k, 0, rows, at) * low, first) for _, rows, at in chains]
        d_mixed = [stack_pair(k.dout[rows, at], first) for _, rows, at in chains]
        shift = [
            k.bias[rows, :] - k.logs[l, w, at.start // 128 : at.start // 128 + 1, :]
            for w, rows, at in chains
        ]
        scores = [dot_nt(qkv_part(k, 1, rows, at), q) for q, (_, rows, at) in zip(query, chains)]
        d_probs = [dot_nt(qkv_part(k, 2, rows, at), d) for d, (_, rows, at) in zip(d_mixed, chains)]
        probs = [jnp.exp(s + more) for s, more in zip(scores, shift)]
        d_values = [dot(p.astype(LOWER), d) for p, d in zip(probs, d_mixed)]
        inner = [p * d for p, d in zip(probs, d_probs)]
        sums = [jnp.sum(i, 0, keepdims=True) for i in inner]
        d_scores = [(i - p * t).astype(LOWER) for i, p, t in zip(inner, probs, sums)]
        d_keyed = [dot(d, q) for d, q in zip(d_scores, query)]
        d_query = [dot_tn(d, qkv_part(k, 1, rows, at)) for d, (_, rows, at) in zip(d_scores, chains)]
        for n, (_, rows, at) in enumerate(chains):
            values = (join_pair(d_query[n], first) * scale, d_keyed[n], d_values[n])
            for m, value in enumerate(values):
                k.work[rows, m * D + at.start : m * D + at.stop] = value.astype(LOWER)

    each_pair(pair, between)


def backward_attn_grads(k, l):
    for j in range(3):
        part = dot(k.normed_t[...], k.work[:, j * D : (j + 1) * D])
        store_blocks(k.wa, l + 1, range(BLOCKS), 16 * j, 16, part)


def backward_input(k, l, grad):
    def chunk(c, rows):
        d_normed = jnp.zeros((CHUNK, D), WIDE)
        for j in range(3):
            d_part = k.work[rows, j * D : (j + 1) * D]
            k.sgl[l, 4 + j : 5 + j, :] += col_sum(d_part.astype(WIDE))
            d_normed = d_normed + dot_nt(d_part, k.w_qkv(l, j))
        xhat, scale = norm_parts(k.xs[slot(l), rows, :])
        k.sgl[l, 0:1, :] += col_sum(d_normed * xhat)
        k.sgl[l, 1:2, :] += col_sum(d_normed)
        k.xs[grad, rows, :] += norm_back(xhat, scale, k.row(l, 0), d_normed)

    each_chunk(chunk)


def small_stage(k, out, grad):
    out[...] = jnp.zeros_like(out)
    out[0:EMB, :] = dot_tn(k.feats[...], k.xs[grad], HIGH)[0:EMB]
    out[FIN : FIN + 2, :] = k.sgh[0:2, :]
    out[HEADW : HEADW + A, :] = k.sgw[0, 0:A, :]
    out[HEADW + A : HEADW + 2 * A, :] = k.sgw[1, 0:A, :]
    for l in range(LAYERS):
        out[BASE + l * PER : BASE + (l + 1) * PER, :] = k.sgl[l, 0:PER, :]
    out[NROWS : NROWS + 3, :] = k.sgh[2:5, :]


WORK_SHAPES = dict(
    wa=((LAYERS + 1, 4, 8, ATTN, D), LOWER),
    wf=((LAYERS, 4, 8, FFN, D), LOWER),
    xs=((3, ROWS, D), WIDE),
    qkv=((ROWS, 3 * D), LOWER),
    normed_t=((D, ROWS), LOWER),
    mixed_t=((D, ROWS), LOWER),
    slope=((ROWS, FF), LOWER),
    act_t=((FF, ROWS), LOWER),
    second_t=((D, ROWS), LOWER),
    mid=((D // 128, ROWS, 128), WIDE),
    logs=((LAYERS, WINS, 8, 128), WIDE),
    work=((ROWS, FF), LOWER),
    left=((ROWS, D), LOWER),
    dout=((ROWS, D), LOWER),
    feats=((ROWS, 128), WIDE),
    heads=((STATES, 128), WIDE),
    bias=((ROWS, 128), WIDE),
    headw=((2, 128, D), LOWER),
    lrows=((LAYERS, 16, D), WIDE),
    sgl=((LAYERS, 16, D), WIDE),
    sgh=((8, D), WIDE),
    sgw=((2, 8, D), WIDE),
    meta=((128, 128), WIDE),
    buf=((2, 128, 128), WIDE),
)
KEEP_ATTN = ("qkv", "normed_t", "mixed_t")
KEEP_FFN = ("slope", "act_t", "second_t", "mid")
KEEP = KEEP_ATTN + KEEP_FFN


MESH = pl.DeviceIdType.MESH
NZ, NY, NX, NC = 4, 2, 2, 2
NR = NY * NX * NC
SHARD = PACK
PARTS, DEEP = 3, 64
HALF = DEEP // 2


class Place:
    def __init__(self):
        dp, fsdp = lax.axis_index("dp"), lax.axis_index("fsdp")
        self.z, self.y = dp // NY, dp % NY
        self.x, self.c = fsdp // NC, fsdp % NC
        self.a, self.b = 2 * self.c + self.x, 4 * self.y + self.z
        self.r = 4 * self.y + fsdp
        self.to_z = [(((self.z + d) % NZ) * NY + self.y, fsdp) for d in range(1, NZ)]
        self.odd = self.z % 2
        self.to_pair = ((self.z + 1 - 2 * self.odd) * NY + self.y, fsdp)
        self.plane = []
        for d in range(1, 8):
            y, x, c = [
                1 - v if d & bit else v for v, bit in ((self.y, 4), (self.x, 2), (self.c, 1))
            ]
            self.plane.append((self.z * NY + y, x * NC + c))
        self.to_c, self.to_x, self.to_y = self.plane[0], self.plane[1], self.plane[3]

    def barrier(self):
        sem = pltpu.get_barrier_semaphore()
        for partner in self.plane + self.to_z:
            pl.semaphore_signal(sem, inc=1, device_id=partner, device_id_type=MESH)
        pl.semaphore_wait(sem, len(self.plane) + len(self.to_z))


def remote(src, dst, send, recv, to):
    return pltpu.make_async_remote_copy(
        src_ref=src, dst_ref=dst, send_sem=send, recv_sem=recv, device_id=to, device_id_type=MESH
    )


def part_ref(weights, part):
    return weights[min(part, 1)], (0, 0, DEEP)[part]


class Gather:
    COPIES = 13

    def __init__(self, place, weights, send, recv):
        self.at, self.weights, self.send, self.recv = place, weights, send, recv

    def copy(self, l, part, n):
        at = self.at
        array, row = part_ref(self.weights, part)
        a, b, rows, to = at.a, pl.ds(4 * at.y, 4), pl.ds(row, DEEP), at.to_c
        if n < 3:
            b, to = at.b, at.to_z[n]
        elif n < 5:
            to = (at.to_x, at.to_y)[n - 3]
        if n in (6, 8, 10, 11, 12):
            a = 2 * at.c + 1 - at.x
        if n in (7, 9, 10, 11, 12):
            b = pl.ds(4 * (1 - at.y), 4)
        if n in (6, 7):
            first = row + at.odd * HALF + (n - 6) * (HALF // 2)
            rows = pl.ds(pl.multiple_of(first, HALF // 2), HALF // 2)
            to = (at.to_y, at.to_x)[n - 6]
        if n in (10, 11):
            rows = pl.ds(pl.multiple_of(row + at.odd * HALF, HALF), HALF)
        if n == 11:
            to = at.to_pair
        if n == 12:
            rows = pl.ds(pl.multiple_of(row + (1 - at.odd) * HALF, HALF), HALF)
        ref = array.at[l, a, b, rows, :]
        q = PARTS * l + part
        return remote(ref, ref, self.send.at[q, n], self.recv.at[q, n], to)

    def start(self, l, part, *ns):
        for n in ns:
            self.copy(l, part, n).start()

    def wait(self, l, part, *ns):
        for n in ns:
            self.copy(l, part, n).wait_recv()

    def first(self, l, part):
        self.start(l, part, 0, 1, 2)

    def second(self, l, part):
        self.wait(l, part, 0, 1, 2)
        self.start(l, part, 3, 4, 5)

    def third(self, l, part):
        self.wait(l, part, 3)
        self.start(l, part, 6, 8)
        self.wait(l, part, 4)
        self.start(l, part, 7, 9)

    def fourth(self, l, part):
        self.wait(l, part, 6, 7)
        self.start(l, part, 11, 10)

    def fifth(self, l, part):
        self.wait(l, part, 11)
        self.start(l, part, 12)

    def last(self, l, part):
        self.wait(l, part, 5, 8, 9, 10, 12)

    def sent(self, l, part):
        for n in range(self.COPIES):
            self.copy(l, part, n).wait_send()


class Reduce:
    COPIES = 8

    def __init__(self, place, grads, landing, send, recv, credit):
        self.at, self.grads, self.landing = place, grads, landing
        self.send, self.recv, self.credit = send, recv, credit

    def refs(self, l, part):
        array, row = part_ref(self.grads, part)
        grads = array.at[l + 1 - min(part, 1), :, :, pl.ds(row, DEEP), :]
        return (grads, *self.landing[part])

    def copy(self, l, part, n):
        at, half = self.at, HALF
        g, r0, r1a, r1b, r2, r3 = self.refs(l, part)
        top, low, other = pl.ds(0, half), pl.ds(half, half), pl.ds(4 * (1 - at.y), 4)
        if n == 0:
            src, dst, to = g.at[pl.ds(2 * (1 - at.c), 2)], r0, at.to_c
        elif n == 1:
            src, dst, to = r0.at[1 - at.x, :, top, :], r1a, at.to_x
        elif n == 2:
            src, dst, to = r0.at[:, other, low, :], r1b, at.to_y
        elif n == 3:
            src, dst, to = r1a.at[other], r2.at[:, top, :], at.to_y
        elif n == 4:
            src, dst, to = r1b.at[1 - at.x], r2.at[:, low, :], at.to_x
        else:
            src, dst, to = r2.at[(at.z + n - 4) % NZ], r3.at[n - 5], at.to_z[n - 5]
        q = PARTS * l + part
        return remote(src, dst, self.send.at[q, n], self.recv.at[q, n], to)

    def may_send(self, l, part, *partners):
        @pl.when(l < LAYERS - 1)
        def _():
            for n in partners:
                pl.semaphore_wait(self.credit.at[part, n], 1)

    def allow(self, l, part, *credits):
        at = self.at

        @pl.when(l > 0)
        def _():
            for n, to in credits:
                pl.semaphore_signal(
                    self.credit.at[part, n], inc=1, device_id=to, device_id_type=MESH
                )

    def start(self, l, part):
        self.may_send(l, part, 0)
        self.copy(l, part, 0).start()

    def first(self, l, part):
        at, half = self.at, HALF
        g, r0, _, _, _, _ = self.refs(l, part)
        top, low = pl.ds(0, half), pl.ds(half, half)
        self.copy(l, part, 0).wait_recv()

        x = 1 - at.x
        total = g[2 * at.c + x, :, top].astype(WIDE) + r0[x, :, top].astype(WIDE)
        r0[x, :, top] = total.astype(LOWER)
        self.may_send(l, part, 1, 2)
        self.copy(l, part, 1).start()
        other = pl.ds(4 * (1 - at.y), 4)
        for x in range(NX):
            total = g[2 * at.c + x, other, low].astype(WIDE) + r0[x, other, low].astype(WIDE)
            r0[x, other, low] = total.astype(LOWER)
        self.copy(l, part, 2).start()

    def second(self, l, part):
        at, half = self.at, HALF
        g, r0, r1a, r1b, _, _ = self.refs(l, part)
        top, low = pl.ds(0, half), pl.ds(half, half)

        x, other, column = 1 - at.x, pl.ds(4 * (1 - at.y), 4), pl.ds(4 * at.y, 4)
        self.copy(l, part, 1).wait_recv()
        total = g[at.a, other, top].astype(WIDE) + r0[at.x, other, top].astype(WIDE)
        r1a[other] = (total + r1a[other].astype(WIDE)).astype(LOWER)
        self.may_send(l, part, 6, 7)
        self.copy(l, part, 3).start()
        self.copy(l, part, 2).wait_recv()
        total = g[2 * at.c + x, column, low].astype(WIDE) + r0[x, column, low].astype(WIDE)
        r1b[x] = (total + r1b[x].astype(WIDE)).astype(LOWER)
        self.copy(l, part, 4).start()

    def chip_sums(self, l, part, z):
        at, half = self.at, HALF
        g, r0, r1a, r1b, r2, _ = self.refs(l, part)
        top, low, b = pl.ds(0, half), pl.ds(half, half), 4 * at.y + z
        upper = g[at.a, b, top].astype(WIDE) + r0[at.x, b, top].astype(WIDE)
        lower = g[at.a, b, low].astype(WIDE) + r0[at.x, b, low].astype(WIDE)
        return (
            upper + r1a[b].astype(WIDE) + r2[z, top].astype(WIDE),
            lower + r1b[at.x, z].astype(WIDE) + r2[z, low].astype(WIDE),
        )

    def third(self, l, part, out):
        at, half, row = self.at, HALF, DEEP * part
        r2 = self.landing[part][3]
        for n in (3, 4):
            self.copy(l, part, n).wait_recv()
        self.may_send(l, part, 3, 4, 5)
        for n in range(3):
            z = (at.z + n + 1) % NZ
            upper, lower = self.chip_sums(l, part, z)
            r2[z, pl.ds(0, half)] = upper.astype(LOWER)
            r2[z, pl.ds(half, half)] = lower.astype(LOWER)
            self.copy(l, part, 5 + n).start()
        upper, lower = self.chip_sums(l, part, at.z)
        out[l, row : row + half, :] = upper
        out[l, row + half : row + 2 * half, :] = lower
        for n in range(5):
            self.copy(l, part, n).wait_send()
        self.allow(l, part, (0, at.to_c), (1, at.to_x), (2, at.to_y))

    def last(self, l, part, out, squares):
        at, row = self.at, DEEP * part
        r3 = self.landing[part][4]
        rows = slice(row, row + DEEP)
        total = out[l, rows, :]
        for n in range(3):
            self.copy(l, part, 5 + n).wait_recv()
            total = total + r3[n].astype(WIDE)
        out[l, rows, :] = total
        squares[0:1, :] += col_sum(total * total)
        for n in range(5, self.COPIES):
            self.copy(l, part, n).wait_send()
        late = [(6, at.to_x), (7, at.to_y)] + [(5 - n, at.to_z[n]) for n in range(3)]
        self.allow(l, part, *late)


class Total:
    COPIES = 7

    def __init__(self, place, ref, rows, send, recv):
        self.at, self.ref, self.rows = place, ref, rows // 2
        self.send, self.recv = send, recv

    def half(self, n):
        return self.ref.at[pl.ds(pl.multiple_of(n * self.rows, 8), self.rows), :]

    def whole(self):
        return self.ref.at[pl.ds(0, 2 * self.rows), :]

    def copy(self, n):
        at = self.at
        mine, other = self.half(at.c), self.half(1 - at.c)
        src, dst, to = (
            (other, self.half(2), at.to_c),
            (self.half(8), self.half(3), at.to_x),
            (self.half(9), self.half(4), at.to_y),
            (self.half(10), self.half(5), at.to_z[0]),
            (self.half(10), self.half(6), at.to_z[1]),
            (self.half(10), self.half(7), at.to_z[2]),
            (mine, self.half(11), at.to_c),
        )[n]
        return remote(src, dst, self.send.at[n], self.recv.at[n], to)

    def start(self):
        self.copy(0).start()

    def step(self, n):
        self.copy(n).wait_recv()
        own = self.half(self.at.c) if n == 0 else self.half(7 + n)
        self.half(8 + n)[...] = own[...] + self.half(2 + n)[...]
        for m in ((1,), (2,), (3, 4, 5))[n]:
            self.copy(m).start()

    def back(self):
        for m in (3, 4, 5):
            self.copy(m).wait_recv()
        self.copy(0).wait_send()
        total = None
        for z in range(NZ):
            term = self.half(10)[...]
            for n in range(3):
                from_z = (self.at.z + NZ - 1 - n) % NZ
                term = jnp.where(from_z == z, self.half(5 + n)[...], term)
            total = term if total is None else total + term
        self.half(self.at.c)[...] = total
        self.copy(6).start()

    def last(self):
        self.copy(6).wait_recv()
        self.half(1 - self.at.c)[...] = self.half(11)[...]
        for n in range(1, self.COPIES):
            self.copy(n).wait_send()


class Norm:
    COPIES = 10

    def __init__(self, place, plane, column, send, recv):
        self.at, self.plane, self.column = place, plane, column
        self.send, self.recv = send, recv

    def copy(self, n):
        at = self.at
        if n < 7:
            ref, to = self.plane.at[at.r], at.plane[n]
        else:
            ref, to = self.column.at[at.z], at.to_z[n - 7]
        return remote(ref, ref, self.send.at[n], self.recv.at[n], to)

    def start(self, tile):
        self.plane[self.at.r] = tile
        for n in range(7):
            self.copy(n).start()

    def total(self, ref, ns):
        for n in ns:
            self.copy(n).wait_recv()
        total = ref[0]
        for n in range(1, ref.shape[0]):
            total = total + ref[n]
        return total

    def step(self):
        self.column[self.at.z] = self.total(self.plane, range(7))
        for n in range(7, self.COPIES):
            self.copy(n).start()

    def last(self):
        total = self.total(self.column, range(7, self.COPIES))
        for n in range(self.COPIES):
            self.copy(n).wait_send()
        return total


LANDING = (
    (NX, 8, DEEP, D),
    (8, HALF, D),
    (NX, NZ, HALF, D),
    (NZ, DEEP, D),
    (3, DEEP, D),
)


def stage_rows(qkv, out, up, down, l):
    return (
        [(qkv.at[l, :, pl.ds(j * D, D)], 16 * j, 16) for j in range(3)]
        + [(out.at[l], 48, 16)]
        + [(up.at[l, :, pl.ds(j * D, D)], 64 + 16 * j, 16) for j in range(4)]
        + [(down.at[l], 128, 64)]
    )


BEGIN, SETUP, START, QKV_HALF, QKV, WINDOWS_HALF, WINDOWS, UP_HALF, UP, DOWN = range(10)
FIRST, SECOND, THIRD, FOURTH, FIFTH, LAST, SEND = range(7)
GATHER_PLAN = {
    (-1, BEGIN): [(FIRST, 0, 0), (FIRST, 0, 1)],
    (-1, SETUP): [(SECOND, 0, 0), (FIRST, 0, 2)],
    (0, START): [(THIRD, 0, 0), (SECOND, 0, 1), (FOURTH, 0, 0), (FIRST, 1, 0), (FIFTH, 0, 0), (LAST, 0, 0)],
    (0, QKV_HALF): [(SECOND, 0, 2), (THIRD, 0, 1), (FIRST, 1, 1)],
    (0, QKV): [(FOURTH, 0, 1), (SECOND, 1, 0), (FIRST, 1, 2)],
    (0, WINDOWS_HALF): [(FIFTH, 0, 1), (THIRD, 0, 2), (LAST, 0, 1), (SECOND, 1, 1), (FIRST, 2, 0)],
    (0, WINDOWS): [(FOURTH, 0, 2), (THIRD, 1, 0)],
    (0, UP_HALF): [(FIFTH, 0, 2), (SECOND, 1, 2), (FIRST, 2, 1), (FOURTH, 1, 0)],
    (0, UP): [(LAST, 0, 2), (THIRD, 1, 1), (FIFTH, 1, 0), (SECOND, 2, 0)],
    (0, DOWN): [(FIRST, 2, 2), (FOURTH, 1, 1)],
    (1, START): [(LAST, 1, 0)],
    (1, QKV_HALF): [(SECOND, 2, 1), (THIRD, 1, 2)],
    (1, QKV): [(FIFTH, 1, 1)],
    (1, WINDOWS_HALF): [(LAST, 1, 1), (SECOND, 2, 2), (FOURTH, 1, 2), (THIRD, 2, 0)],
    (1, WINDOWS): [(FIFTH, 1, 2)],
    (1, UP_HALF): [(LAST, 1, 2), (FOURTH, 2, 0)],
    (1, UP): [(THIRD, 2, 1), (FIFTH, 2, 0)],
    (1, DOWN): [(LAST, 2, 0), (FOURTH, 2, 1)],
    (2, QKV_HALF): [(THIRD, 2, 2), (FIFTH, 2, 1)],
    (2, QKV): [(FOURTH, 2, 2)],
    (2, WINDOWS_HALF): [(LAST, 2, 1), (FIFTH, 2, 2)],
    (2, WINDOWS): [(LAST, 2, 2)],
}


def train_kernel(refs, alone):
    k = Kit(**refs)

    def kept(names, l, back):
        copies = []
        for name in names:
            here, there = refs[name], refs["keep_" + name].at[l]
            src, dst = (there, here) if back else (here, there)
            copies.append(pltpu.make_async_copy(src, dst, k.keep_sem.at[KEEP.index(name)]))
        return copies

    def start(copies):
        for copy in copies:
            copy.start()

    def wait(copies):
        for copy in copies:
            copy.wait()

    def kept_x(back):
        here, there = k.xs.at[0], k.keep_x
        src, dst = (there, here) if back else (here, there)
        return [pltpu.make_async_copy(src, dst, k.keep_sem.at[len(KEEP)])]

    arrays = [(l, n) for l in range(LAYERS) for n in (0, 1)]
    parts = [(l, part) for l in range(LAYERS) for part in range(PARTS)]
    weights = (k.wa, k.wf)
    if alone:
        loads = [
            pltpu.make_async_copy((k.all_a, k.all_f)[n].at[l], weights[n].at[l], k.load_sem.at[2 * l + n])
            for l, n in arrays
        ]
        stores = [
            pltpu.make_async_copy(
                weights[n].at[l + 1 - n], (k.grad_a, k.grad_f)[n].at[l], k.load_sem.at[2 * l + n]
            )
            for l, n in arrays
        ]
        start(loads)
    else:
        place = Place()
        gather = Gather(place, weights, k.gather_send, k.gather_recv)
        reduce = Reduce(
            place, weights, k.landing, k.reduce_send, k.reduce_recv, k.credit
        )
        sums = Total(place, k.xs.at[1], SMALL, k.sum_send, k.sum_recv)
        norm = Norm(place, k.norm_plane, k.norm_column, k.norm_send, k.norm_recv)

    def run(plan):
        stages = (
            gather.first,
            gather.second,
            gather.third,
            gather.fourth,
            gather.fifth,
            gather.last,
        )
        for stage, l, part in plan:
            stages[stage](l, part)

    def poll(l, point):
        if alone:
            return
        for layer in range(LAYERS):
            plan = GATHER_PLAN.get((layer, point))
            if plan:

                @pl.when(l == layer)
                def _(plan=plan):
                    run(plan)

    if not alone:
        staged = []
        for l in range(LAYERS):
            for n, (src, row, count) in enumerate(stage_rows(k.qkv_w, k.out_w, k.up_w, k.down_w, l)):
                dst = k.xs.at[2, pl.ds(l * PACK + row, count), :]
                staged.append(pltpu.make_async_copy(src, dst, k.stage_sem.at[l, n]))
        start(staged)
        place.barrier()
        for l in range(LAYERS):
            wait(staged[9 * l : 9 * l + 9])
            row = l * PACK
            for part in range(PARTS):
                array, first = part_ref(weights, part)
                mine = k.xs[2, row + DEEP * part : row + DEEP * (part + 1), :].astype(LOWER)
                array[l, place.a, place.b, first : first + DEEP, :] = mine
                if (FIRST, l, part) in GATHER_PLAN[-1, BEGIN]:
                    gather.first(l, part)
        k.squares_sum[...] = jnp.zeros_like(k.squares_sum)

    setup_stage(k)
    start(kept_x(False))
    if not alone:
        run(GATHER_PLAN[-1, SETUP])

    grad = 2

    def forward(l, carry):
        if alone:
            pltpu.make_async_copy(k.all_a.at[l], k.wa.at[l], k.load_sem.at[2 * l]).wait()

        @pl.when(l > 0)
        def _():
            wait(kept(KEEP_ATTN, l - 1, False))

        poll(l, START)
        forward_qkv(k, l, lambda: poll(l, QKV_HALF))
        poll(l, QKV)
        forward_windows(k, l, lambda: poll(l, WINDOWS_HALF))

        @pl.when(l < LAYERS - 1)
        def _():
            start(kept(KEEP_ATTN, l, False))

        @pl.when(l > 0)
        def _():
            wait(kept(KEEP_FFN, l - 1, False))

        @pl.when(l == 1)
        def _():
            wait(kept_x(False))

        if alone:
            pltpu.make_async_copy(k.all_f.at[l], k.wf.at[l], k.load_sem.at[2 * l + 1]).wait()
        poll(l, WINDOWS)

        @pl.when(l < LAYERS - 1)
        def _():
            forward_up(k, l, lambda: poll(l, UP_HALF))

        @pl.when(l == LAYERS - 1)
        def _():
            forward_up_states(k, l, grad)

        poll(l, UP)

        @pl.when(l < LAYERS - 1)
        def _():
            forward_down(k, l, (l + 1) % 2)

        @pl.when(l == LAYERS - 1)
        def _():
            down_rows(k, l, slice(0, STATES), grad)

        @pl.when(l < LAYERS - 1)
        def _():
            start(kept(KEEP_FFN, l, False))

        poll(l, DOWN)
        return carry

    lax.fori_loop(0, LAYERS, forward, 0)
    if not alone:
        for l, part in parts:
            gather.sent(l, part)
    head_stage(k, grad)

    def run_reduce(stage, l, part):
        if stage == THIRD:
            reduce.third(l, part, k.shard)
        elif stage == LAST:
            reduce.last(l, part, k.shard, k.squares_sum)
        else:
            {SEND: reduce.start, FIRST: reduce.first, SECOND: reduce.second}[stage](l, part)

    def backward(n, carry):
        l = LAYERS - 1 - n

        def behind(name, *stages):
            @pl.when(n > 0)
            def _():
                for stage, part, *more in stages:
                    stage(l + 1, part, *more)

        @pl.when(n > 0)
        def _():
            wait(kept(KEEP_FFN, l, True))

        def now(stage, part, early=None):
            if alone:
                return
            if early is None:
                run_reduce(stage, l, part)
                return

            @pl.when((n == LAYERS - 1) if early else (n < LAYERS - 1))
            def _():
                run_reduce(stage, l, part)

        def then(stage, part):
            if not alone:

                @pl.when(n > 0)
                def _():
                    run_reduce(stage, l + 1, part)

        def in_ffn():
            then(LAST, 2)
            then(THIRD, 1)
            then(FIRST, 0)

        def in_windows():
            now(FIRST, 1, False)
            now(SECOND, 2, True)

        states = slice(0, STATES)

        @pl.when(n > 0)
        def _():
            backward_ffn(k, l, grad, in_ffn)
            backward_down_grads(k, l)

        @pl.when(n == 0)
        def _():
            ffn_back_rows(k, l, states, grad)
            backward_down_grads(k, l, states)

        now(SEND, 2)
        then(LAST, 1)
        then(SECOND, 0)

        @pl.when(n > 0)
        def _():
            backward_up_grads(k, l)

        @pl.when(n == 0)
        def _():
            backward_up_grads(k, l, states)

        @pl.when((n > 0) & (n < LAYERS - 1))
        def _():
            start(kept(KEEP_FFN, l - 1, True))

        now(SEND, 1)
        now(FIRST, 2, True)

        @pl.when(n > 0)
        def _():
            wait(kept(KEEP_ATTN, l, True))

        @pl.when(n > 0)
        def _():
            backward_out(k, l, grad)

        @pl.when(n == 0)
        def _():
            backward_out_states(k, l, grad)
            start(kept(KEEP_FFN, l - 1, True))

        now(FIRST, 2, False)
        now(FIRST, 1, True)
        then(THIRD, 0)
        backward_windows(k, l, in_windows)
        now(SECOND, 2, False)
        now(THIRD, 2, True)
        then(LAST, 0)
        backward_attn_grads(k, l)

        @pl.when(n < LAYERS - 1)
        def _():
            start(kept(KEEP_ATTN, l - 1, True))

        now(SEND, 0)
        now(THIRD, 2, False)
        now(SECOND, 1, True)

        @pl.when(n == LAYERS - 1)
        def _():
            wait(kept_x(True))

        backward_input(k, l, grad)

        @pl.when(n == 0)
        def _():
            start(kept_x(True))

        now(SECOND, 1, False)
        now(FIRST, 0, True)
        now(THIRD, 1, True)
        return carry

    lax.fori_loop(0, LAYERS, backward, 0)
    if alone:
        start(stores)
        small_stage(k, k.small_out, grad)
        wait(stores)
        return
    small_stage(k, sums.whole(), grad)
    sums.start()
    reduce.last(0, 2, k.shard, k.squares_sum)
    reduce.second(0, 0)
    sums.step(0)
    reduce.third(0, 0, k.shard)
    sums.step(1)
    reduce.last(0, 1, k.shard, k.squares_sum)
    sums.step(2)
    reduce.last(0, 0, k.shard, k.squares_sum)
    squares = k.squares_sum[...]
    norm.start(sum(squares[:, n * 128 : (n + 1) * 128] for n in range(D // 128)))
    sums.back()
    norm.step()
    sums.last()
    k.small_out[...] = sums.whole()[...]
    k.squares[...] = norm.last()


def train_pass(inputs, weights, alone):
    whole = pl.BlockSpec(memory_space=pltpu.VMEM)
    scalars = pl.BlockSpec(memory_space=pltpu.SMEM)
    anywhere = pl.BlockSpec(memory_space=pl.ANY)
    dma = pltpu.SemaphoreType.DMA
    count = PARTS * LAYERS
    names = ["states", "actions", "returns", "starts", "repeats", "valid"]
    names += ["log_temp", "small", "head_bias"]
    out_shape = {"small_out": ((SMALL, D), WIDE)}
    for name in KEEP:
        shape, dtype = WORK_SHAPES[name]
        out_shape["keep_" + name] = ((LAYERS - 1,) + shape, dtype)
    out_shape["keep_x"] = ((ROWS, D), WIDE)
    scratch = {name: pltpu.VMEM(*shape) for name, shape in WORK_SHAPES.items()}
    scratch["keep_sem"] = dma((len(KEEP) + 1,))
    if alone:
        names += ["all_a", "all_f"]
        out_shape["grad_a"] = ((LAYERS, 4, 8, ATTN, D), LOWER)
        out_shape["grad_f"] = ((LAYERS, 4, 8, FFN, D), LOWER)
        scratch["load_sem"] = dma((count,))
    else:
        names += ["qkv_w", "out_w", "up_w", "down_w"]
        out_shape["shard"] = ((LAYERS, PACK, D), WIDE)
        out_shape["squares"] = ((8, 128), WIDE)
        for part in range(PARTS):
            for n, shape in enumerate(LANDING):
                scratch["land_%d_%d" % (part, n)] = pltpu.VMEM(shape, LOWER)
        scratch["stage_sem"] = dma((LAYERS, 9))
        scratch["squares_sum"] = pltpu.VMEM((8, D), WIDE)
        for name, copies in (("gather", Gather.COPIES), ("reduce", Reduce.COPIES)):
            scratch[name + "_send"] = dma((count, copies))
            scratch[name + "_recv"] = dma((count, copies))
        scratch["credit"] = pltpu.SemaphoreType.REGULAR((PARTS, 8))
        scratch["norm_plane"] = pltpu.VMEM((8, 8, 128), WIDE)
        scratch["norm_column"] = pltpu.VMEM((NZ, 8, 128), WIDE)
        for name, copies in (("sum", Total.COPIES), ("norm", Norm.COPIES)):
            scratch[name + "_send"] = dma((copies,))
            scratch[name + "_recv"] = dma((copies,))
    spaces = dict.fromkeys(("starts", "repeats", "head_bias", "log_temp"), scalars)
    for name in ("all_a", "all_f", "grad_a", "grad_f", "qkv_w", "out_w", "up_w", "down_w"):
        spaces[name] = anywhere
    for name in KEEP + ("x",):
        spaces["keep_" + name] = anywhere
    every = names + list(out_shape) + list(scratch)

    def kernel(*given):
        refs = dict(zip(every, given))
        refs["landing"] = [
            [refs.get("land_%d_%d" % (part, n)) for n in range(len(LANDING))] for part in range(PARTS)
        ]
        train_kernel(refs, alone)

    results = pl.pallas_call(
        kernel,
        name="train_pass",
        out_shape=tuple(jax.ShapeDtypeStruct(*shape) for shape in out_shape.values()),
        in_specs=[spaces.get(name, whole) for name in names],
        out_specs=tuple(spaces.get(name, whole) for name in out_shape),
        scratch_shapes=list(scratch.values()),
        compiler_params=pltpu.CompilerParams(
            vmem_limit_bytes=VMEM_BYTES,
            collective_id=None if alone else 0,
            has_side_effects=not alone,
        ),
        cost_estimate=pl.CostEstimate(
            flops=6 * 10**10, bytes_accessed=4 * 10**7, transcendentals=10**7
        ),
    )(*inputs, *weights)
    return dict(zip(out_shape, results))


def adam_parts(weight, grad, first, second, rate):
    first = BETA_ONE * first + (1.0 - BETA_ONE) * grad
    second = BETA_TWO * second + (1.0 - BETA_TWO) * grad * grad
    fix_one = 1.0 - BETA_ONE**STEP
    fix_two = 1.0 - BETA_TWO**STEP
    fresh = weight - rate * (
        first * (1.0 / fix_one) / (jnp.sqrt(second * (1.0 / fix_two)) + ADAM_EPS) + DECAY * weight
    )
    return fresh, first, second


def adam_kernel(*refs):
    shard, small_grad, squares, groups, log_temp = refs[:5]
    small, small_first, small_second, bias, bias_first, bias_second = refs[5:11]
    far_in, far_out = refs[11:23], refs[32:48]
    near_in, near_out, load, store = refs[48:60], refs[60:76], refs[76], refs[77]
    loads = [pltpu.make_async_copy(a, b, load.at[n]) for n, (a, b) in enumerate(zip(far_in, near_in))]
    stores = [
        pltpu.make_async_copy(a, b, store.at[n]) for n, (a, b) in enumerate(zip(near_out, far_out))
    ]
    kinds = (3, 2, 0, 1)
    for kind in kinds:
        for n in range(3):
            loads[4 * n + kind].start()
    mats, firsts, seconds = near_in[0:4], near_in[4:8], near_in[8:12]
    totals, norm, next_temp, s_next, s_first, s_second, b_next, b_first, b_second = refs[23:32]
    m_next, m_copy, m_first, m_second = [near_out[4 * n : 4 * n + 4] for n in range(4)]
    extra = small_grad[NROWS : NROWS + 3, 0:128]
    lane = iota((1, 128), 1)
    bias_mean = jnp.where(lane < A, extra[1:2], 0.0)
    bias_spread = jnp.where(lane < A, extra[2:3], 0.0)

    def all_sum(v):
        return jnp.sum(jnp.sum(v, 0, keepdims=True), 1, keepdims=True)

    grads = small_grad[0:NROWS, :]
    square = (
        all_sum(squares[0:1, :])
        + all_sum(grads * grads)
        + all_sum(bias_mean * bias_mean)
        + all_sum(bias_spread * bias_spread)
    )
    length = jnp.sqrt(square)
    clip = jnp.minimum(1.0, CLIP / (length + 1e-06))

    def rate_of(l, kind):
        group = jnp.full((1, 1), groups[l, kind], jnp.int32).astype(WIDE)
        return LEARN * jnp.exp2(-group)

    def update(l, kind, rows, cols, grad):
        at = (l, rows, cols)
        fresh, first, second = adam_parts(
            mats[kind][at], clip * grad, firsts[kind][at], seconds[kind][at], rate_of(l, kind)
        )
        m_next[kind][at] = fresh
        m_copy[kind][at] = fresh.astype(LOWER)
        m_first[kind][at] = first
        m_second[kind][at] = second

    every, wide = slice(0, 16), (3, 1, 4)
    for kind in kinds:
        for n in range(3):
            loads[4 * n + kind].wait()
        for l in range(LAYERS):
            if kind == 3:
                update(l, 3, slice(0, 64), slice(0, D), shard[l, 128:192, :])
                continue
            for j in range(wide[kind]):
                row = (0, 48, 64)[kind] + 16 * j
                cols = slice(j * D, (j + 1) * D)
                update(l, kind, every, cols, shard[l, row : row + 16, :])
        for n in range(4):
            stores[4 * n + kind].start()

    s_next[...], s_first[...], s_second[...] = adam_parts(
        small[...], clip * grads, small_first[...], small_second[...], LEARN
    )

    def scalar(v, n):
        return jnp.sum(jnp.where(lane == n, v, 0.0))

    def row(ref):
        v = jnp.zeros((1, 128), WIDE)
        for n in range(2 * A):
            v = jnp.where(lane == n, ref[n], v)
        return v

    grad = bias_mean + pltpu.roll(bias_spread, A, 1)
    results = adam_parts(row(bias), clip * grad, row(bias_first), row(bias_second), LEARN)
    for ref, result in zip((b_next, b_first, b_second), results):
        for n in range(2 * A):
            ref[n] = scalar(result, n)
    sums = extra[0:1]
    for n in range(3):
        totals[n] = scalar(sums, n)
    norm[0] = jnp.sum(length)
    logs = jnp.full((1, 1), log_temp[0], WIDE)
    ratio = jnp.full((1, 1), scalar(sums, 1), WIDE) / jnp.full((1, 1), scalar(sums, 2), WIDE)
    next_temp[0] = jnp.sum(logs - TEMP_RATE * jnp.exp(logs) * (ratio + A))
    for copy in stores:
        copy.wait()


def adam_all(shard, small_grad, squares, groups, log_temp, smalls, biases, mats, firsts, seconds):
    scalars = pl.BlockSpec(memory_space=pltpu.SMEM)

    whole = pl.BlockSpec(memory_space=pltpu.VMEM)
    anywhere = pl.BlockSpec(memory_space=pl.ANY)

    def like(array, dtype=WIDE):
        return jax.ShapeDtypeStruct(array.shape, dtype)

    stacks = list(mats) + list(firsts) + list(seconds)
    small, bias = smalls[0], biases[0]
    return pl.pallas_call(
        adam_kernel,
        name="adam",
        out_shape=(
            (jax.ShapeDtypeStruct((3,), WIDE),)
            + (jax.ShapeDtypeStruct((1,), WIDE),) * 2
            + (like(small),) * 3
            + (like(bias),) * 3
            + tuple(like(m) for m in mats)
            + tuple(like(m, LOWER) for m in mats)
            + tuple(like(m) for m in mats) * 2
        ),
        in_specs=[whole] * 3 + [scalars] * 2 + [whole] * 3 + [scalars] * 3 + [anywhere] * 12,
        out_specs=(scalars,) * 3 + (whole,) * 3 + (scalars,) * 3 + (anywhere,) * 16,
        scratch_shapes=[pltpu.VMEM(a.shape, WIDE) for a in stacks]
        + [pltpu.VMEM(m.shape, dtype) for dtype in (WIDE, LOWER, WIDE, WIDE) for m in mats]
        + [pltpu.SemaphoreType.DMA((12,)), pltpu.SemaphoreType.DMA((16,))],
        compiler_params=pltpu.CompilerParams(vmem_limit_bytes=VMEM_BYTES),
        cost_estimate=pl.CostEstimate(flops=10**7, bytes_accessed=8 * 10**6, transcendentals=10**6),
    )(shard, small_grad, squares, groups, log_temp, *smalls, *biases, *stacks)


def gather_packed(mats, axes, count):
    group = count // BLOCKS
    pieces = []
    for mat in mats:
        rows, wide = mat.shape[1], mat.shape[2] // D
        piece = mat.astype(LOWER).reshape(LAYERS, rows, wide, D)
        piece = lax.all_gather(piece, axes, axis=1, tiled=True)
        piece = piece.reshape(LAYERS, NZ, NY, NX, NC, group * rows, wide, D)
        piece = piece.transpose(0, 4, 3, 2, 1, 6, 5, 7)
        pieces.append(piece.reshape(LAYERS, 4, 8, wide * group * rows, D))
    return jnp.concatenate(pieces[:2], 3), jnp.concatenate(pieces[2:], 3)


def scatter_packed(grads, mats, axes):
    results, first = [], 0
    for n, mat in enumerate(mats):
        rows, wide = mat.shape[1], mat.shape[2] // D
        total = lax.psum(1, axes) * rows
        deep = total // BLOCKS
        first = 0 if n % 2 == 0 else first
        piece = grads[n // 2][:, :, :, first : first + wide * deep].astype(WIDE)
        first += wide * deep
        piece = piece.reshape(LAYERS, NC, NX, NY, NZ, wide, deep, D)
        piece = piece.transpose(0, 4, 3, 2, 1, 6, 5, 7).reshape(LAYERS, total, wide * D)
        results.append(lax.psum_scatter(piece, axes, scatter_dimension=1, tiled=True))
    return results


def local(
    buf_states,
    buf_actions,
    buf_returns,
    window_starts,
    window_repeats,
    valid_steps,
    matrix_groups,
    log_temp,
    small_rows,
    head_bias,
    qkv_weight,
    out_weight,
    up_weight,
    down_weight,
    small_first,
    bias_first,
    qkv_first,
    out_first,
    up_first,
    down_first,
    small_second,
    bias_second,
    qkv_second,
    out_second,
    up_second,
    down_second,
):
    axes = ("dp", "fsdp")
    mats = (qkv_weight, out_weight, up_weight, down_weight)
    firsts = (qkv_first, out_first, up_first, down_first)
    seconds = (qkv_second, out_second, up_second, down_second)
    pass_inputs = (
        buf_states.T,
        buf_actions.T,
        buf_returns[None],
        window_starts,
        window_repeats,
        valid_steps,
        log_temp,
        small_rows,
        head_bias,
    )
    if FF // down_weight.shape[1] == BLOCKS and lax.psum(1, "fsdp") == NX * NC:
        made = train_pass(pass_inputs, mats, False)
        return adam_all(
            made["shard"],
            made["small_out"],
            made["squares"],
            matrix_groups,
            log_temp,
            (small_rows, small_first, small_second),
            (head_bias, bias_first, bias_second),
            mats,
            firsts,
            seconds,
        )
    packed = gather_packed(mats, axes, FF // down_weight.shape[1])
    made = train_pass(pass_inputs, packed, True)
    big = scatter_packed((made["grad_a"], made["grad_f"]), mats, axes)
    small = made["small_out"]
    small = lax.psum(small, axes)
    small_grad, totals = small[:NROWS], small[NROWS, :3]
    bias_grad = jnp.concatenate([small[NROWS + 1, :A], small[NROWS + 2, :A]])
    square = sum((jnp.sum(piece * piece) for piece in big))
    square = (
        lax.psum(square, axes) + jnp.sum(small_grad * small_grad) + jnp.sum(bias_grad * bias_grad)
    )
    grad_norm = jnp.sqrt(square)
    clip = jnp.minimum(1.0, CLIP / (grad_norm + 1e-06))
    rates = LEARN * jnp.exp2(-matrix_groups.astype(WIDE))
    results = [
        adam_parts(
            mats[kind], clip * big[kind], firsts[kind], seconds[kind], rates[:, kind][:, None, None]
        )
        for kind in range(4)
    ]
    small_new = adam_parts(small_rows, clip * small_grad, small_first, small_second, LEARN)
    bias_new = adam_parts(head_bias, clip * bias_grad, bias_first, bias_second, LEARN)
    next_temp = log_temp - TEMP_RATE * jnp.exp(log_temp) * (totals[1] / totals[2] + A)
    return (
        (totals, grad_norm[None], next_temp)
        + small_new
        + bias_new
        + tuple(r[0] for r in results)
        + tuple(r[0].astype(LOWER) for r in results)
        + tuple(r[1] for r in results)
        + tuple(r[2] for r in results)
    )


def solution(mesh):
    rows = P(("dp", "fsdp"), None)
    vector = P(("dp", "fsdp"))
    stack = P(None, ("dp", "fsdp"), None)
    same = P()
    in_specs = (
        (rows, rows, vector, vector, vector, rows)
        + (same,) * 4
        + (stack,) * 4
        + (same,) * 2
        + (stack,) * 4
        + (same,) * 2
        + (stack,) * 4
    )
    out_specs = (same,) * 9 + (stack,) * 16
    return jax.shard_map(local, mesh=mesh, in_specs=in_specs, out_specs=out_specs, check_vma=False)
```

```python
import math

import jax
import jax.numpy as jnp
from jax import lax
from jax.experimental import pallas as pl
from jax.experimental.pallas import tpu as pltpu
from jax.sharding import PartitionSpec as P

D = 512
H = 8
HD = 64
FF = 2048
S = 11
A = 3
K = 20
STEP = 10

EPS = 1e-05
CLIP = 1.0
LEARN = 0.03
BETA_ONE = 0.5
BETA_TWO = 0.7
DECAY = 0.01
ADAM_EPS = 1e-08
TEMP_RATE = 0.1
MASKED = -1e30
HALF_LOG_TAU = 0.5 * math.log(2.0 * math.pi)
GELU_C = math.sqrt(2.0 / math.pi)
GELU_A = 0.044715
HIGH = lax.Precision.HIGHEST
LOWER = jnp.bfloat16
WIDE = jnp.float32

LAYERS = 3
WINS = 16
BUF_DEV = 64
SLOT = 64
ROWS = WINS * SLOT
CHUNK = 512
CHUNKS = ROWS // CHUNK
STATE_SLOT = 24
STATES = WINS * STATE_SLOT
BLOCKS = 32
PACK = 192
ATTN, FFN = 64, 128
EMB = S + A + 1 + K + 3
FIN = EMB
HEADW = EMB + 2
BASE = EMB + 2 + 2 * A
PER = 9 + FF // D
NROWS = BASE + LAYERS * PER
SMALL = 96
HEAD_AT = 64
EMB_AT = ROWS - 128
VMEM_BYTES = 64 * 1024 * 1024


def dot(a, b, precision=None):
    return lax.dot_general(
        a, b, (((1,), (0,)), ((), ())), precision=precision, preferred_element_type=WIDE
    )


def dot_nt(a, b, precision=None):
    return lax.dot_general(
        a, b, (((1,), (1,)), ((), ())), precision=precision, preferred_element_type=WIDE
    )


def dot_tn(a, b, precision=None):
    return lax.dot_general(
        a, b, (((0,), (0,)), ((), ())), precision=precision, preferred_element_type=WIDE
    )


def iota(shape, dim):
    return lax.broadcasted_iota(jnp.int32, shape, dim)


def col_sum(v):
    return jnp.sum(v, 0, keepdims=True)


def row_mean(v):
    return jnp.mean(v, -1, keepdims=True)


def norm_parts(x):
    center = x - row_mean(x)
    scale = lax.rsqrt(row_mean(center * center) + EPS)
    return center * scale, scale


def norm_back(xhat, scale, gain, grad):
    scaled = grad * gain
    return scale * (scaled - row_mean(scaled) - xhat * row_mean(scaled * xhat))


def token_rows(at, count):
    row = at + iota((count, 128), 0)
    place = row & (SLOT - 1)
    step = (place * 21846) >> 16
    return row >> 6, step, place - 3 * step, place < 3 * K


def chunk_rows(c):
    return pl.ds(pl.multiple_of(c * CHUNK, CHUNK), CHUNK)


def owner_place(i):
    z, y, x, c = i // 8, (i // 4) % 2, (i // 2) % 2, i % 2
    return 2 * c + x, 4 * y + z


class Kit:
    def __init__(self, **refs):
        self.__dict__.update(refs)

    def row(self, l, k):
        return self.lrows[l, k : k + 1, :]

    def blocks(self, ref, l, first, count, owners):
        places = [owner_place(i) for i in owners]
        return jnp.concatenate([ref[l, a, b, first : first + count, :] for a, b in places], 0)

    def w_qkv(self, l, j):
        return self.blocks(self.wa, l, 16 * j, 16, range(BLOCKS))

    def w_out(self, l):
        return self.blocks(self.wa, l, 48, 16, range(BLOCKS))

    def w_up(self, l, j):
        return self.blocks(self.wf, l, 16 * j, 16, range(BLOCKS))

    def w_down(self, l, j):
        return self.blocks(self.wf, l, 64, 64, range(8 * j, 8 * j + 8))


def slot(l):
    return l % 2


def setup_stage(k):
    k.xs[2, EMB_AT:ROWS, :] = jnp.zeros((128, D), WIDE)
    k.xs[2, EMB_AT : EMB_AT + EMB, :] = k.small[0:EMB, :]
    k.headw[...] = jnp.zeros_like(k.headw)
    k.headw[0, 0:A, :] = k.small[HEADW : HEADW + A, :].astype(LOWER)
    k.headw[1, 0:A, :] = k.small[HEADW + A : HEADW + 2 * A, :].astype(LOWER)
    for l in range(LAYERS):
        k.lrows[l, 0:PER, :] = k.small[BASE + l * PER : BASE + (l + 1) * PER, :]
    low_half = iota((SLOT, 128), 1) < HD
    for n, factor in enumerate((HD**-0.5, 1.0)):
        k.pairs[2 * n] = jnp.where(low_half, factor, 0.0).astype(LOWER)
        k.pairs[2 * n + 1] = jnp.where(low_half, 0.0, factor).astype(LOWER)
    k.sgl[...] = jnp.zeros_like(k.sgl)
    k.sgh[...] = jnp.zeros_like(k.sgh)
    k.sgw[...] = jnp.zeros_like(k.sgw)

    lane, sub = iota((WINS, 128), 1), iota((WINS, 128), 0)
    k.meta[...] = jnp.zeros_like(k.meta)
    k.meta[0:WINS, 0:K] = k.valid[...].astype(WIDE)
    meta = k.meta[0:WINS, :]
    for w in range(WINS):
        for n, ref in enumerate((k.starts, k.repeats)):
            meta = jnp.where((sub == w) & (lane == K + n), ref[w].astype(WIDE), meta)
    k.meta[0:WINS, :] = meta
    meta = k.meta[...].astype(LOWER)
    k.buf[...] = jnp.zeros_like(k.buf)
    k.buf[0, 0:S, 0:BUF_DEV] = k.states[...]
    k.buf[0, S + A : S + A + 1, 0:BUF_DEV] = k.returns[...]
    k.buf[1, 0:A, 0:BUF_DEV] = k.actions[...]

    def chunk(c, carry):
        rows = chunk_rows(c)
        win, step, kind, real = token_rows(c * CHUNK, CHUNK)
        lane = iota((CHUNK, 128), 1)
        tok = dot((lane == win).astype(WIDE).astype(LOWER), meta)
        start, repeat = tok[:, K : K + 1], tok[:, K + 1 : K + 2]
        valid = jnp.sum(jnp.where(lane == step, tok, 0.0), -1, keepdims=True)
        key = iota((CHUNK, 128), 0) & (SLOT - 1)
        query = lane & (SLOT - 1)
        allowed = (key <= query) & (((valid > 0.5) & real) | (key == query))
        k.bias[rows, :] = jnp.where(allowed, 0.0, MASKED)
        place = start.astype(jnp.int32) + step
        source = ((lane == place) & real).astype(WIDE)
        raw = dot_nt(source, k.buf[0], HIGH)
        acts = dot_nt(source, k.buf[1], HIGH)
        mine = (
            ((lane < S) & (kind == 1))
            | ((lane >= S) & (lane < S + A) & (kind == 2))
            | ((lane == S + A) & (kind == 0))
        )
        raw = raw + pltpu.roll(acts, S, 1)
        marks = ((lane == S + A + 1 + step) | (lane == S + A + 1 + K + kind)) & real
        feats = jnp.where(mine, raw, 0.0) + marks.astype(WIDE)
        weight = jnp.where((kind == 1) & real, repeat * valid, 0.0)
        acts = pltpu.roll(acts, HEAD_AT, 1)
        ours = (lane >= HEAD_AT) & (lane < HEAD_AT + A)
        feats = jnp.where(ours, acts, jnp.where(lane == HEAD_AT + A, weight, feats))
        k.feats[rows, :] = feats
        k.xs[0, rows, :] = dot(feats, k.xs[2, EMB_AT:ROWS, :], HIGH)
        return carry

    lax.fori_loop(0, CHUNKS, chunk, 0)


def stack_pair(v, masks):
    return jnp.concatenate([v * masks[0], v * masks[1]], 0)


def join_pair(v, first):
    return jnp.where(first, v[:SLOT], v[SLOT:])


def window_rows(w):
    return pl.ds(pl.multiple_of(w * SLOT, SLOT), SLOT)


def each_chunk(body, between=None):
    def step(c, carry):
        body(c, chunk_rows(c))
        if between is not None:

            @pl.when(c < CHUNKS - 1)
            def _():
                between()

        return carry

    lax.fori_loop(0, CHUNKS, step, 0)


def each_pair(body, between=None):
    def pair(n, carry):
        chains = [
            (2 * n + w, window_rows(2 * n + w), slice(p * 128, (p + 1) * 128))
            for w in range(2)
            for p in range(H // 2)
        ]
        body(pl.ds(pl.multiple_of(n * 128, 128), 128), chains)
        if between is not None:

            @pl.when(n == WINS // 4 - 1)
            def _():
                between()

        return carry

    lax.fori_loop(0, WINS // 2, pair, 0)


def forward_qkv(k, l, between):
    def chunk(c, rows):
        xhat, _ = norm_parts(k.xs[slot(l), rows, :])
        normed = (xhat * k.row(l, 0) + k.row(l, 1)).astype(LOWER)
        k.normed_t[:, rows] = normed.T
        for j in range(3):
            part = dot(normed, k.w_qkv(l, j)) + k.row(l, 4 + j)
            k.qkv[rows, j * D : (j + 1) * D] = part.astype(LOWER)

    each_chunk(chunk, between)


def qkv_part(k, n, rows, at):
    return k.qkv[rows, n * D + at.start : n * D + at.stop]


def forward_windows(k, l, between):
    first = iota((SLOT, 128), 1) < HD
    scaled = (k.pairs[0], k.pairs[1])

    def pair(both, chains):
        query = [stack_pair(qkv_part(k, 0, rows, at), scaled) for _, rows, at in chains]
        scores = [
            dot_nt(qkv_part(k, 1, rows, at), q) + k.bias[rows, :]
            for q, (_, rows, at) in zip(query, chains)
        ]
        peaks = [jnp.max(s, 0, keepdims=True) for s in scores]
        expos = [jnp.exp(s - peak) for s, peak in zip(scores, peaks)]
        totals = [jnp.sum(e, 0, keepdims=True) for e in expos]
        probs = [(e * (1.0 / total)).astype(LOWER) for e, total in zip(expos, totals)]
        outs = [dot_tn(p, qkv_part(k, 2, rows, at)) for p, (_, rows, at) in zip(probs, chains)]
        for peak, total, out, (w, rows, at) in zip(peaks, totals, outs, chains):
            p = at.start // 128
            k.logs[l, w, p : p + 1, :] = peak + jnp.log(total)
            k.left[rows, at] = join_pair(out, first).astype(LOWER)
        k.mixed_t[:, both] = k.left[both, :].T

    each_pair(pair, between)


TILES = [slice(n * 128, (n + 1) * 128) for n in range(D // 128)]


def load_mid(k, rows):
    return jnp.concatenate([k.mid[n, rows, :] for n in range(len(TILES))], 1)


def store_mid(k, rows, value):
    for n, tile in enumerate(TILES):
        k.mid[n, rows, :] = value[:, tile]


def take_states(src, dst, cols):
    dst[0:STATES, cols] = jnp.zeros((STATES, 128), WIDE)
    for w in range(WINS):
        rows = slice(w * STATE_SLOT, w * STATE_SLOT + K)
        dst[rows, cols] = src[pl.ds(w * SLOT + 1, K, stride=3), :]


def put_states(k, value):
    for n, tile in enumerate(TILES):
        dst = k.mid.at[n]
        dst[...] = jnp.zeros((ROWS, 128), WIDE)
        for w in range(WINS):
            rows = slice(w * STATE_SLOT, w * STATE_SLOT + K)
            dst[pl.ds(w * SLOT + 1, K, stride=3), :] = value[rows, tile]


def forward_up(k, l, between):
    each_chunk(lambda c, rows: up_rows(k, l, rows, k.xs[slot(l), rows, :], k.left[rows, :]), between)


def up_rows(k, l, rows, x, mixed):
    mid = x + dot(mixed, k.w_out(l)) + k.row(l, 7)
    store_mid(k, rows, mid)
    xhat, _ = norm_parts(mid)
    second = (xhat * k.row(l, 2) + k.row(l, 3)).astype(LOWER)
    k.second_t[:, rows] = second.T
    ahead = dot(second, k.w_up(l, 0))
    for j in range(4):
        cols = slice(j * D, (j + 1) * D)
        h = ahead + k.row(l, 8 + j)
        if j < 3:
            ahead = dot(second, k.w_up(l, j + 1))
        square = h * h
        over = 1.0 + jnp.tanh(h * (GELU_C + GELU_C * GELU_A * square))
        half = 0.5 * h
        acted = (half * over).astype(LOWER)
        slope = over * (0.5 + half * (2.0 - over) * (GELU_C + 3.0 * GELU_A * GELU_C * square))
        k.work[rows, cols] = acted
        k.slope[rows, cols] = slope.astype(LOWER)
        k.act_t[cols, rows] = acted.T


def forward_down(k, l, dest):
    each_chunk(lambda c, rows: down_rows(k, l, rows, dest))


def down_rows(k, l, rows, dest):
    w_down = jnp.concatenate([k.w_down(l, j) for j in range(4)], 0)
    k.xs[dest, rows, :] = load_mid(k, rows) + k.row(l, 12) + dot(k.work[rows, :], w_down)


def forward_up_states(k, l, spare):
    every, rows = slice(0, ROWS), slice(0, STATES)
    store_mid(k, every, k.left[...].astype(WIDE))
    for n, tile in enumerate(TILES):
        take_states(k.mid.at[n], k.xs.at[spare], tile)
    mixed = k.xs[spare, rows, :].astype(LOWER)
    k.mixed_t[:, rows] = mixed.T
    store_mid(k, every, k.xs[slot(l)])
    for n, tile in enumerate(TILES):
        take_states(k.mid.at[n], k.xs.at[spare], tile)
    up_rows(k, l, rows, k.xs[spare, rows, :], mixed)


def head_stage(k, at):
    gain, bias = k.small[FIN : FIN + 1, :], k.small[FIN + 1 : FIN + 2, :]
    lane = iota((STATES, 128), 1)
    keep = lane < A

    def bias_row(first):
        row = jnp.zeros((1, 128), WIDE)
        at = iota((1, 128), 1)
        for a in range(A):
            row = jnp.where(at == a, k.head_bias[first + a], row)
        return row

    bias_mean, bias_spread = bias_row(0), bias_row(A)
    temp = jnp.exp(jnp.full((1, 128), k.log_temp[0], WIDE))

    rows = slice(0, STATES)
    xhat, scale = norm_parts(k.xs[at, rows, :])
    feats = (xhat * gain + bias).astype(LOWER)
    mean = dot_nt(feats, k.headw[0]) + bias_mean
    spread = jnp.tanh(dot_nt(feats, k.headw[1]) + bias_spread)
    take_states(k.feats, k.heads, slice(0, 128))
    acts = pltpu.roll(k.heads[...], 128 - HEAD_AT, 1)
    weight = acts[:, A : A + 1]
    acts = jnp.where(keep, acts, 0.0)
    target = 0.5 * (jnp.log(1.0 + acts) - jnp.log(1.0 - acts))
    shrink = jnp.exp(-spread)
    zed = (target - mean) * shrink
    terms = 0.5 * zed * zed + spread + HALF_LOG_TAU + jnp.log(1.0 - acts * acts)
    nll = jnp.sum(jnp.where(keep, terms, 0.0), -1, keepdims=True)
    entropy = jnp.sum(jnp.where(keep, spread, 0.0), -1, keepdims=True) + A * (0.5 + HALF_LOG_TAU)
    loss = weight * (nll - temp * entropy)
    sums = jnp.where(lane == 0, loss, jnp.where(lane == 1, weight * entropy, jnp.where(lane == 2, weight, 0.0)))
    d_mean = jnp.where(keep, weight * (-zed * shrink), 0.0).astype(LOWER)
    d_spread = weight * (1.0 - zed * zed - temp) * (1.0 - spread * spread)
    d_spread = jnp.where(keep, d_spread, 0.0).astype(LOWER)
    k.sgh[2:3, 0:128] += col_sum(sums)
    k.sgh[3:4, 0:128] += col_sum(d_mean.astype(WIDE))
    k.sgh[4:5, 0:128] += col_sum(d_spread.astype(WIDE))
    k.sgw[0] += dot_tn(d_mean, feats)[0:8]
    k.sgw[1] += dot_tn(d_spread, feats)[0:8]
    d_feats = dot(d_mean, k.headw[0]) + dot(d_spread, k.headw[1])
    k.sgh[0:1, :] += col_sum(d_feats * xhat)
    k.sgh[1:2, :] += col_sum(d_feats)
    k.xs[at, rows, :] = norm_back(xhat, scale, gain, d_feats)


def store_blocks(ref, l, owners, first, count, value):
    value = value.astype(LOWER)
    for n, i in enumerate(owners):
        a, b = owner_place(i)
        ref[l, a, b, first : first + count, :] = value[n * count : (n + 1) * count]


def backward_ffn(k, l, grad, between=None):
    each_chunk(lambda c, rows: ffn_back_rows(k, l, rows, grad), between)


def ffn_back_rows(k, l, rows, grad):
    d_down = k.xs[grad, rows, :].astype(LOWER)
    k.dout[rows, :] = d_down
    k.sgl[l, 12:13, :] += col_sum(d_down.astype(WIDE))
    d_second = jnp.zeros(d_down.shape, WIDE)
    ahead = dot_nt(d_down, k.w_down(l, 0))
    for j in range(4):
        cols = slice(j * D, (j + 1) * D)
        d_acted = ahead
        if j < 3:
            ahead = dot_nt(d_down, k.w_down(l, j + 1))
        d_hidden = (d_acted * k.slope[rows, cols].astype(WIDE)).astype(LOWER)
        k.work[rows, cols] = d_hidden
        k.sgl[l, 8 + j : 9 + j, :] += col_sum(d_hidden.astype(WIDE))
        d_second = d_second + dot_nt(d_hidden, k.w_up(l, j))
    xhat, scale = norm_parts(load_mid(k, rows))
    k.sgl[l, 2:3, :] += col_sum(d_second * xhat)
    k.sgl[l, 3:4, :] += col_sum(d_second)
    k.xs[grad, rows, :] += norm_back(xhat, scale, k.row(l, 2), d_second)


def backward_down_grads(k, l, rows=slice(0, ROWS)):
    for j in range(4):
        part = dot(k.act_t[j * D : (j + 1) * D, rows], k.dout[rows, :])
        store_blocks(k.wf, l, range(8 * j, 8 * j + 8), 64, 64, part)


def backward_up_grads(k, l, rows=slice(0, ROWS)):
    for j in range(4):
        part = dot(k.second_t[:, rows], k.work[rows, j * D : (j + 1) * D])
        store_blocks(k.wf, l, range(BLOCKS), 16 * j, 16, part)


def backward_out(k, l, grad):
    def before(c, rows):
        d_branch = k.xs[grad, rows, :].astype(LOWER)
        k.left[rows, :] = d_branch
        k.sgl[l, 7:8, :] += col_sum(d_branch.astype(WIDE))
        k.dout[rows, :] = dot_nt(d_branch, k.w_out(l)).astype(LOWER)

    each_chunk(before)
    store_blocks(k.wa, l + 1, range(BLOCKS), 48, 16, dot(k.mixed_t[...], k.left[...]))


def backward_out_states(k, l, grad):
    rows = slice(0, STATES)
    d_mid = k.xs[grad, rows, :]
    d_branch = d_mid.astype(LOWER)
    k.sgl[l, 7:8, :] += col_sum(d_branch.astype(WIDE))
    d_mixed = dot_nt(d_branch, k.w_out(l)).astype(LOWER)
    store_blocks(k.wa, l + 1, range(BLOCKS), 48, 16, dot(k.mixed_t[:, rows], d_branch))
    put_states(k, d_mixed.astype(WIDE))
    k.dout[...] = load_mid(k, slice(0, ROWS)).astype(LOWER)
    put_states(k, d_mid)
    k.xs[grad] = load_mid(k, slice(0, ROWS))


def backward_windows(k, l, between):
    first = iota((SLOT, 128), 1) < HD
    scale = HD**-0.5
    scaled, plain = (k.pairs[0], k.pairs[1]), (k.pairs[2], k.pairs[3])

    def pair(both, chains):
        query = [stack_pair(qkv_part(k, 0, rows, at), scaled) for _, rows, at in chains]
        d_mixed = [stack_pair(k.dout[rows, at], plain) for _, rows, at in chains]
        shift = [
            k.bias[rows, :] - k.logs[l, w, at.start // 128 : at.start // 128 + 1, :]
            for w, rows, at in chains
        ]
        scores = [dot_nt(qkv_part(k, 1, rows, at), q) for q, (_, rows, at) in zip(query, chains)]
        d_probs = [dot_nt(qkv_part(k, 2, rows, at), d) for d, (_, rows, at) in zip(d_mixed, chains)]
        probs = [jnp.exp(s + more) for s, more in zip(scores, shift)]
        d_values = [dot(p.astype(LOWER), d) for p, d in zip(probs, d_mixed)]
        inner = [p * d for p, d in zip(probs, d_probs)]
        sums = [jnp.sum(i, 0, keepdims=True) for i in inner]
        d_scores = [(i - p * t).astype(LOWER) for i, p, t in zip(inner, probs, sums)]
        d_keyed = [dot(d, q) for d, q in zip(d_scores, query)]
        d_query = [dot_tn(d, qkv_part(k, 1, rows, at)) for d, (_, rows, at) in zip(d_scores, chains)]
        for n, (_, rows, at) in enumerate(chains):
            values = (join_pair(d_query[n], first) * scale, d_keyed[n], d_values[n])
            for m, value in enumerate(values):
                k.work[rows, m * D + at.start : m * D + at.stop] = value.astype(LOWER)

    each_pair(pair, between)


def backward_attn_grads(k, l):
    for j in range(3):
        part = dot(k.normed_t[...], k.work[:, j * D : (j + 1) * D])
        store_blocks(k.wa, l + 1, range(BLOCKS), 16 * j, 16, part)


def backward_input(k, l, grad):
    def chunk(c, rows):
        d_normed = jnp.zeros((CHUNK, D), WIDE)
        for j in range(3):
            d_part = k.work[rows, j * D : (j + 1) * D]
            k.sgl[l, 4 + j : 5 + j, :] += col_sum(d_part.astype(WIDE))
            d_normed = d_normed + dot_nt(d_part, k.w_qkv(l, j))
        xhat, scale = norm_parts(k.xs[slot(l), rows, :])
        k.sgl[l, 0:1, :] += col_sum(d_normed * xhat)
        k.sgl[l, 1:2, :] += col_sum(d_normed)
        k.xs[grad, rows, :] += norm_back(xhat, scale, k.row(l, 0), d_normed)

    each_chunk(chunk)


def small_stage(k, out, grad):
    out[...] = jnp.zeros_like(out)
    out[0:EMB, :] = dot_tn(k.feats[...], k.xs[grad], HIGH)[0:EMB]
    out[FIN : FIN + 2, :] = k.sgh[0:2, :]
    out[HEADW : HEADW + A, :] = k.sgw[0, 0:A, :]
    out[HEADW + A : HEADW + 2 * A, :] = k.sgw[1, 0:A, :]
    for l in range(LAYERS):
        out[BASE + l * PER : BASE + (l + 1) * PER, :] = k.sgl[l, 0:PER, :]
    out[NROWS : NROWS + 3, :] = k.sgh[2:5, :]


WORK_SHAPES = dict(
    wa=((LAYERS + 1, 4, 8, ATTN, D), LOWER),
    wf=((LAYERS, 4, 8, FFN, D), LOWER),
    xs=((3, ROWS, D), WIDE),
    qkv=((ROWS, 3 * D), LOWER),
    normed_t=((D, ROWS), LOWER),
    mixed_t=((D, ROWS), LOWER),
    slope=((ROWS, FF), LOWER),
    act_t=((FF, ROWS), LOWER),
    second_t=((D, ROWS), LOWER),
    mid=((D // 128, ROWS, 128), WIDE),
    logs=((LAYERS, WINS, 8, 128), WIDE),
    work=((ROWS, FF), LOWER),
    left=((ROWS, D), LOWER),
    dout=((ROWS, D), LOWER),
    feats=((ROWS, 128), WIDE),
    heads=((STATES, 128), WIDE),
    bias=((ROWS, 128), WIDE),
    pairs=((4, SLOT, 128), LOWER),
    headw=((2, 128, D), LOWER),
    lrows=((LAYERS, 16, D), WIDE),
    sgl=((LAYERS, 16, D), WIDE),
    sgh=((8, D), WIDE),
    sgw=((2, 8, D), WIDE),
    meta=((128, 128), WIDE),
    buf=((2, 128, 128), WIDE),
)
KEEP_ATTN = ("qkv", "normed_t", "mixed_t")
KEEP_FFN = ("slope", "act_t", "second_t", "mid")
KEEP = KEEP_ATTN + KEEP_FFN


MESH = pl.DeviceIdType.MESH
NZ, NY, NX, NC = 4, 2, 2, 2
NR = NY * NX * NC
SHARD = PACK
PARTS, DEEP = 3, 64
HALF = DEEP // 2


class Place:
    def __init__(self):
        dp, fsdp = lax.axis_index("dp"), lax.axis_index("fsdp")
        self.z, self.y = dp // NY, dp % NY
        self.x, self.c = fsdp // NC, fsdp % NC
        self.a, self.b = 2 * self.c + self.x, 4 * self.y + self.z
        self.r = 4 * self.y + fsdp
        self.to_z = [(((self.z + d) % NZ) * NY + self.y, fsdp) for d in range(1, NZ)]
        self.odd = self.z % 2
        self.to_pair = ((self.z + 1 - 2 * self.odd) * NY + self.y, fsdp)
        self.plane = []
        for d in range(1, 8):
            y, x, c = [
                1 - v if d & bit else v for v, bit in ((self.y, 4), (self.x, 2), (self.c, 1))
            ]
            self.plane.append((self.z * NY + y, x * NC + c))
        self.to_c, self.to_x, self.to_y = self.plane[0], self.plane[1], self.plane[3]

    def barrier(self):
        sem = pltpu.get_barrier_semaphore()
        for partner in self.plane + self.to_z:
            pl.semaphore_signal(sem, inc=1, device_id=partner, device_id_type=MESH)
        pl.semaphore_wait(sem, len(self.plane) + len(self.to_z))


def remote(src, dst, send, recv, to):
    return pltpu.make_async_remote_copy(
        src_ref=src, dst_ref=dst, send_sem=send, recv_sem=recv, device_id=to, device_id_type=MESH
    )


def part_ref(weights, part):
    return weights[min(part, 1)], (0, 0, DEEP)[part]


class Gather:
    COPIES = 13

    def __init__(self, place, weights, send, recv):
        self.at, self.weights, self.send, self.recv = place, weights, send, recv

    def copy(self, l, part, n):
        at = self.at
        array, row = part_ref(self.weights, part)
        a, b, rows, to = at.a, pl.ds(4 * at.y, 4), pl.ds(row, DEEP), at.to_c
        if n < 3:
            b, to = at.b, at.to_z[n]
        elif n < 5:
            to = (at.to_x, at.to_y)[n - 3]
        if n in (6, 8, 10, 11, 12):
            a = 2 * at.c + 1 - at.x
        if n in (7, 9, 10, 11, 12):
            b = pl.ds(4 * (1 - at.y), 4)
        if n in (6, 7):
            first = row + at.odd * HALF + (n - 6) * (HALF // 2)
            rows = pl.ds(pl.multiple_of(first, HALF // 2), HALF // 2)
            to = (at.to_y, at.to_x)[n - 6]
        if n in (10, 11):
            rows = pl.ds(pl.multiple_of(row + at.odd * HALF, HALF), HALF)
        if n == 11:
            to = at.to_pair
        if n == 12:
            rows = pl.ds(pl.multiple_of(row + (1 - at.odd) * HALF, HALF), HALF)
        ref = array.at[l, a, b, rows, :]
        q = PARTS * l + part
        return remote(ref, ref, self.send.at[q, n], self.recv.at[q, n], to)

    def start(self, l, part, *ns):
        for n in ns:
            self.copy(l, part, n).start()

    def wait(self, l, part, *ns):
        for n in ns:
            self.copy(l, part, n).wait_recv()

    def first(self, l, part):
        self.start(l, part, 0, 1, 2)

    def second(self, l, part):
        self.wait(l, part, 0, 1, 2)
        self.start(l, part, 3, 4, 5)

    def third(self, l, part):
        self.wait(l, part, 3)
        self.start(l, part, 6, 8)
        self.wait(l, part, 4)
        self.start(l, part, 7, 9)

    def fourth(self, l, part):
        self.wait(l, part, 6, 7)
        self.start(l, part, 11, 10)

    def fifth(self, l, part):
        self.wait(l, part, 11)
        self.start(l, part, 12)

    def last(self, l, part):
        self.wait(l, part, 5, 8, 9, 10, 12)

    def sent(self, l, part):
        for n in range(self.COPIES):
            self.copy(l, part, n).wait_send()


class Reduce:
    COPIES = 8

    def __init__(self, place, grads, landing, send, recv, credit):
        self.at, self.grads, self.landing = place, grads, landing
        self.send, self.recv, self.credit = send, recv, credit

    def refs(self, l, part):
        array, row = part_ref(self.grads, part)
        grads = array.at[l + 1 - min(part, 1), :, :, pl.ds(row, DEEP), :]
        return (grads, *self.landing[part])

    def copy(self, l, part, n):
        at, half = self.at, HALF
        g, r0, r1a, r1b, r2, r3 = self.refs(l, part)
        top, low, other = pl.ds(0, half), pl.ds(half, half), pl.ds(4 * (1 - at.y), 4)
        if n == 0:
            src, dst, to = g.at[pl.ds(2 * (1 - at.c), 2)], r0, at.to_c
        elif n == 1:
            src, dst, to = r0.at[1 - at.x, :, top, :], r1a, at.to_x
        elif n == 2:
            src, dst, to = r0.at[:, other, low, :], r1b, at.to_y
        elif n == 3:
            src, dst, to = r1a.at[other], r2.at[:, top, :], at.to_y
        elif n == 4:
            src, dst, to = r1b.at[1 - at.x], r2.at[:, low, :], at.to_x
        else:
            src, dst, to = r2.at[(at.z + n - 4) % NZ], r3.at[n - 5], at.to_z[n - 5]
        q = PARTS * l + part
        return remote(src, dst, self.send.at[q, n], self.recv.at[q, n], to)

    def may_send(self, l, part, *partners):
        @pl.when(l < LAYERS - 1)
        def _():
            for n in partners:
                pl.semaphore_wait(self.credit.at[part, n], 1)

    def allow(self, l, part, *credits):
        at = self.at

        @pl.when(l > 0)
        def _():
            for n, to in credits:
                pl.semaphore_signal(
                    self.credit.at[part, n], inc=1, device_id=to, device_id_type=MESH
                )

    def start(self, l, part):
        self.may_send(l, part, 0)
        self.copy(l, part, 0).start()

    def first(self, l, part):
        at, half = self.at, HALF
        g, r0, _, _, _, _ = self.refs(l, part)
        top, low = pl.ds(0, half), pl.ds(half, half)
        self.copy(l, part, 0).wait_recv()

        x = 1 - at.x
        total = g[2 * at.c + x, :, top].astype(WIDE) + r0[x, :, top].astype(WIDE)
        r0[x, :, top] = total.astype(LOWER)
        self.may_send(l, part, 1, 2)
        self.copy(l, part, 1).start()
        other = pl.ds(4 * (1 - at.y), 4)
        for x in range(NX):
            total = g[2 * at.c + x, other, low].astype(WIDE) + r0[x, other, low].astype(WIDE)
            r0[x, other, low] = total.astype(LOWER)
        self.copy(l, part, 2).start()

    def second(self, l, part):
        at, half = self.at, HALF
        g, r0, r1a, r1b, _, _ = self.refs(l, part)
        top, low = pl.ds(0, half), pl.ds(half, half)

        x, other, column = 1 - at.x, pl.ds(4 * (1 - at.y), 4), pl.ds(4 * at.y, 4)
        self.copy(l, part, 1).wait_recv()
        total = g[at.a, other, top].astype(WIDE) + r0[at.x, other, top].astype(WIDE)
        r1a[other] = (total + r1a[other].astype(WIDE)).astype(LOWER)
        self.may_send(l, part, 6, 7)
        self.copy(l, part, 3).start()
        self.copy(l, part, 2).wait_recv()
        total = g[2 * at.c + x, column, low].astype(WIDE) + r0[x, column, low].astype(WIDE)
        r1b[x] = (total + r1b[x].astype(WIDE)).astype(LOWER)
        self.copy(l, part, 4).start()

    def chip_sums(self, l, part, z):
        at, half = self.at, HALF
        g, r0, r1a, r1b, r2, _ = self.refs(l, part)
        top, low, b = pl.ds(0, half), pl.ds(half, half), 4 * at.y + z
        upper = g[at.a, b, top].astype(WIDE) + r0[at.x, b, top].astype(WIDE)
        lower = g[at.a, b, low].astype(WIDE) + r0[at.x, b, low].astype(WIDE)
        return (
            upper + r1a[b].astype(WIDE) + r2[z, top].astype(WIDE),
            lower + r1b[at.x, z].astype(WIDE) + r2[z, low].astype(WIDE),
        )

    def third(self, l, part, out):
        at, half, row = self.at, HALF, DEEP * part
        r2 = self.landing[part][3]
        for n in (3, 4):
            self.copy(l, part, n).wait_recv()
        self.may_send(l, part, 3, 4, 5)
        for n in range(3):
            z = (at.z + n + 1) % NZ
            upper, lower = self.chip_sums(l, part, z)
            r2[z, pl.ds(0, half)] = upper.astype(LOWER)
            r2[z, pl.ds(half, half)] = lower.astype(LOWER)
            self.copy(l, part, 5 + n).start()
        upper, lower = self.chip_sums(l, part, at.z)
        out[l, row : row + half, :] = upper
        out[l, row + half : row + 2 * half, :] = lower
        for n in range(5):
            self.copy(l, part, n).wait_send()
        self.allow(l, part, (0, at.to_c), (1, at.to_x), (2, at.to_y))

    def last(self, l, part, out, squares):
        at, row = self.at, DEEP * part
        r3 = self.landing[part][4]
        rows = slice(row, row + DEEP)
        total = out[l, rows, :]
        for n in range(3):
            self.copy(l, part, 5 + n).wait_recv()
            total = total + r3[n].astype(WIDE)
        out[l, rows, :] = total
        squares[0:1, :] += col_sum(total * total)
        for n in range(5, self.COPIES):
            self.copy(l, part, n).wait_send()
        late = [(6, at.to_x), (7, at.to_y)] + [(5 - n, at.to_z[n]) for n in range(3)]
        self.allow(l, part, *late)


class Total:
    COPIES = 7

    def __init__(self, place, ref, rows, send, recv):
        self.at, self.ref, self.rows = place, ref, rows // 2
        self.send, self.recv = send, recv

    def half(self, n):
        return self.ref.at[pl.ds(pl.multiple_of(n * self.rows, 8), self.rows), :]

    def whole(self):
        return self.ref.at[pl.ds(0, 2 * self.rows), :]

    def copy(self, n):
        at = self.at
        mine, other = self.half(at.c), self.half(1 - at.c)
        src, dst, to = (
            (other, self.half(2), at.to_c),
            (self.half(8), self.half(3), at.to_x),
            (self.half(9), self.half(4), at.to_y),
            (self.half(10), self.half(5), at.to_z[0]),
            (self.half(10), self.half(6), at.to_z[1]),
            (self.half(10), self.half(7), at.to_z[2]),
            (mine, self.half(11), at.to_c),
        )[n]
        return remote(src, dst, self.send.at[n], self.recv.at[n], to)

    def start(self):
        self.copy(0).start()

    def step(self, n):
        self.copy(n).wait_recv()
        own = self.half(self.at.c) if n == 0 else self.half(7 + n)
        self.half(8 + n)[...] = own[...] + self.half(2 + n)[...]
        for m in ((1,), (2,), (3, 4, 5))[n]:
            self.copy(m).start()

    def back(self):
        for m in (3, 4, 5):
            self.copy(m).wait_recv()
        self.copy(0).wait_send()
        total = None
        for z in range(NZ):
            term = self.half(10)[...]
            for n in range(3):
                from_z = (self.at.z + NZ - 1 - n) % NZ
                term = jnp.where(from_z == z, self.half(5 + n)[...], term)
            total = term if total is None else total + term
        self.half(self.at.c)[...] = total
        self.copy(6).start()

    def last(self):
        self.copy(6).wait_recv()
        self.half(1 - self.at.c)[...] = self.half(11)[...]
        for n in range(1, self.COPIES):
            self.copy(n).wait_send()


class Norm:
    COPIES = 10

    def __init__(self, place, plane, column, send, recv):
        self.at, self.plane, self.column = place, plane, column
        self.send, self.recv = send, recv

    def copy(self, n):
        at = self.at
        if n < 7:
            ref, to = self.plane.at[at.r], at.plane[n]
        else:
            ref, to = self.column.at[at.z], at.to_z[n - 7]
        return remote(ref, ref, self.send.at[n], self.recv.at[n], to)

    def start(self, tile):
        self.plane[self.at.r] = tile
        for n in range(7):
            self.copy(n).start()

    def total(self, ref, ns):
        for n in ns:
            self.copy(n).wait_recv()
        total = ref[0]
        for n in range(1, ref.shape[0]):
            total = total + ref[n]
        return total

    def step(self):
        self.column[self.at.z] = self.total(self.plane, range(7))
        for n in range(7, self.COPIES):
            self.copy(n).start()

    def last(self):
        total = self.total(self.column, range(7, self.COPIES))
        for n in range(self.COPIES):
            self.copy(n).wait_send()
        return total


LANDING = (
    (NX, 8, DEEP, D),
    (8, HALF, D),
    (NX, NZ, HALF, D),
    (NZ, DEEP, D),
    (3, DEEP, D),
)


def stage_rows(qkv, out, up, down, l):
    return (
        [(qkv.at[l, :, pl.ds(j * D, D)], 16 * j, 16) for j in range(3)]
        + [(out.at[l], 48, 16)]
        + [(up.at[l, :, pl.ds(j * D, D)], 64 + 16 * j, 16) for j in range(4)]
        + [(down.at[l], 128, 64)]
    )


BEGIN, SETUP, START, QKV_HALF, QKV, WINDOWS_HALF, WINDOWS, UP_HALF, UP, DOWN = range(10)
FIRST, SECOND, THIRD, FOURTH, FIFTH, LAST, SEND = range(7)
GATHER_PLAN = {
    (-1, BEGIN): [(FIRST, 0, 0), (FIRST, 0, 1)],
    (-1, SETUP): [(SECOND, 0, 0), (FIRST, 0, 2)],
    (0, START): [(THIRD, 0, 0), (SECOND, 0, 1), (FOURTH, 0, 0), (FIRST, 1, 0), (FIFTH, 0, 0), (LAST, 0, 0)],
    (0, QKV_HALF): [(SECOND, 0, 2), (THIRD, 0, 1), (FIRST, 1, 1)],
    (0, QKV): [(FOURTH, 0, 1), (SECOND, 1, 0), (FIRST, 1, 2)],
    (0, WINDOWS_HALF): [(FIFTH, 0, 1), (THIRD, 0, 2), (LAST, 0, 1), (SECOND, 1, 1), (FIRST, 2, 0)],
    (0, WINDOWS): [(FOURTH, 0, 2), (THIRD, 1, 0)],
    (0, UP_HALF): [(FIFTH, 0, 2), (SECOND, 1, 2), (FIRST, 2, 1), (FOURTH, 1, 0)],
    (0, UP): [(LAST, 0, 2), (THIRD, 1, 1), (FIFTH, 1, 0), (SECOND, 2, 0)],
    (0, DOWN): [(FIRST, 2, 2), (FOURTH, 1, 1)],
    (1, START): [(LAST, 1, 0)],
    (1, QKV_HALF): [(SECOND, 2, 1), (THIRD, 1, 2)],
    (1, QKV): [(FIFTH, 1, 1)],
    (1, WINDOWS_HALF): [(LAST, 1, 1), (SECOND, 2, 2), (FOURTH, 1, 2), (THIRD, 2, 0)],
    (1, WINDOWS): [(FIFTH, 1, 2)],
    (1, UP_HALF): [(LAST, 1, 2), (FOURTH, 2, 0)],
    (1, UP): [(THIRD, 2, 1), (FIFTH, 2, 0)],
    (1, DOWN): [(LAST, 2, 0), (FOURTH, 2, 1)],
    (2, QKV_HALF): [(THIRD, 2, 2), (FIFTH, 2, 1)],
    (2, QKV): [(FOURTH, 2, 2)],
    (2, WINDOWS_HALF): [(LAST, 2, 1), (FIFTH, 2, 2)],
    (2, WINDOWS): [(LAST, 2, 2)],
}


def train_kernel(refs, alone):
    k = Kit(**refs)

    def kept(names, l, back):
        copies = []
        for name in names:
            here, there = refs[name], refs["keep_" + name].at[l]
            src, dst = (there, here) if back else (here, there)
            copies.append(pltpu.make_async_copy(src, dst, k.keep_sem.at[KEEP.index(name)]))
        return copies

    def start(copies):
        for copy in copies:
            copy.start()

    def wait(copies):
        for copy in copies:
            copy.wait()

    def kept_x(back):
        here, there = k.xs.at[0], k.keep_x
        src, dst = (there, here) if back else (here, there)
        return [pltpu.make_async_copy(src, dst, k.keep_sem.at[len(KEEP)])]

    arrays = [(l, n) for l in range(LAYERS) for n in (0, 1)]
    parts = [(l, part) for l in range(LAYERS) for part in range(PARTS)]
    weights = (k.wa, k.wf)
    if alone:
        loads = [
            pltpu.make_async_copy((k.all_a, k.all_f)[n].at[l], weights[n].at[l], k.load_sem.at[2 * l + n])
            for l, n in arrays
        ]
        stores = [
            pltpu.make_async_copy(
                weights[n].at[l + 1 - n], (k.grad_a, k.grad_f)[n].at[l], k.load_sem.at[2 * l + n]
            )
            for l, n in arrays
        ]
        start(loads)
    else:
        place = Place()
        gather = Gather(place, weights, k.gather_send, k.gather_recv)
        reduce = Reduce(
            place, weights, k.landing, k.reduce_send, k.reduce_recv, k.credit
        )
        sums = Total(place, k.xs.at[1], SMALL, k.sum_send, k.sum_recv)
        norm = Norm(place, k.norm_plane, k.norm_column, k.norm_send, k.norm_recv)

    def run(plan):
        stages = (
            gather.first,
            gather.second,
            gather.third,
            gather.fourth,
            gather.fifth,
            gather.last,
        )
        for stage, l, part in plan:
            stages[stage](l, part)

    def poll(l, point):
        if alone:
            return
        for layer in range(LAYERS):
            plan = GATHER_PLAN.get((layer, point))
            if plan:

                @pl.when(l == layer)
                def _(plan=plan):
                    run(plan)

    if not alone:
        staged = []
        for l in range(LAYERS):
            for n, (src, row, count) in enumerate(stage_rows(k.qkv_w, k.out_w, k.up_w, k.down_w, l)):
                dst = k.xs.at[2, pl.ds(l * PACK + row, count), :]
                staged.append(pltpu.make_async_copy(src, dst, k.stage_sem.at[l, n]))
        start(staged)
        place.barrier()
        for l in range(LAYERS):
            wait(staged[9 * l : 9 * l + 9])
            row = l * PACK
            for part in range(PARTS):
                array, first = part_ref(weights, part)
                mine = k.xs[2, row + DEEP * part : row + DEEP * (part + 1), :].astype(LOWER)
                array[l, place.a, place.b, first : first + DEEP, :] = mine
                if (FIRST, l, part) in GATHER_PLAN[-1, BEGIN]:
                    gather.first(l, part)
        k.squares_sum[...] = jnp.zeros_like(k.squares_sum)

    setup_stage(k)
    start(kept_x(False))
    if not alone:
        run(GATHER_PLAN[-1, SETUP])

    grad = 2

    def forward(l, carry):
        if alone:
            pltpu.make_async_copy(k.all_a.at[l], k.wa.at[l], k.load_sem.at[2 * l]).wait()

        @pl.when(l > 0)
        def _():
            wait(kept(KEEP_ATTN, l - 1, False))

        poll(l, START)
        forward_qkv(k, l, lambda: poll(l, QKV_HALF))
        poll(l, QKV)
        forward_windows(k, l, lambda: poll(l, WINDOWS_HALF))

        @pl.when(l < LAYERS - 1)
        def _():
            start(kept(KEEP_ATTN, l, False))

        @pl.when(l > 0)
        def _():
            wait(kept(KEEP_FFN, l - 1, False))

        @pl.when(l == 1)
        def _():
            wait(kept_x(False))

        if alone:
            pltpu.make_async_copy(k.all_f.at[l], k.wf.at[l], k.load_sem.at[2 * l + 1]).wait()
        poll(l, WINDOWS)

        @pl.when(l < LAYERS - 1)
        def _():
            forward_up(k, l, lambda: poll(l, UP_HALF))

        @pl.when(l == LAYERS - 1)
        def _():
            forward_up_states(k, l, grad)

        poll(l, UP)

        @pl.when(l < LAYERS - 1)
        def _():
            forward_down(k, l, (l + 1) % 2)

        @pl.when(l == LAYERS - 1)
        def _():
            down_rows(k, l, slice(0, STATES), grad)

        @pl.when(l < LAYERS - 1)
        def _():
            start(kept(KEEP_FFN, l, False))

        poll(l, DOWN)
        return carry

    lax.fori_loop(0, LAYERS, forward, 0)
    if not alone:
        for l, part in parts:
            gather.sent(l, part)
    head_stage(k, grad)

    def run_reduce(stage, l, part):
        if stage == THIRD:
            reduce.third(l, part, k.shard)
        elif stage == LAST:
            reduce.last(l, part, k.shard, k.squares_sum)
        else:
            {SEND: reduce.start, FIRST: reduce.first, SECOND: reduce.second}[stage](l, part)

    def backward(n, carry):
        l = LAYERS - 1 - n

        def behind(name, *stages):
            @pl.when(n > 0)
            def _():
                for stage, part, *more in stages:
                    stage(l + 1, part, *more)

        @pl.when(n > 0)
        def _():
            wait(kept(KEEP_FFN, l, True))

        def now(stage, part, early=None):
            if alone:
                return
            if early is None:
                run_reduce(stage, l, part)
                return

            @pl.when((n == LAYERS - 1) if early else (n < LAYERS - 1))
            def _():
                run_reduce(stage, l, part)

        def then(stage, part):
            if not alone:

                @pl.when(n > 0)
                def _():
                    run_reduce(stage, l + 1, part)

        def in_ffn():
            then(LAST, 2)
            then(THIRD, 1)
            then(FIRST, 0)

        def in_windows():
            now(FIRST, 1, False)
            now(SECOND, 2, True)

        states = slice(0, STATES)

        @pl.when(n > 0)
        def _():
            backward_ffn(k, l, grad, in_ffn)
            backward_down_grads(k, l)

        @pl.when(n == 0)
        def _():
            ffn_back_rows(k, l, states, grad)
            backward_down_grads(k, l, states)

        now(SEND, 2)
        then(LAST, 1)
        then(SECOND, 0)

        @pl.when(n > 0)
        def _():
            backward_up_grads(k, l)

        @pl.when(n == 0)
        def _():
            backward_up_grads(k, l, states)

        @pl.when((n > 0) & (n < LAYERS - 1))
        def _():
            start(kept(KEEP_FFN, l - 1, True))

        now(SEND, 1)
        now(FIRST, 2, True)

        @pl.when(n > 0)
        def _():
            wait(kept(KEEP_ATTN, l, True))

        @pl.when(n > 0)
        def _():
            backward_out(k, l, grad)

        @pl.when(n == 0)
        def _():
            backward_out_states(k, l, grad)
            start(kept(KEEP_FFN, l - 1, True))

        now(FIRST, 2, False)
        now(FIRST, 1, True)
        then(THIRD, 0)
        backward_windows(k, l, in_windows)
        now(SECOND, 2, False)
        now(THIRD, 2, True)
        then(LAST, 0)
        backward_attn_grads(k, l)

        @pl.when(n < LAYERS - 1)
        def _():
            start(kept(KEEP_ATTN, l - 1, True))

        now(SEND, 0)
        now(THIRD, 2, False)
        now(SECOND, 1, True)

        @pl.when(n == LAYERS - 1)
        def _():
            wait(kept_x(True))

        backward_input(k, l, grad)

        @pl.when(n == 0)
        def _():
            start(kept_x(True))

        now(SECOND, 1, False)
        now(FIRST, 0, True)
        now(THIRD, 1, True)
        return carry

    lax.fori_loop(0, LAYERS, backward, 0)
    if alone:
        start(stores)
        small_stage(k, k.small_out, grad)
        wait(stores)
        return
    small_stage(k, sums.whole(), grad)
    sums.start()
    reduce.last(0, 2, k.shard, k.squares_sum)
    reduce.second(0, 0)
    sums.step(0)
    reduce.third(0, 0, k.shard)
    sums.step(1)
    reduce.last(0, 1, k.shard, k.squares_sum)
    sums.step(2)
    reduce.last(0, 0, k.shard, k.squares_sum)
    squares = k.squares_sum[...]
    norm.start(sum(squares[:, n * 128 : (n + 1) * 128] for n in range(D // 128)))
    sums.back()
    norm.step()
    sums.last()
    k.small_out[...] = sums.whole()[...]
    k.squares[...] = norm.last()


def train_pass(inputs, weights, alone):
    whole = pl.BlockSpec(memory_space=pltpu.VMEM)
    scalars = pl.BlockSpec(memory_space=pltpu.SMEM)
    anywhere = pl.BlockSpec(memory_space=pl.ANY)
    dma = pltpu.SemaphoreType.DMA
    count = PARTS * LAYERS
    names = ["states", "actions", "returns", "starts", "repeats", "valid"]
    names += ["log_temp", "small", "head_bias"]
    out_shape = {"small_out": ((SMALL, D), WIDE)}
    for name in KEEP:
        shape, dtype = WORK_SHAPES[name]
        out_shape["keep_" + name] = ((LAYERS - 1,) + shape, dtype)
    out_shape["keep_x"] = ((ROWS, D), WIDE)
    scratch = {name: pltpu.VMEM(*shape) for name, shape in WORK_SHAPES.items()}
    scratch["keep_sem"] = dma((len(KEEP) + 1,))
    if alone:
        names += ["all_a", "all_f"]
        out_shape["grad_a"] = ((LAYERS, 4, 8, ATTN, D), LOWER)
        out_shape["grad_f"] = ((LAYERS, 4, 8, FFN, D), LOWER)
        scratch["load_sem"] = dma((count,))
    else:
        names += ["qkv_w", "out_w", "up_w", "down_w"]
        out_shape["shard"] = ((LAYERS, PACK, D), WIDE)
        out_shape["squares"] = ((8, 128), WIDE)
        for part in range(PARTS):
            for n, shape in enumerate(LANDING):
                scratch["land_%d_%d" % (part, n)] = pltpu.VMEM(shape, LOWER)
        scratch["stage_sem"] = dma((LAYERS, 9))
        scratch["squares_sum"] = pltpu.VMEM((8, D), WIDE)
        for name, copies in (("gather", Gather.COPIES), ("reduce", Reduce.COPIES)):
            scratch[name + "_send"] = dma((count, copies))
            scratch[name + "_recv"] = dma((count, copies))
        scratch["credit"] = pltpu.SemaphoreType.REGULAR((PARTS, 8))
        scratch["norm_plane"] = pltpu.VMEM((8, 8, 128), WIDE)
        scratch["norm_column"] = pltpu.VMEM((NZ, 8, 128), WIDE)
        for name, copies in (("sum", Total.COPIES), ("norm", Norm.COPIES)):
            scratch[name + "_send"] = dma((copies,))
            scratch[name + "_recv"] = dma((copies,))
    spaces = dict.fromkeys(("starts", "repeats", "head_bias", "log_temp"), scalars)
    for name in ("all_a", "all_f", "grad_a", "grad_f", "qkv_w", "out_w", "up_w", "down_w"):
        spaces[name] = anywhere
    for name in KEEP + ("x",):
        spaces["keep_" + name] = anywhere
    every = names + list(out_shape) + list(scratch)

    def kernel(*given):
        refs = dict(zip(every, given))
        refs["landing"] = [
            [refs.get("land_%d_%d" % (part, n)) for n in range(len(LANDING))] for part in range(PARTS)
        ]
        train_kernel(refs, alone)

    results = pl.pallas_call(
        kernel,
        name="train_pass",
        out_shape=tuple(jax.ShapeDtypeStruct(*shape) for shape in out_shape.values()),
        in_specs=[spaces.get(name, whole) for name in names],
        out_specs=tuple(spaces.get(name, whole) for name in out_shape),
        scratch_shapes=list(scratch.values()),
        compiler_params=pltpu.CompilerParams(
            vmem_limit_bytes=VMEM_BYTES,
            collective_id=None if alone else 0,
            has_side_effects=not alone,
        ),
        cost_estimate=pl.CostEstimate(
            flops=6 * 10**10, bytes_accessed=4 * 10**7, transcendentals=10**7
        ),
    )(*inputs, *weights)
    return dict(zip(out_shape, results))


def adam_parts(weight, grad, first, second, rate):
    first = BETA_ONE * first + (1.0 - BETA_ONE) * grad
    second = BETA_TWO * second + (1.0 - BETA_TWO) * grad * grad
    fix_one = 1.0 - BETA_ONE**STEP
    fix_two = 1.0 - BETA_TWO**STEP
    fresh = weight - rate * (
        first * (1.0 / fix_one) / (jnp.sqrt(second * (1.0 / fix_two)) + ADAM_EPS) + DECAY * weight
    )
    return fresh, first, second


def adam_kernel(*refs):
    shard, small_grad, squares, groups, log_temp = refs[:5]
    small, small_first, small_second, bias, bias_first, bias_second = refs[5:11]
    mats, firsts, seconds = refs[11:15], refs[15:19], refs[19:23]
    totals, norm, next_temp, s_next, s_first, s_second, b_next, b_first, b_second = refs[23:32]
    m_next, m_copy, m_first, m_second = refs[32:36], refs[36:40], refs[40:44], refs[44:48]
    extra = small_grad[NROWS : NROWS + 3, 0:128]
    lane = iota((1, 128), 1)
    bias_mean = jnp.where(lane < A, extra[1:2], 0.0)
    bias_spread = jnp.where(lane < A, extra[2:3], 0.0)

    def all_sum(v):
        return jnp.sum(jnp.sum(v, 0, keepdims=True), 1, keepdims=True)

    grads = small_grad[0:NROWS, :]
    square = (
        all_sum(squares[0:1, :])
        + all_sum(grads * grads)
        + all_sum(bias_mean * bias_mean)
        + all_sum(bias_spread * bias_spread)
    )
    length = jnp.sqrt(square)
    clip = jnp.minimum(1.0, CLIP / (length + 1e-06))

    def rate_of(l, kind):
        group = jnp.full((1, 1), groups[l, kind], jnp.int32).astype(WIDE)
        return LEARN * jnp.exp2(-group)

    def update(l, kind, rows, cols, grad):
        at = (l, rows, cols)
        fresh, first, second = adam_parts(
            mats[kind][at], clip * grad, firsts[kind][at], seconds[kind][at], rate_of(l, kind)
        )
        m_next[kind][at] = fresh
        m_copy[kind][at] = fresh.astype(LOWER)
        m_first[kind][at] = first
        m_second[kind][at] = second

    every = slice(0, 16)
    for l in range(LAYERS):
        for j in range(3):
            update(l, 0, every, slice(j * D, (j + 1) * D), shard[l, 16 * j : 16 * j + 16, :])
        update(l, 1, every, slice(0, D), shard[l, 48:64, :])
        for j in range(4):
            rows = slice(64 + 16 * j, 80 + 16 * j)
            update(l, 2, every, slice(j * D, (j + 1) * D), shard[l, rows, :])
        update(l, 3, slice(0, 64), slice(0, D), shard[l, 128:192, :])

    s_next[...], s_first[...], s_second[...] = adam_parts(
        small[...], clip * grads, small_first[...], small_second[...], LEARN
    )

    def scalar(v, n):
        return jnp.sum(jnp.where(lane == n, v, 0.0))

    def row(ref):
        v = jnp.zeros((1, 128), WIDE)
        for n in range(2 * A):
            v = jnp.where(lane == n, ref[n], v)
        return v

    grad = bias_mean + pltpu.roll(bias_spread, A, 1)
    results = adam_parts(row(bias), clip * grad, row(bias_first), row(bias_second), LEARN)
    for ref, result in zip((b_next, b_first, b_second), results):
        for n in range(2 * A):
            ref[n] = scalar(result, n)
    sums = extra[0:1]
    for n in range(3):
        totals[n] = scalar(sums, n)
    norm[0] = jnp.sum(length)
    logs = jnp.full((1, 1), log_temp[0], WIDE)
    ratio = jnp.full((1, 1), scalar(sums, 1), WIDE) / jnp.full((1, 1), scalar(sums, 2), WIDE)
    next_temp[0] = jnp.sum(logs - TEMP_RATE * jnp.exp(logs) * (ratio + A))


def adam_all(shard, small_grad, squares, groups, log_temp, smalls, biases, mats, firsts, seconds):
    scalars = pl.BlockSpec(memory_space=pltpu.SMEM)

    whole = pl.BlockSpec(memory_space=pltpu.VMEM)

    def like(array, dtype=WIDE):
        return jax.ShapeDtypeStruct(array.shape, dtype)

    stacks = list(mats) + list(firsts) + list(seconds)
    small, bias = smalls[0], biases[0]
    return pl.pallas_call(
        adam_kernel,
        name="adam",
        out_shape=(
            (jax.ShapeDtypeStruct((3,), WIDE),)
            + (jax.ShapeDtypeStruct((1,), WIDE),) * 2
            + (like(small),) * 3
            + (like(bias),) * 3
            + tuple(like(m) for m in mats)
            + tuple(like(m, LOWER) for m in mats)
            + tuple(like(m) for m in mats) * 2
        ),
        in_specs=[whole] * 3 + [scalars] * 2 + [whole] * 3 + [scalars] * 3 + [whole] * 12,
        out_specs=(scalars,) * 3 + (whole,) * 3 + (scalars,) * 3 + (whole,) * 16,
        compiler_params=pltpu.CompilerParams(vmem_limit_bytes=VMEM_BYTES),
        cost_estimate=pl.CostEstimate(flops=10**7, bytes_accessed=8 * 10**6, transcendentals=10**6),
    )(shard, small_grad, squares, groups, log_temp, *smalls, *biases, *stacks)


def gather_packed(mats, axes, count):
    group = count // BLOCKS
    pieces = []
    for mat in mats:
        rows, wide = mat.shape[1], mat.shape[2] // D
        piece = mat.astype(LOWER).reshape(LAYERS, rows, wide, D)
        piece = lax.all_gather(piece, axes, axis=1, tiled=True)
        piece = piece.reshape(LAYERS, NZ, NY, NX, NC, group * rows, wide, D)
        piece = piece.transpose(0, 4, 3, 2, 1, 6, 5, 7)
        pieces.append(piece.reshape(LAYERS, 4, 8, wide * group * rows, D))
    return jnp.concatenate(pieces[:2], 3), jnp.concatenate(pieces[2:], 3)


def scatter_packed(grads, mats, axes):
    results, first = [], 0
    for n, mat in enumerate(mats):
        rows, wide = mat.shape[1], mat.shape[2] // D
        total = lax.psum(1, axes) * rows
        deep = total // BLOCKS
        first = 0 if n % 2 == 0 else first
        piece = grads[n // 2][:, :, :, first : first + wide * deep].astype(WIDE)
        first += wide * deep
        piece = piece.reshape(LAYERS, NC, NX, NY, NZ, wide, deep, D)
        piece = piece.transpose(0, 4, 3, 2, 1, 6, 5, 7).reshape(LAYERS, total, wide * D)
        results.append(lax.psum_scatter(piece, axes, scatter_dimension=1, tiled=True))
    return results


def local(
    buf_states,
    buf_actions,
    buf_returns,
    window_starts,
    window_repeats,
    valid_steps,
    matrix_groups,
    log_temp,
    small_rows,
    head_bias,
    qkv_weight,
    out_weight,
    up_weight,
    down_weight,
    small_first,
    bias_first,
    qkv_first,
    out_first,
    up_first,
    down_first,
    small_second,
    bias_second,
    qkv_second,
    out_second,
    up_second,
    down_second,
):
    axes = ("dp", "fsdp")
    mats = (qkv_weight, out_weight, up_weight, down_weight)
    firsts = (qkv_first, out_first, up_first, down_first)
    seconds = (qkv_second, out_second, up_second, down_second)
    pass_inputs = (
        buf_states.T,
        buf_actions.T,
        buf_returns[None],
        window_starts,
        window_repeats,
        valid_steps,
        log_temp,
        small_rows,
        head_bias,
    )
    if FF // down_weight.shape[1] == BLOCKS and lax.psum(1, "fsdp") == NX * NC:
        made = train_pass(pass_inputs, mats, False)
        return adam_all(
            made["shard"],
            made["small_out"],
            made["squares"],
            matrix_groups,
            log_temp,
            (small_rows, small_first, small_second),
            (head_bias, bias_first, bias_second),
            mats,
            firsts,
            seconds,
        )
    packed = gather_packed(mats, axes, FF // down_weight.shape[1])
    made = train_pass(pass_inputs, packed, True)
    big = scatter_packed((made["grad_a"], made["grad_f"]), mats, axes)
    small = made["small_out"]
    small = lax.psum(small, axes)
    small_grad, totals = small[:NROWS], small[NROWS, :3]
    bias_grad = jnp.concatenate([small[NROWS + 1, :A], small[NROWS + 2, :A]])
    square = sum((jnp.sum(piece * piece) for piece in big))
    square = (
        lax.psum(square, axes) + jnp.sum(small_grad * small_grad) + jnp.sum(bias_grad * bias_grad)
    )
    grad_norm = jnp.sqrt(square)
    clip = jnp.minimum(1.0, CLIP / (grad_norm + 1e-06))
    rates = LEARN * jnp.exp2(-matrix_groups.astype(WIDE))
    results = [
        adam_parts(
            mats[kind], clip * big[kind], firsts[kind], seconds[kind], rates[:, kind][:, None, None]
        )
        for kind in range(4)
    ]
    small_new = adam_parts(small_rows, clip * small_grad, small_first, small_second, LEARN)
    bias_new = adam_parts(head_bias, clip * bias_grad, bias_first, bias_second, LEARN)
    next_temp = log_temp - TEMP_RATE * jnp.exp(log_temp) * (totals[1] / totals[2] + A)
    return (
        (totals, grad_norm[None], next_temp)
        + small_new
        + bias_new
        + tuple(r[0] for r in results)
        + tuple(r[0].astype(LOWER) for r in results)
        + tuple(r[1] for r in results)
        + tuple(r[2] for r in results)
    )


def solution(mesh):
    rows = P(("dp", "fsdp"), None)
    vector = P(("dp", "fsdp"))
    stack = P(None, ("dp", "fsdp"), None)
    same = P()
    in_specs = (
        (rows, rows, vector, vector, vector, rows)
        + (same,) * 4
        + (stack,) * 4
        + (same,) * 2
        + (stack,) * 4
        + (same,) * 2
        + (stack,) * 4
    )
    out_specs = (same,) * 9 + (stack,) * 16
    return jax.shard_map(local, mesh=mesh, in_specs=in_specs, out_specs=out_specs, check_vma=False)
```
